32 devices in a mesh: seq: 8 (over y, x, core), mp: 4 (over z).
Axes of the slice: x: 2, y: 2, z: 4, core: 2. Of those that a mesh axis runs over, the one named last changes fastest.
Arguments:
- tokens: bfloat16 [6, 3072, 1024], P(None, 'seq'), may hold values from -6 to 6
- patches: bfloat16 [6, 1536, 768], P(None, 'seq'), may hold values from -6 to 6
- counts: int32 [6], replicated, may hold values from 512 to 1536, as said below
- norm_gains: float32 [3, 1024], replicated, may hold values from 0.5 to 1.5
- norm_shifts: float32 [3, 1024], replicated, may hold values from -1.75 to 1.75
- cross_query: bfloat16 [1024, 1024], P(None, 'mp'), may hold values from -0.1875 to 0.1875
- cross_kv: bfloat16 [768, 2, 1024], P(None, None, 'mp'), may hold values from -0.21875 to 0.21875
- cross_out: bfloat16 [1024, 1024], P('mp'), may hold values from -3.5 to 3.5
- self_qkv: bfloat16 [1024, 3, 1024], P(None, None, 'mp'), may hold values from -0.1875 to 0.1875
- self_out: bfloat16 [1024, 1024], P('mp'), may hold values from -6 to 6
- mlp_up: bfloat16 [1024, 4096], P(None, 'mp'), may hold values from -0.1875 to 0.1875
- mlp_down: bfloat16 [4096, 1024], P('mp'), may hold values from -0.09375 to 0.09375
- decoder: bfloat16 [1024, 80, 4], P(None, 'mp'), may hold values from -0.1875 to 0.1875
- sample_weights: bfloat16 [6, 3, 8, 561, 256], P(None, None, 'seq'), may hold values from 0 to 1
- tokens_cot: bfloat16 [6, 3072, 1024], P(None, 'seq'), may hold values from -6 to 6
- sample_cot: bfloat16 [6, 3, 80, 8, 256], P(None, None, 'mp', 'seq'), may hold values from -6 to 6
Outputs:
- tokens_out: bfloat16 [6, 3072, 1024], P(None, ('seq', 'mp'))
- sampled: bfloat16 [6, 3, 80, 8, 256], P(None, None, 'mp', 'seq')
- grad_tokens: float32 [6, 3072, 1024], P(None, ('seq', 'mp'))
- grad_patches: float32 [6, 1536, 768], P(None, 'seq')
- grad_norm_gains: float32 [3, 1024], P(None, 'seq')
- grad_norm_shifts: float32 [2, 1024], P(None, 'seq')
- grad_mlp_shift: float32 [1024], P('seq')
- grad_cross_query: float32 [1024, 1024], P('seq', 'mp')
- grad_cross_kv: float32 [768, 2, 1024], P('seq', None, 'mp')
- grad_cross_out: float32 [1024, 1024], P('mp', 'seq')
- grad_self_qkv: float32 [1024, 3, 1024], P('seq', None, 'mp')
- grad_self_out: float32 [1024, 1024], P('mp', 'seq')
- grad_mlp_up: float32 [1024, 4096], P('seq', 'mp')
- grad_mlp_down: float32 [4096, 1024], P('mp', 'seq')
- grad_decoder: float32 [1024, 80, 4], P('seq', 'mp')
The draws below stay inside these ranges and needn't reach their ends.
Inputs may be any that keep to these rules, and one draw needn't show every extreme that they name: `counts`: exactly one object has 1536 foreground patch tokens; every object has 512 or more; slots at or past an object's count hold no patch token of it.
All inputs are finite; a program needn't handle non-finite values.
Results may differ from the reference program's by a relative error of at most 0.029.
Values may be sent and summed in bfloat16 or wider, within the bound.
No kernel may reach another device: no remote copies, remote signals or barrier semaphores. Data moves between devices by JAX's collectives and lax.ppermute only.
A program may use at most 704 MiB of HBM per device.

```python
import math
import jax
import jax.numpy as jnp
from jax import lax

D = 1024
HEADS = 16
FF = 4096
DIMG = 768
CH = 80
PLANE = 32
PMEAN = 1024
PMAX = 1536
SAMP = 256
OBJ = 6
OBJ_TOK = 3072
TILES = 8
TROWS = 16
TCOLS = 8
EXT = 561


def draw_counts(key, part):
    key = jax.random.fold_in(key, 23)
    place_key, first_key, second_key = jax.random.split(key, 3)
    full_place = jax.random.randint(place_key, (), 0, OBJ, dtype=jnp.int32)
    first_draw = jax.random.randint(first_key, (OBJ,), PMEAN // 2, PMAX + 1, dtype=jnp.int32)
    second_draw = jax.random.randint(second_key, (OBJ,), PMEAN // 2, PMAX + 1, dtype=jnp.int32)
    smaller = jnp.minimum(first_draw, second_draw)
    object_index = jnp.arange(OBJ, dtype=jnp.int32)
    return jnp.where(object_index == full_place, jnp.int32(PMAX), smaller).astype(jnp.int32)


def draw_sample_weights(key, part):
    key = jax.random.fold_in(key, 11)
    row_key, col_key = jax.random.split(key)
    draw_shape = (OBJ, 3, TILES, 1, SAMP)
    rows_at = jax.random.uniform(row_key, draw_shape, jnp.float32, 0.0, 2.0 * TROWS)
    cols_at = jax.random.uniform(col_key, draw_shape, jnp.float32, 0.0, 2.0 * TCOLS)
    cell_index = jnp.arange(EXT, dtype=jnp.int32)
    cell_row = (cell_index // (2 * TCOLS + 1)).astype(jnp.float32).reshape(1, 1, 1, EXT, 1)
    cell_col = (cell_index % (2 * TCOLS + 1)).astype(jnp.float32).reshape(1, 1, 1, EXT, 1)
    row_weight = jnp.maximum(1.0 - jnp.abs(rows_at - cell_row), 0.0)
    col_weight = jnp.maximum(1.0 - jnp.abs(cols_at - cell_col), 0.0)
    return (row_weight * col_weight).astype(jnp.bfloat16)


def steps_of(key, shape, shards, least, largest):
    def one(axis_at, blocks):
        draws = jax.random.uniform(jax.random.fold_in(jax.random.fold_in(key, 6), axis_at), (blocks,), jnp.float32, least / len(shards), largest / len(shards))
        return jnp.repeat(jnp.exp(draws), shape[axis_at] // blocks).reshape((-1,) + (1,) * (len(shape) - axis_at - 1))

    gain = one(*shards[0])
    for cut in shards[1:]:
        gain = gain * one(*cut)
    return gain


def gaussian(stream_key, shape, scale, most, cuts=(), held_as=jnp.bfloat16):
    drawn = jax.random.normal(stream_key, shape, jnp.float32) * scale
    if len(cuts) > 0:
        drawn = steps_of(stream_key, shape, cuts, -0.22, 0.18) * drawn
    return jnp.clip(drawn, min=-most, max=most).astype(held_as)


def setup_inputs(seed: int = 0) -> dict:
    keys = jax.random.split(jax.random.key(seed), 17)
    return {
        "tokens": gaussian(keys[0], (OBJ, OBJ_TOK, D), 1.0, 6.0, ((1, 8),)),
        "patches": gaussian(keys[1], (OBJ, PMAX, DIMG), 1.0, 6.0, ((1, 8),)),
        "counts": draw_counts(jax.random.fold_in(keys[16], 71), 0),
        "norm_gains": jnp.clip(1.0 + 0.1 * jax.random.normal(keys[3], (3, D), jnp.float32), 0.5, 1.5),
        "norm_shifts": gaussian(keys[4], (3, D), 0.3, 1.75, (), jnp.float32),
        "cross_query": gaussian(keys[5], (D, D), D ** -0.5, 0.1875, ((1, 4),)),
        "cross_kv": gaussian(keys[6], (DIMG, 2, D), DIMG ** -0.5, 0.21875, ((2, 4),)),
        "cross_out": gaussian(keys[7], (D, D), (max(1, 3 * D // PMEAN)) ** -0.5, 3.5, ((0, 4),)),
        "self_qkv": gaussian(keys[8], (D, 3, D), D ** -0.5, 0.1875, ((2, 4),)),
        "self_out": gaussian(keys[9], (D, D), (max(1, 3 * D // OBJ_TOK)) ** -0.5, 6.0, ((0, 4),)),
        "mlp_up": gaussian(keys[10], (D, FF), D ** -0.5, 0.1875, ((1, 4),)),
        "mlp_down": gaussian(keys[11], (FF, D), FF ** -0.5, 0.09375, ((0, 4),)),
        "decoder": gaussian(keys[12], (D, CH, 4), D ** -0.5, 0.1875, ((1, 4),)),
        "sample_weights": draw_sample_weights(jax.random.fold_in(keys[16], 71), 0),
        "tokens_cot": gaussian(keys[14], (OBJ, OBJ_TOK, D), 1.0, 6.0, ((1, 8),)),
        "sample_cot": gaussian(keys[15], (OBJ, 3, CH, TILES, SAMP), 1.0, 6.0, ((2, 4), (3, 8))),
    }


norm_eps = 1e-05
highest = lax.Precision.HIGHEST

@jax.custom_vjp
def low(v):
    return lax.optimization_barrier(v.astype(jnp.bfloat16)).astype(jnp.float32)

@jax.custom_vjp
def low_back(v):
    return v

def low_keep(v):
    return (low(v), None)

def low_pass(kept, grad):
    return (grad,)

def back_keep(v):
    return (v, None)

def back_low(kept, grad):
    return (low(grad),)
low.defvjp(low_keep, low_pass)
low_back.defvjp(back_keep, back_low)

def layer_norm(values, gain_row, shift_row):
    center = values - lax.optimization_barrier(jnp.mean(values, axis=-1, keepdims=True))
    spread = lax.optimization_barrier(jnp.mean(center * center, axis=-1, keepdims=True))
    return center * lax.rsqrt(spread + norm_eps) * gain_row + shift_row

def matmul(operand, matrix):
    return jnp.einsum('...d,de->...e', operand, matrix, precision=highest)

def split_heads(operand):
    return operand.reshape(operand.shape[:-1] + (HEADS, operand.shape[-1] // HEADS))

def attend_block(query_block, key_rows, value_rows, key_mask, factor):
    scores = low_back(factor * jnp.einsum('qhd,khd->hqk', query_block, key_rows, precision=highest))
    scores = jnp.where(key_mask[None, None, :], scores, -1e+30)
    weights = low(jax.nn.softmax(scores, axis=-1))
    return jnp.einsum('hqk,khd->qhd', weights, value_rows, precision=highest)

def attention(queries, key_rows, value_rows, key_mask):
    factor = 1.0 / math.sqrt(queries.shape[-1])
    block_rows = math.gcd(queries.shape[1], 512)

    def per_object(pieces):
        query_obj, key_obj, value_obj, mask_obj = pieces

        def one_block(query_block):
            return attend_block(query_block, key_obj, value_obj, mask_obj, factor)
        blocks = query_obj.reshape((query_obj.shape[0] // block_rows, block_rows) + query_obj.shape[1:])
        result = lax.map(jax.checkpoint(one_block), blocks)
        return result.reshape(query_obj.shape)
    return lax.map(per_object, (queries, key_rows, value_rows, key_mask))

def sample_planes(pixels, sample_in):
    objects = pixels.shape[0]
    grid_rows = TILES // 4
    cells = pixels.reshape(objects, 3, TROWS, TCOLS, grid_rows, 4, CH, 2, 2)
    planes = cells.transpose(0, 1, 6, 4, 2, 7, 5, 3, 8).reshape(objects, 3, CH, 2 * PLANE, 2 * PLANE)
    padded = jnp.pad(planes, ((0, 0), (0, 0), (0, 0), (0, 1), (0, 1)))
    row_index = ((jnp.arange(grid_rows) * 2 * TROWS)[:, None] + jnp.arange(2 * TROWS + 1)[None, :]).astype(jnp.int32)
    col_index = ((jnp.arange(4) * 2 * TCOLS)[:, None] + jnp.arange(2 * TCOLS + 1)[None, :]).astype(jnp.int32)
    windows = padded[:, :, :, row_index[:, None, :, None], col_index[None, :, None, :]]
    windows = windows.reshape(objects, 3, CH, TILES, EXT)
    return jnp.einsum('opcje,opjes->opcjs', windows, sample_in, precision=highest)

def forward(token_in, patch_in, weights, sample_in, key_mask):
    norm_gains, norm_shifts, cross_query, cross_kv, cross_out, self_qkv, self_out, mlp_up, mlp_down, decoder = weights
    normed = low(layer_norm(token_in, norm_gains[0], norm_shifts[0]))
    queries = low(low_back(matmul(normed, cross_query)))
    key_value = low(low_back(jnp.einsum('osi,ije->osje', patch_in, cross_kv, precision=highest)))
    attended = attention(split_heads(queries), split_heads(key_value[:, :, 0]), split_heads(key_value[:, :, 1]), key_mask)
    attended = low(low_back(attended.reshape(queries.shape)))
    after_cross = token_in + low_back(matmul(attended, cross_out))
    normed = low(layer_norm(after_cross, norm_gains[1], norm_shifts[1]))
    triple = low(low_back(jnp.einsum('otd,dje->otje', normed, self_qkv, precision=highest)))
    open_mask = jnp.zeros(after_cross.shape[:2], jnp.int32) == 0
    attended = attention(split_heads(triple[:, :, 0]), split_heads(triple[:, :, 1]), split_heads(triple[:, :, 2]), open_mask)
    attended = low(low_back(attended.reshape(after_cross.shape)))
    after_self = after_cross + low_back(matmul(attended, self_out))
    normed = low(layer_norm(after_self, norm_gains[2], norm_shifts[2]))
    hidden = low_back(matmul(normed, mlp_up))
    after_mlp = after_self + low_back(matmul(low(jax.nn.gelu(hidden)), mlp_down))
    pixels = low(low_back(jnp.einsum('otd,dcu->otcu', low(after_mlp), decoder, precision=highest)))
    return (after_mlp, sample_planes(pixels, sample_in))

def reference(tokens, patches, counts, norm_gains, norm_shifts, cross_query, cross_kv, cross_out, self_qkv, self_out, mlp_up, mlp_down, decoder, sample_weights, tokens_cot, sample_cot):
    params = tuple((weight.astype(jnp.float32) for weight in (norm_gains, norm_shifts, cross_query, cross_kv, cross_out, self_qkv, self_out, mlp_up, mlp_down, decoder)))

    def per_object(totals, pieces):
        token_obj, patch_obj, count_obj, sample_obj, token_grad, sample_grad = pieces
        key_mask = (jnp.arange(PMAX).astype(jnp.int32) < count_obj)[None, :]

        def object_loss(token_in, patch_in, *weights):
            return forward(token_in[None], patch_in[None], weights, sample_obj[None].astype(jnp.float32), key_mask)
        outputs, pullback = jax.vjp(object_loss, token_obj.astype(jnp.float32), patch_obj.astype(jnp.float32), *params)
        grad_list = pullback((token_grad[None].astype(jnp.float32), sample_grad[None].astype(jnp.float32)))
        totals = tuple((total_grad + grad_part for total_grad, grad_part in zip(totals, grad_list[2:])))
        return (totals, (outputs[0][0], outputs[1][0], grad_list[0], grad_list[1]))
    zero_grads = tuple((jnp.zeros(weight.shape, jnp.float32) for weight in params))
    totals, stacked = lax.scan(per_object, zero_grads, (tokens, patches, counts, sample_weights, tokens_cot, sample_cot))
    tokens_out = stacked[0].astype(jnp.bfloat16)
    sampled = stacked[1].astype(jnp.bfloat16)
    return (tokens_out, sampled, stacked[2], stacked[3], totals[0], totals[1][:2], totals[1][2], totals[2], totals[3], totals[4], totals[5], totals[6], totals[7], totals[8], totals[9])
```

```python
import functools
import math

import jax
import jax.numpy as jnp
from jax import lax
from jax.experimental import pallas as pl
from jax.experimental.pallas import tpu as pltpu
from jax.sharding import PartitionSpec as P


PLANE = 32
HD = 64
LANES = 128
norm_eps = 1e-05
f32 = jnp.float32
bf16 = jnp.bfloat16

NT = (((1,), (1,)), ((), ()))
NN = (((1,), (0,)), ((), ()))
TN = (((0,), (0,)), ((), ()))


def dot(a, b, dims):
    return lax.dot_general(a, b, dims, preferred_element_type=f32)


def mm(a, b):
    return jnp.dot(a, b, preferred_element_type=f32)


def split3(v):
    hi = v.astype(bf16).astype(f32)
    rest = v - hi
    mid = rest.astype(bf16).astype(f32)
    return hi, mid, rest - mid


def spread(base, cols):
    lane = lax.broadcasted_iota(jnp.int32, (base.shape[0], HD), 1)
    tail = jnp.zeros((base.shape[0], HD), f32)
    for at, col in cols.items():
        tail = jnp.where(lane == at, col, tail)
    return jnp.concatenate([base, tail], axis=1).astype(bf16)


def load_keys(n_ref, kv_specs, refs, ka, va, hpd, blocks):
    for ref_at, rows, k_at, v_at, base in kv_specs:
        src = refs[ref_at]

        def build(i, _):
            natural = base + (i ^ n_ref[1]) * rows
            dst = pl.ds(pl.multiple_of(natural, 16), rows)
            slot = natural + lax.broadcasted_iota(jnp.int32, (rows, 1), 0)
            mask = jnp.where(slot < n_ref[0], 0.0, -1e30).astype(f32)
            for h in range(hpd):
                k = src[i, k_at[0] : k_at[0] + rows, k_at[1] + h * HD : k_at[1] + (h + 1) * HD]
                v = src[i, v_at[0] : v_at[0] + rows, v_at[1] + h * HD : v_at[1] + (h + 1) * HD]
                ka[h, dst, :] = spread(k.astype(f32), {0: 1.0, 1: 1.0, 2: 1.0, 3: mask})
                va[h, dst, :] = spread(v.astype(f32), {0: 1.0, 1: 1.0, 2: 1.0})
            return 0

        lax.fori_loop(0, blocks, build, 0)


def fwd_kernel(n_ref, *refs, n_in, blocks, q_spec, kv_specs, hpd, bq, kc, fixed):
    ins, (o_ref, qa_ref, ka, va) = refs[:n_in], refs[n_in:]
    load_keys(n_ref, kv_specs, ins, ka, va, hpd, blocks)
    q_at, rows_q, q_off, q_lane = q_spec

    def build(i, _):
        dst = pl.ds(pl.multiple_of((i ^ n_ref[1]) * rows_q, 16), rows_q)
        for h in range(hpd):
            q = ins[q_at][i, q_off : q_off + rows_q, q_lane + h * HD : q_lane + (h + 1) * HD]
            qa_ref[h, dst, :] = spread(q.astype(f32) * (1.0 / math.sqrt(HD)), {3: 1.0})
        return 0

    lax.fori_loop(0, blocks, build, 0)
    total = ka.shape[1]

    def block(b, _):
        rows = pl.ds(pl.multiple_of(b * bq, bq), bq)

        def chunk(c, carry):
            cols = pl.ds(pl.multiple_of(c * kc, kc), kc)
            out = []
            for h in range(hpd):
                m, acc = carry[h]
                s = dot(qa_ref[h, rows, :], ka[h, cols, :], NT)
                top = jnp.maximum(m, jnp.max(s, axis=1, keepdims=True))
                p = jnp.exp(s - top).astype(bf16)
                out.append((top, acc * jnp.exp(m - top) + dot(p, va[h, cols, :], NN)))
            return tuple(out)

        carry = ((jnp.full((bq, 1), -1e30, f32), jnp.zeros((bq, LANES), f32)),) * hpd
        if fixed:
            for c in range(total // kc):
                carry = chunk(c, carry)
        else:
            carry = lax.fori_loop(0, (n_ref[0] + kc - 1) // kc, chunk, carry)
        outs = []
        for h in range(hpd):
            m, acc = carry[h]
            norm = acc[:, HD : HD + 1]
            outs.append(acc[:, :HD] / norm)
            hi, mid, lo = split3(-(m + jnp.log(norm)))
            qa_ref[h, rows, :] = spread(
                qa_ref[h, rows, :HD].astype(f32), {0: hi, 1: mid, 2: lo, 3: 1.0}
            )
        o_ref[rows, :] = jnp.concatenate(outs, axis=1).astype(bf16)
        return 0

    lax.fori_loop(0, qa_ref.shape[1] // bq, block, 0)


def bwd_kernel(n_ref, *refs, n_in, blocks, do_spec, kv_specs, hpd, bq, kc, fixed):
    ins, (dq_ref, dkv_ref, ka, va, da, dk, dv) = refs[:n_in], refs[n_in:]
    qa_ref, do_ref, o_ref = ins[:3]
    load_keys(n_ref, kv_specs, ins, ka, va, hpd, blocks)
    rows_q, do_off = do_spec

    def build(i, _):
        rows = pl.ds(pl.multiple_of(i * rows_q, 16), rows_q)
        for h in range(hpd):
            d = do_ref[i, do_off : do_off + rows_q, h * HD : (h + 1) * HD].astype(f32)
            o = o_ref[rows, h * HD : (h + 1) * HD].astype(f32)
            hi, mid, lo = split3(-jnp.sum(d * o, axis=1, keepdims=True))
            da[h, rows, :] = spread(d, {0: hi, 1: mid, 2: lo})
        return 0

    lax.fori_loop(0, blocks, build, 0)
    dk[...] = jnp.zeros_like(dk)
    dv[...] = jnp.zeros_like(dv)
    total = ka.shape[1]
    steps = total // kc if fixed else (n_ref[0] + kc - 1) // kc

    def block(b, _):
        rows = pl.ds(pl.multiple_of(b * bq, bq), bq)

        def chunk(c, dqs):
            cols = pl.ds(pl.multiple_of(c * kc, kc), kc)
            out = []
            for h in range(hpd):
                k, q, d = ka[h, cols, :], qa_ref[h, rows, :], da[h, rows, :]
                p = jnp.exp(dot(k, q, NT))
                dp = dot(va[h, cols, :], d, NT)
                dv[h, cols, :] += dot(p.astype(bf16), d, NN)
                g = (p * dp).astype(bf16)
                dk[h, cols, :] += dot(g, q, NN)
                out.append(dqs[h] + dot(k, g, TN))
            return tuple(out)

        dqs = lax.fori_loop(0, steps, chunk, (jnp.zeros((LANES, bq), f32),) * hpd)
        dq = jnp.concatenate([v[:HD, :] for v in dqs], axis=0).T
        dq_ref[rows, :] = (dq * (1.0 / math.sqrt(HD))).astype(bf16)
        return 0

    lax.fori_loop(0, qa_ref.shape[1] // bq, block, 0)
    step = total // blocks

    def finish(i, _):
        rows = pl.ds(pl.multiple_of(i * step, 16), step)
        parts = [dk[h, rows, :HD] for h in range(hpd)] + [dv[h, rows, :HD] for h in range(hpd)]
        dkv_ref[rows, :] = jnp.concatenate(parts, axis=1).astype(bf16)
        return 0

    lax.fori_loop(0, blocks, finish, 0)


VM = pl.BlockSpec(memory_space=pltpu.VMEM)
SM = pl.BlockSpec(memory_space=pltpu.SMEM)


def fit(rows, most):
    return math.gcd(rows, most)


def attend(limits, ins, blocks, q_spec, kv_specs, total, hpd, fixed):
    queries = blocks * q_spec[1]
    kc = fit(total, 1024 if fixed else 512)
    body = functools.partial(
        fwd_kernel,
        n_in=len(ins),
        blocks=blocks,
        q_spec=q_spec,
        kv_specs=kv_specs,
        hpd=hpd,
        bq=fit(queries, 512),
        kc=kc,
        fixed=fixed,
    )
    work = hpd * queries * total
    return pl.pallas_call(
        body,
        out_shape=(
            jax.ShapeDtypeStruct((queries, hpd * HD), bf16),
            jax.ShapeDtypeStruct((hpd, queries, LANES), bf16),
        ),
        in_specs=[SM] + [VM] * len(ins),
        out_specs=(VM, VM),
        scratch_shapes=[pltpu.VMEM((hpd, total, LANES), bf16)] * 2,
        compiler_params=pltpu.CompilerParams(vmem_limit_bytes=44 * 2**20),
        cost_estimate=pl.CostEstimate(
            flops=1024 * work, bytes_accessed=16 * queries * hpd * HD, transcendentals=work
        ),
    )(limits, *ins)


def attend_back(limits, ins, blocks, do_spec, kv_specs, total, hpd, fixed):
    queries = blocks * do_spec[0]
    body = functools.partial(
        bwd_kernel,
        n_in=len(ins),
        blocks=blocks,
        do_spec=do_spec,
        kv_specs=kv_specs,
        hpd=hpd,
        bq=fit(queries, 512),
        kc=fit(total, 512),
        fixed=fixed,
    )
    work = hpd * queries * total
    return pl.pallas_call(
        body,
        out_shape=(
            jax.ShapeDtypeStruct((queries, hpd * HD), bf16),
            jax.ShapeDtypeStruct((total, 2 * hpd * HD), bf16),
        ),
        in_specs=[SM] + [VM] * len(ins),
        out_specs=(VM, VM),
        scratch_shapes=[pltpu.VMEM((hpd, total, LANES), bf16)] * 2
        + [pltpu.VMEM((hpd, queries, LANES), bf16)]
        + [pltpu.VMEM((hpd, total, LANES), f32)] * 2,
        compiler_params=pltpu.CompilerParams(vmem_limit_bytes=52 * 2**20),
        cost_estimate=pl.CostEstimate(
            flops=2560 * work, bytes_accessed=24 * queries * hpd * HD, transcendentals=work
        ),
    )(limits, *ins)


def norm_parts(values):
    center = values - jnp.mean(values, axis=-1, keepdims=True)
    scale = lax.rsqrt(jnp.mean(center * center, axis=-1, keepdims=True) + norm_eps)
    return center * scale, scale


def layer_norm(values, gain_row, shift_row):
    return (norm_parts(values)[0] * gain_row + shift_row).astype(bf16)


def norm_back(values, gain_row, grad_out):
    unit, scale = norm_parts(values)
    lifted = grad_out * gain_row
    grad_in = scale * (
        lifted
        - jnp.mean(lifted, axis=-1, keepdims=True)
        - unit * jnp.mean(lifted * unit, axis=-1, keepdims=True)
    )
    return grad_in, jnp.sum(grad_out * unit, axis=0), jnp.sum(grad_out, axis=0)


def swap_seq(value):
    return lax.all_to_all(value, "seq", split_axis=0, concat_axis=0, tiled=True)


def swap_all(value):
    return lax.all_to_all(value, ("seq", "mp"), split_axis=0, concat_axis=0, tiled=True)


def swap_pair(value):
    count = lax.axis_size("mp")
    return lax.ppermute(value, "mp", [(i, i ^ 1) for i in range(count)])


def gather_rows(piece):
    return lax.all_gather(piece, ("mp", "seq"), axis=0, tiled=True)


def reduce_rows(value):
    return lax.psum_scatter(value.astype(bf16), "seq", scatter_dimension=0, tiled=True)


def reduce_cols(value):
    return lax.psum_scatter(value, "mp", scatter_dimension=1, tiled=True).astype(f32)


def from_behind(value, axis, steps):
    count = lax.axis_size(axis)
    initial, last = (max(0, -steps), min(count, count - steps))
    return lax.ppermute(value, axis, [(source, source + steps) for source in range(initial, last)])


def to_owner(value, rank, seq_rows):
    ranks = lax.axis_size("mp")
    pairs = ranks // 2
    pair, half = rank // 2, rank % 2
    own = seq_rows // ranks
    whole = lax.all_to_all(
        value[:seq_rows].reshape(ranks, own, -1), "mp", split_axis=0, concat_axis=0, tiled=True
    )
    blocks = value[seq_rows:].reshape(pairs, own, -1)
    arrived = []
    for step in range(pairs):
        moves = [(2 * p + h, pairs * h + (p ^ step)) for p in range(pairs) for h in range(2)]
        block = lax.dynamic_index_in_dim(blocks, pair ^ step, 0, keepdims=False)
        arrived.append(lax.ppermute(block, "mp", moves))
    arrived = jnp.stack(arrived)
    place = rank % pairs
    rows = []
    for p in range(pairs):
        rows += [
            whole[2 * p],
            lax.dynamic_index_in_dim(arrived, place ^ p, 0, keepdims=False),
            whole[2 * p + 1],
        ]
    return jnp.stack(rows)


def to_planes(tile_pixels, tile_rows, tile_cols):
    objects, channels = (tile_pixels.shape[0], tile_pixels.shape[2])
    cells = tile_pixels.reshape(objects, 3, tile_rows, tile_cols, channels, 2, 2)
    cells = cells.transpose(0, 1, 4, 2, 5, 3, 6)
    return cells.reshape(objects, 3, channels, 2 * tile_rows, 2 * tile_cols)


def from_planes(planes, tile_rows, tile_cols):
    objects, channels = (planes.shape[0], planes.shape[2])
    cells = planes.reshape(objects, 3, channels, tile_rows, 2, tile_cols, 2)
    cells = cells.transpose(0, 1, 3, 5, 2, 4, 6)
    return cells.reshape(objects, 3 * tile_rows * tile_cols, channels * 4)


def per_device(
    tokens,
    patches,
    counts,
    norm_gains,
    norm_shifts,
    cross_query,
    cross_kv,
    cross_out,
    self_qkv,
    self_out,
    mlp_up,
    mlp_down,
    decoder,
    sample_weights,
    tokens_cot,
    sample_cot,
):
    objects, R, D = tokens.shape
    S, M = lax.axis_size("seq"), lax.axis_size("mp")
    s, m = lax.axis_index("seq"), lax.axis_index("mp")
    pairs = M // 2
    if objects != 3 * pairs or S != 2 * M or D != 1024:
        raise ValueError("unexpected sizes")
    pair, half = m // 2, m % 2
    at_a, at_b = 3 * pair + 2 * half, 3 * pair + 1
    RB = R // 2
    RS = R + RB
    W = D // S
    hpd = W // HD
    slots, width = patches.shape[1], patches.shape[2]
    slot_total = slots * S
    row_total = R * S

    def pick(arr, a, b, h):
        first = lax.dynamic_index_in_dim(arr, a, 0, keepdims=False)
        second = lax.dynamic_slice_in_dim(
            lax.dynamic_index_in_dim(arr, b, 0, keepdims=False), h * RB, RB, 0
        )
        return jnp.concatenate([first, second], axis=0)

    def mine(arr, axis):
        share = arr.shape[axis] // S
        return lax.dynamic_slice_in_dim(arr, s * share, share, axis)

    w_cross_out = gather_rows(mine(cross_out, 0))
    qkv_piece = mine(self_qkv, 2).transpose(1, 2, 0)
    w_qkv = gather_rows(qkv_piece.reshape(-1, D)).reshape(S, M, 3, D // (M * S), D)
    w_qkv = w_qkv.transpose(0, 2, 1, 3, 4).reshape(3 * D, D)
    w_self_out = gather_rows(mine(self_out, 0))
    w_up = gather_rows(mine(mlp_up, 1).T)
    w_down = gather_rows(mine(mlp_down, 0))
    channels = decoder.shape[1]
    cu = 4 * channels
    dec = lax.all_gather(mine(decoder.reshape(D, cu), 0), ("seq", "mp"), axis=0, tiled=False)
    w_dec = dec.reshape(S, M, D // S, cu).transpose(0, 2, 1, 3).reshape(D, M * cu)
    w_query = gather_rows(mine(cross_query, 1).T)
    kv_piece = mine(cross_kv, 2).transpose(1, 2, 0)
    w_kv = gather_rows(kv_piece.reshape(-1, width)).reshape(S, M, 2, D // (M * S), width)
    w_kv = w_kv.transpose(0, 2, 1, 3, 4).reshape(2 * D, width)

    grid_cols = 4
    tile_rows, tile_cols = PLANE * grid_cols // S, PLANE // grid_cols
    ext_rows, ext_cols = 2 * tile_rows + 1, 2 * tile_cols + 1
    weights_in = sample_weights[:, :, 0]
    grad_window = jnp.einsum(
        "opcs,opes->opce", sample_cot[:, :, :, 0], weights_in, preferred_element_type=f32
    ).reshape(objects, 3, channels, ext_rows, ext_cols)
    below_back = from_behind(grad_window[..., -1, :], "seq", grid_cols)
    grad_wide = jnp.concatenate(
        [grad_window[..., :1, :] + below_back[..., None, :], grad_window[..., 1:-1, :]], axis=-2
    )
    right_back = from_behind(grad_wide[..., -1], "seq", 1)
    right_back = jnp.where(s % grid_cols == 0, jnp.zeros_like(right_back), right_back)
    grad_planes = jnp.concatenate(
        [grad_wide[..., :1] + right_back[..., None], grad_wide[..., 1:-1]], axis=-1
    )
    KA, KB = R // S, RB // S
    grad_pix = from_planes(grad_planes.astype(bf16), tile_rows, tile_cols)
    grad_pix = grad_pix.reshape(pairs, 3, S, KA, cu)
    gp_a = jnp.stack([grad_pix[:, 0], grad_pix[:, 2]], axis=1).transpose(2, 0, 1, 3, 4)
    gp_b = grad_pix[:, 1].reshape(pairs, S, 2, KB, cu).transpose(1, 0, 2, 3, 4)
    sent = jnp.concatenate([gp_a, gp_b], axis=3).reshape(S * M, KA + KB, cu)
    back = swap_all(sent).reshape(S, M, KA + KB, cu).transpose(2, 0, 1, 3)
    d_pix = back.reshape(RS, M * cu)

    n1_all = layer_norm(tokens.astype(f32), norm_gains[0], norm_shifts[0])
    q1 = jnp.einsum("ord,de->ore", n1_all, cross_query, preferred_element_type=f32).astype(bf16)
    kv1 = jnp.einsum("osi,ije->osje", patches, cross_kv, preferred_element_type=f32).astype(bf16)
    kv1 = kv1.reshape(objects, slots, 2, -1)
    arrived = []
    for step in range(S):
        to = s ^ step
        lane, rank = to % 2, to // 2
        a, b, h = 3 * (rank // 2) + 2 * (rank % 2), 3 * (rank // 2) + 1, rank % 2
        part = lax.dynamic_slice_in_dim(pick(q1, a, b, h), lane * W, W, 1)
        kv = []
        for o in (a, b):
            one = lax.dynamic_index_in_dim(kv1, o, 0, keepdims=False)
            one = lax.dynamic_slice_in_dim(one, lane * W, W, 2)
            kv += [one[:, 0], one[:, 1]]
        moves = []
        for i in range(S):
            for j in range(M):
                t = i ^ step
                moves.append((i * M + j, (2 * j + t % 2) * M + t // 2))
        arrived.append(lax.ppermute(jnp.concatenate([part] + kv, axis=0), ("seq", "mp"), moves))
    heads_one = jnp.stack(arrived)
    order = 2 * m + s % 2
    n_a = lax.dynamic_index_in_dim(counts, at_a, 0, keepdims=False)
    n_b = lax.dynamic_index_in_dim(counts, at_b, 0, keepdims=False)
    lim_a, lim_b = jnp.stack([n_a, order]), jnp.stack([n_b, order])
    q_a1, q_b1 = (0, R, 0, 0), (0, RB, R, 0)
    kv_a1 = (RS, 0), (RS + slots, 0)
    kv_b1 = (RS + 2 * slots, 0), (RS + 3 * slots, 0)
    o_a1, res_a1 = attend(
        lim_a, [heads_one], S, q_a1, [(0, slots) + kv_a1 + (0,)], slot_total, hpd, False
    )
    o_b1, res_b1 = attend(
        lim_b, [heads_one], S, q_b1, [(0, slots) + kv_b1 + (0,)], slot_total, hpd, False
    )

    def join(a, b):
        return jnp.concatenate([a.reshape(S, R, -1), b.reshape(S, RB, -1)], axis=1)

    def to_rows(value):
        return swap_seq(value).transpose(1, 0, 2).reshape(value.shape[1], -1)

    def to_heads(value):
        return swap_seq(value.reshape(value.shape[0], S, -1).transpose(1, 0, 2))

    x0 = pick(tokens, at_a, at_b, half).astype(f32)
    a1 = to_rows(join(o_a1, o_b1))
    x1 = x0 + mm(a1, w_cross_out)
    n2 = layer_norm(x1, norm_gains[1], norm_shifts[1])

    t2 = dot(n2, w_qkv, NT).astype(bf16)
    heads_two = to_heads(t2)
    pair_kv = swap_pair(heads_two[:, R:, W:])
    open_a = jnp.array([row_total, 0], jnp.int32)
    o_a2, res_a2 = attend(
        open_a, [heads_two], S, (0, R, 0, 0), [(0, R, (0, W), (0, 2 * W), 0)], row_total, hpd, True
    )
    kv_b2 = [(0, RB, (R, W), (R, 2 * W), 0), (1, RB, (0, 0), (0, W), row_total // 2)]
    o_b2, res_b2 = attend(
        open_a, [heads_two, pair_kv], S, (0, RB, R, 0), kv_b2, row_total, hpd, True
    )
    a2 = to_rows(join(o_a2, o_b2))
    x2 = x1 + mm(a2, w_self_out)
    n3 = layer_norm(x2, norm_gains[2], norm_shifts[2])

    u = dot(n3, w_up, NT)
    slope = math.sqrt(2.0 / math.pi)
    bend = jnp.tanh(slope * (u + 0.044715 * u * u * u))
    g = (0.5 * u * (1.0 + bend)).astype(bf16)
    rise = 0.5 * (1.0 + bend) + 0.5 * u * (1.0 - bend * bend) * slope * (1.0 + 0.134145 * u * u)
    rise = rise.astype(bf16)
    x3 = x2 + mm(g, w_down)
    x3b = x3.astype(bf16)
    tokens_out = to_owner(x3b, m, R)

    pix = mm(x3b, w_dec).astype(bf16).reshape(KA + KB, S, M, cu).transpose(1, 2, 0, 3)
    got = swap_all(pix.reshape(S * M, KA + KB, cu)).reshape(S, pairs, 2, KA + KB, cu)
    px_a = got[:, :, :, :KA].transpose(1, 2, 0, 3, 4).reshape(pairs, 2, S * KA, cu)
    px_b = got[:, :, :, KA:].transpose(1, 0, 2, 3, 4).reshape(pairs, S * KA, cu)
    tile = jnp.stack([px_a[:, 0], px_b, px_a[:, 1]], axis=1)
    planes = to_planes(tile.reshape(objects, S * KA, channels, 4), tile_rows, tile_cols)
    from_right = from_behind(planes[..., 0], "seq", -1)
    from_right = jnp.where(s % grid_cols == grid_cols - 1, jnp.zeros_like(from_right), from_right)
    widened = jnp.concatenate([planes, from_right[..., None]], axis=-1)
    from_below = from_behind(widened[..., 0, :], "seq", -grid_cols)
    window = jnp.concatenate([widened, from_below[..., None, :]], axis=-2)
    sampled = jnp.einsum(
        "opce,opes->opcs",
        window.reshape(objects, 3, channels, -1),
        weights_in,
        preferred_element_type=f32,
    ).astype(bf16)[:, :, :, None, :]

    d3 = pick(tokens_cot, at_a, at_b, half).astype(f32) + dot(d_pix, w_dec, NT)
    e3 = d3.astype(bf16)
    du = (dot(e3, w_down, NT) * rise.astype(f32)).astype(bf16)
    grad_decoder = reduce_rows(dot(x3b, d_pix, TN))
    grad_mlp_down = reduce_rows(dot(e3, g, TN))
    grad_mlp_up = reduce_rows(dot(n3, du, TN))
    grad_in, gain_three, shift_three = norm_back(x2, norm_gains[2], mm(du, w_up))
    d2 = d3 + grad_in
    e2 = d2.astype(bf16)

    da2 = to_heads(dot(e2, w_self_out, NT).astype(bf16))
    grad_self_out = reduce_rows(dot(e2, a2, TN))
    dq_a2, dkv_a2 = attend_back(
        open_a,
        [res_a2, da2, o_a2, heads_two],
        S,
        (R, 0),
        [(3, R, (0, W), (0, 2 * W), 0)],
        row_total,
        hpd,
        True,
    )
    kv_b2 = [(3, RB, (R, W), (R, 2 * W), 0), (4, RB, (0, 0), (0, W), row_total // 2)]
    dq_b2, dkv_b2 = attend_back(
        open_a,
        [res_b2, da2, o_b2, heads_two, pair_kv],
        S,
        (RB, R),
        kv_b2,
        row_total,
        hpd,
        True,
    )
    kept, given = dkv_b2[: row_total // 2], dkv_b2[row_total // 2 :]
    dkv_b2 = (kept.astype(f32) + swap_pair(given).astype(f32)).astype(bf16)
    dt2 = to_rows(
        join(
            jnp.concatenate([dq_a2, dkv_a2], axis=1),
            jnp.concatenate([dq_b2, dkv_b2], axis=1),
        )
    )
    grad_self_qkv = reduce_rows(dot(n2, dt2, TN))
    grad_in, gain_two, shift_two = norm_back(x1, norm_gains[1], mm(dt2, w_qkv))
    d1 = d2 + grad_in
    e1 = d1.astype(bf16)

    da1 = to_heads(dot(e1, w_cross_out, NT).astype(bf16))
    grad_cross_out = reduce_rows(dot(e1, a1, TN))
    dq_a1, dkv_a1 = attend_back(
        lim_a,
        [res_a1, da1, o_a1, heads_one],
        S,
        (R, 0),
        [(3, slots) + kv_a1 + (0,)],
        slot_total,
        hpd,
        False,
    )
    dq_b1, dkv_b1 = attend_back(
        lim_b,
        [res_b1, da1, o_b1, heads_one],
        S,
        (RB, R),
        [(3, slots) + kv_b1 + (0,)],
        slot_total,
        hpd,
        False,
    )
    dkv1 = to_rows(
        jnp.concatenate([dkv_a1.reshape(S, slots, -1), dkv_b1.reshape(S, slots, -1)], axis=1)
    )
    both = [lax.dynamic_index_in_dim(patches, o, 0, keepdims=False) for o in (at_a, at_b)]
    grad_cross_kv = reduce_rows(dot(jnp.concatenate(both, axis=0), dkv1, TN))
    patch_part = mm(dkv1, w_kv).astype(bf16)
    patch_all = lax.all_gather(patch_part, "mp", axis=0).astype(f32)
    patch_all = patch_all.reshape(pairs, 2, 2, slots, width)
    patch_grad = jnp.stack(
        [patch_all[:, 0, 0], patch_all[:, 0, 1] + patch_all[:, 1, 1], patch_all[:, 1, 0]], axis=1
    ).reshape(objects, slots, width)

    dq1 = to_rows(join(dq_a1, dq_b1))
    n1 = layer_norm(x0, norm_gains[0], norm_shifts[0])
    grad_cross_query = reduce_rows(dot(n1, dq1, TN))
    grad_in, gain_one, shift_one = norm_back(x0, norm_gains[0], mm(dq1, w_query))
    grad_tokens = to_owner((d1 + grad_in).astype(bf16), m, R).astype(f32)

    rows = jnp.stack([gain_one, gain_two, gain_three, shift_one, shift_two, shift_three])
    rows = jnp.sum(swap_seq(rows.reshape(6, S, D // S).transpose(1, 0, 2)), axis=0)
    rows = lax.all_to_all(
        jnp.broadcast_to(rows, (M,) + rows.shape), "mp", split_axis=0, concat_axis=0, tiled=True
    )
    rows = jnp.sum(rows, axis=0)

    grad_self_qkv = grad_self_qkv.reshape(D // S, M, 2, 3, W)
    grad_self_qkv = reduce_cols(grad_self_qkv.reshape(D // S, -1)).reshape(D // S, 2, 3, W)
    grad_cross_kv = reduce_cols(grad_cross_kv).reshape(width // S, 2, 2, W)
    return (
        tokens_out,
        sampled,
        grad_tokens,
        patch_grad,
        rows[:3],
        rows[3:5],
        rows[5],
        reduce_cols(grad_cross_query),
        grad_cross_kv.transpose(0, 2, 1, 3).reshape(width // S, 2, -1),
        reduce_cols(grad_cross_out).T,
        grad_self_qkv.transpose(0, 2, 1, 3).reshape(D // S, 3, -1),
        reduce_cols(grad_self_out).T,
        reduce_cols(grad_mlp_up),
        reduce_cols(grad_mlp_down).T,
        reduce_cols(grad_decoder).reshape(D // S, channels, 4),
    )


def solution(mesh):
    return jax.shard_map(
        per_device,
        mesh=mesh,
        in_specs=(
            P(None, "seq", None),
            P(None, "seq", None),
            P(),
            P(),
            P(),
            P(None, "mp"),
            P(None, None, "mp"),
            P("mp", None),
            P(None, None, "mp"),
            P("mp", None),
            P(None, "mp"),
            P("mp", None),
            P(None, "mp", None),
            P(None, None, "seq", None, None),
            P(None, "seq", None),
            P(None, None, "mp", "seq", None),
        ),
        out_specs=(
            P(None, ("seq", "mp"), None),
            P(None, None, "mp", "seq", None),
            P(None, ("seq", "mp"), None),
            P(None, "seq", None),
            P(None, "seq"),
            P(None, "seq"),
            P("seq"),
            P("seq", "mp"),
            P("seq", None, "mp"),
            P("mp", "seq"),
            P("seq", None, "mp"),
            P("mp", "seq"),
            P("seq", "mp"),
            P("mp", "seq"),
            P("seq", "mp", None),
        ),
        check_vma=False,
    )
```

```python
import functools
import math

import jax
import jax.numpy as jnp
from jax import lax
from jax.experimental import pallas as pl
from jax.experimental.pallas import tpu as pltpu
from jax.sharding import PartitionSpec as P


PLANE = 32
HD = 64
LANES = 128
norm_eps = 1e-05
f32 = jnp.float32
bf16 = jnp.bfloat16

NT = (((1,), (1,)), ((), ()))
NN = (((1,), (0,)), ((), ()))
TN = (((0,), (0,)), ((), ()))


def dot(a, b, dims):
    return lax.dot_general(a, b, dims, preferred_element_type=f32)


def mm(a, b):
    return jnp.dot(a, b, preferred_element_type=f32)


def split3(v):
    hi = v.astype(bf16).astype(f32)
    rest = v - hi
    mid = rest.astype(bf16).astype(f32)
    return hi, mid, rest - mid


def spread(base, cols):
    lane = lax.broadcasted_iota(jnp.int32, (base.shape[0], HD), 1)
    tail = jnp.zeros((base.shape[0], HD), f32)
    for at, col in cols.items():
        tail = jnp.where(lane == at, col, tail)
    return jnp.concatenate([base, tail], axis=1).astype(bf16)


def load_keys(n_ref, kv_specs, refs, ka, va, hpd, blocks):
    for ref_at, rows, k_at, v_at, base in kv_specs:
        src = refs[ref_at]

        def build(i, _):
            natural = base + (i ^ n_ref[1]) * rows
            dst = pl.ds(pl.multiple_of(natural, 16), rows)
            slot = natural + lax.broadcasted_iota(jnp.int32, (rows, 1), 0)
            mask = jnp.where(slot < n_ref[0], 0.0, -1e30).astype(f32)
            for h in range(hpd):
                k = src[i, k_at[0] : k_at[0] + rows, k_at[1] + h * HD : k_at[1] + (h + 1) * HD]
                v = src[i, v_at[0] : v_at[0] + rows, v_at[1] + h * HD : v_at[1] + (h + 1) * HD]
                ka[h, dst, :] = spread(k.astype(f32), {0: 1.0, 1: 1.0, 2: 1.0, 3: mask})
                va[h, dst, :] = spread(v.astype(f32), {0: 1.0, 1: 1.0, 2: 1.0})
            return 0

        lax.fori_loop(0, blocks, build, 0)


def fwd_kernel(n_ref, *refs, n_in, blocks, q_spec, kv_specs, hpd, bq, kc, fixed):
    ins, (o_ref, qa_ref, ka, va) = refs[:n_in], refs[n_in:]
    load_keys(n_ref, kv_specs, ins, ka, va, hpd, blocks)
    q_at, rows_q, q_off, q_lane = q_spec

    def build(i, _):
        dst = pl.ds(pl.multiple_of((i ^ n_ref[1]) * rows_q, 16), rows_q)
        for h in range(hpd):
            q = ins[q_at][i, q_off : q_off + rows_q, q_lane + h * HD : q_lane + (h + 1) * HD]
            qa_ref[h, dst, :] = spread(q.astype(f32) * (1.0 / math.sqrt(HD)), {3: 1.0})
        return 0

    lax.fori_loop(0, blocks, build, 0)
    total = ka.shape[1]

    def block(b, _):
        rows = pl.ds(pl.multiple_of(b * bq, bq), bq)

        def chunk(c, carry):
            cols = pl.ds(pl.multiple_of(c * kc, kc), kc)
            out = []
            for h in range(hpd):
                m, acc = carry[h]
                s = dot(qa_ref[h, rows, :], ka[h, cols, :], NT)
                top = jnp.maximum(m, jnp.max(s, axis=1, keepdims=True))
                p = jnp.exp(s - top).astype(bf16)
                out.append((top, acc * jnp.exp(m - top) + dot(p, va[h, cols, :], NN)))
            return tuple(out)

        carry = ((jnp.full((bq, 1), -1e30, f32), jnp.zeros((bq, LANES), f32)),) * hpd
        if fixed:
            for c in range(total // kc):
                carry = chunk(c, carry)
        else:
            carry = lax.fori_loop(0, (n_ref[0] + kc - 1) // kc, chunk, carry)
        outs = []
        for h in range(hpd):
            m, acc = carry[h]
            norm = acc[:, HD : HD + 1]
            outs.append(acc[:, :HD] / norm)
            hi, mid, lo = split3(-(m + jnp.log(norm)))
            qa_ref[h, rows, :] = spread(
                qa_ref[h, rows, :HD].astype(f32), {0: hi, 1: mid, 2: lo, 3: 1.0}
            )
        o_ref[rows, :] = jnp.concatenate(outs, axis=1).astype(bf16)
        return 0

    lax.fori_loop(0, qa_ref.shape[1] // bq, block, 0)


def bwd_kernel(n_ref, *refs, n_in, blocks, do_spec, kv_specs, hpd, bq, kc, fixed):
    ins, (dq_ref, dkv_ref, ka, va, da, dk, dv) = refs[:n_in], refs[n_in:]
    qa_ref, do_ref, o_ref = ins[:3]
    load_keys(n_ref, kv_specs, ins, ka, va, hpd, blocks)
    rows_q, do_off = do_spec

    def build(i, _):
        rows = pl.ds(pl.multiple_of(i * rows_q, 16), rows_q)
        for h in range(hpd):
            d = do_ref[i, do_off : do_off + rows_q, h * HD : (h + 1) * HD].astype(f32)
            o = o_ref[rows, h * HD : (h + 1) * HD].astype(f32)
            hi, mid, lo = split3(-jnp.sum(d * o, axis=1, keepdims=True))
            da[h, rows, :] = spread(d, {0: hi, 1: mid, 2: lo})
        return 0

    lax.fori_loop(0, blocks, build, 0)
    dk[...] = jnp.zeros_like(dk)
    dv[...] = jnp.zeros_like(dv)
    total = ka.shape[1]
    steps = total // kc if fixed else (n_ref[0] + kc - 1) // kc

    def block(b, _):
        rows = pl.ds(pl.multiple_of(b * bq, bq), bq)

        def chunk(c, dqs):
            cols = pl.ds(pl.multiple_of(c * kc, kc), kc)
            out = []
            for h in range(hpd):
                k, q, d = ka[h, cols, :], qa_ref[h, rows, :], da[h, rows, :]
                p = jnp.exp(dot(k, q, NT))
                dp = dot(va[h, cols, :], d, NT)
                dv[h, cols, :] += dot(p.astype(bf16), d, NN)
                g = (p * dp).astype(bf16)
                dk[h, cols, :] += dot(g, q, NN)
                out.append(dqs[h] + dot(k, g, TN))
            return tuple(out)

        dqs = lax.fori_loop(0, steps, chunk, (jnp.zeros((LANES, bq), f32),) * hpd)
        dq = jnp.concatenate([v[:HD, :] for v in dqs], axis=0).T
        dq_ref[rows, :] = (dq * (1.0 / math.sqrt(HD))).astype(bf16)
        return 0

    lax.fori_loop(0, qa_ref.shape[1] // bq, block, 0)
    step = total // blocks

    def finish(i, _):
        rows = pl.ds(pl.multiple_of(i * step, 16), step)
        parts = [dk[h, rows, :HD] for h in range(hpd)] + [dv[h, rows, :HD] for h in range(hpd)]
        dkv_ref[rows, :] = jnp.concatenate(parts, axis=1).astype(bf16)
        return 0

    lax.fori_loop(0, blocks, finish, 0)


VM = pl.BlockSpec(memory_space=pltpu.VMEM)
SM = pl.BlockSpec(memory_space=pltpu.SMEM)


def fit(rows, most):
    return math.gcd(rows, most)


def attend(limits, ins, blocks, q_spec, kv_specs, total, hpd, fixed):
    queries = blocks * q_spec[1]
    kc = fit(total, 1024 if fixed else 512)
    body = functools.partial(
        fwd_kernel,
        n_in=len(ins),
        blocks=blocks,
        q_spec=q_spec,
        kv_specs=kv_specs,
        hpd=hpd,
        bq=fit(queries, 512),
        kc=kc,
        fixed=fixed,
    )
    work = hpd * queries * total
    return pl.pallas_call(
        body,
        out_shape=(
            jax.ShapeDtypeStruct((queries, hpd * HD), bf16),
            jax.ShapeDtypeStruct((hpd, queries, LANES), bf16),
        ),
        in_specs=[SM] + [VM] * len(ins),
        out_specs=(VM, VM),
        scratch_shapes=[pltpu.VMEM((hpd, total, LANES), bf16)] * 2,
        compiler_params=pltpu.CompilerParams(vmem_limit_bytes=44 * 2**20),
        cost_estimate=pl.CostEstimate(
            flops=1024 * work, bytes_accessed=16 * queries * hpd * HD, transcendentals=work
        ),
    )(limits, *ins)


def attend_back(limits, ins, blocks, do_spec, kv_specs, total, hpd, fixed):
    queries = blocks * do_spec[0]
    body = functools.partial(
        bwd_kernel,
        n_in=len(ins),
        blocks=blocks,
        do_spec=do_spec,
        kv_specs=kv_specs,
        hpd=hpd,
        bq=fit(queries, 512),
        kc=fit(total, 512),
        fixed=fixed,
    )
    work = hpd * queries * total
    return pl.pallas_call(
        body,
        out_shape=(
            jax.ShapeDtypeStruct((queries, hpd * HD), bf16),
            jax.ShapeDtypeStruct((total, 2 * hpd * HD), bf16),
        ),
        in_specs=[SM] + [VM] * len(ins),
        out_specs=(VM, VM),
        scratch_shapes=[pltpu.VMEM((hpd, total, LANES), bf16)] * 2
        + [pltpu.VMEM((hpd, queries, LANES), bf16)]
        + [pltpu.VMEM((hpd, total, LANES), f32)] * 2,
        compiler_params=pltpu.CompilerParams(vmem_limit_bytes=52 * 2**20),
        cost_estimate=pl.CostEstimate(
            flops=2560 * work, bytes_accessed=24 * queries * hpd * HD, transcendentals=work
        ),
    )(limits, *ins)


def norm_parts(values):
    center = values - jnp.mean(values, axis=-1, keepdims=True)
    scale = lax.rsqrt(jnp.mean(center * center, axis=-1, keepdims=True) + norm_eps)
    return center * scale, scale


def layer_norm(values, gain_row, shift_row):
    return (norm_parts(values)[0] * gain_row + shift_row).astype(bf16)


def norm_back(values, gain_row, grad_out):
    unit, scale = norm_parts(values)
    lifted = grad_out * gain_row
    grad_in = scale * (
        lifted
        - jnp.mean(lifted, axis=-1, keepdims=True)
        - unit * jnp.mean(lifted * unit, axis=-1, keepdims=True)
    )
    gain = jnp.sum(grad_out * unit, axis=0, keepdims=True)
    return grad_in, gain, jnp.sum(grad_out, axis=0, keepdims=True)


def flat(ref):
    return ref[...].reshape(-1, ref.shape[-1])


def joined(ref):
    return jnp.concatenate([ref[i] for i in range(ref.shape[0])], axis=1)


def once(shape, index=None):
    at = (0,) * len(shape) if index is None else index
    return pl.BlockSpec(shape, lambda i: at, pipeline_mode=pl.Buffered(1))


def held(shape):
    return pl.BlockSpec(shape, lambda i: (0,) * len(shape))


def mid_kernel(a_ref, x_ref, norm_ref, wo_ref, wt_ref, x1_ref, n_ref, ac_ref, t_ref):
    @pl.when(pl.program_id(0) == 0)
    def _():
        a = joined(a_ref)
        ac_ref[...] = a
        x1 = x_ref[...].astype(f32) + dot(a, flat(wo_ref), NN)
        x1_ref[...] = x1
        n_ref[...] = layer_norm(x1, norm_ref[0:1, :], norm_ref[1:2, :])

    t_ref[0] = dot(n_ref[...], flat(wt_ref), NT).astype(bf16)


def middle(a, x, norm, w_out, w_triple):
    S, rows, W = a.shape
    D = S * W
    return pl.pallas_call(
        mid_kernel,
        grid=(S,),
        out_shape=(
            jax.ShapeDtypeStruct((rows, D), f32),
            jax.ShapeDtypeStruct((rows, D), bf16),
            jax.ShapeDtypeStruct((rows, D), bf16),
            jax.ShapeDtypeStruct((S, rows, 3 * W), bf16),
        ),
        in_specs=[
            once((S, rows, W)),
            once((rows, D)),
            once((2, D)),
            w_out[1],
            w_triple[1],
        ],
        out_specs=(
            held((rows, D)),
            held((rows, D)),
            held((rows, D)),
            pl.BlockSpec((1, rows, 3 * W), lambda i: (i, 0, 0)),
        ),
        compiler_params=pltpu.CompilerParams(vmem_limit_bytes=40 * 2**20),
        cost_estimate=pl.CostEstimate(
            flops=8 * rows * D * D, bytes_accessed=8 * D * D + 14 * rows * D, transcendentals=0
        ),
    )(a, x, norm, w_out[0], w_triple[0])


def mlp_kernel(
    aa_ref,
    ab_ref,
    xa_ref,
    xb_ref,
    ca_ref,
    cb_ref,
    dp_ref,
    norm_ref,
    ws_ref,
    wd_ref,
    up_ref,
    down_ref,
    n_ref,
    ac_ref,
    g_ref,
    du_ref,
    x3_ref,
    pix_ref,
    e3_ref,
    d2_ref,
    e2_ref,
    da_ref,
    db_ref,
    sum_ref,
    x2,
    d3,
    acc,
    back,
    *,
    steps,
):
    step = pl.program_id(0)
    R = xa_ref.shape[0]
    S, _, W = aa_ref.shape

    @pl.when(step == 0)
    def _():
        for rows, a_ref, x_ref, c_ref in (
            (slice(0, R), aa_ref, xa_ref, ca_ref),
            (slice(R, x2.shape[0]), ab_ref, xb_ref, cb_ref),
        ):
            a = joined(a_ref)
            ac_ref[rows, :] = a
            x = x_ref[...] + dot(a, flat(ws_ref), NN)
            x2[rows, :] = x
            n_ref[rows, :] = layer_norm(x, norm_ref[0:1, :], norm_ref[1:2, :])
            d = c_ref[...].astype(f32) + dot(dp_ref[rows, :], flat(wd_ref), NN)
            d3[rows, :] = d
            e3_ref[rows, :] = d.astype(bf16)
        acc[...] = jnp.zeros_like(acc)
        back[...] = jnp.zeros_like(back)

    up = flat(up_ref)
    u = dot(n_ref[...], up, NT)
    slope = math.sqrt(2.0 / math.pi)
    square = u * u
    bend = jnp.tanh(slope * u * (1.0 + 0.044715 * square))
    half = 0.5 * (1.0 + bend)
    g = (u * half).astype(bf16)
    rise = half + 0.5 * slope * u * (1.0 - bend * bend) * (1.0 + 0.134145 * square)
    du = (dot(e3_ref[...], down_ref[...], NT) * rise).astype(bf16)
    g_ref[...] = g
    du_ref[...] = du
    acc[...] += dot(g, down_ref[...], NN)
    back[...] += dot(du, up, NN)

    @pl.when(step == steps - 1)
    def _():
        x3 = (x2[...] + acc[...]).astype(bf16)
        x3_ref[...] = x3
        pix_ref[...] = dot(x3, flat(wd_ref), NT).astype(bf16)
        grad_in, gain, shift = norm_back(x2[...], norm_ref[0:1, :], back[...])
        d2 = d3[...] + grad_in
        d2_ref[...] = d2
        e2 = d2.astype(bf16)
        e2_ref[...] = e2
        sum_ref[...] = jnp.concatenate([gain, shift], axis=0)
        da = dot(e2, flat(ws_ref), NT).astype(bf16)
        for i in range(S):
            da_ref[i] = da[:R, i * W : (i + 1) * W]
            db_ref[i] = da[R:, i * W : (i + 1) * W]


def feed_forward(a, x1, cot, d_pix, norm, w_out, w_dec, w_up, w_down, steps):
    S, R, W = a[0].shape
    RB = a[1].shape[1]
    D, total, pixels = S * W, R + RB, d_pix.shape[1]
    hidden = w_down.shape[0]
    part = hidden // steps
    row = jax.ShapeDtypeStruct((total, D), bf16)
    wide = jax.ShapeDtypeStruct((total, hidden), bf16)
    blocked = pl.BlockSpec((total, part), lambda i: (0, i))
    full = held((total, D))
    return pl.pallas_call(
        functools.partial(mlp_kernel, steps=steps),
        grid=(steps,),
        out_shape=(
            row,
            row,
            wide,
            wide,
            row,
            jax.ShapeDtypeStruct((total, pixels), bf16),
            row,
            jax.ShapeDtypeStruct((total, D), f32),
            row,
            jax.ShapeDtypeStruct((S, R, W), bf16),
            jax.ShapeDtypeStruct((S, RB, W), bf16),
            jax.ShapeDtypeStruct((2, D), f32),
        ),
        in_specs=[
            once((S, R, W)),
            once((S, RB, W)),
            once((R, D)),
            once((RB, D)),
            once((R, D)),
            once((RB, D)),
            once((total, pixels)),
            once((2, D)),
            w_out[1],
            w_dec[1],
            w_up[1],
            pl.BlockSpec((part, D), lambda i: (i, 0)),
        ],
        out_specs=(
            full,
            full,
            blocked,
            blocked,
            full,
            held((total, pixels)),
            full,
            full,
            full,
            held((S, R, W)),
            held((S, RB, W)),
            held((2, D)),
        ),
        scratch_shapes=[pltpu.VMEM((total, D), f32)] * 4,
        compiler_params=pltpu.CompilerParams(vmem_limit_bytes=60 * 2**20),
        cost_estimate=pl.CostEstimate(
            flops=8 * total * D * hidden + 8 * total * D * D,
            bytes_accessed=4 * D * hidden + 30 * total * D,
            transcendentals=total * hidden,
        ),
    )(*a, *x1, *cot, d_pix, norm, w_out[0], w_dec[0], w_up[0], w_down)


def back_kernel(
    t_ref, x_ref, d_ref, norm_ref, wo_ref, wt_ref, d1_ref, e_ref, da_ref, sum_ref, acc, *, steps
):
    step = pl.program_id(0)
    part = dot(t_ref[0], flat(wt_ref), NN)

    @pl.when(step == 0)
    def _():
        acc[...] = part

    @pl.when(step > 0)
    def _():
        acc[...] += part

    @pl.when(step == steps - 1)
    def _():
        grad_in, gain, shift = norm_back(x_ref[...], norm_ref[0:1, :], acc[...])
        d1 = d_ref[...] + grad_in
        d1_ref[...] = d1
        e = d1.astype(bf16)
        e_ref[...] = e
        sum_ref[...] = jnp.concatenate([gain, shift], axis=0)
        da = dot(e, flat(wo_ref), NT).astype(bf16)
        W = da_ref.shape[2]
        for i in range(steps):
            da_ref[i] = da[:, i * W : (i + 1) * W]


def middle_back(t, x1, d2, at, norm, w_out, w_triple):
    S, rows, wide = t.shape
    D = x1.shape[1]
    W = wide // 3
    return pl.pallas_call(
        functools.partial(back_kernel, steps=S),
        grid=(S,),
        out_shape=(
            jax.ShapeDtypeStruct((rows, D), f32),
            jax.ShapeDtypeStruct((rows, D), bf16),
            jax.ShapeDtypeStruct((S, rows, W), bf16),
            jax.ShapeDtypeStruct((2, D), f32),
        ),
        in_specs=[
            pl.BlockSpec((1, rows, wide), lambda i: (i, 0, 0)),
            once((rows, D)),
            once((rows, D), (at, 0)),
            once((2, D)),
            w_out[1],
            w_triple[1],
        ],
        out_specs=(
            held((rows, D)),
            held((rows, D)),
            held((S, rows, W)),
            held((2, D)),
        ),
        scratch_shapes=[pltpu.VMEM((rows, D), f32)],
        compiler_params=pltpu.CompilerParams(vmem_limit_bytes=40 * 2**20),
        cost_estimate=pl.CostEstimate(
            flops=8 * rows * D * D, bytes_accessed=8 * D * D + 24 * rows * D, transcendentals=0
        ),
    )(t, x1, d2, norm, w_out[0], w_triple[0])


def grads_kernel(*refs, shape, widths):
    count = sum(shape)
    lefts, rights = refs[:count], refs[count : 2 * count]
    out_ref, turned = refs[2 * count], refs[2 * count + 1 :]

    @pl.when(pl.program_id(0) == 0)
    def _():
        for left, t in zip(lefts, turned):
            t[...] = left[...].T

    at = n = 0
    for pieces, width in zip(shape, widths):
        total = 0.0
        for i in range(n, n + pieces):
            right = joined(rights[i]) if len(rights[i].shape) == 3 else rights[i][...]
            total += dot(turned[i][...], right, NN)
        out_ref[:, at : at + width] = total.astype(bf16)
        at, n = at + width, n + pieces


def weight_grads(terms, ranks):
    pieces = [p for term in terms for p in term]
    shape = [len(term) for term in terms]
    widths = [term[0][1].size // term[0][0].shape[0] // ranks for term in terms]
    D, per = pieces[0][0].shape[1], sum(widths)
    lefts = [p[0] for p in pieces]
    rights = [p[1] for p in pieces]
    work = sum(p[0].shape[0] for p in pieces) * D * per * ranks // len(pieces)
    return pl.pallas_call(
        functools.partial(grads_kernel, shape=shape, widths=widths),
        grid=(ranks,),
        out_shape=jax.ShapeDtypeStruct((D, per * ranks), bf16),
        in_specs=[once(v.shape) for v in lefts]
        + [
            pl.BlockSpec((v.shape[0] // ranks,) + v.shape[1:], lambda i: (i, 0, 0))
            if v.ndim == 3
            else pl.BlockSpec((v.shape[0], v.shape[1] // ranks), lambda i: (0, i))
            for v in rights
        ],
        out_specs=pl.BlockSpec((D, per), lambda i: (0, i)),
        scratch_shapes=[pltpu.VMEM(v.shape[::-1], bf16) for v in lefts],
        compiler_params=pltpu.CompilerParams(vmem_limit_bytes=56 * 2**20),
        cost_estimate=pl.CostEstimate(
            flops=2 * work, bytes_accessed=4 * D * per * ranks, transcendentals=0
        ),
    )(*lefts, *rights)


CP = 32


def place(perm, toks, TR, TC):
    own, ext = TR * TC, perm.shape[2]
    tok = lax.broadcasted_iota(jnp.int32, (toks, 1), 0)
    row = jnp.where(tok < own, tok // TC, jnp.where(tok < own + TR, tok - own, TR))
    col = jnp.where(
        tok < own, tok % TC, jnp.where(tok < own + TR, TC, tok - own - TR)
    )
    real = tok <= own + TR + TC
    pixel = lax.broadcasted_iota(jnp.int32, (toks, ext), 1)
    for a in range(2):
        for b in range(2):
            ok = real & ((row < TR) | (a == 0)) & ((col < TC) | (b == 0))
            at = jnp.where(ok, (2 * row + a) * (2 * TC + 1) + 2 * col + b, -1)
            perm[2 * a + b] = jnp.where(pixel == at, 1.0, 0.0).astype(bf16)


def pixel_grad_kernel(cot_ref, w_ref, out_ref, perm, *, TR, TC):
    @pl.when(pl.program_id(0) == 0)
    def _():
        place(perm, out_ref.shape[1], TR, TC)

    grad = dot(cot_ref[0], w_ref[0], NT)
    hi = grad.astype(bf16)
    lo = (grad - hi.astype(f32)).astype(bf16)
    parts = [dot(perm[i], hi, NT) + dot(perm[i], lo, NT) for i in range(4)]
    out_ref[0] = jnp.concatenate(parts, axis=1)


def pixel_sample_kernel(x_ref, w_ref, out_ref, perm, *, TR, TC):
    @pl.when(pl.program_id(0) == 0)
    def _():
        place(perm, x_ref.shape[1], TR, TC)

    x = x_ref[0]
    window = sum(dot(x[:, i * CP : (i + 1) * CP], perm[i], TN) for i in range(4))
    out_ref[0] = dot(window.astype(bf16), w_ref[0], NN).astype(bf16)


def per_plane(body, first, weights, out_rows, out_lanes, out_type, toks, TR, TC):
    planes, ext, samples = weights.shape

    def whole(shape):
        return pl.BlockSpec((1,) + shape, lambda i: (i, 0, 0))

    return pl.pallas_call(
        functools.partial(body, TR=TR, TC=TC),
        grid=(planes,),
        out_shape=jax.ShapeDtypeStruct((planes, out_rows, out_lanes), out_type),
        in_specs=[whole(first.shape[1:]), whole((ext, samples))],
        out_specs=whole((out_rows, out_lanes)),
        scratch_shapes=[pltpu.VMEM((4, toks, ext), bf16)],
        compiler_params=pltpu.CompilerParams(vmem_limit_bytes=24 * 2**20),
        cost_estimate=pl.CostEstimate(
            flops=6 * 10**8, bytes_accessed=7 * 10**6, transcendentals=0
        ),
    )(first, weights)


def swap_seq(value):
    return lax.all_to_all(value, "seq", split_axis=0, concat_axis=0, tiled=True)


def swap_mp(value):
    return lax.all_to_all(value, "mp", split_axis=0, concat_axis=0, tiled=True)


def swap_all(value):
    return lax.all_to_all(value, ("seq", "mp"), split_axis=0, concat_axis=0, tiled=True)


def swap_pair(value):
    count = lax.axis_size("mp")
    return lax.ppermute(value, "mp", [(i, i ^ 1) for i in range(count)])


def gather_rows(piece):
    return lax.all_gather(piece, ("mp", "seq"), axis=0, tiled=False)


def bundle_part(bundle, at, rows, per_step=None):
    pieces, _, D = bundle.shape
    if rows % 16 == 0 and at % rows == 0:
        place = at // rows
        if per_step is None:
            return bundle, once((pieces, rows, D), (0, place, 0))
        return bundle, pl.BlockSpec((per_step, rows, D), lambda i: (i, place, 0))
    value = bundle[:, at : at + rows].reshape(1, -1, D)
    if per_step is None:
        return value, once(value.shape)
    return value, pl.BlockSpec((1, per_step * rows, D), lambda i: (0, i, 0))


def reduce_rows(value):
    return lax.psum_scatter(value, "seq", scatter_dimension=0, tiled=True)


def from_ranks(blocks):
    ranks, rank = lax.axis_size("mp"), lax.axis_index("mp")
    got = []
    for step in range(ranks):
        block = lax.dynamic_index_in_dim(blocks, rank ^ step, 0, keepdims=False)
        if step > 0:
            block = lax.ppermute(block, "mp", [(i, i ^ step) for i in range(ranks)])
        got.append(block)
    return got


def in_order(got, at):
    got = jnp.stack(got)
    return [lax.dynamic_index_in_dim(got, at ^ i, 0, keepdims=False) for i in range(got.shape[0])]


def sum_ranks(value):
    ranks = lax.axis_size("mp")
    parts = value.reshape(value.shape[0], ranks, -1).transpose(1, 0, 2)
    return sum(v.astype(f32) for v in from_ranks(parts))


def gather_seq(value):
    shares, me = lax.axis_size("seq"), lax.axis_index("seq")
    got = [value]
    for step in range(1, shares // 2):
        moves = [(i, i ^ (2 * step)) for i in range(shares)]
        got.append(lax.ppermute(value, "seq", moves))
    got = jnp.stack(got)
    other = lax.ppermute(got, "seq", [(i, i ^ 1) for i in range(shares)])
    both = jnp.stack([got, other], axis=1).reshape((shares,) + value.shape)
    return jnp.stack(
        [lax.dynamic_index_in_dim(both, me ^ i, 0, keepdims=False) for i in range(shares)]
    )


def own_blocks(whole, blocks):
    ranks, rank = lax.axis_size("mp"), lax.axis_index("mp")
    pairs = ranks // 2
    pair = rank // 2
    own = whole.shape[0] // ranks
    whole = in_order(from_ranks(whole.reshape(ranks, own, -1)), rank)
    blocks = blocks.reshape(pairs, own, -1)
    arrived = []
    for step in range(pairs):
        moves = [(2 * p + h, pairs * h + (p ^ step)) for p in range(pairs) for h in range(2)]
        block = lax.dynamic_index_in_dim(blocks, pair ^ step, 0, keepdims=False)
        arrived.append(lax.ppermute(block, "mp", moves))
    arrived = in_order(arrived, rank % pairs)
    rows = []
    for p in range(pairs):
        rows += [whole[2 * p], arrived[p], whole[2 * p + 1]]
    return jnp.stack(rows)


def to_rows(value):
    return swap_seq(value).transpose(1, 0, 2).reshape(value.shape[1], -1)


def after(values, others):
    return lax.optimization_barrier((values, others))[0]


def per_device(
    tokens,
    patches,
    counts,
    norm_gains,
    norm_shifts,
    cross_query,
    cross_kv,
    cross_out,
    self_qkv,
    self_out,
    mlp_up,
    mlp_down,
    decoder,
    sample_weights,
    tokens_cot,
    sample_cot,
):
    objects, R, D = tokens.shape
    S, M = lax.axis_size("seq"), lax.axis_size("mp")
    s, m = lax.axis_index("seq"), lax.axis_index("mp")
    pairs = M // 2
    if objects != 3 * pairs or S != 2 * M or D % (HD * S) != 0:
        raise ValueError("unexpected sizes")
    pair, half = m // 2, m % 2
    at_a, at_b = 3 * pair + 2 * half, 3 * pair + 1
    RB = R // 2
    RS = R + RB
    rows = [R, RB]
    W = D // S
    hpd = W // HD
    slots, width = patches.shape[1], patches.shape[2]
    slot_total = slots * S
    row_total = R * S

    def pick(arr):
        whole = lax.dynamic_index_in_dim(arr, at_b, 0, keepdims=False)
        return [
            lax.dynamic_index_in_dim(arr, at_a, 0, keepdims=False),
            lax.dynamic_slice_in_dim(whole, half * RB, RB, 0),
        ]

    def mine(arr, axis):
        share = arr.shape[axis] // S
        return lax.dynamic_slice_in_dim(arr, s * share, share, axis)

    channels = decoder.shape[1]
    local_dec = jnp.pad(decoder.transpose(2, 1, 0), ((0, 0), (0, CP - channels), (0, 0)))
    local_qkv = self_qkv.reshape(D, 3, 2, W).transpose(2, 1, 3, 0).reshape(-1, D)
    local_kv = cross_kv.reshape(width, 2, 2, W).transpose(2, 1, 3, 0).reshape(-1, width)
    per = D // (S * M)
    up_rows = mlp_up.shape[1] // S
    dec_rows = 4 * CP // S
    lead = jnp.concatenate([mine(cross_query, 1).T, mine(local_kv, 0).reshape(-1, D)], axis=0)
    lead = gather_rows(lead)
    w_query = lead[:, :per].reshape(-1, D)
    w_kv = lead[:, per:].reshape(-1, width)
    first = gather_rows(jnp.concatenate([mine(local_qkv, 0), mine(cross_out, 0)], axis=0))
    w_triple = bundle_part(first, 0, 3 * per, M)
    w_cross_out = bundle_part(first, 3 * per, per)
    second = gather_rows(
        jnp.concatenate(
            [mine(mlp_up, 1).T, mine(self_out, 0), mine(local_dec.reshape(-1, D), 0)], axis=0
        )
    )
    steps = 8
    w_up = bundle_part(second, 0, up_rows, S * M // steps)
    w_self_out = bundle_part(second, up_rows, per)
    w_dec = bundle_part(second, up_rows + per, dec_rows)
    w_down = gather_rows(mine(mlp_down, 0)).reshape(-1, D)

    x0 = pick(tokens)
    both = [lax.dynamic_index_in_dim(patches, o, 0, keepdims=False) for o in (at_a, at_b)]
    patch_all = gather_seq(jnp.concatenate(both, axis=0)).reshape(-1, width)
    x0_all = jnp.concatenate(x0, axis=0)
    n1 = layer_norm(x0_all.astype(f32), norm_gains[0], norm_shifts[0])
    q1 = dot(n1, w_query, NT).astype(bf16)
    heads_one = swap_seq(q1.reshape(RS, S, W).transpose(1, 0, 2))
    own_kv = lax.dynamic_slice_in_dim(w_kv, s * 2 * W, 2 * W, 0)
    keys_one = dot(patch_all, own_kv, NT).astype(bf16).reshape(S, 2 * slots, 2 * W)

    TC = PLANE // 4
    TR = PLANE * 4 // S
    own, rim = TR * TC, TR * TC + TR
    toks = -(-(rim + TC + 1) // 32) * 32
    planes = objects * 3
    weights_in = sample_weights.reshape(planes, *sample_weights.shape[3:])
    cot_in = sample_cot.reshape(planes, channels, -1)
    cot_in = jnp.pad(cot_in, ((0, 0), (0, CP - channels), (0, 0)))
    ext = per_plane(pixel_grad_kernel, cot_in, weights_in, toks, 4 * CP, f32, toks, TR, TC)
    ways = {
        1: [i for i in range(S) if i % 4 != 3],
        4: [i for i in range(S) if i + 4 < S],
        5: [i for i in range(S) if i % 4 != 3 and i + 4 < S],
    }
    rights = lax.ppermute(ext[:, own:rim], "seq", [(i, i + 1) for i in ways[1]])
    belows = lax.ppermute(ext[:, rim : rim + TC], "seq", [(i, i + 4) for i in ways[4]])
    corner = lax.ppermute(ext[:, rim + TC : rim + TC + 1], "seq", [(i, i + 5) for i in ways[5]])
    grid = ext[:, :own].reshape(planes, TR, TC, -1)
    belows = jnp.concatenate([belows[:, :1] + corner, belows[:, 1:]], axis=1)
    grid = grid + jnp.pad(rights[:, :, None], ((0, 0), (0, 0), (0, TC - 1), (0, 0)))
    grid = grid + jnp.pad(belows[:, None], ((0, 0), (0, TR - 1), (0, 0), (0, 0)))
    KA, KB = R // S, RB // S
    cu = 4 * CP
    grad_pix = grid.astype(bf16).reshape(pairs, 3, S, KA, cu)
    gp_a = jnp.stack([grad_pix[:, 0], grad_pix[:, 2]], axis=1).transpose(2, 0, 1, 3, 4)
    gp_b = grad_pix[:, 1].reshape(pairs, S, 2, KB, cu).transpose(1, 0, 2, 3, 4)
    sent = jnp.concatenate([gp_a, gp_b], axis=3).reshape(S * M, KA + KB, cu)
    back = swap_all(sent).reshape(S, M, KA + KB, cu).transpose(2, 0, 1, 3)
    d_pix = back.reshape(RS, M * cu)

    limits = [
        jnp.stack([lax.dynamic_index_in_dim(counts, o, 0, keepdims=False), jnp.int32(0)])
        for o in (at_a, at_b)
    ]
    kv_one = [(slots, (i * slots, 0), (i * slots, W), 0) for i in range(2)]
    o1, res1 = [], []
    for i in range(2):
        out, res = attend(
            limits[i],
            [heads_one, keys_one],
            S,
            (0, rows[i], i * R, 0),
            [(1,) + kv_one[i]],
            slot_total,
            hpd,
            False,
        )
        o1.append(out)
        res1.append(res)

    norms = [jnp.stack([norm_gains[i], norm_shifts[i]]) for i in range(3)]
    mids = [
        middle(swap_seq(o1[i].reshape(S, rows[i], W)), x0[i], norms[1], w_cross_out, w_triple)
        for i in range(2)
    ]
    x1, n2, a1, t2 = zip(*mids)

    heads_two = [swap_seq(v) for v in t2]
    pair_kv = swap_pair(heads_two[1][:, :, W:])
    wide = jnp.array([row_total, 0], jnp.int32)
    kv_a2 = (R, (0, W), (0, 2 * W), 0)
    kv_b2 = (RB, (0, W), (0, 2 * W), 0)
    kv_p2 = (RB, (0, 0), (0, W), row_total // 2)
    o_a2, res_a2 = attend(
        wide, [heads_two[0]], S, (0, R, 0, 0), [(0,) + kv_a2], row_total, hpd, True
    )
    o_b2, res_b2 = attend(
        wide,
        [heads_two[1], pair_kv],
        S,
        (0, RB, 0, 0),
        [(0,) + kv_b2, (1,) + kv_p2],
        row_total,
        hpd,
        True,
    )
    a2 = [swap_seq(o_a2.reshape(S, R, W)), swap_seq(o_b2.reshape(S, RB, W))]

    n3, a2, g, du, x3b, pix, e3, d2, e2, da2_a, da2_b, sums_three = feed_forward(
        a2, x1, pick(tokens_cot), d_pix, norms[2], w_self_out, w_dec, w_up, w_down, steps
    )

    da2 = [swap_seq(da2_a), swap_seq(da2_b)]
    grads_one = weight_grads([[(n3, du)], [(e3, g)], [(e2, a2)], [(x3b, d_pix)]], M)
    da2[0] = after(da2[0], grads_one)
    grads_one = reduce_rows(grads_one)
    dq_a2, dkv_a2 = attend_back(
        wide,
        [res_a2, da2[0], o_a2, heads_two[0]],
        S,
        (R, 0),
        [(3,) + kv_a2],
        row_total,
        hpd,
        True,
    )
    tokens_out = own_blocks(x3b[:R], x3b[R:])
    pix = pix.reshape(KA + KB, S, M, cu).transpose(1, 2, 0, 3)
    got = swap_all(pix.reshape(S * M, KA + KB, cu)).reshape(S, pairs, 2, KA + KB, cu)
    da2[1] = after(da2[1], (tokens_out, got, dkv_a2))
    dq_b2, dkv_b2 = attend_back(
        wide,
        [res_b2, da2[1], o_b2, heads_two[1], pair_kv],
        S,
        (RB, 0),
        [(3,) + kv_b2, (4,) + kv_p2],
        row_total,
        hpd,
        True,
    )
    kept, given = dkv_b2[: row_total // 2], dkv_b2[row_total // 2 :]
    dkv_b2 = (kept.astype(f32) + swap_pair(given).astype(f32)).astype(bf16)
    dt2 = [
        swap_seq(jnp.concatenate([dq_a2, dkv_a2], axis=1).reshape(S, R, 3 * W)),
        swap_seq(jnp.concatenate([dq_b2, dkv_b2], axis=1).reshape(S, RB, 3 * W)),
    ]
    outs = [
        middle_back(dt2[i], x1[i], d2, (0, R // RB)[i], norms[1], w_cross_out, w_triple)
        for i in range(2)
    ]
    d1, e1, da1, sums_two = zip(*outs)
    da1 = [swap_seq(v) for v in da1]

    px_a = got[:, :, :, :KA].transpose(1, 2, 0, 3, 4).reshape(pairs, 2, S * KA, cu)
    px_b = got[:, :, :, KA:].transpose(1, 0, 2, 3, 4).reshape(pairs, S * KA, cu)
    tile = jnp.stack([px_a[:, 0], px_b, px_a[:, 1]], axis=1).reshape(planes, TR, TC, cu)
    rights = lax.ppermute(tile[:, :, 0], "seq", [(i + 1, i) for i in ways[1]])
    belows = lax.ppermute(tile[:, 0], "seq", [(i + 4, i) for i in ways[4]])
    corner = lax.ppermute(tile[:, 0, :1], "seq", [(i + 5, i) for i in ways[5]])
    fill = jnp.zeros((planes, toks - rim - TC - 1, cu), bf16)
    ext = jnp.concatenate([tile.reshape(planes, own, cu), rights, belows, corner, fill], axis=1)
    sampled = per_plane(
        pixel_sample_kernel, ext, weights_in, CP, weights_in.shape[2], bf16, toks, TR, TC
    )
    sampled = sampled[:, :channels].reshape(objects, 3, channels, 1, -1)

    grads_two = weight_grads(
        [[(n2[i], dt2[i]) for i in range(2)], [(e1[i], a1[i]) for i in range(2)]], M
    )
    n1_all = gather_seq(n1).reshape(-1, D)
    da1[1] = after(da1[1], (grads_two, sampled, n1_all))
    grads_two = reduce_rows(grads_two)
    dq1, dkv1 = [], []
    for i in range(2):
        dq, dkv = attend_back(
            limits[i],
            [res1[i], da1[i], o1[i], keys_one],
            S,
            (rows[i], 0),
            [(3,) + kv_one[i]],
            slot_total,
            hpd,
            False,
        )
        dq1.append(dq.reshape(S, rows[i], W))
        dkv1.append(dkv.reshape(S, slots, 2 * W))

    parts = [mm(to_rows(v), w_kv).astype(bf16) for v in dkv1]
    every = [[p] for p in parts]
    for step in range(1, M):
        moves = [(i, i ^ step) for i in range(M)]
        for i in range(2):
            every[i].append(lax.ppermute(parts[i], "mp", moves))
    from_a, from_b = [in_order(v, m) for v in every]
    patch_grad = []
    for p in range(pairs):
        shared = from_b[2 * p].astype(f32) + from_b[2 * p + 1].astype(f32)
        patch_grad += [from_a[2 * p].astype(f32), shared, from_a[2 * p + 1].astype(f32)]
    patch_grad = jnp.stack(patch_grad)

    grads = [mm(to_rows(v), w_query) for v in dq1]
    back_one = [norm_back(x0[i].astype(f32), norm_gains[0], grads[i]) for i in range(2)]
    d0 = [(d1[i] + back_one[i][0]).astype(bf16) for i in range(2)]
    grad_tokens = own_blocks(d0[0], d0[1]).astype(f32)

    order = 2 * m + s % 2
    dq_all = jnp.concatenate(dq1, axis=1).reshape(-1, W)
    dkv_all = jnp.concatenate(dkv1, axis=1).reshape(-1, 2 * W)
    grad_q = dot(n1_all, dq_all, TN).astype(bf16).reshape(S, D // S, W)
    grad_kv = dot(patch_all, dkv_all, TN).astype(bf16)
    grad_kv = grad_kv.reshape(S, width // S, 2 * W)
    grad_kv = jnp.concatenate([grad_kv[..., :W], grad_kv[..., W:]], axis=1)
    by_head = jnp.concatenate([grad_q, grad_kv], axis=1)
    sums = [0.0, 0.0]
    for step in range(S):
        moves = []
        for i in range(S):
            for j in range(M):
                t = i ^ step
                moves.append(((2 * j + t % 2) * M + t // 2, i * M + j))
        piece = lax.dynamic_index_in_dim(by_head, order ^ step, 0, keepdims=False)
        sums[step % 2] += lax.ppermute(piece, ("seq", "mp"), moves).astype(f32)
    swap = s % 2 == 1
    owned = jnp.concatenate(
        [jnp.where(swap, sums[1], sums[0]), jnp.where(swap, sums[0], sums[1])], axis=1
    )
    grad_cross_query = owned[: D // S]
    grad_cross_kv = owned[D // S :].reshape(2, width // S, 2 * W).transpose(1, 0, 2)

    grads_one, grads_two = sum_ranks(grads_one), sum_ranks(grads_two)
    ff = g.shape[1] // M
    grad_mlp_up, grad_mlp_down = grads_one[:, :ff], grads_one[:, ff : 2 * ff].T
    grad_self_out = grads_one[:, 2 * ff : 2 * ff + D // M].T
    grad_decoder = grads_one[:, 2 * ff + D // M :]
    grad_decoder = grad_decoder.reshape(D // S, 4, CP)[:, :, :channels].transpose(0, 2, 1)
    grad_self_qkv = grads_two[:, : 3 * D // M].reshape(D // S, 2, 3, W).transpose(0, 2, 1, 3)
    grad_cross_out = grads_two[:, 3 * D // M :].T

    one = [back_one[0][i] + back_one[1][i] for i in (1, 2)]
    two = sums_two[0] + sums_two[1]
    small = jnp.concatenate(
        [one[0], two[:1], sums_three[:1], one[1], two[1:], sums_three[1:]], axis=0
    )
    small = jnp.sum(swap_seq(small.reshape(6, S, D // S).transpose(1, 0, 2)), axis=0)
    small = sum(from_ranks(jnp.broadcast_to(small, (M,) + small.shape)))

    return (
        tokens_out,
        sampled,
        grad_tokens,
        patch_grad,
        small[:3],
        small[3:5],
        small[5],
        grad_cross_query,
        grad_cross_kv,
        grad_cross_out,
        grad_self_qkv.reshape(D // S, 3, -1),
        grad_self_out,
        grad_mlp_up,
        grad_mlp_down,
        grad_decoder,
    )


def solution(mesh):
    return jax.shard_map(
        per_device,
        mesh=mesh,
        in_specs=(
            P(None, "seq", None),
            P(None, "seq", None),
            P(),
            P(),
            P(),
            P(None, "mp"),
            P(None, None, "mp"),
            P("mp", None),
            P(None, None, "mp"),
            P("mp", None),
            P(None, "mp"),
            P("mp", None),
            P(None, "mp", None),
            P(None, None, "seq", None, None),
            P(None, "seq", None),
            P(None, None, "mp", "seq", None),
        ),
        out_specs=(
            P(None, ("seq", "mp"), None),
            P(None, None, "mp", "seq", None),
            P(None, ("seq", "mp"), None),
            P(None, "seq", None),
            P(None, "seq"),
            P(None, "seq"),
            P("seq"),
            P("seq", "mp"),
            P("seq", None, "mp"),
            P("mp", "seq"),
            P("seq", None, "mp"),
            P("mp", "seq"),
            P("seq", "mp"),
            P("mp", "seq"),
            P("seq", "mp", None),
        ),
        check_vma=False,
    )
```

```python
import functools
import math

import jax
import jax.numpy as jnp
from jax import lax
from jax.experimental import pallas as pl
from jax.experimental.pallas import tpu as pltpu
from jax.sharding import PartitionSpec as P


PLANE = 32
HD = 64
LANES = 128
norm_eps = 1e-05
f32 = jnp.float32
bf16 = jnp.bfloat16

NT = (((1,), (1,)), ((), ()))
NN = (((1,), (0,)), ((), ()))
TN = (((0,), (0,)), ((), ()))


def dot(a, b, dims):
    return lax.dot_general(a, b, dims, preferred_element_type=f32)


def mm(a, b):
    return jnp.dot(a, b, preferred_element_type=f32)


def split3(v):
    hi = v.astype(bf16).astype(f32)
    rest = v - hi
    mid = rest.astype(bf16).astype(f32)
    return hi, mid, rest - mid


def spread(base, cols):
    lane = lax.broadcasted_iota(jnp.int32, (base.shape[0], HD), 1)
    tail = jnp.zeros((base.shape[0], HD), f32)
    for at, col in cols.items():
        tail = jnp.where(lane == at, col, tail)
    return jnp.concatenate([base, tail], axis=1).astype(bf16)


def load_keys(n_ref, kv_specs, refs, ka, va, hpd, blocks):
    for ref_at, rows, k_at, v_at, base in kv_specs:
        src = refs[ref_at]

        def build(i, _):
            natural = base + (i ^ n_ref[1]) * rows
            dst = pl.ds(pl.multiple_of(natural, 16), rows)
            slot = natural + lax.broadcasted_iota(jnp.int32, (rows, 1), 0)
            mask = jnp.where(slot < n_ref[0], 0.0, -1e30).astype(f32)
            for h in range(hpd):
                k = src[i, k_at[0] : k_at[0] + rows, k_at[1] + h * HD : k_at[1] + (h + 1) * HD]
                v = src[i, v_at[0] : v_at[0] + rows, v_at[1] + h * HD : v_at[1] + (h + 1) * HD]
                ka[h, dst, :] = spread(k.astype(f32), {0: 1.0, 1: 1.0, 2: 1.0, 3: mask})
                va[h, dst, :] = spread(v.astype(f32), {0: 1.0, 1: 1.0, 2: 1.0})
            return 0

        lax.fori_loop(0, blocks, build, 0)


def fwd_kernel(n_ref, *refs, n_in, blocks, q_spec, kv_specs, hpd, bq, kc, fixed):
    ins, (o_ref, qa_ref, ka, va) = refs[:n_in], refs[-4:]
    load_keys(n_ref, kv_specs, ins, ka, va, hpd, blocks)
    q_at, rows_q, q_off, q_lane = q_spec

    def build(i, _):
        dst = pl.ds(pl.multiple_of((i ^ n_ref[1]) * rows_q, 16), rows_q)
        for h in range(hpd):
            q = ins[q_at][i, q_off : q_off + rows_q, q_lane + h * HD : q_lane + (h + 1) * HD]
            qa_ref[h, dst, :] = spread(q.astype(f32) * (1.0 / math.sqrt(HD)), {3: 1.0})
        return 0

    lax.fori_loop(0, blocks, build, 0)
    total = ka.shape[1]

    def block(b, _):
        rows = pl.ds(pl.multiple_of(b * bq, bq), bq)

        def chunk(c, carry):
            cols = pl.ds(pl.multiple_of(c * kc, kc), kc)
            out = []
            for h in range(hpd):
                m, acc = carry[h]
                s = dot(qa_ref[h, rows, :], ka[h, cols, :], NT)
                top = jnp.maximum(m, jnp.max(s, axis=1, keepdims=True))
                p = jnp.exp(s - top).astype(bf16)
                out.append((top, acc * jnp.exp(m - top) + dot(p, va[h, cols, :], NN)))
            return tuple(out)

        carry = ((jnp.full((bq, 1), -1e30, f32), jnp.zeros((bq, LANES), f32)),) * hpd
        if fixed:
            for c in range(total // kc):
                carry = chunk(c, carry)
        else:
            carry = lax.fori_loop(0, (n_ref[0] + kc - 1) // kc, chunk, carry)
        outs = []
        for h in range(hpd):
            m, acc = carry[h]
            norm = acc[:, HD : HD + 1]
            outs.append(acc[:, :HD] / norm)
            hi, mid, lo = split3(-(m + jnp.log(norm)))
            qa_ref[h, rows, :] = spread(
                qa_ref[h, rows, :HD].astype(f32), {0: hi, 1: mid, 2: lo, 3: 1.0}
            )
        o_ref[rows, :] = jnp.concatenate(outs, axis=1).astype(bf16)
        return 0

    lax.fori_loop(0, qa_ref.shape[1] // bq, block, 0)


def bwd_kernel(n_ref, *refs, n_in, blocks, do_spec, kv_specs, hpd, bq, kc, fixed):
    ins, (dq_ref, dkv_ref, ka, va, da, dk, dv) = refs[:n_in], refs[-7:]
    qa_ref, do_ref, o_ref = ins[:3]
    load_keys(n_ref, kv_specs, ins, ka, va, hpd, blocks)
    rows_q, do_off = do_spec

    def build(i, _):
        rows = pl.ds(pl.multiple_of(i * rows_q, 16), rows_q)
        for h in range(hpd):
            d = do_ref[i, do_off : do_off + rows_q, h * HD : (h + 1) * HD].astype(f32)
            o = o_ref[rows, h * HD : (h + 1) * HD].astype(f32)
            hi, mid, lo = split3(-jnp.sum(d * o, axis=1, keepdims=True))
            da[h, rows, :] = spread(d, {0: hi, 1: mid, 2: lo})
        return 0

    lax.fori_loop(0, blocks, build, 0)
    dk[...] = jnp.zeros_like(dk)
    dv[...] = jnp.zeros_like(dv)
    total = ka.shape[1]
    steps = total // kc if fixed else (n_ref[0] + kc - 1) // kc

    def block(b, _):
        rows = pl.ds(pl.multiple_of(b * bq, bq), bq)

        def chunk(c, dqs):
            cols = pl.ds(pl.multiple_of(c * kc, kc), kc)
            out = []
            for h in range(hpd):
                k, q, d = ka[h, cols, :], qa_ref[h, rows, :], da[h, rows, :]
                p = jnp.exp(dot(k, q, NT))
                dp = dot(va[h, cols, :], d, NT)
                dv[h, cols, :] += dot(p.astype(bf16), d, NN)
                g = (p * dp).astype(bf16)
                dk[h, cols, :] += dot(g, q, NN)
                out.append(dqs[h] + dot(k, g, TN))
            return tuple(out)

        dqs = lax.fori_loop(0, steps, chunk, (jnp.zeros((LANES, bq), f32),) * hpd)
        dq = jnp.concatenate([v[:HD, :] for v in dqs], axis=0).T
        dq_ref[rows, :] = (dq * (1.0 / math.sqrt(HD))).astype(bf16)
        return 0

    lax.fori_loop(0, qa_ref.shape[1] // bq, block, 0)
    step = total // blocks

    def finish(i, _):
        rows = pl.ds(pl.multiple_of(i * step, 16), step)
        parts = [dk[h, rows, :HD] for h in range(hpd)] + [dv[h, rows, :HD] for h in range(hpd)]
        dkv_ref[rows, :] = jnp.concatenate(parts, axis=1).astype(bf16)
        return 0

    lax.fori_loop(0, blocks, finish, 0)


VM = pl.BlockSpec(memory_space=pltpu.VMEM)
SM = pl.BlockSpec(memory_space=pltpu.SMEM)
AN = pl.BlockSpec(memory_space=pl.ANY)


def fit(rows, most):
    return math.gcd(rows, most)


def attend(limits, ins, blocks, q_spec, kv_specs, total, hpd, fixed, deps=()):
    queries = blocks * q_spec[1]
    kc = fit(total, 1024 if fixed else 512)
    body = functools.partial(
        fwd_kernel,
        n_in=len(ins),
        blocks=blocks,
        q_spec=q_spec,
        kv_specs=kv_specs,
        hpd=hpd,
        bq=fit(queries, 512),
        kc=kc,
        fixed=fixed,
    )
    work = hpd * queries * total
    return pl.pallas_call(
        body,
        out_shape=(
            jax.ShapeDtypeStruct((queries, hpd * HD), bf16),
            jax.ShapeDtypeStruct((hpd, queries, LANES), bf16),
        ),
        in_specs=[SM] + [VM] * len(ins) + [AN] * len(deps),
        out_specs=(VM, VM),
        scratch_shapes=[pltpu.VMEM((hpd, total, LANES), bf16)] * 2,
        compiler_params=pltpu.CompilerParams(vmem_limit_bytes=44 * 2**20),
        cost_estimate=pl.CostEstimate(
            flops=1024 * work, bytes_accessed=16 * queries * hpd * HD, transcendentals=work
        ),
    )(limits, *ins, *deps)


def attend_back(limits, ins, blocks, do_spec, kv_specs, total, hpd, fixed, deps=()):
    queries = blocks * do_spec[0]
    body = functools.partial(
        bwd_kernel,
        n_in=len(ins),
        blocks=blocks,
        do_spec=do_spec,
        kv_specs=kv_specs,
        hpd=hpd,
        bq=fit(queries, 512),
        kc=fit(total, 512),
        fixed=fixed,
    )
    work = hpd * queries * total
    return pl.pallas_call(
        body,
        out_shape=(
            jax.ShapeDtypeStruct((queries, hpd * HD), bf16),
            jax.ShapeDtypeStruct((total, 2 * hpd * HD), bf16),
        ),
        in_specs=[SM] + [VM] * len(ins) + [AN] * len(deps),
        out_specs=(VM, VM),
        scratch_shapes=[pltpu.VMEM((hpd, total, LANES), bf16)] * 2
        + [pltpu.VMEM((hpd, queries, LANES), bf16)]
        + [pltpu.VMEM((hpd, total, LANES), f32)] * 2,
        compiler_params=pltpu.CompilerParams(vmem_limit_bytes=52 * 2**20),
        cost_estimate=pl.CostEstimate(
            flops=2560 * work, bytes_accessed=24 * queries * hpd * HD, transcendentals=work
        ),
    )(limits, *ins, *deps)


def norm_parts(values):
    center = values - jnp.mean(values, axis=-1, keepdims=True)
    scale = lax.rsqrt(jnp.mean(center * center, axis=-1, keepdims=True) + norm_eps)
    return center * scale, scale


def layer_norm(values, gain_row, shift_row):
    return (norm_parts(values)[0] * gain_row + shift_row).astype(bf16)


def norm_back(values, gain_row, grad_out):
    unit, scale = norm_parts(values)
    lifted = grad_out * gain_row
    grad_in = scale * (
        lifted
        - jnp.mean(lifted, axis=-1, keepdims=True)
        - unit * jnp.mean(lifted * unit, axis=-1, keepdims=True)
    )
    gain = jnp.sum(grad_out * unit, axis=0, keepdims=True)
    return grad_in, gain, jnp.sum(grad_out, axis=0, keepdims=True)


def flat(ref):
    return ref[...].reshape(-1, ref.shape[-1])


def joined(ref):
    return jnp.concatenate([ref[i] for i in range(ref.shape[0])], axis=1)


def once(shape, index=None):
    at = (0,) * len(shape) if index is None else index
    return pl.BlockSpec(shape, lambda i: at, pipeline_mode=pl.Buffered(1))


def held(shape):
    return pl.BlockSpec(shape, lambda i: (0,) * len(shape))


def mid_kernel(a_ref, x_ref, norm_ref, wo_ref, wt_ref, x1_ref, n_ref, ac_ref, t_ref):
    @pl.when(pl.program_id(0) == 0)
    def _():
        a = joined(a_ref)
        ac_ref[...] = a
        x1 = x_ref[...].astype(f32) + dot(a, flat(wo_ref), NN)
        x1_ref[...] = x1
        n_ref[...] = layer_norm(x1, norm_ref[0:1, :], norm_ref[1:2, :])

    t_ref[0] = dot(n_ref[...], flat(wt_ref), NT).astype(bf16)


def middle(a, x, norm, w_out, w_triple):
    S, rows, W = a.shape
    D = S * W
    return pl.pallas_call(
        mid_kernel,
        grid=(S,),
        out_shape=(
            jax.ShapeDtypeStruct((rows, D), f32),
            jax.ShapeDtypeStruct((rows, D), bf16),
            jax.ShapeDtypeStruct((rows, D), bf16),
            jax.ShapeDtypeStruct((S, rows, 3 * W), bf16),
        ),
        in_specs=[
            once((S, rows, W)),
            once((rows, D)),
            once((2, D)),
            w_out[1],
            w_triple[1],
        ],
        out_specs=(
            held((rows, D)),
            held((rows, D)),
            held((rows, D)),
            pl.BlockSpec((1, rows, 3 * W), lambda i: (i, 0, 0)),
        ),
        compiler_params=pltpu.CompilerParams(vmem_limit_bytes=40 * 2**20),
        cost_estimate=pl.CostEstimate(
            flops=8 * rows * D * D, bytes_accessed=8 * D * D + 14 * rows * D, transcendentals=0
        ),
    )(a, x, norm, w_out[0], w_triple[0])


def mlp_kernel(
    aa_ref,
    ab_ref,
    xa_ref,
    xb_ref,
    ca_ref,
    cb_ref,
    dp_ref,
    norm_ref,
    ws_ref,
    wd_ref,
    up_ref,
    down_ref,
    n_ref,
    ac_ref,
    g_ref,
    du_ref,
    x3_ref,
    pix_ref,
    e3_ref,
    d2_ref,
    e2_ref,
    da_ref,
    db_ref,
    sum_ref,
    x2,
    d3,
    acc,
    back,
    *,
    steps,
):
    step = pl.program_id(0)
    R = xa_ref.shape[0]
    S, _, W = aa_ref.shape

    @pl.when(step == 0)
    def _():
        for rows, a_ref, x_ref, c_ref in (
            (slice(0, R), aa_ref, xa_ref, ca_ref),
            (slice(R, x2.shape[0]), ab_ref, xb_ref, cb_ref),
        ):
            a = joined(a_ref)
            ac_ref[rows, :] = a
            x = x_ref[...] + dot(a, flat(ws_ref), NN)
            x2[rows, :] = x
            n_ref[rows, :] = layer_norm(x, norm_ref[0:1, :], norm_ref[1:2, :])
            d = c_ref[...].astype(f32) + dot(dp_ref[rows, :], flat(wd_ref), NN)
            d3[rows, :] = d
            e3_ref[rows, :] = d.astype(bf16)
        acc[...] = jnp.zeros_like(acc)
        back[...] = jnp.zeros_like(back)

    up = flat(up_ref)
    u = dot(n_ref[...], up, NT)
    slope = math.sqrt(2.0 / math.pi)
    square = u * u
    bend = jnp.tanh(slope * u * (1.0 + 0.044715 * square))
    half = 0.5 * (1.0 + bend)
    g = (u * half).astype(bf16)
    rise = half + 0.5 * slope * u * (1.0 - bend * bend) * (1.0 + 0.134145 * square)
    du = (dot(e3_ref[...], down_ref[...], NT) * rise).astype(bf16)
    g_ref[...] = g
    du_ref[...] = du
    acc[...] += dot(g, down_ref[...], NN)
    back[...] += dot(du, up, NN)

    @pl.when(step == steps - 1)
    def _():
        x3 = (x2[...] + acc[...]).astype(bf16)
        x3_ref[...] = x3
        pix_ref[...] = dot(x3, flat(wd_ref), NT).astype(bf16)
        grad_in, gain, shift = norm_back(x2[...], norm_ref[0:1, :], back[...])
        d2 = d3[...] + grad_in
        d2_ref[...] = d2
        e2 = d2.astype(bf16)
        e2_ref[...] = e2
        sum_ref[...] = jnp.concatenate([gain, shift], axis=0)
        da = dot(e2, flat(ws_ref), NT).astype(bf16)
        for i in range(S):
            da_ref[i] = da[:R, i * W : (i + 1) * W]
            db_ref[i] = da[R:, i * W : (i + 1) * W]


def feed_forward(a, x1, cot, d_pix, norm, w_out, w_dec, w_up, w_down, steps):
    S, R, W = a[0].shape
    RB = a[1].shape[1]
    D, total, pixels = S * W, R + RB, d_pix.shape[1]
    hidden = w_down.shape[0]
    part = hidden // steps
    row = jax.ShapeDtypeStruct((total, D), bf16)
    wide = jax.ShapeDtypeStruct((total, hidden), bf16)
    blocked = pl.BlockSpec((total, part), lambda i: (0, i))
    full = held((total, D))
    return pl.pallas_call(
        functools.partial(mlp_kernel, steps=steps),
        grid=(steps,),
        out_shape=(
            row,
            row,
            wide,
            wide,
            row,
            jax.ShapeDtypeStruct((total, pixels), bf16),
            row,
            jax.ShapeDtypeStruct((total, D), f32),
            row,
            jax.ShapeDtypeStruct((S, R, W), bf16),
            jax.ShapeDtypeStruct((S, RB, W), bf16),
            jax.ShapeDtypeStruct((2, D), f32),
        ),
        in_specs=[
            once((S, R, W)),
            once((S, RB, W)),
            once((R, D)),
            once((RB, D)),
            once((R, D)),
            once((RB, D)),
            once((total, pixels)),
            once((2, D)),
            w_out[1],
            w_dec[1],
            w_up[1],
            pl.BlockSpec((part, D), lambda i: (i, 0)),
        ],
        out_specs=(
            full,
            full,
            blocked,
            blocked,
            full,
            held((total, pixels)),
            full,
            full,
            full,
            held((S, R, W)),
            held((S, RB, W)),
            held((2, D)),
        ),
        scratch_shapes=[pltpu.VMEM((total, D), f32)] * 4,
        compiler_params=pltpu.CompilerParams(vmem_limit_bytes=60 * 2**20),
        cost_estimate=pl.CostEstimate(
            flops=8 * total * D * hidden + 8 * total * D * D,
            bytes_accessed=4 * D * hidden + 30 * total * D,
            transcendentals=total * hidden,
        ),
    )(*a, *x1, *cot, d_pix, norm, w_out[0], w_dec[0], w_up[0], w_down)


def back_kernel(
    t_ref, x_ref, d_ref, norm_ref, wo_ref, wt_ref, *refs, steps
):
    d1_ref, e_ref, da_ref, sum_ref, acc = refs[-5:]
    step = pl.program_id(0)
    part = dot(t_ref[0], flat(wt_ref), NN)

    @pl.when(step == 0)
    def _():
        acc[...] = part

    @pl.when(step > 0)
    def _():
        acc[...] += part

    @pl.when(step == steps - 1)
    def _():
        grad_in, gain, shift = norm_back(x_ref[...], norm_ref[0:1, :], acc[...])
        d1 = d_ref[...] + grad_in
        d1_ref[...] = d1
        e = d1.astype(bf16)
        e_ref[...] = e
        sum_ref[...] = jnp.concatenate([gain, shift], axis=0)
        da = dot(e, flat(wo_ref), NT).astype(bf16)
        W = da_ref.shape[2]
        for i in range(steps):
            da_ref[i] = da[:, i * W : (i + 1) * W]


def middle_back(t, x1, d2, at, norm, w_out, w_triple, deps=()):
    S, rows, wide = t.shape
    D = x1.shape[1]
    W = wide // 3
    return pl.pallas_call(
        functools.partial(back_kernel, steps=S),
        grid=(S,),
        out_shape=(
            jax.ShapeDtypeStruct((rows, D), f32),
            jax.ShapeDtypeStruct((rows, D), bf16),
            jax.ShapeDtypeStruct((S, rows, W), bf16),
            jax.ShapeDtypeStruct((2, D), f32),
        ),
        in_specs=[
            pl.BlockSpec((1, rows, wide), lambda i: (i, 0, 0)),
            once((rows, D)),
            once((rows, D), (at, 0)),
            once((2, D)),
            w_out[1],
            w_triple[1],
        ]
        + [AN] * len(deps),
        out_specs=(
            held((rows, D)),
            held((rows, D)),
            held((S, rows, W)),
            held((2, D)),
        ),
        scratch_shapes=[pltpu.VMEM((rows, D), f32)],
        compiler_params=pltpu.CompilerParams(vmem_limit_bytes=40 * 2**20),
        cost_estimate=pl.CostEstimate(
            flops=8 * rows * D * D, bytes_accessed=8 * D * D + 24 * rows * D, transcendentals=0
        ),
    )(t, x1, d2, norm, w_out[0], w_triple[0], *deps)


def grads_kernel(*refs, shape, widths):
    count = sum(shape)
    lefts, rights = refs[:count], refs[count : 2 * count]
    out_ref, turned = refs[2 * count], refs[2 * count + 1 :]

    @pl.when(pl.program_id(0) == 0)
    def _():
        for left, t in zip(lefts, turned):
            t[...] = left[...].T

    at = n = 0
    for pieces, width in zip(shape, widths):
        total = 0.0
        for i in range(n, n + pieces):
            right = joined(rights[i]) if len(rights[i].shape) == 3 else rights[i][...]
            total += dot(turned[i][...], right, NN)
        out_ref[:, at : at + width] = total.astype(bf16)
        at, n = at + width, n + pieces


def weight_grads(terms, ranks):
    pieces = [p for term in terms for p in term]
    shape = [len(term) for term in terms]
    widths = [term[0][1].size // term[0][0].shape[0] // ranks for term in terms]
    D, per = pieces[0][0].shape[1], sum(widths)
    lefts = [p[0] for p in pieces]
    rights = [p[1] for p in pieces]
    work = sum(p[0].shape[0] for p in pieces) * D * per * ranks // len(pieces)
    return pl.pallas_call(
        functools.partial(grads_kernel, shape=shape, widths=widths),
        grid=(ranks,),
        out_shape=jax.ShapeDtypeStruct((D, per * ranks), bf16),
        in_specs=[once(v.shape) for v in lefts]
        + [
            pl.BlockSpec((v.shape[0] // ranks,) + v.shape[1:], lambda i: (i, 0, 0))
            if v.ndim == 3
            else pl.BlockSpec((v.shape[0], v.shape[1] // ranks), lambda i: (0, i))
            for v in rights
        ],
        out_specs=pl.BlockSpec((D, per), lambda i: (0, i)),
        scratch_shapes=[pltpu.VMEM(v.shape[::-1], bf16) for v in lefts],
        compiler_params=pltpu.CompilerParams(vmem_limit_bytes=56 * 2**20),
        cost_estimate=pl.CostEstimate(
            flops=2 * work, bytes_accessed=4 * D * per * ranks, transcendentals=0
        ),
    )(*lefts, *rights)


def start_kernel(at_ref, xa_ref, xb_ref, norm_ref, *refs, pieces, weights, parts, rows):
    w_in, refs = refs[:weights], refs[weights:]
    p_in, kv_in, (q_ref, k_ref, n_ref, wq_ref) = refs[:pieces], refs[pieces:-4], refs[-4:]
    seq, rank = at_ref[0], at_ref[1]
    R = xa_ref.shape[0]
    for i in range(weights):
        for j in range(w_in[i].shape[0]):
            at = 0 if weights == 1 else ((rank ^ j) * pieces + (seq ^ i)) * rows
            wq_ref[pl.ds(pl.multiple_of(at, 16), w_in[i].shape[1]), :] = w_in[i][j]
    for block, x_ref in ((slice(0, R), xa_ref), (slice(R, n_ref.shape[0]), xb_ref)):
        n_ref[block, :] = layer_norm(x_ref[...].astype(f32), norm_ref[0:1, :], norm_ref[1:2, :])
    W = q_ref.shape[2]
    for i in range(pieces):
        q_ref[i] = dot(n_ref[...], wq_ref[i * W : (i + 1) * W, :], NT).astype(bf16)
    w_kv = sum(v[...] for v in kv_in)
    for i in range(pieces):
        k_ref[seq ^ i] = dot(p_in[i][...], w_kv, NT).astype(bf16)


def start(at, x0, norm, w_pieces, patch_pieces, kv_parts, W):
    S, D = len(patch_pieces), x0[0].shape[1]
    total = x0[0].shape[0] + x0[1].shape[0]
    slots = patch_pieces[0].shape[0]
    body = functools.partial(
        start_kernel,
        pieces=S,
        weights=len(w_pieces),
        parts=len(kv_parts),
        rows=w_pieces[0].shape[1],
    )
    return pl.pallas_call(
        body,
        out_shape=(
            jax.ShapeDtypeStruct((S, total, W), bf16),
            jax.ShapeDtypeStruct((S, slots, 2 * W), bf16),
            jax.ShapeDtypeStruct((total, D), bf16),
            jax.ShapeDtypeStruct((D, D), bf16),
        ),
        in_specs=[SM] + [VM] * (3 + len(w_pieces) + S + len(kv_parts)),
        out_specs=(VM,) * 4,
        compiler_params=pltpu.CompilerParams(vmem_limit_bytes=44 * 2**20),
        cost_estimate=pl.CostEstimate(
            flops=2 * total * D * D + 4 * S * slots * 768 * W,
            bytes_accessed=6 * D * D + 12 * total * D,
            transcendentals=0,
        ),
    )(at, *x0, norm, *w_pieces, *patch_pieces, *kv_parts)


def finish_kernel(at_ref, qa_ref, qb_ref, ka_ref, kb_ref, *refs, pieces):
    n_in, p_in, out_ref = refs[:pieces], refs[pieces:-1], refs[-1]
    seq = at_ref[0]
    R, slots, W = qa_ref.shape[1], ka_ref.shape[1], qa_ref.shape[2]
    by_q, by_kv = 0.0, 0.0
    for i in range(pieces):
        j = seq ^ i
        by_q += dot(qa_ref[j], n_in[i][:R, :], TN) + dot(qb_ref[j], n_in[i][R:, :], TN)
        by_kv += dot(ka_ref[j], p_in[i][:slots, :], TN) + dot(kb_ref[j], p_in[i][slots:, :], TN)
    grad = by_q.T.astype(bf16)
    rows = grad.shape[0] // pieces
    wide = by_kv.shape[1] // pieces
    grad_k, grad_v = by_kv[:W].T.astype(bf16), by_kv[W:].T.astype(bf16)
    for i in range(pieces):
        out_ref[i, :rows, :] = grad[i * rows : (i + 1) * rows, :]
        out_ref[i, rows : rows + wide, :] = grad_k[i * wide : (i + 1) * wide, :]
        out_ref[i, rows + wide :, :] = grad_v[i * wide : (i + 1) * wide, :]


def finish(at, dq, dkv, n_pieces, patch_pieces):
    S, _, W = dq[0].shape
    D, width = n_pieces[0].shape[1], patch_pieces[0].shape[1]
    rows = D // S + 2 * width // S
    return pl.pallas_call(
        functools.partial(finish_kernel, pieces=S),
        out_shape=jax.ShapeDtypeStruct((S, rows, W), bf16),
        in_specs=[SM] + [VM] * (4 + 2 * S),
        out_specs=VM,
        compiler_params=pltpu.CompilerParams(vmem_limit_bytes=48 * 2**20),
        cost_estimate=pl.CostEstimate(
            flops=3 * 10**9, bytes_accessed=18 * 10**6, transcendentals=0
        ),
    )(at, *dq, *dkv, *n_pieces, *patch_pieces)


CP = 32


def place(perm, toks, TR, TC):
    own, ext = TR * TC, perm.shape[2]
    tok = lax.broadcasted_iota(jnp.int32, (toks, 1), 0)
    row = jnp.where(tok < own, tok // TC, jnp.where(tok < own + TR, tok - own, TR))
    col = jnp.where(
        tok < own, tok % TC, jnp.where(tok < own + TR, TC, tok - own - TR)
    )
    real = tok <= own + TR + TC
    pixel = lax.broadcasted_iota(jnp.int32, (toks, ext), 1)
    for a in range(2):
        for b in range(2):
            ok = real & ((row < TR) | (a == 0)) & ((col < TC) | (b == 0))
            at = jnp.where(ok, (2 * row + a) * (2 * TC + 1) + 2 * col + b, -1)
            perm[2 * a + b] = jnp.where(pixel == at, 1.0, 0.0).astype(bf16)


def pixel_grad_kernel(cot_ref, w_ref, out_ref, perm, *, TR, TC):
    @pl.when(pl.program_id(0) == 0)
    def _():
        place(perm, out_ref.shape[1], TR, TC)

    grad = dot(cot_ref[0], w_ref[0], NT)
    hi = grad.astype(bf16)
    lo = (grad - hi.astype(f32)).astype(bf16)
    parts = [dot(perm[i], hi, NT) + dot(perm[i], lo, NT) for i in range(4)]
    out_ref[0] = jnp.concatenate(parts, axis=1)


def pixel_sample_kernel(x_ref, w_ref, out_ref, perm, *, TR, TC):
    @pl.when(pl.program_id(0) == 0)
    def _():
        place(perm, x_ref.shape[1], TR, TC)

    x = x_ref[0]
    window = sum(dot(x[:, i * CP : (i + 1) * CP], perm[i], TN) for i in range(4))
    out_ref[0] = dot(window.astype(bf16), w_ref[0], NN).astype(bf16)


def per_plane(body, first, weights, out_rows, out_lanes, out_type, toks, TR, TC):
    planes, ext, samples = weights.shape

    def whole(shape):
        return pl.BlockSpec((1,) + shape, lambda i: (i, 0, 0))

    return pl.pallas_call(
        functools.partial(body, TR=TR, TC=TC),
        grid=(planes,),
        out_shape=jax.ShapeDtypeStruct((planes, out_rows, out_lanes), out_type),
        in_specs=[whole(first.shape[1:]), whole((ext, samples))],
        out_specs=whole((out_rows, out_lanes)),
        scratch_shapes=[pltpu.VMEM((4, toks, ext), bf16)],
        compiler_params=pltpu.CompilerParams(vmem_limit_bytes=24 * 2**20),
        cost_estimate=pl.CostEstimate(
            flops=6 * 10**8, bytes_accessed=7 * 10**6, transcendentals=0
        ),
    )(first, weights)


def swap_seq(value):
    return lax.all_to_all(value, "seq", split_axis=0, concat_axis=0, tiled=True)


def swap_mp(value):
    return lax.all_to_all(value, "mp", split_axis=0, concat_axis=0, tiled=True)


def swap_all(value):
    return lax.all_to_all(value, ("seq", "mp"), split_axis=0, concat_axis=0, tiled=True)


def swap_pair(value):
    count = lax.axis_size("mp")
    return lax.ppermute(value, "mp", [(i, i ^ 1) for i in range(count)])


def gather_rows(piece):
    return lax.all_gather(piece, ("mp", "seq"), axis=0, tiled=False)


def bundle_part(bundle, at, rows, per_step=None):
    pieces, _, D = bundle.shape
    if rows % 16 == 0 and at % rows == 0:
        place = at // rows
        if per_step is None:
            return bundle, once((pieces, rows, D), (0, place, 0))
        return bundle, pl.BlockSpec((per_step, rows, D), lambda i: (i, place, 0))
    value = bundle[:, at : at + rows].reshape(1, -1, D)
    if per_step is None:
        return value, once(value.shape)
    return value, pl.BlockSpec((1, per_step * rows, D), lambda i: (0, i, 0))


def reduce_rows(value):
    return lax.psum_scatter(value, "seq", scatter_dimension=0, tiled=True)


def from_ranks(blocks):
    ranks, rank = lax.axis_size("mp"), lax.axis_index("mp")
    got = []
    for step in range(ranks):
        block = lax.dynamic_index_in_dim(blocks, rank ^ step, 0, keepdims=False)
        if step > 0:
            block = lax.ppermute(block, "mp", [(i, i ^ step) for i in range(ranks)])
        got.append(block)
    return got


def in_order(got, at):
    got = jnp.stack(got)
    return [lax.dynamic_index_in_dim(got, at ^ i, 0, keepdims=False) for i in range(got.shape[0])]


def sum_ranks(value):
    return lax.psum_scatter(value, "mp", scatter_dimension=1, tiled=True).astype(f32)


def gather_pieces(value):
    shares = lax.axis_size("seq")
    pieces = []
    for step in range(0, shares, 2):
        moves = [(i, i ^ step) for i in range(shares)]
        pieces.append(value if step == 0 else lax.ppermute(value, "seq", moves))
    cores = [(i, i ^ 1) for i in range(shares)]
    return [p for piece in pieces for p in (piece, lax.ppermute(piece, "seq", cores))]


def own_blocks(whole, blocks):
    ranks, rank = lax.axis_size("mp"), lax.axis_index("mp")
    pairs = ranks // 2
    pair = rank // 2
    own = whole.shape[0] // ranks
    whole = in_order(from_ranks(whole.reshape(ranks, own, -1)), rank)
    blocks = blocks.reshape(pairs, own, -1)
    arrived = []
    for step in range(pairs):
        moves = [(2 * p + h, pairs * h + (p ^ step)) for p in range(pairs) for h in range(2)]
        block = lax.dynamic_index_in_dim(blocks, pair ^ step, 0, keepdims=False)
        arrived.append(lax.ppermute(block, "mp", moves))
    arrived = in_order(arrived, rank % pairs)
    rows = []
    for p in range(pairs):
        rows += [whole[2 * p], arrived[p], whole[2 * p + 1]]
    return jnp.stack(rows)


def to_rows(value):
    return swap_seq(value).transpose(1, 0, 2).reshape(value.shape[1], -1)


def per_device(
    tokens,
    patches,
    counts,
    norm_gains,
    norm_shifts,
    cross_query,
    cross_kv,
    cross_out,
    self_qkv,
    self_out,
    mlp_up,
    mlp_down,
    decoder,
    sample_weights,
    tokens_cot,
    sample_cot,
):
    objects, R, D = tokens.shape
    S, M = lax.axis_size("seq"), lax.axis_size("mp")
    s, m = lax.axis_index("seq"), lax.axis_index("mp")
    pairs = M // 2
    if objects != 3 * pairs or S != 2 * M or D % (HD * S) != 0:
        raise ValueError("unexpected sizes")
    pair, half = m // 2, m % 2
    at_a, at_b = 3 * pair + 2 * half, 3 * pair + 1
    RB = R // 2
    RS = R + RB
    rows = [R, RB]
    W = D // S
    hpd = W // HD
    slots, width = patches.shape[1], patches.shape[2]
    slot_total = slots * S
    row_total = R * S

    def pick(arr):
        whole = lax.dynamic_index_in_dim(arr, at_b, 0, keepdims=False)
        return [
            lax.dynamic_index_in_dim(arr, at_a, 0, keepdims=False),
            lax.dynamic_slice_in_dim(whole, half * RB, RB, 0),
        ]

    def mine(arr, axis):
        share = arr.shape[axis] // S
        return lax.dynamic_slice_in_dim(arr, s * share, share, axis)

    channels = decoder.shape[1]
    local_dec = jnp.pad(decoder.transpose(2, 1, 0), ((0, 0), (0, CP - channels), (0, 0)))
    local_qkv = self_qkv.reshape(D, 3, 2, W).transpose(2, 1, 3, 0).reshape(-1, D)
    local_kv = cross_kv.reshape(width, 2, 2, W).transpose(2, 1, 3, 0).reshape(-1, width)
    per = D // (S * M)
    up_rows = mlp_up.shape[1] // S
    dec_rows = 4 * CP // S
    first = gather_rows(jnp.concatenate([mine(local_qkv, 0), mine(cross_out, 0)], axis=0))
    w_triple = bundle_part(first, 0, 3 * per, M)
    w_cross_out = bundle_part(first, 3 * per, per)
    second = gather_rows(
        jnp.concatenate(
            [mine(mlp_up, 1).T, mine(self_out, 0), mine(local_dec.reshape(-1, D), 0)], axis=0
        )
    )
    steps = 8
    w_up = bundle_part(second, 0, up_rows, S * M // steps)
    w_self_out = bundle_part(second, up_rows, per)
    w_dec = bundle_part(second, up_rows + per, dec_rows)
    w_down = gather_rows(mine(mlp_down, 0)).reshape(-1, D)
    w_kv = gather_rows(mine(local_kv, 0)).reshape(-1, width)

    x0 = pick(tokens)
    norms = [jnp.stack([norm_gains[i], norm_shifts[i]]) for i in range(3)]
    at = jnp.stack([s, m])
    both = [lax.dynamic_index_in_dim(patches, o, 0, keepdims=False) for o in (at_a, at_b)]
    patch_pieces = gather_pieces(jnp.concatenate(both, axis=0))
    piece = mine(cross_query, 1).T
    ranks = [piece]
    for step in range(1, M):
        ranks.append(lax.ppermute(piece, "mp", [(i, i ^ step) for i in range(M)]))
    w_pieces = gather_pieces(jnp.stack(ranks))
    if per % 16 != 0:
        w_pieces = jnp.stack(w_pieces)
        w_pieces = [
            lax.dynamic_index_in_dim(w_pieces, s ^ i, 0, keepdims=False) for i in range(S)
        ]
        w_pieces = jnp.stack(w_pieces, axis=1)
        w_pieces = [
            lax.dynamic_index_in_dim(w_pieces, m ^ i, 0, keepdims=False) for i in range(M)
        ]
        w_pieces = [jnp.stack(w_pieces).reshape(1, D, D)]
    own_kv = lax.dynamic_slice_in_dim(local_kv, (s % 2) * 2 * W, 2 * W, 0)
    kv_parts = [jnp.where(m == s // 2, own_kv, jnp.zeros_like(own_kv))]
    for step in range(1, M):
        moves = [(i * M + i // 2, i * M + ((i // 2) ^ step)) for i in range(S)]
        kv_parts.append(lax.ppermute(own_kv, ("seq", "mp"), moves))
    q1, keys_one, n1, w_query = start(at, x0, norms[0], w_pieces, patch_pieces, kv_parts, W)
    heads_one = swap_seq(q1)

    TC = PLANE // 4
    TR = PLANE * 4 // S
    own, rim = TR * TC, TR * TC + TR
    toks = -(-(rim + TC + 1) // 32) * 32
    planes = objects * 3
    weights_in = sample_weights.reshape(planes, *sample_weights.shape[3:])
    cot_in = sample_cot.reshape(planes, channels, -1)
    cot_in = jnp.pad(cot_in, ((0, 0), (0, CP - channels), (0, 0)))
    ext = per_plane(pixel_grad_kernel, cot_in, weights_in, toks, 4 * CP, f32, toks, TR, TC)
    ways = {
        1: [i for i in range(S) if i % 4 != 3],
        4: [i for i in range(S) if i + 4 < S],
        5: [i for i in range(S) if i % 4 != 3 and i + 4 < S],
    }
    rights = lax.ppermute(ext[:, own:rim], "seq", [(i, i + 1) for i in ways[1]])
    belows = lax.ppermute(ext[:, rim : rim + TC], "seq", [(i, i + 4) for i in ways[4]])
    corner = lax.ppermute(ext[:, rim + TC : rim + TC + 1], "seq", [(i, i + 5) for i in ways[5]])
    grid = ext[:, :own].reshape(planes, TR, TC, -1)
    belows = jnp.concatenate([belows[:, :1] + corner, belows[:, 1:]], axis=1)
    grid = grid + jnp.pad(rights[:, :, None], ((0, 0), (0, 0), (0, TC - 1), (0, 0)))
    grid = grid + jnp.pad(belows[:, None], ((0, 0), (0, TR - 1), (0, 0), (0, 0)))
    KA, KB = R // S, RB // S
    cu = 4 * CP
    grad_pix = grid.astype(bf16).reshape(pairs, 3, S, KA, cu)
    gp_a = jnp.stack([grad_pix[:, 0], grad_pix[:, 2]], axis=1).transpose(2, 0, 1, 3, 4)
    gp_b = grad_pix[:, 1].reshape(pairs, S, 2, KB, cu).transpose(1, 0, 2, 3, 4)
    sent = jnp.concatenate([gp_a, gp_b], axis=3).reshape(S * M, KA + KB, cu)
    back = swap_all(sent).reshape(S, M, KA + KB, cu).transpose(2, 0, 1, 3)
    d_pix = back.reshape(RS, M * cu)

    limits = [
        jnp.stack([lax.dynamic_index_in_dim(counts, o, 0, keepdims=False), jnp.int32(0)])
        for o in (at_a, at_b)
    ]
    kv_one = [(slots, (i * slots, 0), (i * slots, W), 0) for i in range(2)]
    o1, res1 = [], []
    for i in range(2):
        out, res = attend(
            limits[i],
            [heads_one, keys_one],
            S,
            (0, rows[i], i * R, 0),
            [(1,) + kv_one[i]],
            slot_total,
            hpd,
            False,
        )
        o1.append(out)
        res1.append(res)

    mids = [
        middle(swap_seq(o1[i].reshape(S, rows[i], W)), x0[i], norms[1], w_cross_out, w_triple)
        for i in range(2)
    ]
    x1, n2, a1, t2 = zip(*mids)

    heads_two = [swap_seq(v) for v in t2]
    pair_kv = swap_pair(heads_two[1][:, :, W:])
    wide = jnp.array([row_total, 0], jnp.int32)
    kv_a2 = (R, (0, W), (0, 2 * W), 0)
    kv_b2 = (RB, (0, W), (0, 2 * W), 0)
    kv_p2 = (RB, (0, 0), (0, W), row_total // 2)
    o_a2, res_a2 = attend(
        wide, [heads_two[0]], S, (0, R, 0, 0), [(0,) + kv_a2], row_total, hpd, True
    )
    o_b2, res_b2 = attend(
        wide,
        [heads_two[1], pair_kv],
        S,
        (0, RB, 0, 0),
        [(0,) + kv_b2, (1,) + kv_p2],
        row_total,
        hpd,
        True,
    )
    a2 = [swap_seq(o_a2.reshape(S, R, W)), swap_seq(o_b2.reshape(S, RB, W))]

    n3, a2, g, du, x3b, pix, e3, d2, e2, da2_a, da2_b, sums_three = feed_forward(
        a2, x1, pick(tokens_cot), d_pix, norms[2], w_self_out, w_dec, w_up, w_down, steps
    )

    da2 = [swap_seq(da2_a), swap_seq(da2_b)]
    grads_one = weight_grads([[(n3, du)], [(e3, g)], [(e2, a2)], [(x3b, d_pix)]], M)
    dq_a2, dkv_a2 = attend_back(
        wide,
        [res_a2, da2[0], o_a2, heads_two[0]],
        S,
        (R, 0),
        [(3,) + kv_a2],
        row_total,
        hpd,
        True,
        [grads_one],
    )
    grads_one = reduce_rows(grads_one)
    n_pieces = gather_pieces(n1)
    tokens_out = own_blocks(x3b[:R], x3b[R:])
    pix = pix.reshape(KA + KB, S, M, cu).transpose(1, 2, 0, 3)
    got = swap_all(pix.reshape(S * M, KA + KB, cu)).reshape(S, pairs, 2, KA + KB, cu)
    dq_b2, dkv_b2 = attend_back(
        wide,
        [res_b2, da2[1], o_b2, heads_two[1], pair_kv],
        S,
        (RB, 0),
        [(3,) + kv_b2, (4,) + kv_p2],
        row_total,
        hpd,
        True,
        [dq_a2, tokens_out, got] + n_pieces[::2],
    )
    kept, given = dkv_b2[: row_total // 2], dkv_b2[row_total // 2 :]
    dkv_b2 = (kept.astype(f32) + swap_pair(given).astype(f32)).astype(bf16)
    dt2 = [
        swap_seq(jnp.concatenate([dq_a2, dkv_a2], axis=1).reshape(S, R, 3 * W)),
        swap_seq(jnp.concatenate([dq_b2, dkv_b2], axis=1).reshape(S, RB, 3 * W)),
    ]
    def below(i, deps):
        return middle_back(
            dt2[i], x1[i], d2, (0, R // RB)[i], norms[1], w_cross_out, w_triple, deps
        )

    def cross_back(i, da1, deps):
        dq, dkv = attend_back(
            limits[i],
            [res1[i], da1, o1[i], keys_one],
            S,
            (rows[i], 0),
            [(3,) + kv_one[i]],
            slot_total,
            hpd,
            False,
            deps,
        )
        return dq.reshape(S, rows[i], W), dkv.reshape(S, slots, 2 * W)

    low_a = below(0, [])
    cross_a = cross_back(0, swap_seq(low_a[2]), [grads_one] + n_pieces[1::2])
    low_b = below(1, [cross_a[0]])
    d1, e1, da1, sums_two = zip(low_a, low_b)

    px_a = got[:, :, :, :KA].transpose(1, 2, 0, 3, 4).reshape(pairs, 2, S * KA, cu)
    px_b = got[:, :, :, KA:].transpose(1, 0, 2, 3, 4).reshape(pairs, S * KA, cu)
    tile = jnp.stack([px_a[:, 0], px_b, px_a[:, 1]], axis=1).reshape(planes, TR, TC, cu)
    rights = lax.ppermute(tile[:, :, 0], "seq", [(i + 1, i) for i in ways[1]])
    belows = lax.ppermute(tile[:, 0], "seq", [(i + 4, i) for i in ways[4]])
    corner = lax.ppermute(tile[:, 0, :1], "seq", [(i + 5, i) for i in ways[5]])
    fill = jnp.zeros((planes, toks - rim - TC - 1, cu), bf16)
    ext = jnp.concatenate([tile.reshape(planes, own, cu), rights, belows, corner, fill], axis=1)
    sampled = per_plane(
        pixel_sample_kernel, ext, weights_in, CP, weights_in.shape[2], bf16, toks, TR, TC
    )
    sampled = sampled[:, :channels].reshape(objects, 3, channels, 1, -1)

    grads_two = weight_grads(
        [[(n2[i], dt2[i]) for i in range(2)], [(e1[i], a1[i]) for i in range(2)]], M
    )
    cross_b = cross_back(1, swap_seq(da1[1]), [grads_two, sampled])
    dq1, dkv1 = zip(cross_a, cross_b)
    grads_two = reduce_rows(grads_two)

    parts = [mm(to_rows(v), w_kv).astype(bf16) for v in dkv1]
    every = [[p] for p in parts]
    for step in range(1, M):
        moves = [(i, i ^ step) for i in range(M)]
        for i in range(2):
            every[i].append(lax.ppermute(parts[i], "mp", moves))
    from_a, from_b = [in_order(v, m) for v in every]
    patch_grad = []
    for p in range(pairs):
        shared = from_b[2 * p].astype(f32) + from_b[2 * p + 1].astype(f32)
        patch_grad += [from_a[2 * p].astype(f32), shared, from_a[2 * p + 1].astype(f32)]
    patch_grad = jnp.stack(patch_grad)

    grads = [mm(to_rows(v), w_query) for v in dq1]
    back_one = [norm_back(x0[i].astype(f32), norm_gains[0], grads[i]) for i in range(2)]
    d0 = [(d1[i] + back_one[i][0]).astype(bf16) for i in range(2)]
    grad_tokens = own_blocks(d0[0], d0[1]).astype(f32)

    order = 2 * m + s % 2
    by_head = finish(at, dq1, dkv1, n_pieces, patch_pieces)
    sums = [0.0, 0.0]
    for step in range(S):
        moves = []
        for i in range(S):
            for j in range(M):
                t = i ^ step
                moves.append(((2 * j + t % 2) * M + t // 2, i * M + j))
        piece = lax.dynamic_index_in_dim(by_head, order ^ step, 0, keepdims=False)
        sums[step % 2] += lax.ppermute(piece, ("seq", "mp"), moves).astype(f32)
    swap = s % 2 == 1
    owned = jnp.concatenate(
        [jnp.where(swap, sums[1], sums[0]), jnp.where(swap, sums[0], sums[1])], axis=1
    )
    grad_cross_query = owned[: D // S]
    grad_cross_kv = owned[D // S :].reshape(2, width // S, 2 * W).transpose(1, 0, 2)

    grads_one, grads_two = sum_ranks(grads_one), sum_ranks(grads_two)
    ff = g.shape[1] // M
    grad_mlp_up, grad_mlp_down = grads_one[:, :ff], grads_one[:, ff : 2 * ff].T
    grad_self_out = grads_one[:, 2 * ff : 2 * ff + D // M].T
    grad_decoder = grads_one[:, 2 * ff + D // M :]
    grad_decoder = grad_decoder.reshape(D // S, 4, CP)[:, :, :channels].transpose(0, 2, 1)
    grad_self_qkv = grads_two[:, : 3 * D // M].reshape(D // S, 2, 3, W).transpose(0, 2, 1, 3)
    grad_cross_out = grads_two[:, 3 * D // M :].T

    one = [back_one[0][i] + back_one[1][i] for i in (1, 2)]
    two = sums_two[0] + sums_two[1]
    small = jnp.concatenate(
        [one[0], two[:1], sums_three[:1], one[1], two[1:], sums_three[1:]], axis=0
    )
    small = jnp.sum(swap_seq(small.reshape(6, S, D // S).transpose(1, 0, 2)), axis=0)
    small = sum(from_ranks(jnp.broadcast_to(small, (M,) + small.shape)))

    return (
        tokens_out,
        sampled,
        grad_tokens,
        patch_grad,
        small[:3],
        small[3:5],
        small[5],
        grad_cross_query,
        grad_cross_kv,
        grad_cross_out,
        grad_self_qkv.reshape(D // S, 3, -1),
        grad_self_out,
        grad_mlp_up,
        grad_mlp_down,
        grad_decoder,
    )


def solution(mesh):
    return jax.shard_map(
        per_device,
        mesh=mesh,
        in_specs=(
            P(None, "seq", None),
            P(None, "seq", None),
            P(),
            P(),
            P(),
            P(None, "mp"),
            P(None, None, "mp"),
            P("mp", None),
            P(None, None, "mp"),
            P("mp", None),
            P(None, "mp"),
            P("mp", None),
            P(None, "mp", None),
            P(None, None, "seq", None, None),
            P(None, "seq", None),
            P(None, None, "mp", "seq", None),
        ),
        out_specs=(
            P(None, ("seq", "mp"), None),
            P(None, None, "mp", "seq", None),
            P(None, ("seq", "mp"), None),
            P(None, "seq", None),
            P(None, "seq"),
            P(None, "seq"),
            P("seq"),
            P("seq", "mp"),
            P("seq", None, "mp"),
            P("mp", "seq"),
            P("seq", None, "mp"),
            P("mp", "seq"),
            P("seq", "mp"),
            P("mp", "seq"),
            P("seq", "mp", None),
        ),
        check_vma=False,
    )
```

```python
import functools
import math

import jax
import jax.numpy as jnp
from jax import lax
from jax.experimental import pallas as pl
from jax.experimental.pallas import tpu as pltpu
from jax.sharding import PartitionSpec as P


PLANE = 32
HD = 64
LANES = 128
norm_eps = 1e-05
f32 = jnp.float32
bf16 = jnp.bfloat16

NT = (((1,), (1,)), ((), ()))
NN = (((1,), (0,)), ((), ()))
TN = (((0,), (0,)), ((), ()))


def dot(a, b, dims):
    return lax.dot_general(a, b, dims, preferred_element_type=f32)


def mm(a, b):
    return jnp.dot(a, b, preferred_element_type=f32)


def split3(v):
    hi = v.astype(bf16).astype(f32)
    rest = v - hi
    mid = rest.astype(bf16).astype(f32)
    return hi, mid, rest - mid


def spread(base, cols):
    lane = lax.broadcasted_iota(jnp.int32, (base.shape[0], HD), 1)
    tail = jnp.zeros((base.shape[0], HD), f32)
    for at, col in cols.items():
        tail = jnp.where(lane == at, col, tail)
    return jnp.concatenate([base, tail], axis=1).astype(bf16)


def load_keys(n_ref, kv_specs, refs, ka, va, hpd, blocks):
    for ref_at, rows, k_at, v_at, base in kv_specs:
        src = refs[ref_at]

        def build(i, _):
            natural = base + (i ^ n_ref[1]) * rows
            dst = pl.ds(pl.multiple_of(natural, 16), rows)
            slot = natural + lax.broadcasted_iota(jnp.int32, (rows, 1), 0)
            mask = jnp.where(slot < n_ref[0], 0.0, -1e30).astype(f32)
            for h in range(hpd):
                k = src[i, k_at[0] : k_at[0] + rows, k_at[1] + h * HD : k_at[1] + (h + 1) * HD]
                v = src[i, v_at[0] : v_at[0] + rows, v_at[1] + h * HD : v_at[1] + (h + 1) * HD]
                ka[h, dst, :] = spread(k.astype(f32), {0: 1.0, 1: 1.0, 2: 1.0, 3: mask})
                va[h, dst, :] = spread(v.astype(f32), {0: 1.0, 1: 1.0, 2: 1.0})
            return 0

        lax.fori_loop(0, blocks, build, 0)


def fwd_kernel(n_ref, *refs, n_in, blocks, q_spec, kv_specs, hpd, bq, kc, fixed):
    ins, (o_ref, qa_ref, ka, va) = refs[:n_in], refs[-4:]
    load_keys(n_ref, kv_specs, ins, ka, va, hpd, blocks)
    q_at, rows_q, q_off, q_lane = q_spec

    def build(i, _):
        dst = pl.ds(pl.multiple_of((i ^ n_ref[1]) * rows_q, 16), rows_q)
        for h in range(hpd):
            q = ins[q_at][i, q_off : q_off + rows_q, q_lane + h * HD : q_lane + (h + 1) * HD]
            qa_ref[h, dst, :] = spread(q.astype(f32) * (1.0 / math.sqrt(HD)), {3: 1.0})
        return 0

    lax.fori_loop(0, blocks, build, 0)
    total = ka.shape[1]

    def block(b, _):
        rows = pl.ds(pl.multiple_of(b * bq, bq), bq)

        def chunk(c, carry):
            cols = pl.ds(pl.multiple_of(c * kc, kc), kc)
            out = []
            for h in range(hpd):
                m, acc = carry[h]
                s = dot(qa_ref[h, rows, :], ka[h, cols, :], NT)
                top = jnp.maximum(m, jnp.max(s, axis=1, keepdims=True))
                p = jnp.exp(s - top).astype(bf16)
                out.append((top, acc * jnp.exp(m - top) + dot(p, va[h, cols, :], NN)))
            return tuple(out)

        carry = ((jnp.full((bq, 1), -1e30, f32), jnp.zeros((bq, LANES), f32)),) * hpd
        if fixed:
            for c in range(total // kc):
                carry = chunk(c, carry)
        else:
            carry = lax.fori_loop(0, (n_ref[0] + kc - 1) // kc, chunk, carry)
        outs = []
        for h in range(hpd):
            m, acc = carry[h]
            norm = acc[:, HD : HD + 1]
            outs.append(acc[:, :HD] / norm)
            hi, mid, lo = split3(-(m + jnp.log(norm)))
            qa_ref[h, rows, :] = spread(
                qa_ref[h, rows, :HD].astype(f32), {0: hi, 1: mid, 2: lo, 3: 1.0}
            )
        o_ref[rows, :] = jnp.concatenate(outs, axis=1).astype(bf16)
        return 0

    lax.fori_loop(0, qa_ref.shape[1] // bq, block, 0)


def bwd_kernel(n_ref, *refs, n_in, blocks, do_spec, kv_specs, hpd, bq, kc, fixed):
    ins, (dq_ref, dkv_ref, ka, va, da, dk, dv) = refs[:n_in], refs[-7:]
    qa_ref, do_ref, o_ref = ins[:3]
    load_keys(n_ref, kv_specs, ins, ka, va, hpd, blocks)
    rows_q, do_off = do_spec

    def build(i, _):
        rows = pl.ds(pl.multiple_of(i * rows_q, 16), rows_q)
        for h in range(hpd):
            d = do_ref[i, do_off : do_off + rows_q, h * HD : (h + 1) * HD].astype(f32)
            o = o_ref[rows, h * HD : (h + 1) * HD].astype(f32)
            hi, mid, lo = split3(-jnp.sum(d * o, axis=1, keepdims=True))
            da[h, rows, :] = spread(d, {0: hi, 1: mid, 2: lo})
        return 0

    lax.fori_loop(0, blocks, build, 0)
    dk[...] = jnp.zeros_like(dk)
    dv[...] = jnp.zeros_like(dv)
    total = ka.shape[1]
    steps = total // kc if fixed else (n_ref[0] + kc - 1) // kc

    def block(b, _):
        rows = pl.ds(pl.multiple_of(b * bq, bq), bq)

        def chunk(c, dqs):
            cols = pl.ds(pl.multiple_of(c * kc, kc), kc)
            out = []
            for h in range(hpd):
                k, q, d = ka[h, cols, :], qa_ref[h, rows, :], da[h, rows, :]
                p = jnp.exp(dot(k, q, NT))
                dp = dot(va[h, cols, :], d, NT)
                dv[h, cols, :] += dot(p.astype(bf16), d, NN)
                g = (p * dp).astype(bf16)
                dk[h, cols, :] += dot(g, q, NN)
                out.append(dqs[h] + dot(k, g, TN))
            return tuple(out)

        dqs = lax.fori_loop(0, steps, chunk, (jnp.zeros((LANES, bq), f32),) * hpd)
        dq = jnp.concatenate([v[:HD, :] for v in dqs], axis=0).T
        dq_ref[rows, :] = (dq * (1.0 / math.sqrt(HD))).astype(bf16)
        return 0

    lax.fori_loop(0, qa_ref.shape[1] // bq, block, 0)
    step = total // blocks

    def finish(i, _):
        rows = pl.ds(pl.multiple_of(i * step, 16), step)
        parts = [dk[h, rows, :HD] for h in range(hpd)] + [dv[h, rows, :HD] for h in range(hpd)]
        dkv_ref[rows, :] = jnp.concatenate(parts, axis=1).astype(bf16)
        return 0

    lax.fori_loop(0, blocks, finish, 0)


VM = pl.BlockSpec(memory_space=pltpu.VMEM)
SM = pl.BlockSpec(memory_space=pltpu.SMEM)
AN = pl.BlockSpec(memory_space=pl.ANY)


def fit(rows, most):
    return math.gcd(rows, most)


def attend(limits, ins, blocks, q_spec, kv_specs, total, hpd, fixed, deps=()):
    queries = blocks * q_spec[1]
    kc = fit(total, 1024 if fixed else 512)
    body = functools.partial(
        fwd_kernel,
        n_in=len(ins),
        blocks=blocks,
        q_spec=q_spec,
        kv_specs=kv_specs,
        hpd=hpd,
        bq=fit(queries, 512),
        kc=kc,
        fixed=fixed,
    )
    work = hpd * queries * total
    return pl.pallas_call(
        body,
        out_shape=(
            jax.ShapeDtypeStruct((queries, hpd * HD), bf16),
            jax.ShapeDtypeStruct((hpd, queries, LANES), bf16),
        ),
        in_specs=[SM] + [VM] * len(ins) + [AN] * len(deps),
        out_specs=(VM, VM),
        scratch_shapes=[pltpu.VMEM((hpd, total, LANES), bf16)] * 2,
        compiler_params=pltpu.CompilerParams(vmem_limit_bytes=44 * 2**20),
        cost_estimate=pl.CostEstimate(
            flops=1024 * work, bytes_accessed=16 * queries * hpd * HD, transcendentals=work
        ),
    )(limits, *ins, *deps)


def attend_back(limits, ins, blocks, do_spec, kv_specs, total, hpd, fixed, deps=()):
    queries = blocks * do_spec[0]
    body = functools.partial(
        bwd_kernel,
        n_in=len(ins),
        blocks=blocks,
        do_spec=do_spec,
        kv_specs=kv_specs,
        hpd=hpd,
        bq=fit(queries, 512),
        kc=fit(total, 512),
        fixed=fixed,
    )
    work = hpd * queries * total
    return pl.pallas_call(
        body,
        out_shape=(
            jax.ShapeDtypeStruct((queries, hpd * HD), bf16),
            jax.ShapeDtypeStruct((total, 2 * hpd * HD), bf16),
        ),
        in_specs=[SM] + [VM] * len(ins) + [AN] * len(deps),
        out_specs=(VM, VM),
        scratch_shapes=[pltpu.VMEM((hpd, total, LANES), bf16)] * 2
        + [pltpu.VMEM((hpd, queries, LANES), bf16)]
        + [pltpu.VMEM((hpd, total, LANES), f32)] * 2,
        compiler_params=pltpu.CompilerParams(vmem_limit_bytes=52 * 2**20),
        cost_estimate=pl.CostEstimate(
            flops=2560 * work, bytes_accessed=24 * queries * hpd * HD, transcendentals=work
        ),
    )(limits, *ins, *deps)


def norm_parts(values):
    center = values - jnp.mean(values, axis=-1, keepdims=True)
    scale = lax.rsqrt(jnp.mean(center * center, axis=-1, keepdims=True) + norm_eps)
    return center * scale, scale


def layer_norm(values, gain_row, shift_row):
    return (norm_parts(values)[0] * gain_row + shift_row).astype(bf16)


def norm_back(values, gain_row, grad_out):
    unit, scale = norm_parts(values)
    lifted = grad_out * gain_row
    grad_in = scale * (
        lifted
        - jnp.mean(lifted, axis=-1, keepdims=True)
        - unit * jnp.mean(lifted * unit, axis=-1, keepdims=True)
    )
    gain = jnp.sum(grad_out * unit, axis=0, keepdims=True)
    return grad_in, gain, jnp.sum(grad_out, axis=0, keepdims=True)


def flat(ref):
    return ref[...].reshape(-1, ref.shape[-1])


def joined(ref):
    return jnp.concatenate([ref[i] for i in range(ref.shape[0])], axis=1)


def once(shape, index=None):
    at = (0,) * len(shape) if index is None else index
    return pl.BlockSpec(shape, lambda i: at, pipeline_mode=pl.Buffered(1))


def held(shape):
    return pl.BlockSpec(shape, lambda i: (0,) * len(shape))


def mid_kernel(a_ref, x_ref, norm_ref, wo_ref, wt_ref, x1_ref, n_ref, ac_ref, t_ref):
    @pl.when(pl.program_id(0) == 0)
    def _():
        a = joined(a_ref)
        ac_ref[...] = a
        x1 = x_ref[...].astype(f32) + dot(a, flat(wo_ref), NN)
        x1_ref[...] = x1
        n_ref[...] = layer_norm(x1, norm_ref[0:1, :], norm_ref[1:2, :])

    t_ref[0] = dot(n_ref[...], flat(wt_ref), NT).astype(bf16)


def middle(a, x, norm, w_out, w_triple):
    S, rows, W = a.shape
    D = S * W
    return pl.pallas_call(
        mid_kernel,
        grid=(S,),
        out_shape=(
            jax.ShapeDtypeStruct((rows, D), f32),
            jax.ShapeDtypeStruct((rows, D), bf16),
            jax.ShapeDtypeStruct((rows, D), bf16),
            jax.ShapeDtypeStruct((S, rows, 3 * W), bf16),
        ),
        in_specs=[
            once((S, rows, W)),
            once((rows, D)),
            once((2, D)),
            once(*w_out[1]),
            w_triple[1],
        ],
        out_specs=(
            held((rows, D)),
            held((rows, D)),
            held((rows, D)),
            pl.BlockSpec((1, rows, 3 * W), lambda i: (i, 0, 0)),
        ),
        compiler_params=pltpu.CompilerParams(vmem_limit_bytes=40 * 2**20),
        cost_estimate=pl.CostEstimate(
            flops=8 * rows * D * D, bytes_accessed=8 * D * D + 14 * rows * D, transcendentals=0
        ),
    )(a, x, norm, w_out[0], w_triple[0])


def mlp_kernel(
    at_ref,
    aa_ref,
    ab_ref,
    xa_ref,
    xb_ref,
    ca_ref,
    cb_ref,
    dp_ref,
    norm_ref,
    ws_ref,
    wd_ref,
    *refs,
    steps,
):
    pieces, refs = refs[:steps], refs[steps:]
    n_ref, ac_ref, g_ref, du_ref, x3_ref, pix_ref, e3_ref, d2_ref, e2_ref = refs[:9]
    da_ref, db_ref, sum_ref, x2, d3, acc, back, held_w, sems = refs[9:]
    step = pl.program_id(0)
    R = xa_ref.shape[0]
    S, _, W = aa_ref.shape

    def fetch(i):
        return pltpu.make_async_copy(pieces[i], held_w.at[i % 2], sems.at[i % 2])

    @pl.when(step == 0)
    def _():
        fetch(0).start()
        for rows, a_ref, x_ref, c_ref in (
            (slice(0, R), aa_ref, xa_ref, ca_ref),
            (slice(R, x2.shape[0]), ab_ref, xb_ref, cb_ref),
        ):
            a = joined(a_ref)
            ac_ref[rows, :] = a
            x = x_ref[...] + dot(a, flat(ws_ref), NN)
            x2[rows, :] = x
            n_ref[rows, :] = layer_norm(x, norm_ref[0:1, :], norm_ref[1:2, :])
            d = c_ref[...].astype(f32) + dot(dp_ref[rows, :], flat(wd_ref), NN)
            d3[rows, :] = d
            e3_ref[rows, :] = d.astype(bf16)
        acc[...] = jnp.zeros_like(acc)
        back[...] = jnp.zeros_like(back)

    for i in range(steps):

        @pl.when(step == i)
        def _():
            fetch(i).wait()
            if i + 1 < steps:
                fetch(i + 1).start()

    part = held_w.shape[1] // 2
    up = held_w[step % 2, :part, :]
    down = held_w[step % 2, part:, :]
    u = dot(n_ref[...], up, NT)
    slope = math.sqrt(2.0 / math.pi)
    square = u * u
    bend = jnp.tanh(slope * u * (1.0 + 0.044715 * square))
    half = 0.5 * (1.0 + bend)
    g = (u * half).astype(bf16)
    rise = half + 0.5 * slope * u * (1.0 - bend * bend) * (1.0 + 0.134145 * square)
    du = (dot(e3_ref[...], down, NT) * rise).astype(bf16)
    g_ref[...] = g
    du_ref[...] = du
    acc[...] += dot(g, down, NN)
    back[...] += dot(du, up, NN)

    @pl.when(step == steps - 1)
    def _():
        x3 = (x2[...] + acc[...]).astype(bf16)
        x3_ref[...] = x3
        pix_ref[...] = dot(x3, flat(wd_ref), NT).astype(bf16)
        grad_in, gain, shift = norm_back(x2[...], norm_ref[0:1, :], back[...])
        d2 = d3[...] + grad_in
        d2_ref[...] = d2
        e2 = d2.astype(bf16)
        e2_ref[...] = e2
        sum_ref[...] = jnp.concatenate([gain, shift], axis=0)
        da = dot(e2, flat(ws_ref), NT).astype(bf16)
        for i in range(S):
            da_ref[i] = da[:R, i * W : (i + 1) * W]
            db_ref[i] = da[R:, i * W : (i + 1) * W]


def feed_forward(at, a, x1, cot, d_pix, norm, w_out, w_dec, pieces):
    S, R, W = a[0].shape
    RB = a[1].shape[1]
    D, total, pixels = S * W, R + RB, d_pix.shape[1]
    steps = len(pieces)
    part = pieces[0].shape[0] // 2
    hidden = steps * part
    row = jax.ShapeDtypeStruct((total, D), bf16)
    wide = jax.ShapeDtypeStruct((total, hidden), bf16)

    def const(shape, index=None):
        place = (0,) * len(shape) if index is None else index
        return pl.BlockSpec(shape, lambda i, at: place, pipeline_mode=pl.Buffered(1))

    def keep(shape):
        return pl.BlockSpec(shape, lambda i, at: (0,) * len(shape))

    blocked = pl.BlockSpec(
        (total, part), lambda i, at: (0, (at[0] ^ (i // 2)) * 2 + (at[1] ^ (i % 2)))
    )
    full = keep((total, D))
    return pl.pallas_call(
        functools.partial(mlp_kernel, steps=steps),
        grid_spec=pltpu.PrefetchScalarGridSpec(
            num_scalar_prefetch=1,
            grid=(steps,),
            in_specs=[
                const((S, R, W)),
                const((S, RB, W)),
                const((R, D)),
                const((RB, D)),
                const((R, D)),
                const((RB, D)),
                const((total, pixels)),
                const((2, D)),
                const(*w_out[1]),
                const(*w_dec[1]),
            ]
            + [AN] * steps,
            out_specs=(
                full,
                full,
                blocked,
                blocked,
                full,
                keep((total, pixels)),
                full,
                full,
                full,
                keep((S, R, W)),
                keep((S, RB, W)),
                keep((2, D)),
            ),
            scratch_shapes=[pltpu.VMEM((total, D), f32)] * 4
            + [pltpu.VMEM((2,) + pieces[0].shape, bf16), pltpu.SemaphoreType.DMA((2,))],
        ),
        out_shape=(
            row,
            row,
            wide,
            wide,
            row,
            jax.ShapeDtypeStruct((total, pixels), bf16),
            row,
            jax.ShapeDtypeStruct((total, D), f32),
            row,
            jax.ShapeDtypeStruct((S, R, W), bf16),
            jax.ShapeDtypeStruct((S, RB, W), bf16),
            jax.ShapeDtypeStruct((2, D), f32),
        ),
        compiler_params=pltpu.CompilerParams(vmem_limit_bytes=60 * 2**20),
        cost_estimate=pl.CostEstimate(
            flops=8 * total * D * hidden + 8 * total * D * D,
            bytes_accessed=4 * D * hidden + 30 * total * D,
            transcendentals=total * hidden,
        ),
    )(at, *a, *x1, *cot, d_pix, norm, w_out[0], w_dec[0], *pieces)


def pack_kernel(at_ref, up_ref, down_ref, *refs):
    out_ref = refs[-1]
    half = out_ref.shape[0] // 2
    odd = at_ref[0] == 1
    up = jnp.where(odd, up_ref[:, half:], up_ref[:, :half])
    out_ref[:half, :] = up.T
    out_ref[half:, :] = down_ref[pl.ds(pl.multiple_of(at_ref[0] * half, 16), half), :]


def pack(core, up, down, deps):
    return pl.pallas_call(
        pack_kernel,
        out_shape=jax.ShapeDtypeStruct(down.shape, bf16),
        in_specs=[SM, VM, VM] + [AN] * len(deps),
        out_specs=VM,
        compiler_params=pltpu.CompilerParams(vmem_limit_bytes=24 * 2**20),
        cost_estimate=pl.CostEstimate(
            flops=0, bytes_accessed=6 * down.size, transcendentals=0
        ),
    )(core.reshape(1), up, down, *deps)


def hold_kernel(x_ref, *refs):
    refs[-1][...] = x_ref[...]


def hold(value, deps):
    return pl.pallas_call(
        hold_kernel,
        out_shape=jax.ShapeDtypeStruct(value.shape, value.dtype),
        in_specs=[VM] + [AN] * len(deps),
        out_specs=VM,
        cost_estimate=pl.CostEstimate(
            flops=0, bytes_accessed=2 * value.size * value.dtype.itemsize, transcendentals=0
        ),
        compiler_params=pltpu.CompilerParams(vmem_limit_bytes=16 * 2**20),
    )(value, *deps)


def mlp_grads_kernel(at_ref, n_ref, e_ref, g_ref, du_ref, *refs, ranks, cores, shares):
    more, (outs, n_t, e_t) = refs[: -ranks - 2], (refs[-ranks - 2 : -2], refs[-2], refs[-1])
    odd = (at_ref[1] ^ cores) == 1
    W = n_ref.shape[1] // shares
    for src, dst in ((n_ref, n_t), (e_ref, e_t)):
        for i in range(shares // 2):
            both = src[:, 2 * i * W : (2 * i + 2) * W]
            dst[i * W : (i + 1) * W, :] = jnp.where(odd, both[:, W:], both[:, :W]).T
    part = g_ref.shape[1] // ranks
    for step in range(ranks):
        cols = pl.ds(pl.multiple_of((at_ref[0] ^ step) * part, 128), part)
        up, down = dot(n_t[...], du_ref[:, cols], NN), dot(e_t[...], g_ref[:, cols], NN)
        if more:
            up += more[step][:, :part].astype(f32)
            down += more[step][:, part:].astype(f32)
        outs[step][:, :part] = up.astype(bf16)
        outs[step][:, part:] = down.astype(bf16)


def mlp_grads(at, n3, e3, g, du, ranks, shares, cores, more=()):
    total, D = n3.shape
    hidden = g.shape[1]
    shape = (D // 2, 2 * hidden // ranks)
    return pl.pallas_call(
        functools.partial(mlp_grads_kernel, ranks=ranks, cores=cores, shares=shares),
        out_shape=(jax.ShapeDtypeStruct(shape, bf16),) * ranks,
        in_specs=[SM] + [VM] * (4 + len(more)),
        out_specs=(VM,) * ranks,
        scratch_shapes=[pltpu.VMEM((D // 2, total), bf16)] * 2,
        compiler_params=pltpu.CompilerParams(vmem_limit_bytes=56 * 2**20),
        cost_estimate=pl.CostEstimate(
            flops=2 * total * D * hidden, bytes_accessed=4 * total * hidden + 2 * D * hidden, transcendentals=0
        ),
    )(at, n3, e3, g, du, *more)


def back_kernel(
    t_ref, x_ref, d_ref, norm_ref, wo_ref, wt_ref, *refs, steps
):
    d1_ref, e_ref, da_ref, sum_ref, acc = refs[-5:]
    step = pl.program_id(0)
    part = dot(t_ref[0], flat(wt_ref), NN)

    @pl.when(step == 0)
    def _():
        acc[...] = part

    @pl.when(step > 0)
    def _():
        acc[...] += part

    @pl.when(step == steps - 1)
    def _():
        grad_in, gain, shift = norm_back(x_ref[...], norm_ref[0:1, :], acc[...])
        d1 = d_ref[...] + grad_in
        d1_ref[...] = d1
        e = d1.astype(bf16)
        e_ref[...] = e
        sum_ref[...] = jnp.concatenate([gain, shift], axis=0)
        da = dot(e, flat(wo_ref), NT).astype(bf16)
        W = da_ref.shape[2]
        for i in range(steps):
            da_ref[i] = da[:, i * W : (i + 1) * W]


def middle_back(t, x1, d2, at, norm, w_out, w_triple, deps=()):
    S, rows, wide = t.shape
    D = x1.shape[1]
    W = wide // 3
    return pl.pallas_call(
        functools.partial(back_kernel, steps=S),
        grid=(S,),
        out_shape=(
            jax.ShapeDtypeStruct((rows, D), f32),
            jax.ShapeDtypeStruct((rows, D), bf16),
            jax.ShapeDtypeStruct((S, rows, W), bf16),
            jax.ShapeDtypeStruct((2, D), f32),
        ),
        in_specs=[
            pl.BlockSpec((1, rows, wide), lambda i: (i, 0, 0)),
            once((rows, D)),
            once((rows, D), (at, 0)),
            once((2, D)),
            once(*w_out[1]),
            w_triple[1],
        ]
        + [AN] * len(deps),
        out_specs=(
            held((rows, D)),
            held((rows, D)),
            held((S, rows, W)),
            held((2, D)),
        ),
        scratch_shapes=[pltpu.VMEM((rows, D), f32)],
        compiler_params=pltpu.CompilerParams(vmem_limit_bytes=40 * 2**20),
        cost_estimate=pl.CostEstimate(
            flops=8 * rows * D * D, bytes_accessed=8 * D * D + 24 * rows * D, transcendentals=0
        ),
    )(t, x1, d2, norm, w_out[0], w_triple[0], *deps)


def grads_kernel(*refs, shape, widths):
    count = sum(shape)
    lefts, rights = refs[:count], refs[count : 2 * count]
    out_ref, turned = refs[2 * count], refs[2 * count + 1 :]

    @pl.when(pl.program_id(0) == 0)
    def _():
        for left, t in zip(lefts, turned):
            t[...] = left[...].T

    at = n = 0
    for pieces, width in zip(shape, widths):
        total = 0.0
        for i in range(n, n + pieces):
            right = joined(rights[i]) if len(rights[i].shape) == 3 else rights[i][...]
            total += dot(turned[i][...], right, NN)
        out_ref[:, at : at + width] = total.astype(bf16)
        at, n = at + width, n + pieces


def weight_grads(terms, ranks):
    pieces = [p for term in terms for p in term]
    shape = [len(term) for term in terms]
    widths = [term[0][1].size // term[0][0].shape[0] // ranks for term in terms]
    D, per = pieces[0][0].shape[1], sum(widths)
    lefts = [p[0] for p in pieces]
    rights = [p[1] for p in pieces]
    work = sum(p[0].shape[0] for p in pieces) * D * per * ranks // len(pieces)
    return pl.pallas_call(
        functools.partial(grads_kernel, shape=shape, widths=widths),
        grid=(ranks,),
        out_shape=jax.ShapeDtypeStruct((D, per * ranks), bf16),
        in_specs=[once(v.shape) for v in lefts]
        + [
            pl.BlockSpec((v.shape[0] // ranks,) + v.shape[1:], lambda i: (i, 0, 0))
            if v.ndim == 3
            else pl.BlockSpec((v.shape[0], v.shape[1] // ranks), lambda i: (0, i))
            for v in rights
        ],
        out_specs=pl.BlockSpec((D, per), lambda i: (0, i)),
        scratch_shapes=[pltpu.VMEM(v.shape[::-1], bf16) for v in lefts],
        compiler_params=pltpu.CompilerParams(vmem_limit_bytes=56 * 2**20),
        cost_estimate=pl.CostEstimate(
            flops=2 * work, bytes_accessed=4 * D * per * ranks, transcendentals=0
        ),
    )(*lefts, *rights)


def start_kernel(at_ref, xa_ref, xb_ref, norm_ref, wk_ref, wq_in, *refs, pieces, width):
    p_in, (q_ref, k_ref, n_ref, wq_ref, wkv_ref) = refs[:pieces], refs[pieces:]
    seq = at_ref[0]
    R = xa_ref.shape[0]
    W = q_ref.shape[2]
    wq_ref[...] = flat(wq_in)
    wkv_ref[...] = flat(wk_ref)[:, :width]
    for block, x_ref in ((slice(0, R), xa_ref), (slice(R, n_ref.shape[0]), xb_ref)):
        n_ref[block, :] = layer_norm(x_ref[...].astype(f32), norm_ref[0:1, :], norm_ref[1:2, :])
    for i in range(pieces):
        q_ref[i] = dot(n_ref[...], wq_ref[i * W : (i + 1) * W, :], NT).astype(bf16)
    own = wkv_ref[pl.ds(pl.multiple_of(seq * 2 * W, 16), 2 * W), :]
    for i in range(pieces):
        k_ref[seq ^ i] = dot(p_in[i][...], own, NT).astype(bf16)


def start(at, x0, norm, w_kv, w_query, patch_pieces, W):
    S, D = len(patch_pieces), x0[0].shape[1]
    total = x0[0].shape[0] + x0[1].shape[0]
    slots, width = patch_pieces[0].shape
    whole = [x0[0].shape, x0[1].shape, norm.shape]
    outs = [(S, total, W), (S, slots, 2 * W), (total, D), (D, D), (2 * D, width)]
    return pl.pallas_call(
        functools.partial(start_kernel, pieces=S, width=width),
        grid=(1,),
        out_shape=tuple(jax.ShapeDtypeStruct(v, bf16) for v in outs),
        in_specs=[SM]
        + [once(v) for v in whole]
        + [once(*w_kv[1]), once(*w_query[1])]
        + [once((slots, width))] * S,
        out_specs=tuple(held(v) for v in outs),
        compiler_params=pltpu.CompilerParams(vmem_limit_bytes=56 * 2**20),
        cost_estimate=pl.CostEstimate(
            flops=2 * total * D * D + 4 * S * slots * width * W,
            bytes_accessed=6 * D * D + 12 * total * D,
            transcendentals=0,
        ),
    )(at, *x0, norm, w_kv[0], w_query[0], *patch_pieces)


def finish_kernel(at_ref, qa_ref, qb_ref, ka_ref, kb_ref, *refs, pieces):
    n_in, p_in, out_ref = refs[:pieces], refs[pieces:-1], refs[-1]
    seq = at_ref[0]
    R, slots, W = qa_ref.shape[1], ka_ref.shape[1], qa_ref.shape[2]
    by_q, by_kv = 0.0, 0.0
    for i in range(pieces):
        j = seq ^ i
        by_q += dot(qa_ref[j], n_in[i][:R, :], TN) + dot(qb_ref[j], n_in[i][R:, :], TN)
        by_kv += dot(ka_ref[j], p_in[i][:slots, :], TN) + dot(kb_ref[j], p_in[i][slots:, :], TN)
    grad = by_q.T.astype(bf16)
    rows = grad.shape[0] // pieces
    wide = by_kv.shape[1] // pieces
    grad_k, grad_v = by_kv[:W].T.astype(bf16), by_kv[W:].T.astype(bf16)
    for i in range(pieces):
        out_ref[i, :rows, :] = grad[i * rows : (i + 1) * rows, :]
        out_ref[i, rows : rows + wide, :] = grad_k[i * wide : (i + 1) * wide, :]
        out_ref[i, rows + wide :, :] = grad_v[i * wide : (i + 1) * wide, :]


def finish(at, dq, dkv, n_pieces, patch_pieces):
    S, _, W = dq[0].shape
    D, width = n_pieces[0].shape[1], patch_pieces[0].shape[1]
    rows = D // S + 2 * width // S
    return pl.pallas_call(
        functools.partial(finish_kernel, pieces=S),
        out_shape=jax.ShapeDtypeStruct((S, rows, W), bf16),
        in_specs=[SM] + [VM] * (4 + 2 * S),
        out_specs=VM,
        compiler_params=pltpu.CompilerParams(vmem_limit_bytes=48 * 2**20),
        cost_estimate=pl.CostEstimate(
            flops=3 * 10**9, bytes_accessed=18 * 10**6, transcendentals=0
        ),
    )(at, *dq, *dkv, *n_pieces, *patch_pieces)


CP = 32


def place(perm, toks, TR, TC):
    own, ext = TR * TC, perm.shape[2]
    tok = lax.broadcasted_iota(jnp.int32, (toks, 1), 0)
    row = jnp.where(tok < own, tok // TC, jnp.where(tok < own + TR, tok - own, TR))
    col = jnp.where(
        tok < own, tok % TC, jnp.where(tok < own + TR, TC, tok - own - TR)
    )
    real = tok <= own + TR + TC
    pixel = lax.broadcasted_iota(jnp.int32, (toks, ext), 1)
    for a in range(2):
        for b in range(2):
            ok = real & ((row < TR) | (a == 0)) & ((col < TC) | (b == 0))
            at = jnp.where(ok, (2 * row + a) * (2 * TC + 1) + 2 * col + b, -1)
            perm[2 * a + b] = jnp.where(pixel == at, 1.0, 0.0).astype(bf16)


def pixel_grad_kernel(cot_ref, w_ref, out_ref, perm, *, TR, TC):
    @pl.when(pl.program_id(0) == 0)
    def _():
        place(perm, out_ref.shape[1], TR, TC)

    grad = dot(cot_ref[0], w_ref[0], NT)
    hi = grad.astype(bf16)
    lo = (grad - hi.astype(f32)).astype(bf16)
    parts = [dot(perm[i], hi, NT) + dot(perm[i], lo, NT) for i in range(4)]
    out_ref[0] = jnp.concatenate(parts, axis=1)


def pixel_sample_kernel(x_ref, w_ref, out_ref, perm, *, TR, TC):
    @pl.when(pl.program_id(0) == 0)
    def _():
        place(perm, x_ref.shape[1], TR, TC)

    x = x_ref[0]
    window = sum(dot(x[:, i * CP : (i + 1) * CP], perm[i], TN) for i in range(4))
    out_ref[0] = dot(window.astype(bf16), w_ref[0], NN).astype(bf16)


def per_plane(body, first, weights, out_rows, out_lanes, out_type, toks, TR, TC):
    planes, ext, samples = weights.shape

    def whole(shape):
        return pl.BlockSpec((1,) + shape, lambda i: (i, 0, 0))

    return pl.pallas_call(
        functools.partial(body, TR=TR, TC=TC),
        grid=(planes,),
        out_shape=jax.ShapeDtypeStruct((planes, out_rows, out_lanes), out_type),
        in_specs=[whole(first.shape[1:]), whole((ext, samples))],
        out_specs=whole((out_rows, out_lanes)),
        scratch_shapes=[pltpu.VMEM((4, toks, ext), bf16)],
        compiler_params=pltpu.CompilerParams(vmem_limit_bytes=24 * 2**20),
        cost_estimate=pl.CostEstimate(
            flops=6 * 10**8, bytes_accessed=7 * 10**6, transcendentals=0
        ),
    )(first, weights)


def swap_seq(value):
    return lax.all_to_all(value, "seq", split_axis=0, concat_axis=0, tiled=True)


def swap_mp(value):
    return lax.all_to_all(value, "mp", split_axis=0, concat_axis=0, tiled=True)


def swap_all(value):
    return lax.all_to_all(value, ("seq", "mp"), split_axis=0, concat_axis=0, tiled=True)


def swap_pair(value):
    count = lax.axis_size("mp")
    return lax.ppermute(value, "mp", [(i, i ^ 1) for i in range(count)])


def gather_rows(piece):
    return lax.all_gather(piece, ("mp", "seq"), axis=0, tiled=False)


def bundle_part(bundle, at, rows):
    pieces, _, D = bundle.shape
    if rows % 16 == 0 and at % rows == 0:
        return bundle, ((pieces, rows, D), (0, at // rows, 0))
    value = bundle[:, at : at + rows].reshape(1, -1, D)
    return value, (value.shape, None)


def by_step(part, steps):
    (pieces, rows, D), at = part[1]
    if pieces > 1:
        return part[0], pl.BlockSpec((pieces // steps, rows, D), lambda i: (i, at[1], 0))
    return part[0], pl.BlockSpec((1, rows // steps, D), lambda i: (0, i, 0))


def reduce_rows(value):
    return lax.psum_scatter(value, "seq", scatter_dimension=0, tiled=True)


def from_ranks(blocks):
    ranks, rank = lax.axis_size("mp"), lax.axis_index("mp")
    got = []
    for step in range(ranks):
        block = lax.dynamic_index_in_dim(blocks, rank ^ step, 0, keepdims=False)
        if step > 0:
            block = lax.ppermute(block, "mp", [(i, i ^ step) for i in range(ranks)])
        got.append(block)
    return got


def in_order(got, at):
    got = jnp.stack(got)
    return [lax.dynamic_index_in_dim(got, at ^ i, 0, keepdims=False) for i in range(got.shape[0])]


def sum_ranks(value):
    return lax.psum_scatter(value, "mp", scatter_dimension=1, tiled=True).astype(f32)


def gather_pieces(value):
    shares = lax.axis_size("seq")
    pieces = []
    for step in range(0, shares, 2):
        moves = [(i, i ^ step) for i in range(shares)]
        pieces.append(value if step == 0 else lax.ppermute(value, "seq", moves))
    cores = [(i, i ^ 1) for i in range(shares)]
    return [p for piece in pieces for p in (piece, lax.ppermute(piece, "seq", cores))]


def own_blocks(whole, blocks):
    ranks, rank = lax.axis_size("mp"), lax.axis_index("mp")
    pairs = ranks // 2
    pair = rank // 2
    own = whole.shape[0] // ranks
    whole = in_order(from_ranks(whole.reshape(ranks, own, -1)), rank)
    blocks = blocks.reshape(pairs, own, -1)
    arrived = []
    for step in range(pairs):
        moves = [(2 * p + h, pairs * h + (p ^ step)) for p in range(pairs) for h in range(2)]
        block = lax.dynamic_index_in_dim(blocks, pair ^ step, 0, keepdims=False)
        arrived.append(lax.ppermute(block, "mp", moves))
    arrived = in_order(arrived, rank % pairs)
    rows = []
    for p in range(pairs):
        rows += [whole[2 * p], arrived[p], whole[2 * p + 1]]
    return jnp.stack(rows)


def to_rows(value):
    return swap_seq(value).transpose(1, 0, 2).reshape(value.shape[1], -1)


def per_device(
    tokens,
    patches,
    counts,
    norm_gains,
    norm_shifts,
    cross_query,
    cross_kv,
    cross_out,
    self_qkv,
    self_out,
    mlp_up,
    mlp_down,
    decoder,
    sample_weights,
    tokens_cot,
    sample_cot,
):
    objects, R, D = tokens.shape
    S, M = lax.axis_size("seq"), lax.axis_size("mp")
    s, m = lax.axis_index("seq"), lax.axis_index("mp")
    pairs = M // 2
    if objects != 3 * pairs or S != 2 * M or D % (HD * S) != 0:
        raise ValueError("unexpected sizes")
    pair, half = m // 2, m % 2
    at_a, at_b = 3 * pair + 2 * half, 3 * pair + 1
    RB = R // 2
    RS = R + RB
    rows = [R, RB]
    W = D // S
    hpd = W // HD
    slots, width = patches.shape[1], patches.shape[2]
    slot_total = slots * S
    row_total = R * S

    def pick(arr):
        whole = lax.dynamic_index_in_dim(arr, at_b, 0, keepdims=False)
        return [
            lax.dynamic_index_in_dim(arr, at_a, 0, keepdims=False),
            lax.dynamic_slice_in_dim(whole, half * RB, RB, 0),
        ]

    def mine(arr, axis):
        share = arr.shape[axis] // S
        return lax.dynamic_slice_in_dim(arr, s * share, share, axis)

    channels = decoder.shape[1]
    local_dec = jnp.pad(decoder.transpose(2, 1, 0), ((0, 0), (0, CP - channels), (0, 0)))
    local_qkv = self_qkv.reshape(D, 3, 2, W).transpose(2, 1, 3, 0).reshape(-1, D)
    local_kv = cross_kv.reshape(width, 2, 2, W).transpose(2, 1, 3, 0).reshape(-1, width)
    per = D // (S * M)
    dec_rows = 4 * CP // S
    kv_rows = 2 * per
    local_kv = jnp.pad(local_kv, ((0, 0), (0, D - width)))
    lead = gather_rows(jnp.concatenate([mine(local_kv, 0), mine(cross_query, 1).T], axis=0))
    w_kv, w_query = bundle_part(lead, 0, kv_rows), bundle_part(lead, kv_rows, per)
    first = gather_rows(
        jnp.concatenate(
            [
                mine(local_qkv, 0),
                mine(cross_out, 0),
                mine(self_out, 0),
                mine(local_dec.reshape(-1, D), 0),
            ],
            axis=0,
        )
    )
    w_triple = by_step(bundle_part(first, 0, 3 * per), S)
    w_cross_out = bundle_part(first, 3 * per, per)
    w_self_out = bundle_part(first, 4 * per, per)
    w_dec = bundle_part(first, 5 * per, dec_rows)

    x0 = pick(tokens)
    norms = [jnp.stack([norm_gains[i], norm_shifts[i]]) for i in range(3)]
    at = jnp.stack([s, m])
    both = [lax.dynamic_index_in_dim(patches, o, 0, keepdims=False) for o in (at_a, at_b)]
    patch_pieces = gather_pieces(jnp.concatenate(both, axis=0))
    q1, keys_one, n1, w_query, w_kv = start(at, x0, norms[0], w_kv, w_query, patch_pieces, W)
    heads_one = swap_seq(q1)
    core = s % 2
    cores = [(i, i ^ 1) for i in range(S)]
    mlp = pack(core, mlp_up, mlp_down, [q1])
    mlp_pieces = []
    for step in range(M):
        moves = [(i, i ^ step) for i in range(M)]
        one = mlp if step == 0 else lax.ppermute(mlp, "mp", moves)
        mlp_pieces += [one, lax.ppermute(one, "seq", cores)]

    TC = PLANE // 4
    TR = PLANE * 4 // S
    own, rim = TR * TC, TR * TC + TR
    toks = -(-(rim + TC + 1) // 32) * 32
    planes = objects * 3
    weights_in = sample_weights.reshape(planes, *sample_weights.shape[3:])
    cot_in = sample_cot.reshape(planes, channels, -1)
    cot_in = jnp.pad(cot_in, ((0, 0), (0, CP - channels), (0, 0)))
    ext = per_plane(pixel_grad_kernel, cot_in, weights_in, toks, 4 * CP, f32, toks, TR, TC)
    ways = {
        1: [i for i in range(S) if i % 4 != 3],
        4: [i for i in range(S) if i + 4 < S],
        5: [i for i in range(S) if i % 4 != 3 and i + 4 < S],
    }
    rights = lax.ppermute(ext[:, own:rim], "seq", [(i, i + 1) for i in ways[1]])
    belows = lax.ppermute(ext[:, rim : rim + TC], "seq", [(i, i + 4) for i in ways[4]])
    corner = lax.ppermute(ext[:, rim + TC : rim + TC + 1], "seq", [(i, i + 5) for i in ways[5]])
    grid = ext[:, :own].reshape(planes, TR, TC, -1)
    belows = jnp.concatenate([belows[:, :1] + corner, belows[:, 1:]], axis=1)
    grid = grid + jnp.pad(rights[:, :, None], ((0, 0), (0, 0), (0, TC - 1), (0, 0)))
    grid = grid + jnp.pad(belows[:, None], ((0, 0), (0, TR - 1), (0, 0), (0, 0)))
    KA, KB = R // S, RB // S
    cu = 4 * CP
    grad_pix = grid.astype(bf16).reshape(pairs, 3, S, KA, cu)
    gp_a = jnp.stack([grad_pix[:, 0], grad_pix[:, 2]], axis=1).transpose(2, 0, 1, 3, 4)
    gp_b = grad_pix[:, 1].reshape(pairs, S, 2, KB, cu).transpose(1, 0, 2, 3, 4)
    sent = jnp.concatenate([gp_a, gp_b], axis=3).reshape(S * M, KA + KB, cu)
    back = swap_all(sent).reshape(S, M, KA + KB, cu).transpose(2, 0, 1, 3)
    d_pix = back.reshape(RS, M * cu)

    limits = [
        jnp.stack([lax.dynamic_index_in_dim(counts, o, 0, keepdims=False), jnp.int32(0)])
        for o in (at_a, at_b)
    ]
    kv_one = [(slots, (i * slots, 0), (i * slots, W), 0) for i in range(2)]
    o1, res1 = [], []
    for i in range(2):
        out, res = attend(
            limits[i],
            [heads_one, keys_one],
            S,
            (0, rows[i], i * R, 0),
            [(1,) + kv_one[i]],
            slot_total,
            hpd,
            False,
        )
        o1.append(out)
        res1.append(res)

    mids = [
        middle(swap_seq(o1[i].reshape(S, rows[i], W)), x0[i], norms[1], w_cross_out, w_triple)
        for i in range(2)
    ]
    x1, n2, a1, t2 = zip(*mids)

    heads_two = [swap_seq(v) for v in t2]
    pair_kv = swap_pair(heads_two[1][:, :, W:])
    wide = jnp.array([row_total, 0], jnp.int32)
    kv_a2 = (R, (0, W), (0, 2 * W), 0)
    kv_b2 = (RB, (0, W), (0, 2 * W), 0)
    kv_p2 = (RB, (0, 0), (0, W), row_total // 2)
    o_a2, res_a2 = attend(
        wide, [heads_two[0]], S, (0, R, 0, 0), [(0,) + kv_a2], row_total, hpd, True
    )
    o_b2, res_b2 = attend(
        wide,
        [heads_two[1], pair_kv],
        S,
        (0, RB, 0, 0),
        [(0,) + kv_b2, (1,) + kv_p2],
        row_total,
        hpd,
        True,
        [o_a2],
    )
    a2 = [swap_seq(o_a2.reshape(S, R, W)), swap_seq(o_b2.reshape(S, RB, W))]

    place = jnp.stack([m, core])
    n3, a2, g, du, x3b, pix, e3, d2, e2, da2_a, da2_b, sums_three = feed_forward(
        place, a2, x1, pick(tokens_cot), d_pix, norms[2], w_self_out, w_dec, mlp_pieces
    )

    da2 = [swap_seq(da2_a), swap_seq(da2_b)]
    given = mlp_grads(place, n3, e3, g, du, M, S, 1)
    given = [lax.ppermute(v, "seq", cores) for v in given]
    n1_late = hold(n1, da2)
    sent = mlp_grads(place, n3, e3, g, du, M, S, 0, given)
    by_rank = [sent[0]]
    for step in range(1, M):
        by_rank.append(lax.ppermute(sent[step], "mp", [(i, i ^ step) for i in range(M)]))
    dq_a2, dkv_a2 = attend_back(
        wide,
        [res_a2, da2[0], o_a2, heads_two[0]],
        S,
        (R, 0),
        [(3,) + kv_a2],
        row_total,
        hpd,
        True,
        [sent[0]],
    )
    grads_one = weight_grads([[(e2, a2)], [(x3b, d_pix)]], M)
    grads_one = reduce_rows(grads_one)
    n_pieces = gather_pieces(n1_late)
    tokens_out = own_blocks(x3b[:R], x3b[R:])
    pix = pix.reshape(KA + KB, S, M, cu).transpose(1, 2, 0, 3)
    got = swap_all(pix.reshape(S * M, KA + KB, cu)).reshape(S, pairs, 2, KA + KB, cu)
    dq_b2, dkv_b2 = attend_back(
        wide,
        [res_b2, da2[1], o_b2, heads_two[1], pair_kv],
        S,
        (RB, 0),
        [(3,) + kv_b2, (4,) + kv_p2],
        row_total,
        hpd,
        True,
        [dq_a2, tokens_out, got] + n_pieces[::2],
    )
    kept, given = dkv_b2[: row_total // 2], dkv_b2[row_total // 2 :]
    dkv_b2 = (kept.astype(f32) + swap_pair(given).astype(f32)).astype(bf16)
    dt2 = [
        swap_seq(jnp.concatenate([dq_a2, dkv_a2], axis=1).reshape(S, R, 3 * W)),
        swap_seq(jnp.concatenate([dq_b2, dkv_b2], axis=1).reshape(S, RB, 3 * W)),
    ]
    def below(i, deps):
        return middle_back(
            dt2[i], x1[i], d2, (0, R // RB)[i], norms[1], w_cross_out, w_triple, deps
        )

    def cross_back(i, da1, deps):
        dq, dkv = attend_back(
            limits[i],
            [res1[i], da1, o1[i], keys_one],
            S,
            (rows[i], 0),
            [(3,) + kv_one[i]],
            slot_total,
            hpd,
            False,
            deps,
        )
        return dq.reshape(S, rows[i], W), dkv.reshape(S, slots, 2 * W)

    low_a = below(0, [])
    mlp_sum = sum(v.astype(f32) for v in by_rank).astype(bf16).reshape(S // 2, D // S, -1)
    cross_a = cross_back(0, swap_seq(low_a[2]), [grads_one, mlp_sum] + n_pieces[1::2])
    by_chip = []
    for step in range(0, S, 2):
        block = lax.dynamic_index_in_dim(mlp_sum, (s ^ step) // 2, 0, keepdims=False)
        if step > 0:
            block = lax.ppermute(block, "seq", [(i, i ^ step) for i in range(S)])
        by_chip.append(block)
    mlp_sum = sum(v.astype(f32) for v in by_chip)
    low_b = below(1, [cross_a[0]])
    d1, e1, da1, sums_two = zip(low_a, low_b)

    px_a = got[:, :, :, :KA].transpose(1, 2, 0, 3, 4).reshape(pairs, 2, S * KA, cu)
    px_b = got[:, :, :, KA:].transpose(1, 0, 2, 3, 4).reshape(pairs, S * KA, cu)
    tile = jnp.stack([px_a[:, 0], px_b, px_a[:, 1]], axis=1).reshape(planes, TR, TC, cu)
    rights = lax.ppermute(tile[:, :, 0], "seq", [(i + 1, i) for i in ways[1]])
    belows = lax.ppermute(tile[:, 0], "seq", [(i + 4, i) for i in ways[4]])
    corner = lax.ppermute(tile[:, 0, :1], "seq", [(i + 5, i) for i in ways[5]])
    fill = jnp.zeros((planes, toks - rim - TC - 1, cu), bf16)
    ext = jnp.concatenate([tile.reshape(planes, own, cu), rights, belows, corner, fill], axis=1)
    sampled = per_plane(
        pixel_sample_kernel, ext, weights_in, CP, weights_in.shape[2], bf16, toks, TR, TC
    )
    sampled = sampled[:, :channels].reshape(objects, 3, channels, 1, -1)

    grads_two = weight_grads(
        [[(n2[i], dt2[i]) for i in range(2)], [(e1[i], a1[i]) for i in range(2)]], M
    )
    cross_b = cross_back(1, swap_seq(da1[1]), [grads_two, sampled])
    dq1, dkv1 = zip(cross_a, cross_b)
    grads_two = reduce_rows(grads_two)

    parts = [mm(to_rows(v), w_kv).astype(bf16) for v in dkv1]
    every = [[p] for p in parts]
    for step in range(1, M):
        moves = [(i, i ^ step) for i in range(M)]
        for i in range(2):
            every[i].append(lax.ppermute(parts[i], "mp", moves))
    from_a, from_b = [in_order(v, m) for v in every]
    patch_grad = []
    for p in range(pairs):
        shared = from_b[2 * p].astype(f32) + from_b[2 * p + 1].astype(f32)
        patch_grad += [from_a[2 * p].astype(f32), shared, from_a[2 * p + 1].astype(f32)]
    patch_grad = jnp.stack(patch_grad)

    grads = [mm(to_rows(v), w_query) for v in dq1]
    back_one = [norm_back(x0[i].astype(f32), norm_gains[0], grads[i]) for i in range(2)]
    d0 = [(d1[i] + back_one[i][0]).astype(bf16) for i in range(2)]
    grad_tokens = own_blocks(d0[0], d0[1]).astype(f32)

    order = 2 * m + s % 2
    by_head = finish(at, dq1, dkv1, n_pieces, patch_pieces)
    sums = [0.0, 0.0]
    for step in range(S):
        moves = []
        for i in range(S):
            for j in range(M):
                t = i ^ step
                moves.append(((2 * j + t % 2) * M + t // 2, i * M + j))
        piece = lax.dynamic_index_in_dim(by_head, order ^ step, 0, keepdims=False)
        sums[step % 2] += lax.ppermute(piece, ("seq", "mp"), moves).astype(f32)
    swap = s % 2 == 1
    owned = jnp.concatenate(
        [jnp.where(swap, sums[1], sums[0]), jnp.where(swap, sums[0], sums[1])], axis=1
    )
    grad_cross_query = owned[: D // S]
    grad_cross_kv = owned[D // S :].reshape(2, width // S, 2 * W).transpose(1, 0, 2)

    grads_one, grads_two = sum_ranks(grads_one), sum_ranks(grads_two)
    ff = g.shape[1] // M
    grad_mlp_up, grad_mlp_down = mlp_sum[:, :ff], mlp_sum[:, ff:].T
    grad_self_out = grads_one[:, : D // M].T
    grad_decoder = grads_one[:, D // M :]
    grad_decoder = grad_decoder.reshape(D // S, 4, CP)[:, :, :channels].transpose(0, 2, 1)
    grad_self_qkv = grads_two[:, : 3 * D // M].reshape(D // S, 2, 3, W).transpose(0, 2, 1, 3)
    grad_cross_out = grads_two[:, 3 * D // M :].T

    one = [back_one[0][i] + back_one[1][i] for i in (1, 2)]
    two = sums_two[0] + sums_two[1]
    small = jnp.concatenate(
        [one[0], two[:1], sums_three[:1], one[1], two[1:], sums_three[1:]], axis=0
    )
    small = jnp.sum(swap_seq(small.reshape(6, S, D // S).transpose(1, 0, 2)), axis=0)
    small = sum(from_ranks(jnp.broadcast_to(small, (M,) + small.shape)))

    return (
        tokens_out,
        sampled,
        grad_tokens,
        patch_grad,
        small[:3],
        small[3:5],
        small[5],
        grad_cross_query,
        grad_cross_kv,
        grad_cross_out,
        grad_self_qkv.reshape(D // S, 3, -1),
        grad_self_out,
        grad_mlp_up,
        grad_mlp_down,
        grad_decoder,
    )


def solution(mesh):
    return jax.shard_map(
        per_device,
        mesh=mesh,
        in_specs=(
            P(None, "seq", None),
            P(None, "seq", None),
            P(),
            P(),
            P(),
            P(None, "mp"),
            P(None, None, "mp"),
            P("mp", None),
            P(None, None, "mp"),
            P("mp", None),
            P(None, "mp"),
            P("mp", None),
            P(None, "mp", None),
            P(None, None, "seq", None, None),
            P(None, "seq", None),
            P(None, None, "mp", "seq", None),
        ),
        out_specs=(
            P(None, ("seq", "mp"), None),
            P(None, None, "mp", "seq", None),
            P(None, ("seq", "mp"), None),
            P(None, "seq", None),
            P(None, "seq"),
            P(None, "seq"),
            P("seq"),
            P("seq", "mp"),
            P("seq", None, "mp"),
            P("mp", "seq"),
            P("seq", None, "mp"),
            P("mp", "seq"),
            P("seq", "mp"),
            P("mp", "seq"),
            P("seq", "mp", None),
        ),
        check_vma=False,
    )
```

```python
import functools
import math

import jax
import jax.numpy as jnp
from jax import lax
from jax.experimental import pallas as pl
from jax.experimental.pallas import tpu as pltpu
from jax.sharding import PartitionSpec as P


PLANE = 32
HD = 64
LANES = 128
norm_eps = 1e-05
f32 = jnp.float32
bf16 = jnp.bfloat16

NT = (((1,), (1,)), ((), ()))
NN = (((1,), (0,)), ((), ()))
TN = (((0,), (0,)), ((), ()))


def dot(a, b, dims):
    return lax.dot_general(a, b, dims, preferred_element_type=f32)


def mm(a, b):
    return jnp.dot(a, b, preferred_element_type=f32)


def split3(v):
    hi = v.astype(bf16).astype(f32)
    rest = v - hi
    mid = rest.astype(bf16).astype(f32)
    return hi, mid, rest - mid


def spread(base, cols):
    lane = lax.broadcasted_iota(jnp.int32, (base.shape[0], HD), 1)
    tail = jnp.zeros((base.shape[0], HD), f32)
    for at, col in cols.items():
        tail = jnp.where(lane == at, col, tail)
    return jnp.concatenate([base, tail], axis=1).astype(bf16)


def load_keys(n_ref, kv_specs, refs, ka, va, hpd, blocks):
    for ref_at, rows, k_at, v_at, base in kv_specs:
        src = refs[ref_at]

        def build(i, _):
            natural = base + (i ^ n_ref[1]) * rows
            dst = pl.ds(pl.multiple_of(natural, 16), rows)
            slot = natural + lax.broadcasted_iota(jnp.int32, (rows, 1), 0)
            mask = jnp.where(slot < n_ref[0], 0.0, -1e30).astype(f32)
            for h in range(hpd):
                k = src[i, k_at[0] : k_at[0] + rows, k_at[1] + h * HD : k_at[1] + (h + 1) * HD]
                v = src[i, v_at[0] : v_at[0] + rows, v_at[1] + h * HD : v_at[1] + (h + 1) * HD]
                ka[h, dst, :] = spread(k.astype(f32), {0: 1.0, 1: 1.0, 2: 1.0, 3: mask})
                va[h, dst, :] = spread(v.astype(f32), {0: 1.0, 1: 1.0, 2: 1.0})
            return 0

        lax.fori_loop(0, blocks, build, 0)


def fwd_kernel(n_ref, *refs, n_in, blocks, q_spec, kv_specs, hpd, bq, kc, fixed):
    ins, (o_ref, qa_ref, ka, va) = refs[:n_in], refs[-4:]
    load_keys(n_ref, kv_specs, ins, ka, va, hpd, blocks)
    q_at, rows_q, q_off, q_lane = q_spec

    def build(i, _):
        dst = pl.ds(pl.multiple_of((i ^ n_ref[1]) * rows_q, 16), rows_q)
        for h in range(hpd):
            q = ins[q_at][i, q_off : q_off + rows_q, q_lane + h * HD : q_lane + (h + 1) * HD]
            qa_ref[h, dst, :] = spread(q.astype(f32) * (1.0 / math.sqrt(HD)), {3: 1.0})
        return 0

    lax.fori_loop(0, blocks, build, 0)
    total = ka.shape[1]

    def block(b, _):
        rows = pl.ds(pl.multiple_of(b * bq, bq), bq)

        def chunk(c, carry):
            cols = pl.ds(pl.multiple_of(c * kc, kc), kc)
            out = []
            for h in range(hpd):
                m, acc = carry[h]
                s = dot(qa_ref[h, rows, :], ka[h, cols, :], NT)
                top = jnp.maximum(m, jnp.max(s, axis=1, keepdims=True))
                p = jnp.exp(s - top).astype(bf16)
                out.append((top, acc * jnp.exp(m - top) + dot(p, va[h, cols, :], NN)))
            return tuple(out)

        carry = ((jnp.full((bq, 1), -1e30, f32), jnp.zeros((bq, LANES), f32)),) * hpd
        if fixed:
            for c in range(total // kc):
                carry = chunk(c, carry)
        else:
            carry = lax.fori_loop(0, (n_ref[0] + kc - 1) // kc, chunk, carry)
        outs = []
        for h in range(hpd):
            m, acc = carry[h]
            norm = acc[:, HD : HD + 1]
            outs.append(acc[:, :HD] / norm)
            hi, mid, lo = split3(-(m + jnp.log(norm)))
            qa_ref[h, rows, :] = spread(
                qa_ref[h, rows, :HD].astype(f32), {0: hi, 1: mid, 2: lo, 3: 1.0}
            )
        o_ref[rows, :] = jnp.concatenate(outs, axis=1).astype(bf16)
        return 0

    lax.fori_loop(0, qa_ref.shape[1] // bq, block, 0)


def bwd_kernel(n_ref, *refs, n_in, blocks, do_spec, kv_specs, hpd, bq, kc, fixed):
    ins, (dq_ref, dkv_ref, ka, va, da, dk, dv) = refs[:n_in], refs[-7:]
    qa_ref, do_ref, o_ref = ins[:3]
    load_keys(n_ref, kv_specs, ins, ka, va, hpd, blocks)
    rows_q, do_off = do_spec

    def build(i, _):
        rows = pl.ds(pl.multiple_of(i * rows_q, 16), rows_q)
        for h in range(hpd):
            d = do_ref[i, do_off : do_off + rows_q, h * HD : (h + 1) * HD].astype(f32)
            o = o_ref[rows, h * HD : (h + 1) * HD].astype(f32)
            hi, mid, lo = split3(-jnp.sum(d * o, axis=1, keepdims=True))
            da[h, rows, :] = spread(d, {0: hi, 1: mid, 2: lo})
        return 0

    lax.fori_loop(0, blocks, build, 0)
    dk[...] = jnp.zeros_like(dk)
    dv[...] = jnp.zeros_like(dv)
    total = ka.shape[1]
    steps = total // kc if fixed else (n_ref[0] + kc - 1) // kc

    def block(b, _):
        rows = pl.ds(pl.multiple_of(b * bq, bq), bq)

        def chunk(c, dqs):
            cols = pl.ds(pl.multiple_of(c * kc, kc), kc)
            out = []
            for h in range(hpd):
                k, q, d = ka[h, cols, :], qa_ref[h, rows, :], da[h, rows, :]
                p = jnp.exp(dot(k, q, NT))
                dp = dot(va[h, cols, :], d, NT)
                dv[h, cols, :] += dot(p.astype(bf16), d, NN)
                g = (p * dp).astype(bf16)
                dk[h, cols, :] += dot(g, q, NN)
                out.append(dqs[h] + dot(k, g, TN))
            return tuple(out)

        dqs = lax.fori_loop(0, steps, chunk, (jnp.zeros((LANES, bq), f32),) * hpd)
        dq = jnp.concatenate([v[:HD, :] for v in dqs], axis=0).T
        dq_ref[rows, :] = (dq * (1.0 / math.sqrt(HD))).astype(bf16)
        return 0

    lax.fori_loop(0, qa_ref.shape[1] // bq, block, 0)
    step = total // blocks

    def finish(i, _):
        rows = pl.ds(pl.multiple_of(i * step, 16), step)
        parts = [dk[h, rows, :HD] for h in range(hpd)] + [dv[h, rows, :HD] for h in range(hpd)]
        dkv_ref[rows, :] = jnp.concatenate(parts, axis=1).astype(bf16)
        return 0

    lax.fori_loop(0, blocks, finish, 0)


VM = pl.BlockSpec(memory_space=pltpu.VMEM)
SM = pl.BlockSpec(memory_space=pltpu.SMEM)
AN = pl.BlockSpec(memory_space=pl.ANY)


def fit(rows, most):
    return math.gcd(rows, most)


def attend(limits, ins, blocks, q_spec, kv_specs, total, hpd, fixed, deps=()):
    queries = blocks * q_spec[1]
    kc = fit(total, 1024 if fixed else 512)
    body = functools.partial(
        fwd_kernel,
        n_in=len(ins),
        blocks=blocks,
        q_spec=q_spec,
        kv_specs=kv_specs,
        hpd=hpd,
        bq=fit(queries, 512),
        kc=kc,
        fixed=fixed,
    )
    work = hpd * queries * total
    return pl.pallas_call(
        body,
        out_shape=(
            jax.ShapeDtypeStruct((queries, hpd * HD), bf16),
            jax.ShapeDtypeStruct((hpd, queries, LANES), bf16),
        ),
        in_specs=[SM] + [VM] * len(ins) + [AN] * len(deps),
        out_specs=(VM, VM),
        scratch_shapes=[pltpu.VMEM((hpd, total, LANES), bf16)] * 2,
        compiler_params=pltpu.CompilerParams(vmem_limit_bytes=44 * 2**20),
        cost_estimate=pl.CostEstimate(
            flops=1024 * work, bytes_accessed=16 * queries * hpd * HD, transcendentals=work
        ),
    )(limits, *ins, *deps)


def attend_back(limits, ins, blocks, do_spec, kv_specs, total, hpd, fixed, deps=()):
    queries = blocks * do_spec[0]
    body = functools.partial(
        bwd_kernel,
        n_in=len(ins),
        blocks=blocks,
        do_spec=do_spec,
        kv_specs=kv_specs,
        hpd=hpd,
        bq=fit(queries, 512),
        kc=fit(total, 512),
        fixed=fixed,
    )
    work = hpd * queries * total
    return pl.pallas_call(
        body,
        out_shape=(
            jax.ShapeDtypeStruct((queries, hpd * HD), bf16),
            jax.ShapeDtypeStruct((total, 2 * hpd * HD), bf16),
        ),
        in_specs=[SM] + [VM] * len(ins) + [AN] * len(deps),
        out_specs=(VM, VM),
        scratch_shapes=[pltpu.VMEM((hpd, total, LANES), bf16)] * 2
        + [pltpu.VMEM((hpd, queries, LANES), bf16)]
        + [pltpu.VMEM((hpd, total, LANES), f32)] * 2,
        compiler_params=pltpu.CompilerParams(vmem_limit_bytes=52 * 2**20),
        cost_estimate=pl.CostEstimate(
            flops=2560 * work, bytes_accessed=24 * queries * hpd * HD, transcendentals=work
        ),
    )(limits, *ins, *deps)


def norm_parts(values):
    center = values - jnp.mean(values, axis=-1, keepdims=True)
    scale = lax.rsqrt(jnp.mean(center * center, axis=-1, keepdims=True) + norm_eps)
    return center * scale, scale


def layer_norm(values, gain_row, shift_row):
    return (norm_parts(values)[0] * gain_row + shift_row).astype(bf16)


def norm_back(values, gain_row, grad_out):
    unit, scale = norm_parts(values)
    lifted = grad_out * gain_row
    grad_in = scale * (
        lifted
        - jnp.mean(lifted, axis=-1, keepdims=True)
        - unit * jnp.mean(lifted * unit, axis=-1, keepdims=True)
    )
    gain = jnp.sum(grad_out * unit, axis=0, keepdims=True)
    return grad_in, gain, jnp.sum(grad_out, axis=0, keepdims=True)


def flat(ref):
    return ref[...].reshape(-1, ref.shape[-1])


def joined(ref):
    return jnp.concatenate([ref[i] for i in range(ref.shape[0])], axis=1)


def once(shape, index=None):
    at = (0,) * len(shape) if index is None else index
    return pl.BlockSpec(shape, lambda i: at, pipeline_mode=pl.Buffered(1))


def held(shape):
    return pl.BlockSpec(shape, lambda i: (0,) * len(shape))


def mid_kernel(a_ref, x_ref, norm_ref, wo_ref, wt_ref, x1_ref, n_ref, ac_ref, t_ref):
    @pl.when(pl.program_id(0) == 0)
    def _():
        a = joined(a_ref)
        ac_ref[...] = a
        x1 = x_ref[...].astype(f32) + dot(a, flat(wo_ref), NN)
        x1_ref[...] = x1
        n_ref[...] = layer_norm(x1, norm_ref[0:1, :], norm_ref[1:2, :])

    t_ref[0] = dot(n_ref[...], flat(wt_ref), NT).astype(bf16)


def middle(a, x, norm, w_out, w_triple):
    S, rows, W = a.shape
    D = S * W
    return pl.pallas_call(
        mid_kernel,
        grid=(S,),
        out_shape=(
            jax.ShapeDtypeStruct((rows, D), f32),
            jax.ShapeDtypeStruct((rows, D), bf16),
            jax.ShapeDtypeStruct((rows, D), bf16),
            jax.ShapeDtypeStruct((S, rows, 3 * W), bf16),
        ),
        in_specs=[
            once((S, rows, W)),
            once((rows, D)),
            once((2, D)),
            once(*w_out[1]),
            w_triple[1],
        ],
        out_specs=(
            held((rows, D)),
            held((rows, D)),
            held((rows, D)),
            pl.BlockSpec((1, rows, 3 * W), lambda i: (i, 0, 0)),
        ),
        compiler_params=pltpu.CompilerParams(vmem_limit_bytes=40 * 2**20),
        cost_estimate=pl.CostEstimate(
            flops=8 * rows * D * D, bytes_accessed=8 * D * D + 14 * rows * D, transcendentals=0
        ),
    )(a, x, norm, w_out[0], w_triple[0])


def mlp_kernel(
    aa_ref,
    ab_ref,
    xa_ref,
    xb_ref,
    ca_ref,
    cb_ref,
    dp_ref,
    norm_ref,
    ws_ref,
    wd_ref,
    up_ref,
    down_ref,
    n_ref,
    ac_ref,
    g_ref,
    du_ref,
    x3_ref,
    pix_ref,
    e3_ref,
    d2_ref,
    e2_ref,
    da_ref,
    db_ref,
    sum_ref,
    x2,
    d3,
    acc,
    back,
    *,
    steps,
):
    step = pl.program_id(0)
    R = xa_ref.shape[0]
    S, _, W = aa_ref.shape

    @pl.when(step == 0)
    def _():
        for rows, a_ref, x_ref, c_ref in (
            (slice(0, R), aa_ref, xa_ref, ca_ref),
            (slice(R, x2.shape[0]), ab_ref, xb_ref, cb_ref),
        ):
            a = joined(a_ref)
            ac_ref[rows, :] = a
            x = x_ref[...] + dot(a, flat(ws_ref), NN)
            x2[rows, :] = x
            n_ref[rows, :] = layer_norm(x, norm_ref[0:1, :], norm_ref[1:2, :])
            d = c_ref[...].astype(f32) + dot(dp_ref[rows, :], flat(wd_ref), NN)
            d3[rows, :] = d
            e3_ref[rows, :] = d.astype(bf16)
        acc[...] = jnp.zeros_like(acc)
        back[...] = jnp.zeros_like(back)

    up = flat(up_ref)
    down = flat(down_ref)
    u = dot(n_ref[...], up, NT)
    slope = math.sqrt(2.0 / math.pi)
    square = u * u
    bend = jnp.tanh(slope * u * (1.0 + 0.044715 * square))
    half = 0.5 * (1.0 + bend)
    g = (u * half).astype(bf16)
    rise = half + 0.5 * slope * u * (1.0 - bend * bend) * (1.0 + 0.134145 * square)
    du = (dot(e3_ref[...], down, NT) * rise).astype(bf16)
    g_ref[...] = g
    du_ref[...] = du
    acc[...] += dot(g, down, NN)
    back[...] += dot(du, up, NN)

    @pl.when(step == steps - 1)
    def _():
        x3 = (x2[...] + acc[...]).astype(bf16)
        x3_ref[...] = x3
        pix_ref[...] = dot(x3, flat(wd_ref), NT).astype(bf16)
        grad_in, gain, shift = norm_back(x2[...], norm_ref[0:1, :], back[...])
        d2 = d3[...] + grad_in
        d2_ref[...] = d2
        e2 = d2.astype(bf16)
        e2_ref[...] = e2
        sum_ref[...] = jnp.concatenate([gain, shift], axis=0)
        da = dot(e2, flat(ws_ref), NT).astype(bf16)
        for i in range(S):
            da_ref[i] = da[:R, i * W : (i + 1) * W]
            db_ref[i] = da[R:, i * W : (i + 1) * W]


def feed_forward(a, x1, cot, d_pix, norm, w_out, w_dec, w_up, w_down, hidden, steps):
    S, R, W = a[0].shape
    RB = a[1].shape[1]
    D, total, pixels = S * W, R + RB, d_pix.shape[1]
    part = hidden // steps
    row = jax.ShapeDtypeStruct((total, D), bf16)
    wide = jax.ShapeDtypeStruct((total, hidden), bf16)
    blocked = pl.BlockSpec((total, part), lambda i: (0, i))
    full = held((total, D))
    return pl.pallas_call(
        functools.partial(mlp_kernel, steps=steps),
        grid=(steps,),
        out_shape=(
            row,
            row,
            wide,
            wide,
            row,
            jax.ShapeDtypeStruct((total, pixels), bf16),
            row,
            jax.ShapeDtypeStruct((total, D), f32),
            row,
            jax.ShapeDtypeStruct((S, R, W), bf16),
            jax.ShapeDtypeStruct((S, RB, W), bf16),
            jax.ShapeDtypeStruct((2, D), f32),
        ),
        in_specs=[
            once((S, R, W)),
            once((S, RB, W)),
            once((R, D)),
            once((RB, D)),
            once((R, D)),
            once((RB, D)),
            once((total, pixels)),
            once((2, D)),
            once(*w_out[1]),
            once(*w_dec[1]),
            w_up[1],
            w_down[1],
        ],
        out_specs=(
            full,
            full,
            blocked,
            blocked,
            full,
            held((total, pixels)),
            full,
            full,
            full,
            held((S, R, W)),
            held((S, RB, W)),
            held((2, D)),
        ),
        scratch_shapes=[pltpu.VMEM((total, D), f32)] * 4,
        compiler_params=pltpu.CompilerParams(vmem_limit_bytes=60 * 2**20),
        cost_estimate=pl.CostEstimate(
            flops=8 * total * D * hidden + 8 * total * D * D,
            bytes_accessed=4 * D * hidden + 30 * total * D,
            transcendentals=total * hidden,
        ),
    )(*a, *x1, *cot, d_pix, norm, w_out[0], w_dec[0], w_up[0], w_down[0])


def hold_kernel(*refs):
    pass


def hold(value, deps):
    return pl.pallas_call(
        hold_kernel,
        out_shape=jax.ShapeDtypeStruct(value.shape, value.dtype),
        in_specs=[AN] * (1 + len(deps)),
        out_specs=AN,
        input_output_aliases={0: 0},
        cost_estimate=pl.CostEstimate(flops=0, bytes_accessed=0, transcendentals=0),
    )(value, *deps)


def back_kernel(
    t_ref, x_ref, d_ref, norm_ref, wo_ref, wt_ref, *refs, steps
):
    d1_ref, e_ref, da_ref, sum_ref, acc = refs[-5:]
    step = pl.program_id(0)
    part = dot(t_ref[0], flat(wt_ref), NN)

    @pl.when(step == 0)
    def _():
        acc[...] = part

    @pl.when(step > 0)
    def _():
        acc[...] += part

    @pl.when(step == steps - 1)
    def _():
        grad_in, gain, shift = norm_back(x_ref[...], norm_ref[0:1, :], acc[...])
        d1 = d_ref[...] + grad_in
        d1_ref[...] = d1
        e = d1.astype(bf16)
        e_ref[...] = e
        sum_ref[...] = jnp.concatenate([gain, shift], axis=0)
        da = dot(e, flat(wo_ref), NT).astype(bf16)
        W = da_ref.shape[2]
        for i in range(steps):
            da_ref[i] = da[:, i * W : (i + 1) * W]


def middle_back(t, x1, d2, at, norm, w_out, w_triple, deps=()):
    S, rows, wide = t.shape
    D = x1.shape[1]
    W = wide // 3
    return pl.pallas_call(
        functools.partial(back_kernel, steps=S),
        grid=(S,),
        out_shape=(
            jax.ShapeDtypeStruct((rows, D), f32),
            jax.ShapeDtypeStruct((rows, D), bf16),
            jax.ShapeDtypeStruct((S, rows, W), bf16),
            jax.ShapeDtypeStruct((2, D), f32),
        ),
        in_specs=[
            pl.BlockSpec((1, rows, wide), lambda i: (i, 0, 0)),
            once((rows, D)),
            once((rows, D), (at, 0)),
            once((2, D)),
            once(*w_out[1]),
            w_triple[1],
        ]
        + [AN] * len(deps),
        out_specs=(
            held((rows, D)),
            held((rows, D)),
            held((S, rows, W)),
            held((2, D)),
        ),
        scratch_shapes=[pltpu.VMEM((rows, D), f32)],
        compiler_params=pltpu.CompilerParams(vmem_limit_bytes=40 * 2**20),
        cost_estimate=pl.CostEstimate(
            flops=8 * rows * D * D, bytes_accessed=8 * D * D + 24 * rows * D, transcendentals=0
        ),
    )(t, x1, d2, norm, w_out[0], w_triple[0], *deps)


def grads_kernel(*refs, shape, widths):
    count = sum(shape)
    lefts, rights = refs[:count], refs[count : 2 * count]
    out_ref, turned = refs[2 * count], refs[2 * count + 1 :]

    @pl.when(pl.program_id(0) == 0)
    def _():
        for left, t in zip(lefts, turned):
            t[...] = left[...].T

    at = n = 0
    for pieces, width in zip(shape, widths):
        total = 0.0
        for i in range(n, n + pieces):
            right = joined(rights[i]) if len(rights[i].shape) == 3 else rights[i][...]
            total += dot(turned[i][...], right, NN)
        out_ref[:, at : at + width] = total.astype(bf16)
        at, n = at + width, n + pieces


def weight_grads(terms, ranks):
    pieces = [p for term in terms for p in term]
    shape = [len(term) for term in terms]
    widths = [term[0][1].size // term[0][0].shape[0] // ranks for term in terms]
    D, per = pieces[0][0].shape[1], sum(widths)
    lefts = [p[0] for p in pieces]
    rights = [p[1] for p in pieces]
    work = sum(p[0].shape[0] for p in pieces) * D * per * ranks // len(pieces)
    return pl.pallas_call(
        functools.partial(grads_kernel, shape=shape, widths=widths),
        grid=(ranks,),
        out_shape=jax.ShapeDtypeStruct((D, per * ranks), bf16),
        in_specs=[once(v.shape) for v in lefts]
        + [
            pl.BlockSpec((v.shape[0] // ranks,) + v.shape[1:], lambda i: (i, 0, 0))
            if v.ndim == 3
            else pl.BlockSpec((v.shape[0], v.shape[1] // ranks), lambda i: (0, i))
            for v in rights
        ],
        out_specs=pl.BlockSpec((D, per), lambda i: (0, i)),
        scratch_shapes=[pltpu.VMEM(v.shape[::-1], bf16) for v in lefts],
        compiler_params=pltpu.CompilerParams(vmem_limit_bytes=56 * 2**20),
        cost_estimate=pl.CostEstimate(
            flops=2 * work, bytes_accessed=4 * D * per * ranks, transcendentals=0
        ),
    )(*lefts, *rights)


def start_kernel(at_ref, xa_ref, xb_ref, norm_ref, wk_ref, wq_in, *refs, pieces, width):
    p_in, (q_ref, k_ref, n_ref, wq_ref, wkv_ref) = refs[:pieces], refs[pieces:]
    seq = at_ref[0]
    R = xa_ref.shape[0]
    W = q_ref.shape[2]
    wq_ref[...] = flat(wq_in)
    wkv_ref[...] = flat(wk_ref)[:, :width]
    for block, x_ref in ((slice(0, R), xa_ref), (slice(R, n_ref.shape[0]), xb_ref)):
        n_ref[block, :] = layer_norm(x_ref[...].astype(f32), norm_ref[0:1, :], norm_ref[1:2, :])
    for i in range(pieces):
        q_ref[i] = dot(n_ref[...], wq_ref[i * W : (i + 1) * W, :], NT).astype(bf16)
    own = wkv_ref[pl.ds(pl.multiple_of(seq * 2 * W, 16), 2 * W), :]
    for i in range(pieces):
        k_ref[seq ^ i] = dot(p_in[i][...], own, NT).astype(bf16)


def start(at, x0, norm, w_kv, w_query, patch_pieces, W):
    S, D = len(patch_pieces), x0[0].shape[1]
    total = x0[0].shape[0] + x0[1].shape[0]
    slots, width = patch_pieces[0].shape
    whole = [x0[0].shape, x0[1].shape, norm.shape]
    outs = [(S, total, W), (S, slots, 2 * W), (total, D), (D, D), (2 * D, width)]
    return pl.pallas_call(
        functools.partial(start_kernel, pieces=S, width=width),
        grid=(1,),
        out_shape=tuple(jax.ShapeDtypeStruct(v, bf16) for v in outs),
        in_specs=[SM]
        + [once(v) for v in whole]
        + [once(*w_kv[1]), once(*w_query[1])]
        + [once((slots, width))] * S,
        out_specs=tuple(held(v) for v in outs),
        compiler_params=pltpu.CompilerParams(vmem_limit_bytes=56 * 2**20),
        cost_estimate=pl.CostEstimate(
            flops=2 * total * D * D + 4 * S * slots * width * W,
            bytes_accessed=6 * D * D + 12 * total * D,
            transcendentals=0,
        ),
    )(at, *x0, norm, w_kv[0], w_query[0], *patch_pieces)


def finish_kernel(at_ref, ka_ref, kb_ref, *refs, pieces):
    p_in, out_ref = refs[:pieces], refs[-1]
    seq = at_ref[0]
    slots, W = ka_ref.shape[1], ka_ref.shape[2] // 2
    by_kv = 0.0
    for i in range(pieces):
        j = seq ^ i
        by_kv += dot(ka_ref[j], p_in[i][:slots, :], TN) + dot(kb_ref[j], p_in[i][slots:, :], TN)
    wide = by_kv.shape[1] // pieces
    grad_k, grad_v = by_kv[:W].T.astype(bf16), by_kv[W:].T.astype(bf16)
    for i in range(pieces):
        out_ref[i, :wide, :] = grad_k[i * wide : (i + 1) * wide, :]
        out_ref[i, wide:, :] = grad_v[i * wide : (i + 1) * wide, :]


def finish(at, dkv, patch_pieces):
    S, W = dkv[0].shape[0], dkv[0].shape[2] // 2
    rows = 2 * patch_pieces[0].shape[1] // S
    return pl.pallas_call(
        functools.partial(finish_kernel, pieces=S),
        out_shape=jax.ShapeDtypeStruct((S, rows, W), bf16),
        in_specs=[SM] + [VM] * (2 + S),
        out_specs=VM,
        compiler_params=pltpu.CompilerParams(vmem_limit_bytes=32 * 2**20),
        cost_estimate=pl.CostEstimate(
            flops=13 * 10**8, bytes_accessed=8 * 10**6, transcendentals=0
        ),
    )(at, *dkv, *patch_pieces)


CP = 32


def place(perm, toks, TR, TC):
    own, ext = TR * TC, perm.shape[2]
    tok = lax.broadcasted_iota(jnp.int32, (toks, 1), 0)
    row = jnp.where(tok < own, tok // TC, jnp.where(tok < own + TR, tok - own, TR))
    col = jnp.where(
        tok < own, tok % TC, jnp.where(tok < own + TR, TC, tok - own - TR)
    )
    real = tok <= own + TR + TC
    pixel = lax.broadcasted_iota(jnp.int32, (toks, ext), 1)
    for a in range(2):
        for b in range(2):
            ok = real & ((row < TR) | (a == 0)) & ((col < TC) | (b == 0))
            at = jnp.where(ok, (2 * row + a) * (2 * TC + 1) + 2 * col + b, -1)
            perm[2 * a + b] = jnp.where(pixel == at, 1.0, 0.0).astype(bf16)


def pixel_grad_kernel(cot_ref, w_ref, out_ref, perm, *, TR, TC):
    @pl.when(pl.program_id(0) == 0)
    def _():
        place(perm, out_ref.shape[1], TR, TC)

    grad = dot(cot_ref[0], w_ref[0], NT)
    hi = grad.astype(bf16)
    lo = (grad - hi.astype(f32)).astype(bf16)
    parts = [dot(perm[i], hi, NT) + dot(perm[i], lo, NT) for i in range(4)]
    out_ref[0] = jnp.concatenate(parts, axis=1)


def pixel_sample_kernel(x_ref, w_ref, out_ref, perm, *, TR, TC):
    @pl.when(pl.program_id(0) == 0)
    def _():
        place(perm, x_ref.shape[1], TR, TC)

    x = x_ref[0]
    window = sum(dot(x[:, i * CP : (i + 1) * CP], perm[i], TN) for i in range(4))
    out_ref[0] = dot(window.astype(bf16), w_ref[0], NN).astype(bf16)


def per_plane(body, first, weights, out_rows, out_lanes, out_type, toks, TR, TC):
    planes, ext, samples = weights.shape

    def whole(shape):
        return pl.BlockSpec((1,) + shape, lambda i: (i, 0, 0))

    return pl.pallas_call(
        functools.partial(body, TR=TR, TC=TC),
        grid=(planes,),
        out_shape=jax.ShapeDtypeStruct((planes, out_rows, out_lanes), out_type),
        in_specs=[whole(first.shape[1:]), whole((ext, samples))],
        out_specs=whole((out_rows, out_lanes)),
        scratch_shapes=[pltpu.VMEM((4, toks, ext), bf16)],
        compiler_params=pltpu.CompilerParams(vmem_limit_bytes=24 * 2**20),
        cost_estimate=pl.CostEstimate(
            flops=6 * 10**8, bytes_accessed=7 * 10**6, transcendentals=0
        ),
    )(first, weights)


def swap_seq(value):
    return lax.all_to_all(value, "seq", split_axis=0, concat_axis=0, tiled=True)


def swap_mp(value):
    return lax.all_to_all(value, "mp", split_axis=0, concat_axis=0, tiled=True)


def swap_all(value):
    return lax.all_to_all(value, ("seq", "mp"), split_axis=0, concat_axis=0, tiled=True)


def swap_pair(value):
    count = lax.axis_size("mp")
    return lax.ppermute(value, "mp", [(i, i ^ 1) for i in range(count)])


def gather_rows(piece):
    return lax.all_gather(piece, ("mp", "seq"), axis=0, tiled=False)


def bundle_part(bundle, at, rows):
    pieces, _, D = bundle.shape
    if rows % 16 == 0 and at % rows == 0:
        return bundle, ((pieces, rows, D), (0, at // rows, 0))
    value = bundle[:, at : at + rows].reshape(1, -1, D)
    return value, (value.shape, None)


def by_step(part, steps):
    (pieces, rows, D), at = part[1]
    if pieces > 1:
        return part[0], pl.BlockSpec((pieces // steps, rows, D), lambda i: (i, at[1], 0))
    return part[0], pl.BlockSpec((1, rows // steps, D), lambda i: (0, i, 0))


def reduce_rows(value):
    return lax.psum_scatter(value, "seq", scatter_dimension=0, tiled=True)


def from_ranks(blocks):
    ranks, rank = lax.axis_size("mp"), lax.axis_index("mp")
    got = []
    for step in range(ranks):
        block = lax.dynamic_index_in_dim(blocks, rank ^ step, 0, keepdims=False)
        if step > 0:
            block = lax.ppermute(block, "mp", [(i, i ^ step) for i in range(ranks)])
        got.append(block)
    return got


def in_order(got, at):
    got = jnp.stack(got)
    return [lax.dynamic_index_in_dim(got, at ^ i, 0, keepdims=False) for i in range(got.shape[0])]


def sum_ranks(value):
    return lax.psum_scatter(value, "mp", scatter_dimension=1, tiled=True).astype(f32)


def gather_pieces(value):
    shares = lax.axis_size("seq")
    pieces = []
    for step in range(0, shares, 2):
        moves = [(i, i ^ step) for i in range(shares)]
        pieces.append(value if step == 0 else lax.ppermute(value, "seq", moves))
    cores = [(i, i ^ 1) for i in range(shares)]
    return [p for piece in pieces for p in (piece, lax.ppermute(piece, "seq", cores))]


def own_blocks(whole, blocks):
    ranks, rank = lax.axis_size("mp"), lax.axis_index("mp")
    pairs = ranks // 2
    pair = rank // 2
    own = whole.shape[0] // ranks
    whole = in_order(from_ranks(whole.reshape(ranks, own, -1)), rank)
    blocks = blocks.reshape(pairs, own, -1)
    arrived = []
    for step in range(pairs):
        moves = [(2 * p + h, pairs * h + (p ^ step)) for p in range(pairs) for h in range(2)]
        block = lax.dynamic_index_in_dim(blocks, pair ^ step, 0, keepdims=False)
        arrived.append(lax.ppermute(block, "mp", moves))
    arrived = in_order(arrived, rank % pairs)
    rows = []
    for p in range(pairs):
        rows += [whole[2 * p], arrived[p], whole[2 * p + 1]]
    return jnp.stack(rows)


def to_rows(value):
    return swap_seq(value).transpose(1, 0, 2).reshape(value.shape[1], -1)


def per_device(
    tokens,
    patches,
    counts,
    norm_gains,
    norm_shifts,
    cross_query,
    cross_kv,
    cross_out,
    self_qkv,
    self_out,
    mlp_up,
    mlp_down,
    decoder,
    sample_weights,
    tokens_cot,
    sample_cot,
):
    objects, R, D = tokens.shape
    S, M = lax.axis_size("seq"), lax.axis_size("mp")
    s, m = lax.axis_index("seq"), lax.axis_index("mp")
    pairs = M // 2
    if objects != 3 * pairs or S != 2 * M or D % (HD * S) != 0:
        raise ValueError("unexpected sizes")
    pair, half = m // 2, m % 2
    at_a, at_b = 3 * pair + 2 * half, 3 * pair + 1
    RB = R // 2
    RS = R + RB
    rows = [R, RB]
    W = D // S
    hpd = W // HD
    slots, width = patches.shape[1], patches.shape[2]
    slot_total = slots * S
    row_total = R * S

    def pick(arr):
        whole = lax.dynamic_index_in_dim(arr, at_b, 0, keepdims=False)
        return [
            lax.dynamic_index_in_dim(arr, at_a, 0, keepdims=False),
            lax.dynamic_slice_in_dim(whole, half * RB, RB, 0),
        ]

    def mine(arr, axis):
        share = arr.shape[axis] // S
        return lax.dynamic_slice_in_dim(arr, s * share, share, axis)

    channels = decoder.shape[1]
    local_dec = jnp.pad(decoder.transpose(2, 1, 0), ((0, 0), (0, CP - channels), (0, 0)))
    local_qkv = self_qkv.reshape(D, 3, 2, W).transpose(2, 1, 3, 0).reshape(-1, D)
    local_kv = cross_kv.reshape(width, 2, 2, W).transpose(2, 1, 3, 0).reshape(-1, width)
    per = D // (S * M)
    dec_rows = 4 * CP // S
    kv_rows = 2 * per
    local_kv = jnp.pad(local_kv, ((0, 0), (0, D - width)))
    lead = gather_rows(jnp.concatenate([mine(local_kv, 0), mine(cross_query, 1).T], axis=0))
    w_kv, w_query = bundle_part(lead, 0, kv_rows), bundle_part(lead, kv_rows, per)
    first = gather_rows(
        jnp.concatenate(
            [
                mine(local_qkv, 0),
                mine(cross_out, 0),
                mine(self_out, 0),
                mine(local_dec.reshape(-1, D), 0),
            ],
            axis=0,
        )
    )
    up_rows = mlp_up.shape[1] // S
    second = gather_rows(jnp.concatenate([mine(mlp_up, 1).T, mine(mlp_down, 0)], axis=0))
    steps = 8
    w_up = by_step(bundle_part(second, 0, up_rows), steps)
    w_down = by_step(bundle_part(second, up_rows, up_rows), steps)
    w_triple = by_step(bundle_part(first, 0, 3 * per), S)
    w_cross_out = bundle_part(first, 3 * per, per)
    w_self_out = bundle_part(first, 4 * per, per)
    w_dec = bundle_part(first, 5 * per, dec_rows)

    x0 = pick(tokens)
    norms = [jnp.stack([norm_gains[i], norm_shifts[i]]) for i in range(3)]
    at = jnp.stack([s, m])
    both = [lax.dynamic_index_in_dim(patches, o, 0, keepdims=False) for o in (at_a, at_b)]
    patch_pieces = gather_pieces(jnp.concatenate(both, axis=0))
    q1, keys_one, n1, w_query, w_kv = start(at, x0, norms[0], w_kv, w_query, patch_pieces, W)
    heads_one = swap_seq(q1)

    TC = PLANE // 4
    TR = PLANE * 4 // S
    own, rim = TR * TC, TR * TC + TR
    toks = -(-(rim + TC + 1) // 32) * 32
    planes = objects * 3
    weights_in = sample_weights.reshape(planes, *sample_weights.shape[3:])
    cot_in = sample_cot.reshape(planes, channels, -1)
    cot_in = jnp.pad(cot_in, ((0, 0), (0, CP - channels), (0, 0)))
    ext = per_plane(pixel_grad_kernel, cot_in, weights_in, toks, 4 * CP, f32, toks, TR, TC)
    ways = {
        1: [i for i in range(S) if i % 4 != 3],
        4: [i for i in range(S) if i + 4 < S],
        5: [i for i in range(S) if i % 4 != 3 and i + 4 < S],
    }
    rights = lax.ppermute(ext[:, own:rim], "seq", [(i, i + 1) for i in ways[1]])
    belows = lax.ppermute(ext[:, rim : rim + TC], "seq", [(i, i + 4) for i in ways[4]])
    corner = lax.ppermute(ext[:, rim + TC : rim + TC + 1], "seq", [(i, i + 5) for i in ways[5]])
    grid = ext[:, :own].reshape(planes, TR, TC, -1)
    belows = jnp.concatenate([belows[:, :1] + corner, belows[:, 1:]], axis=1)
    grid = grid + jnp.pad(rights[:, :, None], ((0, 0), (0, 0), (0, TC - 1), (0, 0)))
    grid = grid + jnp.pad(belows[:, None], ((0, 0), (0, TR - 1), (0, 0), (0, 0)))
    KA, KB = R // S, RB // S
    cu = 4 * CP
    grad_pix = grid.astype(bf16).reshape(pairs, 3, S, KA, cu)
    gp_a = jnp.stack([grad_pix[:, 0], grad_pix[:, 2]], axis=1).transpose(2, 0, 1, 3, 4)
    gp_b = grad_pix[:, 1].reshape(pairs, S, 2, KB, cu).transpose(1, 0, 2, 3, 4)
    sent = jnp.concatenate([gp_a, gp_b], axis=3).reshape(S * M, KA + KB, cu)
    back = swap_all(sent).reshape(S, M, KA + KB, cu).transpose(2, 0, 1, 3)
    d_pix = back.reshape(RS, M * cu)

    limits = [
        jnp.stack([lax.dynamic_index_in_dim(counts, o, 0, keepdims=False), jnp.int32(0)])
        for o in (at_a, at_b)
    ]
    kv_one = [(slots, (i * slots, 0), (i * slots, W), 0) for i in range(2)]
    o1, res1 = [], []
    for i in range(2):
        out, res = attend(
            limits[i],
            [heads_one, keys_one],
            S,
            (0, rows[i], i * R, 0),
            [(1,) + kv_one[i]],
            slot_total,
            hpd,
            False,
        )
        o1.append(out)
        res1.append(res)

    mids = [
        middle(swap_seq(o1[i].reshape(S, rows[i], W)), x0[i], norms[1], w_cross_out, w_triple)
        for i in range(2)
    ]
    x1, n2, a1, t2 = zip(*mids)

    heads_two = [swap_seq(v) for v in t2]
    pair_kv = swap_pair(heads_two[1][:, :, W:])
    wide = jnp.array([row_total, 0], jnp.int32)
    kv_a2 = (R, (0, W), (0, 2 * W), 0)
    kv_b2 = (RB, (0, W), (0, 2 * W), 0)
    kv_p2 = (RB, (0, 0), (0, W), row_total // 2)
    o_a2, res_a2 = attend(
        wide, [heads_two[0]], S, (0, R, 0, 0), [(0,) + kv_a2], row_total, hpd, True
    )
    o_b2, res_b2 = attend(
        wide,
        [heads_two[1], pair_kv],
        S,
        (0, RB, 0, 0),
        [(0,) + kv_b2, (1,) + kv_p2],
        row_total,
        hpd,
        True,
        [o_a2],
    )
    a2 = [swap_seq(o_a2.reshape(S, R, W)), swap_seq(o_b2.reshape(S, RB, W))]

    hidden = mlp_up.shape[1] * M
    n3, a2, g, du, x3b, pix, e3, d2, e2, da2_a, da2_b, sums_three = feed_forward(
        a2,
        x1,
        pick(tokens_cot),
        d_pix,
        norms[2],
        w_self_out,
        w_dec,
        w_up,
        w_down,
        hidden,
        steps,
    )

    da2 = [swap_seq(da2_a), swap_seq(da2_b)]
    grads_one = weight_grads([[(n3, du)], [(e3, g)], [(e2, a2)], [(x3b, d_pix)]], M)
    grads_one = hold(grads_one, da2)
    x3b, pix = hold(x3b, [grads_one]), hold(pix, [grads_one])
    dq_a2, dkv_a2 = attend_back(
        wide,
        [res_a2, da2[0], o_a2, heads_two[0]],
        S,
        (R, 0),
        [(3,) + kv_a2],
        row_total,
        hpd,
        True,
        [grads_one],
    )
    grads_one = reduce_rows(grads_one)
    tokens_out = own_blocks(x3b[:R], x3b[R:])
    pix = pix.reshape(KA + KB, S, M, cu).transpose(1, 2, 0, 3)
    got = swap_all(pix.reshape(S * M, KA + KB, cu)).reshape(S, pairs, 2, KA + KB, cu)
    dq_b2, dkv_b2 = attend_back(
        wide,
        [res_b2, da2[1], o_b2, heads_two[1], pair_kv],
        S,
        (RB, 0),
        [(3,) + kv_b2, (4,) + kv_p2],
        row_total,
        hpd,
        True,
        [dq_a2, got],
    )
    kept, given = dkv_b2[: row_total // 2], dkv_b2[row_total // 2 :]
    dkv_b2 = (kept.astype(f32) + swap_pair(given).astype(f32)).astype(bf16)
    dt2 = [
        swap_seq(jnp.concatenate([dq_a2, dkv_a2], axis=1).reshape(S, R, 3 * W)),
        swap_seq(jnp.concatenate([dq_b2, dkv_b2], axis=1).reshape(S, RB, 3 * W)),
    ]
    def below(i, deps):
        return middle_back(
            dt2[i], x1[i], d2, (0, R // RB)[i], norms[1], w_cross_out, w_triple, deps
        )

    def cross_back(i, da1, deps):
        dq, dkv = attend_back(
            limits[i],
            [res1[i], da1, o1[i], keys_one],
            S,
            (rows[i], 0),
            [(3,) + kv_one[i]],
            slot_total,
            hpd,
            False,
            deps,
        )
        return dq.reshape(S, rows[i], W), dkv.reshape(S, slots, 2 * W)

    low_a = below(0, [])
    cross_a = cross_back(0, swap_seq(low_a[2]), [grads_one, tokens_out])
    grads_one = sum_ranks(grads_one)
    low_b = below(1, [cross_a[0]])
    d1, e1, da1, sums_two = zip(low_a, low_b)

    grads_two = weight_grads(
        [[(n2[i], dt2[i]) for i in range(2)], [(e1[i], a1[i]) for i in range(2)]], M
    )
    cross_b = cross_back(1, swap_seq(da1[1]), [grads_two, grads_one])
    dq1, dkv1 = zip(cross_a, cross_b)
    grads_two = reduce_rows(grads_two)

    px_a = got[:, :, :, :KA].transpose(1, 2, 0, 3, 4).reshape(pairs, 2, S * KA, cu)
    px_b = got[:, :, :, KA:].transpose(1, 0, 2, 3, 4).reshape(pairs, S * KA, cu)
    tile = jnp.stack([px_a[:, 0], px_b, px_a[:, 1]], axis=1).reshape(planes, TR, TC, cu)
    rights = lax.ppermute(tile[:, :, 0], "seq", [(i + 1, i) for i in ways[1]])
    belows = lax.ppermute(tile[:, 0], "seq", [(i + 4, i) for i in ways[4]])
    corner = lax.ppermute(tile[:, 0, :1], "seq", [(i + 5, i) for i in ways[5]])
    fill = jnp.zeros((planes, toks - rim - TC - 1, cu), bf16)
    ext = jnp.concatenate([tile.reshape(planes, own, cu), rights, belows, corner, fill], axis=1)
    ext = hold(ext, [dq1[1]])
    sampled = per_plane(
        pixel_sample_kernel, ext, weights_in, CP, weights_in.shape[2], bf16, toks, TR, TC
    )
    sampled = sampled[:, :channels].reshape(objects, 3, channels, 1, -1)

    parts = [mm(to_rows(v), w_kv).astype(bf16) for v in dkv1]
    every = [[p] for p in parts]
    for step in range(1, M):
        moves = [(i, i ^ step) for i in range(M)]
        for i in range(2):
            every[i].append(lax.ppermute(parts[i], "mp", moves))
    from_a, from_b = [in_order(v, m) for v in every]
    patch_grad = []
    for p in range(pairs):
        shared = from_b[2 * p].astype(f32) + from_b[2 * p + 1].astype(f32)
        patch_grad += [from_a[2 * p].astype(f32), shared, from_a[2 * p + 1].astype(f32)]
    patch_grad = jnp.stack(patch_grad)

    dq1 = [to_rows(v) for v in dq1]
    grads = [mm(v, w_query) for v in dq1]
    back_one = [norm_back(x0[i].astype(f32), norm_gains[0], grads[i]) for i in range(2)]
    d0 = [(d1[i] + back_one[i][0]).astype(bf16) for i in range(2)]
    grad_tokens = own_blocks(d0[0], d0[1]).astype(f32)

    order = 2 * m + s % 2
    by_head = finish(at, dkv1, patch_pieces)
    sums = [0.0, 0.0]
    for step in range(S):
        moves = []
        for i in range(S):
            for j in range(M):
                t = i ^ step
                moves.append(((2 * j + t % 2) * M + t // 2, i * M + j))
        piece = lax.dynamic_index_in_dim(by_head, order ^ step, 0, keepdims=False)
        sums[step % 2] += lax.ppermute(piece, ("seq", "mp"), moves).astype(f32)
    swap = s % 2 == 1
    owned = jnp.concatenate(
        [jnp.where(swap, sums[1], sums[0]), jnp.where(swap, sums[0], sums[1])], axis=1
    )
    grad_cross_kv = owned.reshape(2, width // S, 2 * W).transpose(1, 0, 2)
    grad_q = dot(n1[:R], dq1[0], TN) + dot(n1[R:], dq1[1], TN)
    grad_q = swap_seq(grad_q.astype(bf16).reshape(S, D // S, D))
    grad_q = jnp.sum(grad_q.astype(f32), axis=0).astype(bf16).reshape(D // S, M, -1)
    grad_cross_query = sum(v.astype(f32) for v in from_ranks(grad_q.transpose(1, 0, 2)))

    grads_two = sum_ranks(grads_two)
    ff = hidden // M
    grad_mlp_up, grad_mlp_down = grads_one[:, :ff], grads_one[:, ff : 2 * ff].T
    grad_self_out = grads_one[:, 2 * ff : 2 * ff + D // M].T
    grad_decoder = grads_one[:, 2 * ff + D // M :]
    grad_decoder = grad_decoder.reshape(D // S, 4, CP)[:, :, :channels].transpose(0, 2, 1)
    grad_self_qkv = grads_two[:, : 3 * D // M].reshape(D // S, 2, 3, W).transpose(0, 2, 1, 3)
    grad_cross_out = grads_two[:, 3 * D // M :].T

    one = [back_one[0][i] + back_one[1][i] for i in (1, 2)]
    two = sums_two[0] + sums_two[1]
    small = jnp.concatenate(
        [one[0], two[:1], sums_three[:1], one[1], two[1:], sums_three[1:]], axis=0
    )
    small = jnp.sum(swap_seq(small.reshape(6, S, D // S).transpose(1, 0, 2)), axis=0)
    small = sum(from_ranks(jnp.broadcast_to(small, (M,) + small.shape)))

    return (
        tokens_out,
        sampled,
        grad_tokens,
        patch_grad,
        small[:3],
        small[3:5],
        small[5],
        grad_cross_query,
        grad_cross_kv,
        grad_cross_out,
        grad_self_qkv.reshape(D // S, 3, -1),
        grad_self_out,
        grad_mlp_up,
        grad_mlp_down,
        grad_decoder,
    )


def solution(mesh):
    return jax.shard_map(
        per_device,
        mesh=mesh,
        in_specs=(
            P(None, "seq", None),
            P(None, "seq", None),
            P(),
            P(),
            P(),
            P(None, "mp"),
            P(None, None, "mp"),
            P("mp", None),
            P(None, None, "mp"),
            P("mp", None),
            P(None, "mp"),
            P("mp", None),
            P(None, "mp", None),
            P(None, None, "seq", None, None),
            P(None, "seq", None),
            P(None, None, "mp", "seq", None),
        ),
        out_specs=(
            P(None, ("seq", "mp"), None),
            P(None, None, "mp", "seq", None),
            P(None, ("seq", "mp"), None),
            P(None, "seq", None),
            P(None, "seq"),
            P(None, "seq"),
            P("seq"),
            P("seq", "mp"),
            P("seq", None, "mp"),
            P("mp", "seq"),
            P("seq", None, "mp"),
            P("mp", "seq"),
            P("seq", "mp"),
            P("mp", "seq"),
            P("seq", "mp", None),
        ),
        check_vma=False,
    )
```

```python
import functools
import math

import jax
import jax.numpy as jnp
from jax import lax
from jax.experimental import pallas as pl
from jax.experimental.pallas import tpu as pltpu
from jax.sharding import PartitionSpec as P


PLANE = 32
HD = 64
LANES = 128
norm_eps = 1e-05
f32 = jnp.float32
bf16 = jnp.bfloat16

NT = (((1,), (1,)), ((), ()))
NN = (((1,), (0,)), ((), ()))
TN = (((0,), (0,)), ((), ()))


def dot(a, b, dims):
    return lax.dot_general(a, b, dims, preferred_element_type=f32)


def mm(a, b):
    return jnp.dot(a, b, preferred_element_type=f32)


def split3(v):
    hi = v.astype(bf16).astype(f32)
    rest = v - hi
    mid = rest.astype(bf16).astype(f32)
    return hi, mid, rest - mid


def spread(base, cols):
    lane = lax.broadcasted_iota(jnp.int32, (base.shape[0], HD), 1)
    tail = jnp.zeros((base.shape[0], HD), f32)
    for at, col in cols.items():
        tail = jnp.where(lane == at, col, tail)
    return jnp.concatenate([base, tail], axis=1).astype(bf16)


def load_keys(n_ref, kv_specs, refs, ka, va, hpd, blocks):
    for ref_at, rows, k_at, v_at, base in kv_specs:
        src = refs[ref_at]

        def build(i, _):
            natural = base + (i ^ n_ref[1]) * rows
            dst = pl.ds(pl.multiple_of(natural, 16), rows)
            slot = natural + lax.broadcasted_iota(jnp.int32, (rows, 1), 0)
            mask = jnp.where(slot < n_ref[0], 0.0, -1e30).astype(f32)
            for h in range(hpd):
                k = src[i, k_at[0] : k_at[0] + rows, k_at[1] + h * HD : k_at[1] + (h + 1) * HD]
                v = src[i, v_at[0] : v_at[0] + rows, v_at[1] + h * HD : v_at[1] + (h + 1) * HD]
                ka[h, dst, :] = spread(k.astype(f32), {0: 1.0, 1: 1.0, 2: 1.0, 3: mask})
                va[h, dst, :] = spread(v.astype(f32), {0: 1.0, 1: 1.0, 2: 1.0})
            return 0

        lax.fori_loop(0, blocks, build, 0)


def fwd_kernel(n_ref, *refs, n_in, blocks, q_spec, kv_specs, hpd, bq, kc, fixed):
    ins, (o_ref, qa_ref, ka, va) = refs[:n_in], refs[-4:]
    load_keys(n_ref, kv_specs, ins, ka, va, hpd, blocks)
    q_at, rows_q, q_off, q_lane = q_spec

    def build(i, _):
        dst = pl.ds(pl.multiple_of((i ^ n_ref[1]) * rows_q, 16), rows_q)
        for h in range(hpd):
            q = ins[q_at][i, q_off : q_off + rows_q, q_lane + h * HD : q_lane + (h + 1) * HD]
            qa_ref[h, dst, :] = spread(q.astype(f32) * (1.0 / math.sqrt(HD)), {3: 1.0})
        return 0

    lax.fori_loop(0, blocks, build, 0)
    total = ka.shape[1]

    def block(b, _):
        rows = pl.ds(pl.multiple_of(b * bq, bq), bq)

        def chunk(c, carry):
            cols = pl.ds(pl.multiple_of(c * kc, kc), kc)
            out = []
            for h in range(hpd):
                m, acc = carry[h]
                s = dot(qa_ref[h, rows, :], ka[h, cols, :], NT)
                top = jnp.maximum(m, jnp.max(s, axis=1, keepdims=True))
                p = jnp.exp(s - top).astype(bf16)
                out.append((top, acc * jnp.exp(m - top) + dot(p, va[h, cols, :], NN)))
            return tuple(out)

        carry = ((jnp.full((bq, 1), -1e30, f32), jnp.zeros((bq, LANES), f32)),) * hpd
        if fixed:
            for c in range(total // kc):
                carry = chunk(c, carry)
        else:
            carry = lax.fori_loop(0, (n_ref[0] + kc - 1) // kc, chunk, carry)
        outs = []
        for h in range(hpd):
            m, acc = carry[h]
            norm = acc[:, HD : HD + 1]
            outs.append(acc[:, :HD] / norm)
            hi, mid, lo = split3(-(m + jnp.log(norm)))
            qa_ref[h, rows, :] = spread(
                qa_ref[h, rows, :HD].astype(f32), {0: hi, 1: mid, 2: lo, 3: 1.0}
            )
        o_ref[rows, :] = jnp.concatenate(outs, axis=1).astype(bf16)
        return 0

    lax.fori_loop(0, qa_ref.shape[1] // bq, block, 0)


def bwd_kernel(n_ref, *refs, n_in, blocks, do_spec, kv_specs, hpd, bq, kc, fixed):
    ins, (dq_ref, dkv_ref, ka, va, da, dk, dv) = refs[:n_in], refs[-7:]
    qa_ref, do_ref, o_ref = ins[:3]
    load_keys(n_ref, kv_specs, ins, ka, va, hpd, blocks)
    rows_q, do_off = do_spec

    def build(i, _):
        rows = pl.ds(pl.multiple_of(i * rows_q, 16), rows_q)
        for h in range(hpd):
            d = do_ref[i, do_off : do_off + rows_q, h * HD : (h + 1) * HD].astype(f32)
            o = o_ref[rows, h * HD : (h + 1) * HD].astype(f32)
            hi, mid, lo = split3(-jnp.sum(d * o, axis=1, keepdims=True))
            da[h, rows, :] = spread(d, {0: hi, 1: mid, 2: lo})
        return 0

    lax.fori_loop(0, blocks, build, 0)
    dk[...] = jnp.zeros_like(dk)
    dv[...] = jnp.zeros_like(dv)
    total = ka.shape[1]
    steps = total // kc if fixed else (n_ref[0] + kc - 1) // kc

    def block(b, _):
        rows = pl.ds(pl.multiple_of(b * bq, bq), bq)

        def chunk(c, dqs):
            cols = pl.ds(pl.multiple_of(c * kc, kc), kc)
            out = []
            for h in range(hpd):
                k, q, d = ka[h, cols, :], qa_ref[h, rows, :], da[h, rows, :]
                p = jnp.exp(dot(k, q, NT))
                dp = dot(va[h, cols, :], d, NT)
                dv[h, cols, :] += dot(p.astype(bf16), d, NN)
                g = (p * dp).astype(bf16)
                dk[h, cols, :] += dot(g, q, NN)
                out.append(dqs[h] + dot(k, g, TN))
            return tuple(out)

        dqs = lax.fori_loop(0, steps, chunk, (jnp.zeros((LANES, bq), f32),) * hpd)
        dq = jnp.concatenate([v[:HD, :] for v in dqs], axis=0).T
        dq_ref[rows, :] = (dq * (1.0 / math.sqrt(HD))).astype(bf16)
        return 0

    lax.fori_loop(0, qa_ref.shape[1] // bq, block, 0)
    step = total // blocks

    def finish(i, _):
        rows = pl.ds(pl.multiple_of(i * step, 16), step)
        parts = [dk[h, rows, :HD] for h in range(hpd)] + [dv[h, rows, :HD] for h in range(hpd)]
        dkv_ref[rows, :] = jnp.concatenate(parts, axis=1).astype(bf16)
        return 0

    lax.fori_loop(0, blocks, finish, 0)


VM = pl.BlockSpec(memory_space=pltpu.VMEM)
SM = pl.BlockSpec(memory_space=pltpu.SMEM)
BRIEF = pl.CostEstimate(flops=10**6, bytes_accessed=10**5, transcendentals=0)
AN = pl.BlockSpec(memory_space=pl.ANY)


def fit(rows, most):
    return math.gcd(rows, most)


def attend(limits, ins, blocks, q_spec, kv_specs, total, hpd, fixed, deps=()):
    queries = blocks * q_spec[1]
    kc = fit(total, 1024 if fixed else 512)
    body = functools.partial(
        fwd_kernel,
        n_in=len(ins),
        blocks=blocks,
        q_spec=q_spec,
        kv_specs=kv_specs,
        hpd=hpd,
        bq=fit(queries, 512),
        kc=kc,
        fixed=fixed,
    )
    work = hpd * queries * total
    return pl.pallas_call(
        body,
        out_shape=(
            jax.ShapeDtypeStruct((queries, hpd * HD), bf16),
            jax.ShapeDtypeStruct((hpd, queries, LANES), bf16),
        ),
        in_specs=[SM] + [VM] * len(ins) + [AN] * len(deps),
        out_specs=(VM, VM),
        scratch_shapes=[pltpu.VMEM((hpd, total, LANES), bf16)] * 2,
        compiler_params=pltpu.CompilerParams(vmem_limit_bytes=44 * 2**20),
        cost_estimate=BRIEF,
    )(limits, *ins, *deps)


def attend_back(limits, ins, blocks, do_spec, kv_specs, total, hpd, fixed, deps=()):
    queries = blocks * do_spec[0]
    body = functools.partial(
        bwd_kernel,
        n_in=len(ins),
        blocks=blocks,
        do_spec=do_spec,
        kv_specs=kv_specs,
        hpd=hpd,
        bq=fit(queries, 512),
        kc=fit(total, 512),
        fixed=fixed,
    )
    work = hpd * queries * total
    return pl.pallas_call(
        body,
        out_shape=(
            jax.ShapeDtypeStruct((queries, hpd * HD), bf16),
            jax.ShapeDtypeStruct((total, 2 * hpd * HD), bf16),
        ),
        in_specs=[SM] + [VM] * len(ins) + [AN] * len(deps),
        out_specs=(VM, VM),
        scratch_shapes=[pltpu.VMEM((hpd, total, LANES), bf16)] * 2
        + [pltpu.VMEM((hpd, queries, LANES), bf16)]
        + [pltpu.VMEM((hpd, total, LANES), f32)] * 2,
        compiler_params=pltpu.CompilerParams(vmem_limit_bytes=52 * 2**20),
        cost_estimate=BRIEF,
    )(limits, *ins, *deps)


def norm_parts(values):
    center = values - jnp.mean(values, axis=-1, keepdims=True)
    scale = lax.rsqrt(jnp.mean(center * center, axis=-1, keepdims=True) + norm_eps)
    return center * scale, scale


def layer_norm(values, gain_row, shift_row):
    return (norm_parts(values)[0] * gain_row + shift_row).astype(bf16)


def norm_back(values, gain_row, grad_out):
    unit, scale = norm_parts(values)
    lifted = grad_out * gain_row
    grad_in = scale * (
        lifted
        - jnp.mean(lifted, axis=-1, keepdims=True)
        - unit * jnp.mean(lifted * unit, axis=-1, keepdims=True)
    )
    gain = jnp.sum(grad_out * unit, axis=0, keepdims=True)
    return grad_in, gain, jnp.sum(grad_out, axis=0, keepdims=True)


def flat(ref):
    return ref[...].reshape(-1, ref.shape[-1])


def joined(ref):
    return jnp.concatenate([ref[i] for i in range(ref.shape[0])], axis=1)


def once(shape, index=None):
    at = (0,) * len(shape) if index is None else index
    return pl.BlockSpec(shape, lambda i: at, pipeline_mode=pl.Buffered(1))


def held(shape):
    return pl.BlockSpec(shape, lambda i: (0,) * len(shape))


def mid_kernel(a_ref, x_ref, norm_ref, wo_ref, wt_ref, x1_ref, n_ref, ac_ref, t_ref):
    @pl.when(pl.program_id(0) == 0)
    def _():
        a = joined(a_ref)
        ac_ref[...] = a
        x1 = x_ref[...].astype(f32) + dot(a, flat(wo_ref), NN)
        x1_ref[...] = x1
        n_ref[...] = layer_norm(x1, norm_ref[0:1, :], norm_ref[1:2, :])

    t_ref[0] = dot(n_ref[...], flat(wt_ref), NT).astype(bf16)


def middle(a, x, norm, w_out, w_triple):
    S, rows, W = a.shape
    D = S * W
    return pl.pallas_call(
        mid_kernel,
        grid=(S,),
        out_shape=(
            jax.ShapeDtypeStruct((rows, D), f32),
            jax.ShapeDtypeStruct((rows, D), bf16),
            jax.ShapeDtypeStruct((rows, D), bf16),
            jax.ShapeDtypeStruct((S, rows, 3 * W), bf16),
        ),
        in_specs=[
            once((S, rows, W)),
            once((rows, D)),
            once((2, D)),
            once(*w_out[1]),
            w_triple[1],
        ],
        out_specs=(
            held((rows, D)),
            held((rows, D)),
            held((rows, D)),
            pl.BlockSpec((1, rows, 3 * W), lambda i: (i, 0, 0)),
        ),
        compiler_params=pltpu.CompilerParams(vmem_limit_bytes=40 * 2**20),
        cost_estimate=BRIEF,
    )(a, x, norm, w_out[0], w_triple[0])


def mlp_kernel(
    aa_ref,
    ab_ref,
    xa_ref,
    xb_ref,
    ca_ref,
    cb_ref,
    dp_ref,
    norm_ref,
    ws_ref,
    wd_ref,
    up_ref,
    down_ref,
    n_ref,
    ac_ref,
    g_ref,
    du_ref,
    x3_ref,
    pix_ref,
    e3_ref,
    d2_ref,
    e2_ref,
    da_ref,
    sum_ref,
    x2,
    d3,
    acc,
    back,
    *,
    steps,
):
    step = pl.program_id(0)
    R = xa_ref.shape[0]
    S, _, W = aa_ref.shape

    @pl.when(step == 0)
    def _():
        for rows, a_ref, x_ref, c_ref in (
            (slice(0, R), aa_ref, xa_ref, ca_ref),
            (slice(R, x2.shape[0]), ab_ref, xb_ref, cb_ref),
        ):
            a = joined(a_ref)
            ac_ref[rows, :] = a
            x = x_ref[...] + dot(a, flat(ws_ref), NN)
            x2[rows, :] = x
            n_ref[rows, :] = layer_norm(x, norm_ref[0:1, :], norm_ref[1:2, :])
            d = c_ref[...].astype(f32) + dot(dp_ref[rows, :], flat(wd_ref), NN)
            d3[rows, :] = d
            e3_ref[rows, :] = d.astype(bf16)
        acc[...] = jnp.zeros_like(acc)
        back[...] = jnp.zeros_like(back)

    up = flat(up_ref)
    down = flat(down_ref)
    u = dot(n_ref[...], up, NT)
    slope = math.sqrt(2.0 / math.pi)
    square = u * u
    bend = jnp.tanh(slope * u * (1.0 + 0.044715 * square))
    half = 0.5 * (1.0 + bend)
    g = (u * half).astype(bf16)
    rise = half + 0.5 * slope * u * (1.0 - bend * bend) * (1.0 + 0.134145 * square)
    du = (dot(e3_ref[...], down, NT) * rise).astype(bf16)
    g_ref[...] = g
    du_ref[...] = du
    acc[...] += dot(g, down, NN)
    back[...] += dot(du, up, NN)

    @pl.when(step == steps - 1)
    def _():
        x3 = (x2[...] + acc[...]).astype(bf16)
        x3_ref[...] = x3
        pix_ref[...] = dot(x3, flat(wd_ref), NT).astype(bf16)
        grad_in, gain, shift = norm_back(x2[...], norm_ref[0:1, :], back[...])
        d2 = d3[...] + grad_in
        d2_ref[...] = d2
        e2 = d2.astype(bf16)
        e2_ref[...] = e2
        sum_ref[...] = jnp.concatenate([gain, shift], axis=0)
        da = dot(e2, flat(ws_ref), NT).astype(bf16)
        for i in range(S):
            da_ref[i] = da[:, i * W : (i + 1) * W]


def feed_forward(a, x1, cot, d_pix, norm, w_out, w_dec, w_up, w_down, hidden, steps):
    S, R, W = a[0].shape
    RB = a[1].shape[1]
    D, total, pixels = S * W, R + RB, d_pix.shape[1]
    part = hidden // steps
    row = jax.ShapeDtypeStruct((total, D), bf16)
    wide = jax.ShapeDtypeStruct((total, hidden), bf16)
    blocked = pl.BlockSpec((total, part), lambda i: (0, i))
    full = held((total, D))
    return pl.pallas_call(
        functools.partial(mlp_kernel, steps=steps),
        grid=(steps,),
        out_shape=(
            row,
            row,
            wide,
            wide,
            row,
            jax.ShapeDtypeStruct((total, pixels), bf16),
            row,
            jax.ShapeDtypeStruct((total, D), f32),
            row,
            jax.ShapeDtypeStruct((S, total, W), bf16),
            jax.ShapeDtypeStruct((2, D), f32),
        ),
        in_specs=[
            once((S, R, W)),
            once((S, RB, W)),
            once((R, D)),
            once((RB, D)),
            once((R, D)),
            once((RB, D)),
            once((total, pixels)),
            once((2, D)),
            once(*w_out[1]),
            once(*w_dec[1]),
            w_up[1],
            w_down[1],
        ],
        out_specs=(
            full,
            full,
            blocked,
            blocked,
            full,
            held((total, pixels)),
            full,
            full,
            full,
            held((S, total, W)),
            held((2, D)),
        ),
        scratch_shapes=[pltpu.VMEM((total, D), f32)] * 4,
        compiler_params=pltpu.CompilerParams(vmem_limit_bytes=60 * 2**20),
        cost_estimate=BRIEF,
    )(*a, *x1, *cot, d_pix, norm, w_out[0], w_dec[0], w_up[0], w_down[0])


def hold_kernel(*refs):
    pass


def hold(value, deps):
    return pl.pallas_call(
        hold_kernel,
        out_shape=jax.ShapeDtypeStruct(value.shape, value.dtype),
        in_specs=[AN] * (1 + len(deps)),
        out_specs=AN,
        input_output_aliases={0: 0},
        cost_estimate=BRIEF,
    )(value, *deps)


def back_kernel(
    t_ref, x_ref, d_ref, norm_ref, wo_ref, wt_ref, *refs, steps
):
    d1_ref, e_ref, da_ref, sum_ref, acc = refs[-5:]
    step = pl.program_id(0)
    part = dot(t_ref[0], flat(wt_ref), NN)

    @pl.when(step == 0)
    def _():
        acc[...] = part

    @pl.when(step > 0)
    def _():
        acc[...] += part

    @pl.when(step == steps - 1)
    def _():
        grad_in, gain, shift = norm_back(x_ref[...], norm_ref[0:1, :], acc[...])
        d1 = d_ref[...] + grad_in
        d1_ref[...] = d1
        e = d1.astype(bf16)
        e_ref[...] = e
        sum_ref[...] = jnp.concatenate([gain, shift], axis=0)
        da = dot(e, flat(wo_ref), NT).astype(bf16)
        W = da_ref.shape[2]
        for i in range(steps):
            da_ref[i] = da[:, i * W : (i + 1) * W]


def middle_back(t, x1, d2, at, norm, w_out, w_triple, deps=()):
    S, rows, wide = t.shape
    D = x1.shape[1]
    W = wide // 3
    return pl.pallas_call(
        functools.partial(back_kernel, steps=S),
        grid=(S,),
        out_shape=(
            jax.ShapeDtypeStruct((rows, D), f32),
            jax.ShapeDtypeStruct((rows, D), bf16),
            jax.ShapeDtypeStruct((S, rows, W), bf16),
            jax.ShapeDtypeStruct((2, D), f32),
        ),
        in_specs=[
            pl.BlockSpec((1, rows, wide), lambda i: (i, 0, 0)),
            once((rows, D)),
            once((rows, D), (at, 0)),
            once((2, D)),
            once(*w_out[1]),
            w_triple[1],
        ]
        + [AN] * len(deps),
        out_specs=(
            held((rows, D)),
            held((rows, D)),
            held((S, rows, W)),
            held((2, D)),
        ),
        scratch_shapes=[pltpu.VMEM((rows, D), f32)],
        compiler_params=pltpu.CompilerParams(vmem_limit_bytes=40 * 2**20),
        cost_estimate=BRIEF,
    )(t, x1, d2, norm, w_out[0], w_triple[0], *deps)


def grads_kernel(*refs, shape, widths):
    count = sum(shape)
    lefts, rights = refs[:count], refs[count : 2 * count]
    out_ref, turned = refs[-1 - count], refs[-count:]

    @pl.when(pl.program_id(0) == 0)
    def _():
        for left, t in zip(lefts, turned):
            t[...] = left[...].T

    at = n = 0
    for pieces, width in zip(shape, widths):
        total = 0.0
        for i in range(n, n + pieces):
            right = joined(rights[i]) if len(rights[i].shape) == 3 else rights[i][...]
            total += dot(turned[i][...], right, NN)
        out_ref[:, at : at + width] = total.astype(bf16)
        at, n = at + width, n + pieces


def weight_grads(terms, ranks, deps=()):
    pieces = [p for term in terms for p in term]
    shape = [len(term) for term in terms]
    widths = [term[0][1].size // term[0][0].shape[0] // ranks for term in terms]
    D, per = pieces[0][0].shape[1], sum(widths)
    lefts = [p[0] for p in pieces]
    rights = [p[1] for p in pieces]
    work = sum(p[0].shape[0] for p in pieces) * D * per * ranks // len(pieces)
    return pl.pallas_call(
        functools.partial(grads_kernel, shape=shape, widths=widths),
        grid=(ranks,),
        out_shape=jax.ShapeDtypeStruct((D, per * ranks), bf16),
        in_specs=[once(v.shape) for v in lefts]
        + [
            pl.BlockSpec((v.shape[0] // ranks,) + v.shape[1:], lambda i: (i, 0, 0))
            if v.ndim == 3
            else pl.BlockSpec((v.shape[0], v.shape[1] // ranks), lambda i: (0, i))
            for v in rights
        ]
        + [AN] * len(deps),
        out_specs=pl.BlockSpec((D, per), lambda i: (0, i)),
        scratch_shapes=[pltpu.VMEM(v.shape[::-1], bf16) for v in lefts],
        compiler_params=pltpu.CompilerParams(vmem_limit_bytes=56 * 2**20),
        cost_estimate=BRIEF,
    )(*lefts, *rights, *deps)


def start_kernel(at_ref, xa_ref, xb_ref, norm_ref, wk_ref, wq_in, *refs, pieces, width):
    p_in, (q_ref, k_ref, n_ref, wq_ref, wkv_ref) = refs[:pieces], refs[-5:]
    seq = at_ref[0]
    R = xa_ref.shape[0]
    W = q_ref.shape[2]
    wq_ref[...] = flat(wq_in)
    wkv_ref[...] = flat(wk_ref)[:, :width]
    for block, x_ref in ((slice(0, R), xa_ref), (slice(R, n_ref.shape[0]), xb_ref)):
        n_ref[block, :] = layer_norm(x_ref[...].astype(f32), norm_ref[0:1, :], norm_ref[1:2, :])
    for i in range(pieces):
        q_ref[i] = dot(n_ref[...], wq_ref[i * W : (i + 1) * W, :], NT).astype(bf16)
    own = wkv_ref[pl.ds(pl.multiple_of(seq * 2 * W, 16), 2 * W), :]
    for i in range(pieces):
        k_ref[seq ^ i] = dot(p_in[i][...], own, NT).astype(bf16)


def start(at, x0, norm, w_kv, w_query, patch_pieces, W, deps):
    S, D = len(patch_pieces), x0[0].shape[1]
    total = x0[0].shape[0] + x0[1].shape[0]
    slots, width = patch_pieces[0].shape
    whole = [x0[0].shape, x0[1].shape, norm.shape]
    outs = [(S, total, W), (S, slots, 2 * W), (total, D), (D, D), (2 * D, width)]
    return pl.pallas_call(
        functools.partial(start_kernel, pieces=S, width=width),
        grid=(1,),
        out_shape=tuple(jax.ShapeDtypeStruct(v, bf16) for v in outs),
        in_specs=[SM]
        + [once(v) for v in whole]
        + [once(*w_kv[1]), once(*w_query[1])]
        + [once((slots, width))] * S
        + [AN] * len(deps),
        out_specs=tuple(held(v) for v in outs),
        compiler_params=pltpu.CompilerParams(vmem_limit_bytes=56 * 2**20),
        cost_estimate=BRIEF,
    )(at, *x0, norm, w_kv[0], w_query[0], *patch_pieces, *deps)


def finish_kernel(at_ref, ka_ref, kb_ref, *refs, pieces):
    p_in, out_ref = refs[:pieces], refs[-1]
    seq = at_ref[0]
    slots, W = ka_ref.shape[1], ka_ref.shape[2] // 2
    by_kv = 0.0
    for i in range(pieces):
        j = seq ^ i
        by_kv += dot(ka_ref[j], p_in[i][:slots, :], TN) + dot(kb_ref[j], p_in[i][slots:, :], TN)
    wide = by_kv.shape[1] // pieces
    grad_k, grad_v = by_kv[:W].T.astype(bf16), by_kv[W:].T.astype(bf16)
    for i in range(pieces):
        out_ref[i, :wide, :] = grad_k[i * wide : (i + 1) * wide, :]
        out_ref[i, wide:, :] = grad_v[i * wide : (i + 1) * wide, :]


def finish(at, dkv, patch_pieces):
    S, W = dkv[0].shape[0], dkv[0].shape[2] // 2
    rows = 2 * patch_pieces[0].shape[1] // S
    return pl.pallas_call(
        functools.partial(finish_kernel, pieces=S),
        out_shape=jax.ShapeDtypeStruct((S, rows, W), bf16),
        in_specs=[SM] + [VM] * (2 + S),
        out_specs=VM,
        compiler_params=pltpu.CompilerParams(vmem_limit_bytes=32 * 2**20),
        cost_estimate=BRIEF,
    )(at, *dkv, *patch_pieces)


def end_kernel(
    at_ref,
    qa_ref,
    b_ref,
    ka_ref,
    wq_ref,
    wkv_ref,
    xa_ref,
    xb_ref,
    n_ref,
    da_ref,
    db_ref,
    small_ref,
    gain_ref,
    head_ref,
    *refs,
    ranks,
):
    outs_a, outs_b = refs[:ranks], refs[ranks : ranks + ranks // 2]
    part_ref, pay_ref, n_t, dq = refs[ranks + ranks // 2 :]
    S, R, W = qa_ref.shape
    own = R // ranks
    dq[:R, :] = joined(qa_ref)
    dq[R:, :] = jnp.concatenate([b_ref[i, :, :W] for i in range(S)], axis=1)
    n_t[...] = n_ref[...].T
    back = dot(dq[...], wq_ref[...], NN)
    gain = gain_ref[...]
    got_a = norm_back(xa_ref[...].astype(f32), gain, back[:R])
    got_b = norm_back(xb_ref[...].astype(f32), gain, back[R:])
    da_ref[...] += got_a[0]
    db_ref[...] += got_b[0]
    for i in range(ranks):
        rows = pl.ds(pl.multiple_of((at_ref[1] ^ i) * own, 8), own)
        outs_a[i][...] = da_ref[rows, :].astype(bf16)
    for i in range(ranks // 2):
        rows = pl.ds(pl.multiple_of((at_ref[1] // 2 ^ i) * own, 8), own)
        outs_b[i][...] = db_ref[rows, :].astype(bf16)
    for i, keys in enumerate((joined(ka_ref), None)):
        if keys is None:
            keys = jnp.concatenate([b_ref[j, :, W:] for j in range(S)], axis=1)
        part_ref[i] = dot(keys, wkv_ref[...], NN).astype(bf16)
    rows = n_t.shape[0] // S
    for i in range(0, S, 2):
        pair = dot(n_t[...], dq[:, i * W : (i + 2) * W], NN).astype(bf16)
        for j in range(S):
            block = pair[j * rows : (j + 1) * rows, :]
            pay_ref[j, i * rows : (i + 1) * rows, :] = block[:, :W]
            pay_ref[j, (i + 1) * rows : (i + 2) * rows, :] = block[:, W:]
    at = S * rows
    heads = head_ref.shape[1]
    lift = jnp.concatenate([got_a[1] + got_b[1], got_a[2] + got_b[2]], axis=0)
    sums = jnp.concatenate([lift, small_ref[...], jnp.zeros((2, n_t.shape[0]), f32)], axis=0)
    hi = sums.astype(bf16).astype(f32)
    both = jnp.concatenate([hi, sums - hi], axis=0).astype(bf16)
    for j in range(S):
        pay_ref[j, at : at + heads, :] = head_ref[j]
        pay_ref[j, at + heads :, :] = both[:, j * W : (j + 1) * W]


def end(at, dq_a, both_b, dkv_a, w_query, w_kv, x0, n1, d1, small, gain, by_head, ranks):
    S, R, W = dq_a.shape
    RB = both_b.shape[1]
    D, total = S * W, R + RB
    own = R // ranks
    slots, width = dkv_a.shape[1], w_kv.shape[1]
    rows = D + by_head.shape[1] + 16
    outs = [(own, D)] * (ranks + ranks // 2) + [(2, slots, width), (S, rows, W)]
    whole = [dq_a, both_b, dkv_a, w_query, w_kv, *x0, n1, *d1, small, gain, by_head]
    return pl.pallas_call(
        functools.partial(end_kernel, ranks=ranks),
        out_shape=tuple(jax.ShapeDtypeStruct(v, bf16) for v in outs),
        in_specs=[SM] + [VM] * len(whole),
        out_specs=(VM,) * len(outs),
        scratch_shapes=[pltpu.VMEM((D, total), bf16), pltpu.VMEM((total, D), bf16)],
        compiler_params=pltpu.CompilerParams(vmem_limit_bytes=56 * 2**20),
        cost_estimate=BRIEF,
    )(at, *whole)


def mix_kernel(at_ref, x_ref, *outs, heads):
    S, rows, W = x_ref.shape
    blocks = rows - heads - 16
    pair = blocks // len(outs)
    small = sum(x_ref[j, blocks + heads :, :].astype(f32) for j in range(S))
    total = small[:8] + small[8:]
    hi = total.astype(bf16).astype(f32)
    for i in range(len(outs)):
        rank = at_ref[1] ^ i
        src = pl.ds(pl.multiple_of(rank * pair, 16), pair)
        outs[i][:pair, :] = sum(x_ref[j, src, :].astype(f32) for j in range(S)).astype(bf16)
        for k in range(2):
            outs[i][pair + k * heads : pair + (k + 1) * heads, :] = x_ref[
                2 * rank + k, blocks : blocks + heads, :
            ]
        outs[i][pair + 2 * heads :, :] = jnp.concatenate([hi, total - hi], axis=0).astype(bf16)


def mix(at, got, ranks, heads):
    S, rows, W = got.shape
    shape = ((rows - heads - 16) // ranks + 2 * heads + 16, W)
    return pl.pallas_call(
        functools.partial(mix_kernel, heads=heads),
        out_shape=(jax.ShapeDtypeStruct(shape, bf16),) * ranks,
        in_specs=[SM, VM],
        out_specs=(VM,) * ranks,
        compiler_params=pltpu.CompilerParams(vmem_limit_bytes=24 * 2**20),
        cost_estimate=BRIEF,
    )(at, got)


def last_kernel(*refs, heads):
    ins, (q_ref, k_ref, v_ref, small_ref) = refs[:-4], refs[-4:]
    total = sum(v[...].astype(f32) for v in ins)
    pair = total.shape[0] - 2 * heads - 16
    q_ref[...] = jnp.concatenate([total[: pair // 2], total[pair // 2 : pair]], axis=1)
    one, two = total[pair : pair + heads], total[pair + heads : pair + 2 * heads]
    k_ref[...] = jnp.concatenate([one[: heads // 2], two[: heads // 2]], axis=1)
    v_ref[...] = jnp.concatenate([one[heads // 2 :], two[heads // 2 :]], axis=1)
    small_ref[...] = total[pair + 2 * heads : pair + 2 * heads + 8] + total[pair + 2 * heads + 8 :]


def last(parts, heads):
    rows, W = parts[0].shape
    pair = rows - 2 * heads - 16
    outs = [(pair // 2, 2 * W), (heads // 2, 2 * W), (heads // 2, 2 * W), (8, W)]
    return pl.pallas_call(
        functools.partial(last_kernel, heads=heads),
        out_shape=tuple(jax.ShapeDtypeStruct(v, f32) for v in outs),
        in_specs=[VM] * len(parts),
        out_specs=(VM,) * 4,
        compiler_params=pltpu.CompilerParams(vmem_limit_bytes=24 * 2**20),
        cost_estimate=BRIEF,
    )(*parts)


def place_kernel(at_ref, *refs, ranks):
    whole, halves, out_ref = refs[:ranks], refs[ranks:-1], refs[-1]
    for i in range(ranks):
        src = at_ref[1] ^ i
        out_ref[3 * (src // 2) + 2 * (src % 2)] = whole[i][...].astype(out_ref.dtype)
    for i in range(ranks // 2):
        src = at_ref[1] % (ranks // 2) ^ i
        out_ref[3 * src + 1] = halves[i][...].astype(out_ref.dtype)


def place_rows(at, whole, halves, kind, deps=()):
    ranks = len(whole)
    shape = (3 * ranks // 2,) + whole[0].shape

    def kernel(at_ref, *refs):
        place_kernel(at_ref, *refs[: ranks + ranks // 2], refs[-1], ranks=ranks)

    return pl.pallas_call(
        kernel,
        out_shape=jax.ShapeDtypeStruct(shape, kind),
        in_specs=[SM] + [VM] * (ranks + ranks // 2) + [AN] * len(deps),
        out_specs=VM,
        compiler_params=pltpu.CompilerParams(vmem_limit_bytes=24 * 2**20),
        cost_estimate=BRIEF,
    )(at, *whole, *halves, *deps)


def patches_kernel(at_ref, *refs):
    ins, out_ref = refs[:-1], refs[-1]
    pairs = len(ins) // 2
    for i in range(pairs):
        out_ref[3 * i + 1] = jnp.zeros(out_ref.shape[1:], f32)
    for i in range(len(ins)):
        src = at_ref[1] ^ i
        out_ref[3 * (src // 2) + 2 * (src % 2)] = ins[i][0].astype(f32)
        out_ref[3 * (src // 2) + 1] += ins[i][1].astype(f32)


def place_patches(at, parts):
    shape = (3 * len(parts) // 2,) + parts[0].shape[1:]
    return pl.pallas_call(
        patches_kernel,
        out_shape=jax.ShapeDtypeStruct(shape, f32),
        in_specs=[SM] + [VM] * len(parts),
        out_specs=VM,
        compiler_params=pltpu.CompilerParams(vmem_limit_bytes=24 * 2**20),
        cost_estimate=BRIEF,
    )(at, *parts)


CP = 32


def place(perm, toks, TR, TC):
    own, ext = TR * TC, perm.shape[2]
    tok = lax.broadcasted_iota(jnp.int32, (toks, 1), 0)
    row = jnp.where(tok < own, tok // TC, jnp.where(tok < own + TR, tok - own, TR))
    col = jnp.where(
        tok < own, tok % TC, jnp.where(tok < own + TR, TC, tok - own - TR)
    )
    real = tok <= own + TR + TC
    pixel = lax.broadcasted_iota(jnp.int32, (toks, ext), 1)
    for a in range(2):
        for b in range(2):
            ok = real & ((row < TR) | (a == 0)) & ((col < TC) | (b == 0))
            at = jnp.where(ok, (2 * row + a) * (2 * TC + 1) + 2 * col + b, -1)
            perm[2 * a + b] = jnp.where(pixel == at, 1.0, 0.0).astype(bf16)


def pixel_grad_kernel(cot_ref, w_ref, out_ref, perm, *, TR, TC):
    @pl.when(pl.program_id(0) == 0)
    def _():
        place(perm, out_ref.shape[1], TR, TC)

    grad = dot(cot_ref[0], w_ref[0], NT)
    hi = grad.astype(bf16)
    lo = (grad - hi.astype(f32)).astype(bf16)
    parts = [dot(perm[i], hi, NT) + dot(perm[i], lo, NT) for i in range(4)]
    out_ref[0] = jnp.concatenate(parts, axis=1)


def pixel_sample_kernel(x_ref, w_ref, out_ref, perm, *, TR, TC):
    @pl.when(pl.program_id(0) == 0)
    def _():
        place(perm, x_ref.shape[1], TR, TC)

    x = x_ref[0]
    window = sum(dot(x[:, i * CP : (i + 1) * CP], perm[i], TN) for i in range(4))
    out_ref[0] = dot(window.astype(bf16), w_ref[0], NN).astype(bf16)


def per_plane(body, first, weights, out_rows, out_lanes, out_type, toks, TR, TC):
    planes, ext, samples = weights.shape

    def whole(shape):
        return pl.BlockSpec((1,) + shape, lambda i: (i, 0, 0))

    return pl.pallas_call(
        functools.partial(body, TR=TR, TC=TC),
        grid=(planes,),
        out_shape=jax.ShapeDtypeStruct((planes, out_rows, out_lanes), out_type),
        in_specs=[whole(first.shape[1:]), whole((ext, samples))],
        out_specs=whole((out_rows, out_lanes)),
        scratch_shapes=[pltpu.VMEM((4, toks, ext), bf16)],
        compiler_params=pltpu.CompilerParams(vmem_limit_bytes=24 * 2**20),
        cost_estimate=BRIEF,
    )(first, weights)


def swap_seq(value):
    return lax.all_to_all(value, "seq", split_axis=0, concat_axis=0, tiled=True)


def swap_mp(value):
    return lax.all_to_all(value, "mp", split_axis=0, concat_axis=0, tiled=True)


def swap_all(value):
    return lax.all_to_all(value, ("seq", "mp"), split_axis=0, concat_axis=0, tiled=True)


def swap_pair(value):
    count = lax.axis_size("mp")
    return lax.ppermute(value, "mp", [(i, i ^ 1) for i in range(count)])


def gather_rows(piece):
    return lax.all_gather(piece, ("mp", "seq"), axis=0, tiled=False)


def bundle_part(bundle, at, rows):
    pieces, _, D = bundle.shape
    if rows % 16 == 0 and at % rows == 0:
        return bundle, ((pieces, rows, D), (0, at // rows, 0))
    value = bundle[:, at : at + rows].reshape(1, -1, D)
    return value, (value.shape, None)


def by_step(part, steps):
    (pieces, rows, D), at = part[1]
    if pieces > 1:
        return part[0], pl.BlockSpec((pieces // steps, rows, D), lambda i: (i, at[1], 0))
    return part[0], pl.BlockSpec((1, rows // steps, D), lambda i: (0, i, 0))


def reduce_rows(value):
    return lax.psum_scatter(value, "seq", scatter_dimension=0, tiled=True)


def to_ranks(blocks):
    moves = [[(i, i ^ step) for i in range(len(blocks))] for step in range(len(blocks))]
    return [v if i == 0 else lax.ppermute(v, "mp", moves[i]) for i, v in enumerate(blocks)]


def to_halves(blocks):
    pairs = len(blocks)
    arrived = []
    for step in range(pairs):
        moves = [(2 * p + h, pairs * h + (p ^ step)) for p in range(pairs) for h in range(2)]
        arrived.append(lax.ppermute(blocks[step], "mp", moves))
    return arrived


def sum_ranks(value):
    return lax.psum_scatter(value, "mp", scatter_dimension=1, tiled=True).astype(f32)


def gather_pieces(value):
    shares = lax.axis_size("seq")
    pieces = []
    for step in range(0, shares, 2):
        moves = [(i, i ^ step) for i in range(shares)]
        pieces.append(value if step == 0 else lax.ppermute(value, "seq", moves))
    cores = [(i, i ^ 1) for i in range(shares)]
    return [p for piece in pieces for p in (piece, lax.ppermute(piece, "seq", cores))]


def per_device(
    tokens,
    patches,
    counts,
    norm_gains,
    norm_shifts,
    cross_query,
    cross_kv,
    cross_out,
    self_qkv,
    self_out,
    mlp_up,
    mlp_down,
    decoder,
    sample_weights,
    tokens_cot,
    sample_cot,
):
    objects, R, D = tokens.shape
    S, M = lax.axis_size("seq"), lax.axis_size("mp")
    s, m = lax.axis_index("seq"), lax.axis_index("mp")
    pairs = M // 2
    if objects != 3 * pairs or S != 2 * M or D % (HD * S) != 0:
        raise ValueError("unexpected sizes")
    pair, half = m // 2, m % 2
    at_a, at_b = 3 * pair + 2 * half, 3 * pair + 1
    RB = R // 2
    RS = R + RB
    rows = [R, RB]
    W = D // S
    hpd = W // HD
    slots, width = patches.shape[1], patches.shape[2]
    slot_total = slots * S
    row_total = R * S

    def pick(arr):
        whole = lax.dynamic_index_in_dim(arr, at_b, 0, keepdims=False)
        return [
            lax.dynamic_index_in_dim(arr, at_a, 0, keepdims=False),
            lax.dynamic_slice_in_dim(whole, half * RB, RB, 0),
        ]

    def mine(arr, axis):
        share = arr.shape[axis] // S
        return lax.dynamic_slice_in_dim(arr, s * share, share, axis)

    channels = decoder.shape[1]
    local_dec = jnp.pad(decoder.transpose(2, 1, 0), ((0, 0), (0, CP - channels), (0, 0)))
    local_qkv = self_qkv.reshape(D, 3, 2, W).transpose(2, 1, 3, 0).reshape(-1, D)
    per = D // (S * M)
    dec_rows = 4 * CP // S
    kv_rows = 2 * per
    at = s * kv_rows
    kv_piece = lax.dynamic_slice(
        cross_kv, (0, (at // W) % 2, at // (2 * W) * W + at % W), (width, 1, kv_rows)
    )
    kv_piece = jnp.pad(kv_piece[:, 0].T, ((0, 0), (0, D - width)))
    lead = gather_rows(jnp.concatenate([kv_piece, mine(cross_query, 1).T], axis=0))
    w_kv, w_query = bundle_part(lead, 0, kv_rows), bundle_part(lead, kv_rows, per)
    first = gather_rows(
        jnp.concatenate(
            [mine(local_qkv, 0), mine(cross_out, 0)], axis=0
        )
    )
    up_rows = mlp_up.shape[1] // S
    second = gather_rows(
        jnp.concatenate(
            [
                mine(mlp_up, 1).T,
                mine(mlp_down, 0),
                mine(self_out, 0),
                mine(local_dec.reshape(-1, D), 0),
            ],
            axis=0,
        )
    )
    steps = 8
    w_up = by_step(bundle_part(second, 0, up_rows), steps)
    w_down = by_step(bundle_part(second, up_rows, up_rows), steps)
    w_triple = by_step(bundle_part(first, 0, 3 * per), S)
    w_cross_out = bundle_part(first, 3 * per, per)
    w_self_out = bundle_part(second, 2 * up_rows, per)
    w_dec = bundle_part(second, 2 * up_rows + per, dec_rows)

    x0 = pick(tokens)
    norms = [jnp.stack([norm_gains[i], norm_shifts[i]]) for i in range(3)]
    at = jnp.stack([s, m])
    both = [lax.dynamic_index_in_dim(patches, o, 0, keepdims=False) for o in (at_a, at_b)]
    patch_pieces = gather_pieces(jnp.concatenate(both, axis=0))
    TC = PLANE // 4
    TR = PLANE * 4 // S
    own, rim = TR * TC, TR * TC + TR
    toks = -(-(rim + TC + 1) // 32) * 32
    planes = objects * 3
    weights_in = sample_weights.reshape(planes, *sample_weights.shape[3:])
    cot_in = sample_cot.reshape(planes, channels, -1)
    cot_in = jnp.pad(cot_in, ((0, 0), (0, CP - channels), (0, 0)))
    ext = per_plane(pixel_grad_kernel, cot_in, weights_in, toks, 4 * CP, f32, toks, TR, TC)
    ways = {
        1: [i for i in range(S) if i % 4 != 3],
        4: [i for i in range(S) if i + 4 < S],
        5: [i for i in range(S) if i % 4 != 3 and i + 4 < S],
    }
    rights = lax.ppermute(ext[:, own:rim], "seq", [(i, i + 1) for i in ways[1]])
    belows = lax.ppermute(ext[:, rim : rim + TC], "seq", [(i, i + 4) for i in ways[4]])
    corner = lax.ppermute(ext[:, rim + TC : rim + TC + 1], "seq", [(i, i + 5) for i in ways[5]])
    grid = ext[:, :own].reshape(planes, TR, TC, -1)
    belows = jnp.concatenate([belows[:, :1] + corner, belows[:, 1:]], axis=1)
    grid = grid + jnp.pad(rights[:, :, None], ((0, 0), (0, 0), (0, TC - 1), (0, 0)))
    grid = grid + jnp.pad(belows[:, None], ((0, 0), (0, TR - 1), (0, 0), (0, 0)))
    KA, KB = R // S, RB // S
    cu = 4 * CP
    grad_pix = grid.astype(bf16).reshape(pairs, 3, S, KA, cu)
    gp_a = jnp.stack([grad_pix[:, 0], grad_pix[:, 2]], axis=1).transpose(2, 0, 1, 3, 4)
    gp_b = grad_pix[:, 1].reshape(pairs, S, 2, KB, cu).transpose(1, 0, 2, 3, 4)
    sent = jnp.concatenate([gp_a, gp_b], axis=3).reshape(S * M, KA + KB, cu)

    q1, keys_one, n1, w_query, w_kv = start(
        at, x0, norms[0], w_kv, w_query, patch_pieces, W, [sent]
    )
    heads_one = swap_seq(q1)
    back = swap_all(hold(sent, [heads_one]))
    d_pix = back.reshape(S, M, KA + KB, cu).transpose(2, 0, 1, 3).reshape(RS, M * cu)

    limits = [
        jnp.stack([lax.dynamic_index_in_dim(counts, o, 0, keepdims=False), jnp.int32(0)])
        for o in (at_a, at_b)
    ]
    kv_one = [(slots, (i * slots, 0), (i * slots, W), 0) for i in range(2)]
    o1, res1 = [], []
    for i in range(2):
        out, res = attend(
            limits[i],
            [heads_one, keys_one],
            S,
            (0, rows[i], i * R, 0),
            [(1,) + kv_one[i]],
            slot_total,
            hpd,
            False,
            [(back,), ()][i],
        )
        o1.append(out)
        res1.append(res)

    mids = [
        middle(swap_seq(o1[i].reshape(S, rows[i], W)), x0[i], norms[1], w_cross_out, w_triple)
        for i in range(2)
    ]
    x1, n2, a1, t2 = zip(*mids)

    heads_two = [swap_seq(v) for v in t2]
    pair_kv = swap_pair(heads_two[1][:, :, W:])
    wide = jnp.array([row_total, 0], jnp.int32)
    kv_a2 = (R, (0, W), (0, 2 * W), 0)
    kv_b2 = (RB, (0, W), (0, 2 * W), 0)
    kv_p2 = (RB, (0, 0), (0, W), row_total // 2)
    o_a2, res_a2 = attend(
        wide, [heads_two[0]], S, (0, R, 0, 0), [(0,) + kv_a2], row_total, hpd, True
    )
    o_b2, res_b2 = attend(
        wide,
        [heads_two[1], pair_kv],
        S,
        (0, RB, 0, 0),
        [(0,) + kv_b2, (1,) + kv_p2],
        row_total,
        hpd,
        True,
        [o_a2],
    )
    a2_a = swap_seq(o_a2.reshape(S, R, W))
    a2 = [a2_a, swap_seq(hold(o_b2.reshape(S, RB, W), [a2_a]))]

    hidden = mlp_up.shape[1] * M
    n3, a2, g, du, x3b, pix, e3, d2, e2, da2, sums_three = feed_forward(
        a2,
        x1,
        pick(tokens_cot),
        d_pix,
        norms[2],
        w_self_out,
        w_dec,
        w_up,
        w_down,
        hidden,
        steps,
    )

    da2 = swap_seq(da2)
    grads_one = weight_grads([[(n3, du)], [(e3, g)], [(e2, a2)], [(x3b, d_pix)]], M)
    grads_one = hold(grads_one, [da2])
    pix = hold(pix, [grads_one])
    dq_a2, dkv_a2 = attend_back(
        wide,
        [res_a2, da2, o_a2, heads_two[0]],
        S,
        (R, 0),
        [(3,) + kv_a2],
        row_total,
        hpd,
        True,
        [grads_one],
    )
    grads_one = reduce_rows(grads_one)
    pix = pix.reshape(KA + KB, S, M, cu).transpose(1, 2, 0, 3)
    got = swap_all(pix.reshape(S * M, KA + KB, cu)).reshape(S, pairs, 2, KA + KB, cu)
    half_total = row_total // 2
    kv_p2 = (RB, (0, 0), (0, W), 0)
    dq_p2, dkv_p2 = attend_back(
        wide,
        [res_b2, da2, o_b2, pair_kv],
        S,
        (RB, R),
        [(3,) + kv_p2],
        half_total,
        hpd,
        True,
        [dq_a2, got],
    )
    given = swap_pair(dkv_p2)
    dq_b2, dkv_b2 = attend_back(
        wide,
        [res_b2, da2, o_b2, heads_two[1]],
        S,
        (RB, R),
        [(3,) + kv_b2],
        half_total,
        hpd,
        True,
        [dq_p2],
    )
    dq_b2 = (dq_b2.astype(f32) + dq_p2.astype(f32)).astype(bf16)
    dkv_b2 = (dkv_b2.astype(f32) + given.astype(f32)).astype(bf16)
    dt2 = [
        swap_seq(jnp.concatenate([dq_a2, dkv_a2], axis=1).reshape(S, R, 3 * W)),
        jnp.concatenate([dq_b2, dkv_b2], axis=1).reshape(S, RB, 3 * W),
    ]

    def below(i, deps):
        return middle_back(
            dt2[i], x1[i], d2, (0, R // RB)[i], norms[1], w_cross_out, w_triple, deps
        )

    def cross_back(i, da1, deps):
        dq, dkv = attend_back(
            limits[i],
            [res1[i], da1, o1[i], keys_one],
            S,
            (rows[i], 0),
            [(3,) + kv_one[i]],
            slot_total,
            hpd,
            False,
            deps,
        )
        return dq.reshape(S, rows[i], W), dkv.reshape(S, slots, 2 * W)

    low_a = below(0, [dq_b2])
    x3b = hold(x3b, [low_a[0]])
    blocks_a, blocks_b = x3b[:R].reshape(M, R // M, D), x3b[R:].reshape(pairs, R // M, D)
    blocks_a = [lax.dynamic_index_in_dim(blocks_a, m ^ i, 0, keepdims=False) for i in range(M)]
    blocks_b = [
        lax.dynamic_index_in_dim(blocks_b, pair ^ i, 0, keepdims=False) for i in range(pairs)
    ]
    blocks_a, blocks_b = to_ranks(blocks_a), to_halves(blocks_b)
    da1_a = swap_seq(low_a[2])
    dt2[1] = swap_seq(hold(dt2[1], [da1_a]))
    dq1_a, dkv1_a = cross_back(0, da1_a, [])
    grads_one = sum_ranks(hold(grads_one, [low_a[0]]))
    low_b = below(1, [dkv1_a])
    da1_b = swap_seq(low_b[2])
    dq1_a = swap_seq(hold(dq1_a, [da1_b]))
    dkv1_a_rows = swap_seq(hold(dkv1_a, [da1_b]))
    d1, e1, da1, sums_two = zip(low_a, low_b)

    grads_two = weight_grads(
        [[(n2[i], dt2[i]) for i in range(2)], [(e1[i], a1[i]) for i in range(2)]], M, [grads_one] + blocks_a + blocks_b
    )
    dq1_b, dkv1_b = cross_back(1, da1_b, [grads_two])
    dkv1 = (dkv1_a, dkv1_b)
    grads_two = reduce_rows(grads_two)
    both_b = swap_seq(jnp.concatenate([dq1_b, dkv1_b], axis=2))
    two = sums_two[0] + sums_two[1]
    small = jnp.concatenate([two, sums_three], axis=0)
    by_head = finish(at, dkv1, patch_pieces)
    done = end(
        at,
        dq1_a,
        both_b,
        dkv1_a_rows,
        w_query,
        w_kv,
        x0,
        n1,
        d1,
        small,
        norm_gains[:1],
        by_head,
        M,
    )
    got_last = swap_seq(done[-1])
    grad_tokens = place_rows(at, to_ranks(done[:M]), to_halves(done[M : M + pairs]), f32)
    patch_grad = place_patches(at, to_ranks([done[-2]] * M))
    heads = by_head.shape[1]
    final = last(to_ranks(mix(at, got_last, M, heads)), heads)
    grad_cross_query, grad_keys, grad_values, small = final
    grad_cross_kv = jnp.stack([grad_keys, grad_values], axis=1)

    px_a = got[:, :, :, :KA].transpose(1, 2, 0, 3, 4).reshape(pairs, 2, S * KA, cu)
    px_b = got[:, :, :, KA:].transpose(1, 0, 2, 3, 4).reshape(pairs, S * KA, cu)
    tile = jnp.stack([px_a[:, 0], px_b, px_a[:, 1]], axis=1).reshape(planes, TR, TC, cu)
    rights = lax.ppermute(tile[:, :, 0], "seq", [(i + 1, i) for i in ways[1]])
    belows = lax.ppermute(tile[:, 0], "seq", [(i + 4, i) for i in ways[4]])
    corner = lax.ppermute(tile[:, 0, :1], "seq", [(i + 5, i) for i in ways[5]])
    fill = jnp.zeros((planes, toks - rim - TC - 1, cu), bf16)
    ext = jnp.concatenate([tile.reshape(planes, own, cu), rights, belows, corner, fill], axis=1)
    ext = hold(ext, [done[-1]])
    tokens_out = place_rows(at, blocks_a, blocks_b, bf16, [done[-1]])
    sampled = per_plane(
        pixel_sample_kernel, ext, weights_in, CP, weights_in.shape[2], bf16, toks, TR, TC
    )
    sampled = sampled[:, :channels].reshape(objects, 3, channels, 1, -1)

    grads_two = sum_ranks(grads_two)
    ff = hidden // M
    grad_mlp_up, grad_mlp_down = grads_one[:, :ff], grads_one[:, ff : 2 * ff].T
    grad_self_out = grads_one[:, 2 * ff : 2 * ff + D // M].T
    grad_decoder = grads_one[:, 2 * ff + D // M :]
    grad_decoder = grad_decoder.reshape(D // S, 4, CP)[:, :, :channels].transpose(0, 2, 1)
    grad_self_qkv = grads_two[:, : 3 * D // M].reshape(D // S, 2, 3, W).transpose(0, 2, 1, 3)
    grad_cross_out = grads_two[:, 3 * D // M :].T

    return (
        tokens_out,
        sampled,
        grad_tokens,
        patch_grad,
        jnp.stack([small[0], small[2], small[4]]),
        jnp.stack([small[1], small[3]]),
        small[5],
        grad_cross_query,
        grad_cross_kv,
        grad_cross_out,
        grad_self_qkv.reshape(D // S, 3, -1),
        grad_self_out,
        grad_mlp_up,
        grad_mlp_down,
        grad_decoder,
    )


def solution(mesh):
    return jax.shard_map(
        per_device,
        mesh=mesh,
        in_specs=(
            P(None, "seq", None),
            P(None, "seq", None),
            P(),
            P(),
            P(),
            P(None, "mp"),
            P(None, None, "mp"),
            P("mp", None),
            P(None, None, "mp"),
            P("mp", None),
            P(None, "mp"),
            P("mp", None),
            P(None, "mp", None),
            P(None, None, "seq", None, None),
            P(None, "seq", None),
            P(None, None, "mp", "seq", None),
        ),
        out_specs=(
            P(None, ("seq", "mp"), None),
            P(None, None, "mp", "seq", None),
            P(None, ("seq", "mp"), None),
            P(None, "seq", None),
            P(None, "seq"),
            P(None, "seq"),
            P("seq"),
            P("seq", "mp"),
            P("seq", None, "mp"),
            P("mp", "seq"),
            P("seq", None, "mp"),
            P("mp", "seq"),
            P("seq", "mp"),
            P("mp", "seq"),
            P("seq", "mp", None),
        ),
        check_vma=False,
    )
```

```python
import functools
import math

import jax
import jax.numpy as jnp
from jax import lax
from jax.experimental import pallas as pl
from jax.experimental.pallas import tpu as pltpu
from jax.sharding import PartitionSpec as P


PLANE = 32
HD = 64
LANES = 128
norm_eps = 1e-05
f32 = jnp.float32
bf16 = jnp.bfloat16

NT = (((1,), (1,)), ((), ()))
NN = (((1,), (0,)), ((), ()))
TN = (((0,), (0,)), ((), ()))


def dot(a, b, dims):
    return lax.dot_general(a, b, dims, preferred_element_type=f32)


def mm(a, b):
    return jnp.dot(a, b, preferred_element_type=f32)


def split3(v):
    hi = v.astype(bf16).astype(f32)
    rest = v - hi
    mid = rest.astype(bf16).astype(f32)
    return hi, mid, rest - mid


def spread(base, cols):
    lane = lax.broadcasted_iota(jnp.int32, (base.shape[0], HD), 1)
    tail = jnp.zeros((base.shape[0], HD), f32)
    for at, col in cols.items():
        tail = jnp.where(lane == at, col, tail)
    return jnp.concatenate([base, tail], axis=1).astype(bf16)


def load_keys(n_ref, kv_specs, refs, ka, va, hpd, blocks):
    for ref_at, rows, k_at, v_at, base in kv_specs:
        src = refs[ref_at]

        def build(i, _):
            natural = base + (i ^ n_ref[1]) * rows
            dst = pl.ds(pl.multiple_of(natural, 16), rows)
            slot = natural + lax.broadcasted_iota(jnp.int32, (rows, 1), 0)
            mask = jnp.where(slot < n_ref[0], 0.0, -1e30).astype(f32)
            for h in range(hpd):
                k = src[i, k_at[0] : k_at[0] + rows, k_at[1] + h * HD : k_at[1] + (h + 1) * HD]
                v = src[i, v_at[0] : v_at[0] + rows, v_at[1] + h * HD : v_at[1] + (h + 1) * HD]
                ka[h, dst, :] = spread(k.astype(f32), {0: 1.0, 1: 1.0, 2: 1.0, 3: mask})
                va[h, dst, :] = spread(v.astype(f32), {0: 1.0, 1: 1.0, 2: 1.0})
            return 0

        lax.fori_loop(0, blocks, build, 0)


def fwd_kernel(n_ref, *refs, n_in, blocks, q_spec, kv_specs, hpd, bq, kc, fixed):
    ins, (o_ref, qa_ref, ka, va) = refs[:n_in], refs[-4:]
    load_keys(n_ref, kv_specs, ins, ka, va, hpd, blocks)
    q_at, rows_q, q_off, q_lane = q_spec

    def build(i, _):
        dst = pl.ds(pl.multiple_of((i ^ n_ref[1]) * rows_q, 16), rows_q)
        for h in range(hpd):
            q = ins[q_at][i, q_off : q_off + rows_q, q_lane + h * HD : q_lane + (h + 1) * HD]
            qa_ref[h, dst, :] = spread(q.astype(f32) * (1.0 / math.sqrt(HD)), {3: 1.0})
        return 0

    lax.fori_loop(0, blocks, build, 0)
    total = ka.shape[1]

    def block(b, _):
        rows = pl.ds(pl.multiple_of(b * bq, bq), bq)

        def chunk(c, carry):
            cols = pl.ds(pl.multiple_of(c * kc, kc), kc)
            out = []
            for h in range(hpd):
                m, acc = carry[h]
                s = dot(qa_ref[h, rows, :], ka[h, cols, :], NT)
                top = jnp.maximum(m, jnp.max(s, axis=1, keepdims=True))
                p = jnp.exp(s - top).astype(bf16)
                out.append((top, acc * jnp.exp(m - top) + dot(p, va[h, cols, :], NN)))
            return tuple(out)

        carry = ((jnp.full((bq, 1), -1e30, f32), jnp.zeros((bq, LANES), f32)),) * hpd
        if fixed:
            for c in range(total // kc):
                carry = chunk(c, carry)
        else:
            carry = lax.fori_loop(0, (n_ref[0] + kc - 1) // kc, chunk, carry)
        outs = []
        for h in range(hpd):
            m, acc = carry[h]
            norm = acc[:, HD : HD + 1]
            outs.append(acc[:, :HD] / norm)
            hi, mid, lo = split3(-(m + jnp.log(norm)))
            qa_ref[h, rows, :] = spread(
                qa_ref[h, rows, :HD].astype(f32), {0: hi, 1: mid, 2: lo, 3: 1.0}
            )
        o_ref[rows, :] = jnp.concatenate(outs, axis=1).astype(bf16)
        return 0

    lax.fori_loop(0, qa_ref.shape[1] // bq, block, 0)


def bwd_kernel(n_ref, *refs, n_in, n_dep, blocks, do_spec, kv_specs, hpd, bq, kc, fixed, form):
    ins, (*outs, ka, va, da, dk, dv, dq) = refs[:n_in], refs[n_in + n_dep :]
    qa_ref, do_ref, o_ref = ins[:3]
    load_keys(n_ref, kv_specs, ins, ka, va, hpd, blocks)
    rows_q, do_off = do_spec

    def build(i, _):
        rows = pl.ds(pl.multiple_of(i * rows_q, 16), rows_q)
        for h in range(hpd):
            d = do_ref[i, do_off : do_off + rows_q, h * HD : (h + 1) * HD].astype(f32)
            o = o_ref[rows, h * HD : (h + 1) * HD].astype(f32)
            hi, mid, lo = split3(-jnp.sum(d * o, axis=1, keepdims=True))
            da[h, rows, :] = spread(d, {0: hi, 1: mid, 2: lo})
        return 0

    lax.fori_loop(0, blocks, build, 0)
    dk[...] = jnp.zeros_like(dk)
    dv[...] = jnp.zeros_like(dv)
    total = ka.shape[1]
    steps = total // kc if fixed else (n_ref[0] + kc - 1) // kc

    def block(b, _):
        rows = pl.ds(pl.multiple_of(b * bq, bq), bq)

        def chunk(c, dqs):
            cols = pl.ds(pl.multiple_of(c * kc, kc), kc)
            out = []
            for h in range(hpd):
                k, q, d = ka[h, cols, :], qa_ref[h, rows, :], da[h, rows, :]
                p = jnp.exp(dot(k, q, NT))
                dp = dot(va[h, cols, :], d, NT)
                dv[h, cols, :] += dot(p.astype(bf16), d, NN)
                g = (p * dp).astype(bf16)
                dk[h, cols, :] += dot(g, q, NN)
                out.append(dqs[h] + dot(k, g, TN))
            return tuple(out)

        dqs = lax.fori_loop(0, steps, chunk, (jnp.zeros((LANES, bq), f32),) * hpd)
        grad = jnp.concatenate([v[:HD, :] for v in dqs], axis=0).T
        dq[rows, :] = (grad * (1.0 / math.sqrt(HD))).astype(bf16)
        return 0

    lax.fori_loop(0, qa_ref.shape[1] // bq, block, 0)
    step = total // blocks

    def finish(i, _):
        rows = pl.ds(pl.multiple_of(i * step, 16), step)
        q_rows = pl.ds(pl.multiple_of(i * rows_q, 16), rows_q)
        k, v = [
            jnp.concatenate([d[h, rows, :HD] for h in range(hpd)], axis=1).astype(bf16)
            for d in (dk, dv)
        ]
        if form == "split":
            outs[0][q_rows, :] = dq[q_rows, :]
            outs[1][rows, :] = jnp.concatenate([k, v], axis=1)
        elif form == "lanes":
            outs[0][i] = jnp.concatenate([dq[q_rows, :], k, v], axis=1)
        else:
            outs[0][i, :rows_q, :] = dq[q_rows, :]
            outs[0][i, rows_q : rows_q + step, :] = k
            outs[0][i, rows_q + step :, :] = v
        return 0

    lax.fori_loop(0, blocks, finish, 0)


VM = pl.BlockSpec(memory_space=pltpu.VMEM)
SM = pl.BlockSpec(memory_space=pltpu.SMEM)
BRIEF = pl.CostEstimate(flops=10**6, bytes_accessed=10**5, transcendentals=0)
AN = pl.BlockSpec(memory_space=pl.ANY)


def fit(rows, most):
    return math.gcd(rows, most)


def attend(limits, ins, blocks, q_spec, kv_specs, total, hpd, fixed, deps=()):
    queries = blocks * q_spec[1]
    kc = fit(total, 1024 if fixed else 512)
    body = functools.partial(
        fwd_kernel,
        n_in=len(ins),
        blocks=blocks,
        q_spec=q_spec,
        kv_specs=kv_specs,
        hpd=hpd,
        bq=fit(queries, 512),
        kc=kc,
        fixed=fixed,
    )
    work = hpd * queries * total
    return pl.pallas_call(
        body,
        out_shape=(
            jax.ShapeDtypeStruct((queries, hpd * HD), bf16),
            jax.ShapeDtypeStruct((hpd, queries, LANES), bf16),
        ),
        in_specs=[SM] + [VM] * len(ins) + [AN] * len(deps),
        out_specs=(VM, VM),
        scratch_shapes=[pltpu.VMEM((hpd, total, LANES), bf16)] * 2,
        compiler_params=pltpu.CompilerParams(vmem_limit_bytes=44 * 2**20),
        cost_estimate=BRIEF,
    )(limits, *ins, *deps)


def attend_back(limits, ins, blocks, do_spec, kv_specs, total, hpd, fixed, deps=(), form="split"):
    queries = blocks * do_spec[0]
    W, step = hpd * HD, total // blocks
    shapes = {
        "split": [(queries, W), (total, 2 * W)],
        "lanes": [(blocks, step, 3 * W)],
        "rows": [(blocks, do_spec[0] + 2 * step, W)],
    }[form]
    body = functools.partial(
        bwd_kernel,
        n_in=len(ins),
        n_dep=len(deps),
        blocks=blocks,
        do_spec=do_spec,
        kv_specs=kv_specs,
        hpd=hpd,
        bq=fit(queries, 512),
        kc=fit(total, 512),
        fixed=fixed,
        form=form,
    )
    out = pl.pallas_call(
        body,
        out_shape=tuple(jax.ShapeDtypeStruct(v, bf16) for v in shapes),
        in_specs=[SM] + [VM] * len(ins) + [AN] * len(deps),
        out_specs=(VM,) * len(shapes),
        scratch_shapes=[pltpu.VMEM((hpd, total, LANES), bf16)] * 2
        + [pltpu.VMEM((hpd, queries, LANES), bf16)]
        + [pltpu.VMEM((hpd, total, LANES), f32)] * 2
        + [pltpu.VMEM((queries, W), bf16)],
        compiler_params=pltpu.CompilerParams(vmem_limit_bytes=52 * 2**20),
        cost_estimate=BRIEF,
    )(limits, *ins, *deps)
    return out if len(out) > 1 else out[0]


def norm_parts(values):
    center = values - jnp.mean(values, axis=-1, keepdims=True)
    scale = lax.rsqrt(jnp.mean(center * center, axis=-1, keepdims=True) + norm_eps)
    return center * scale, scale


def layer_norm(values, gain_row, shift_row):
    return (norm_parts(values)[0] * gain_row + shift_row).astype(bf16)


def norm_back(values, gain_row, grad_out):
    unit, scale = norm_parts(values)
    lifted = grad_out * gain_row
    grad_in = scale * (
        lifted
        - jnp.mean(lifted, axis=-1, keepdims=True)
        - unit * jnp.mean(lifted * unit, axis=-1, keepdims=True)
    )
    gain = jnp.sum(grad_out * unit, axis=0, keepdims=True)
    return grad_in, gain, jnp.sum(grad_out, axis=0, keepdims=True)


def flat(ref):
    return ref[...].reshape(-1, ref.shape[-1])


def joined(ref):
    return jnp.concatenate([ref[i] for i in range(ref.shape[0])], axis=1)


def once(shape, index=None):
    at = (0,) * len(shape) if index is None else index
    return pl.BlockSpec(shape, lambda i: at, pipeline_mode=pl.Buffered(1))


def held(shape):
    return pl.BlockSpec(shape, lambda i: (0,) * len(shape))


def mid_kernel(a_ref, x_ref, norm_ref, wo_ref, wt_ref, *refs):
    x1_ref, n_ref, ac_ref, t_ref = refs[-4:]

    @pl.when(pl.program_id(0) == 0)
    def _():
        a = joined(a_ref)
        ac_ref[...] = a
        x1 = x_ref[...].astype(f32) + dot(a, flat(wo_ref), NN)
        x1_ref[...] = x1
        n_ref[...] = layer_norm(x1, norm_ref[0:1, :], norm_ref[1:2, :])

    t_ref[0] = dot(n_ref[...], flat(wt_ref), NT).astype(bf16)


def middle(a, x, norm, w_out, w_triple, deps=()):
    S, rows, W = a.shape
    D = S * W
    return pl.pallas_call(
        mid_kernel,
        grid=(S,),
        out_shape=(
            jax.ShapeDtypeStruct((rows, D), f32),
            jax.ShapeDtypeStruct((rows, D), bf16),
            jax.ShapeDtypeStruct((rows, D), bf16),
            jax.ShapeDtypeStruct((S, rows, 3 * W), bf16),
        ),
        in_specs=[
            once((S, rows, W)),
            once((rows, D)),
            once((2, D)),
            once(*w_out[1]),
            w_triple[1],
        ]
        + [AN] * len(deps),
        out_specs=(
            held((rows, D)),
            held((rows, D)),
            held((rows, D)),
            pl.BlockSpec((1, rows, 3 * W), lambda i: (i, 0, 0)),
        ),
        compiler_params=pltpu.CompilerParams(vmem_limit_bytes=40 * 2**20),
        cost_estimate=BRIEF,
    )(a, x, norm, w_out[0], w_triple[0], *deps)


def mlp_kernel(
    aa_ref,
    ab_ref,
    xa_ref,
    xb_ref,
    ca_ref,
    cb_ref,
    dp_ref,
    norm_ref,
    ws_ref,
    wd_ref,
    up_ref,
    down_ref,
    n_ref,
    ac_ref,
    g_ref,
    du_ref,
    x3_ref,
    pix_ref,
    e3_ref,
    d2_ref,
    e2_ref,
    da_ref,
    sum_ref,
    x2,
    d3,
    acc,
    back,
    *,
    steps,
):
    step = pl.program_id(0)
    R = xa_ref.shape[0]
    S, _, W = aa_ref.shape

    @pl.when(step == 0)
    def _():
        for rows, a_ref, x_ref, c_ref in (
            (slice(0, R), aa_ref, xa_ref, ca_ref),
            (slice(R, x2.shape[0]), ab_ref, xb_ref, cb_ref),
        ):
            a = joined(a_ref)
            ac_ref[rows, :] = a
            x = x_ref[...] + dot(a, flat(ws_ref), NN)
            x2[rows, :] = x
            n_ref[rows, :] = layer_norm(x, norm_ref[0:1, :], norm_ref[1:2, :])
            d = c_ref[...].astype(f32) + dot(dp_ref[rows, :], flat(wd_ref), NN)
            d3[rows, :] = d
            e3_ref[rows, :] = d.astype(bf16)
        acc[...] = jnp.zeros_like(acc)
        back[...] = jnp.zeros_like(back)

    up = flat(up_ref)
    down = flat(down_ref)
    u = dot(n_ref[...], up, NT)
    slope = math.sqrt(2.0 / math.pi)
    square = u * u
    bend = jnp.tanh(slope * u * (1.0 + 0.044715 * square))
    half = 0.5 * (1.0 + bend)
    g = (u * half).astype(bf16)
    rise = half + 0.5 * slope * u * (1.0 - bend * bend) * (1.0 + 0.134145 * square)
    du = (dot(e3_ref[...], down, NT) * rise).astype(bf16)
    g_ref[...] = g
    du_ref[...] = du
    acc[...] += dot(g, down, NN)
    back[...] += dot(du, up, NN)

    @pl.when(step == steps - 1)
    def _():
        x3 = (x2[...] + acc[...]).astype(bf16)
        x3_ref[...] = x3
        pix_ref[...] = dot(x3, flat(wd_ref), NT).astype(bf16)
        grad_in, gain, shift = norm_back(x2[...], norm_ref[0:1, :], back[...])
        d2 = d3[...] + grad_in
        d2_ref[...] = d2
        e2 = d2.astype(bf16)
        e2_ref[...] = e2
        sum_ref[...] = jnp.concatenate([gain, shift], axis=0)
        da = dot(e2, flat(ws_ref), NT).astype(bf16)
        for i in range(S):
            da_ref[i] = da[:, i * W : (i + 1) * W]


def feed_forward(a, x1, cot, d_pix, norm, w_out, w_dec, w_up, w_down, hidden, steps):
    S, R, W = a[0].shape
    RB = a[1].shape[1]
    D, total, pixels = S * W, R + RB, d_pix.shape[1]
    part = hidden // steps
    row = jax.ShapeDtypeStruct((total, D), bf16)
    wide = jax.ShapeDtypeStruct((total, hidden), bf16)
    blocked = pl.BlockSpec((total, part), lambda i: (0, i))
    full = held((total, D))
    return pl.pallas_call(
        functools.partial(mlp_kernel, steps=steps),
        grid=(steps,),
        out_shape=(
            row,
            row,
            wide,
            wide,
            row,
            jax.ShapeDtypeStruct((total, pixels), bf16),
            row,
            jax.ShapeDtypeStruct((total, D), f32),
            row,
            jax.ShapeDtypeStruct((S, total, W), bf16),
            jax.ShapeDtypeStruct((2, D), f32),
        ),
        in_specs=[
            once((S, R, W)),
            once((S, RB, W)),
            once((R, D)),
            once((RB, D)),
            once((R, D)),
            once((RB, D)),
            once((total, pixels)),
            once((2, D)),
            once(*w_out[1]),
            once(*w_dec[1]),
            w_up[1],
            w_down[1],
        ],
        out_specs=(
            full,
            full,
            blocked,
            blocked,
            full,
            held((total, pixels)),
            full,
            full,
            full,
            held((S, total, W)),
            held((2, D)),
        ),
        scratch_shapes=[pltpu.VMEM((total, D), f32)] * 4,
        compiler_params=pltpu.CompilerParams(vmem_limit_bytes=60 * 2**20),
        cost_estimate=BRIEF,
    )(*a, *x1, *cot, d_pix, norm, w_out[0], w_dec[0], w_up[0], w_down[0])


def hold_kernel(*refs):
    pass


def hold(value, deps):
    return pl.pallas_call(
        hold_kernel,
        out_shape=jax.ShapeDtypeStruct(value.shape, value.dtype),
        in_specs=[AN] * (1 + len(deps)),
        out_specs=AN,
        input_output_aliases={0: 0},
        cost_estimate=BRIEF,
    )(value, *deps)


def back_kernel(
    t_ref, x_ref, d_ref, norm_ref, wo_ref, wt_ref, *refs, steps
):
    d1_ref, e_ref, da_ref, sum_ref, acc = refs[-5:]
    step = pl.program_id(0)
    part = dot(t_ref[0], flat(wt_ref), NN)

    @pl.when(step == 0)
    def _():
        acc[...] = part

    @pl.when(step > 0)
    def _():
        acc[...] += part

    @pl.when(step == steps - 1)
    def _():
        grad_in, gain, shift = norm_back(x_ref[...], norm_ref[0:1, :], acc[...])
        d1 = d_ref[...] + grad_in
        d1_ref[...] = d1
        e = d1.astype(bf16)
        e_ref[...] = e
        sum_ref[...] = jnp.concatenate([gain, shift], axis=0)
        da = dot(e, flat(wo_ref), NT).astype(bf16)
        W = da_ref.shape[2]
        for i in range(steps):
            da_ref[i] = da[:, i * W : (i + 1) * W]


def middle_back(t, x1, d2, at, norm, w_out, w_triple, deps=()):
    S, rows, wide = t.shape
    D = x1.shape[1]
    W = wide // 3
    return pl.pallas_call(
        functools.partial(back_kernel, steps=S),
        grid=(S,),
        out_shape=(
            jax.ShapeDtypeStruct((rows, D), f32),
            jax.ShapeDtypeStruct((rows, D), bf16),
            jax.ShapeDtypeStruct((S, rows, W), bf16),
            jax.ShapeDtypeStruct((2, D), f32),
        ),
        in_specs=[
            pl.BlockSpec((1, rows, wide), lambda i: (i, 0, 0)),
            once((rows, D)),
            once((rows, D), (at, 0)),
            once((2, D)),
            once(*w_out[1]),
            w_triple[1],
        ]
        + [AN] * len(deps),
        out_specs=(
            held((rows, D)),
            held((rows, D)),
            held((S, rows, W)),
            held((2, D)),
        ),
        scratch_shapes=[pltpu.VMEM((rows, D), f32)],
        compiler_params=pltpu.CompilerParams(vmem_limit_bytes=40 * 2**20),
        cost_estimate=BRIEF,
    )(t, x1, d2, norm, w_out[0], w_triple[0], *deps)


def grads_kernel(*refs, shape, widths):
    count = sum(shape)
    lefts, rights = refs[:count], refs[count : 2 * count]
    out_ref, turned = refs[-1 - count], refs[-count:]

    @pl.when(pl.program_id(0) == 0)
    def _():
        for left, t in zip(lefts, turned):
            t[...] = left[...].T

    at = n = 0
    for pieces, width in zip(shape, widths):
        total = 0.0
        for i in range(n, n + pieces):
            right = joined(rights[i]) if len(rights[i].shape) == 3 else rights[i][...]
            total += dot(turned[i][...], right, NN)
        out_ref[:, at : at + width] = total.astype(bf16)
        at, n = at + width, n + pieces


def weight_grads(terms, ranks, deps=()):
    pieces = [p for term in terms for p in term]
    shape = [len(term) for term in terms]
    widths = [term[0][1].size // term[0][0].shape[0] // ranks for term in terms]
    D, per = pieces[0][0].shape[1], sum(widths)
    lefts = [p[0] for p in pieces]
    rights = [p[1] for p in pieces]
    work = sum(p[0].shape[0] for p in pieces) * D * per * ranks // len(pieces)
    return pl.pallas_call(
        functools.partial(grads_kernel, shape=shape, widths=widths),
        grid=(ranks,),
        out_shape=jax.ShapeDtypeStruct((D, per * ranks), bf16),
        in_specs=[once(v.shape) for v in lefts]
        + [
            pl.BlockSpec((v.shape[0] // ranks,) + v.shape[1:], lambda i: (i, 0, 0))
            if v.ndim == 3
            else pl.BlockSpec((v.shape[0], v.shape[1] // ranks), lambda i: (0, i))
            for v in rights
        ]
        + [AN] * len(deps),
        out_specs=pl.BlockSpec((D, per), lambda i: (0, i)),
        scratch_shapes=[pltpu.VMEM(v.shape[::-1], bf16) for v in lefts],
        compiler_params=pltpu.CompilerParams(vmem_limit_bytes=56 * 2**20),
        cost_estimate=BRIEF,
    )(*lefts, *rights, *deps)


def start_kernel(at_ref, xa_ref, xb_ref, norm_ref, wk_ref, wq_in, *refs, pieces, width):
    p_in, (q_ref, k_ref, n_ref, wq_ref, wkv_ref) = refs[:pieces], refs[-5:]
    seq = at_ref[0]
    R = xa_ref.shape[0]
    W = q_ref.shape[2]
    wq_ref[...] = flat(wq_in)
    wkv_ref[...] = flat(wk_ref)[:, :width]
    for block, x_ref in ((slice(0, R), xa_ref), (slice(R, n_ref.shape[0]), xb_ref)):
        n_ref[block, :] = layer_norm(x_ref[...].astype(f32), norm_ref[0:1, :], norm_ref[1:2, :])
    for i in range(pieces):
        q_ref[i] = dot(n_ref[...], wq_ref[i * W : (i + 1) * W, :], NT).astype(bf16)
    own = wkv_ref[pl.ds(pl.multiple_of(seq * 2 * W, 16), 2 * W), :]
    for i in range(pieces):
        k_ref[seq ^ i] = dot(p_in[i][...], own, NT).astype(bf16)


def start(at, x0, norm, w_kv, w_query, patch_pieces, W, deps):
    S, D = len(patch_pieces), x0[0].shape[1]
    total = x0[0].shape[0] + x0[1].shape[0]
    slots, width = patch_pieces[0].shape
    whole = [x0[0].shape, x0[1].shape, norm.shape]
    outs = [(S, total, W), (S, slots, 2 * W), (total, D), (D, D), (2 * D, width)]
    return pl.pallas_call(
        functools.partial(start_kernel, pieces=S, width=width),
        grid=(1,),
        out_shape=tuple(jax.ShapeDtypeStruct(v, bf16) for v in outs),
        in_specs=[SM]
        + [once(v) for v in whole]
        + [once(*w_kv[1]), once(*w_query[1])]
        + [once((slots, width))] * S
        + [AN] * len(deps),
        out_specs=tuple(held(v) for v in outs),
        compiler_params=pltpu.CompilerParams(vmem_limit_bytes=56 * 2**20),
        cost_estimate=BRIEF,
    )(at, *x0, norm, w_kv[0], w_query[0], *patch_pieces, *deps)


def finish_kernel(at_ref, a_ref, b_ref, *refs, pieces, rows):
    p_in, out_ref = refs[:pieces], refs[-1]
    seq = at_ref[0]
    W = a_ref.shape[2]
    slots = (a_ref.shape[1] - rows[0]) // 2
    sums = [0.0, 0.0]
    for i in range(pieces):
        for j, (ref, at) in enumerate(((a_ref, rows[0]), (b_ref, rows[1]))):
            p = p_in[i][j * slots : (j + 1) * slots, :]
            for k in range(2):
                sums[k] += dot(ref[seq ^ i, at + k * slots : at + (k + 1) * slots, :], p, TN)
    wide = sums[0].shape[1] // pieces
    for k in range(2):
        grad = sums[k].T.astype(bf16)
        for i in range(pieces):
            out_ref[i, k * wide : (k + 1) * wide, :] = grad[i * wide : (i + 1) * wide, :]


def finish(at, cross, rows, patch_pieces, deps):
    S, _, W = cross[0].shape
    out = (S, 2 * patch_pieces[0].shape[1] // S, W)
    return pl.pallas_call(
        functools.partial(finish_kernel, pieces=S, rows=rows),
        out_shape=jax.ShapeDtypeStruct(out, bf16),
        in_specs=[SM] + [VM] * (2 + S) + [AN] * len(deps),
        out_specs=VM,
        compiler_params=pltpu.CompilerParams(vmem_limit_bytes=32 * 2**20),
        cost_estimate=BRIEF,
    )(at, *cross, *patch_pieces, *deps)


def end_kernel(
    at_ref, g_ref, wq_ref, wkv_ref, x_ref, n_ref, d_ref, gain_ref, *refs, blocks, more, n_dep
):
    extra, refs = refs[:more], refs[more + n_dep :]
    outs, part_ref, refs = refs[:blocks], refs[blocks], refs[blocks + 1 :]
    outs_more, (n_t, dq, total) = refs[:-3], refs[-3:]
    S, _, W = g_ref.shape
    rows = x_ref.shape[0]
    slots = (g_ref.shape[1] - rows) // 2
    own = rows // blocks
    dq[...] = jnp.concatenate([g_ref[i, :rows, :] for i in range(S)], axis=1)
    n_t[...] = n_ref[...].T
    grad, gain, shift = norm_back(
        x_ref[...].astype(f32), gain_ref[...], dot(dq[...], wq_ref[...], NN)
    )
    total[...] = d_ref[...] + grad
    place = at_ref[1] // 2 if more else at_ref[1]
    for i in range(blocks):
        outs[i][...] = total[pl.ds(pl.multiple_of((place ^ i) * own, 8), own), :].astype(bf16)
    keys = []
    for i in range(S):
        keys += [g_ref[i, rows : rows + slots, :], g_ref[i, rows + slots :, :]]
    part_ref[...] = dot(jnp.concatenate(keys, axis=1), wkv_ref[...], NN).astype(bf16)
    lift = jnp.concatenate([gain, shift], axis=0)
    tall = n_t.shape[0] // S
    for i in range(0, S, 2):
        pair = dot(n_t[...], dq[:, i * W : (i + 2) * W], NN)
        if more:
            pair += extra[0][i // 2]
            for j in range(S):
                block = pair[j * tall : (j + 1) * tall, :].astype(bf16)
                outs_more[0][j, i * tall : (i + 1) * tall, :] = block[:, :W]
                outs_more[0][j, (i + 1) * tall : (i + 2) * tall, :] = block[:, W:]
        else:
            outs_more[0][i // 2] = pair
    if not more:
        outs_more[1][...] = lift
        return
    at = S * tall
    heads = extra[3].shape[1]
    zero = jnp.zeros((2, n_t.shape[0]), f32)
    sums = jnp.concatenate([lift + extra[1][...], extra[2][...], zero], axis=0)
    hi = sums.astype(bf16).astype(f32)
    both = jnp.concatenate([hi, sums - hi], axis=0).astype(bf16)
    for j in range(S):
        outs_more[0][j, at : at + heads, :] = extra[3][j]
        outs_more[0][j, at + heads :, :] = both[:, j * W : (j + 1) * W]


def end(at, got, place, w_query, w_kv, x0, n1, d1, gain, blocks, deps, more=()):
    S, _, W = got.shape
    rows, D = x0.shape
    slots, width = (got.shape[1] - rows) // 2, w_kv.shape[1]
    outs = [((rows // blocks, D), bf16)] * blocks + [((slots, width), bf16)]
    if more:
        outs += [((S, D + more[3].shape[1] + 16, W), bf16)]
    else:
        outs += [((S // 2, D, 2 * W), f32), ((2, D), f32)]
    whole = [got, w_query, w_kv, x0, n1, d1, gain, *more]
    specs = [once(v.shape) for v in whole]
    specs[4] = once((rows, D), (place, 0))
    return pl.pallas_call(
        functools.partial(end_kernel, blocks=blocks, more=len(more), n_dep=len(deps)),
        grid=(1,),
        out_shape=tuple(jax.ShapeDtypeStruct(*v) for v in outs),
        in_specs=[SM] + specs + [AN] * len(deps),
        out_specs=tuple(held(v[0]) for v in outs),
        scratch_shapes=[
            pltpu.VMEM((D, rows), bf16),
            pltpu.VMEM((rows, D), bf16),
            pltpu.VMEM((rows, D), f32),
        ],
        compiler_params=pltpu.CompilerParams(vmem_limit_bytes=56 * 2**20),
        cost_estimate=BRIEF,
    )(at, *whole, *deps)


def mix_kernel(at_ref, x_ref, *refs, heads, ranks):
    outs = refs[-ranks:]
    S, rows, W = x_ref.shape
    blocks = rows - heads - 16
    pair = blocks // len(outs)
    small = sum(x_ref[j, blocks + heads :, :].astype(f32) for j in range(S))
    total = small[:8] + small[8:]
    hi = total.astype(bf16).astype(f32)
    for i in range(len(outs)):
        rank = at_ref[1] ^ i
        src = pl.ds(pl.multiple_of(rank * pair, 16), pair)
        outs[i][:pair, :] = sum(x_ref[j, src, :].astype(f32) for j in range(S)).astype(bf16)
        for k in range(2):
            outs[i][pair + k * heads : pair + (k + 1) * heads, :] = x_ref[
                2 * rank + k, blocks : blocks + heads, :
            ]
        outs[i][pair + 2 * heads :, :] = jnp.concatenate([hi, total - hi], axis=0).astype(bf16)


def mix(at, got, ranks, heads, deps):
    S, rows, W = got.shape
    shape = ((rows - heads - 16) // ranks + 2 * heads + 16, W)
    return pl.pallas_call(
        functools.partial(mix_kernel, heads=heads, ranks=ranks),
        out_shape=(jax.ShapeDtypeStruct(shape, bf16),) * ranks,
        in_specs=[SM, VM] + [AN] * len(deps),
        out_specs=(VM,) * ranks,
        compiler_params=pltpu.CompilerParams(vmem_limit_bytes=24 * 2**20),
        cost_estimate=BRIEF,
    )(at, got, *deps)


def last_kernel(*refs, heads):
    ins, (q_ref, k_ref, v_ref, small_ref) = refs[:-4], refs[-4:]
    total = sum(v[...].astype(f32) for v in ins)
    pair = total.shape[0] - 2 * heads - 16
    q_ref[...] = jnp.concatenate([total[: pair // 2], total[pair // 2 : pair]], axis=1)
    one, two = total[pair : pair + heads], total[pair + heads : pair + 2 * heads]
    k_ref[...] = jnp.concatenate([one[: heads // 2], two[: heads // 2]], axis=1)
    v_ref[...] = jnp.concatenate([one[heads // 2 :], two[heads // 2 :]], axis=1)
    small_ref[...] = total[pair + 2 * heads : pair + 2 * heads + 8] + total[pair + 2 * heads + 8 :]


def last(parts, heads):
    rows, W = parts[0].shape
    pair = rows - 2 * heads - 16
    outs = [(pair // 2, 2 * W), (heads // 2, 2 * W), (heads // 2, 2 * W), (8, W)]
    return pl.pallas_call(
        functools.partial(last_kernel, heads=heads),
        out_shape=tuple(jax.ShapeDtypeStruct(v, f32) for v in outs),
        in_specs=[VM] * len(parts),
        out_specs=(VM,) * 4,
        compiler_params=pltpu.CompilerParams(vmem_limit_bytes=24 * 2**20),
        cost_estimate=BRIEF,
    )(*parts)


def place_kernel(at_ref, *refs, ranks):
    whole, halves, out_ref = refs[:ranks], refs[ranks:-1], refs[-1]
    for i in range(ranks):
        src = at_ref[1] ^ i
        out_ref[3 * (src // 2) + 2 * (src % 2)] = whole[i][...].astype(out_ref.dtype)
    for i in range(ranks // 2):
        src = at_ref[1] % (ranks // 2) ^ i
        out_ref[3 * src + 1] = halves[i][...].astype(out_ref.dtype)


def place_rows(at, whole, halves, kind, deps=()):
    ranks = len(whole)
    shape = (3 * ranks // 2,) + whole[0].shape

    def kernel(at_ref, *refs):
        place_kernel(at_ref, *refs[: ranks + ranks // 2], refs[-1], ranks=ranks)

    return pl.pallas_call(
        kernel,
        out_shape=jax.ShapeDtypeStruct(shape, kind),
        in_specs=[SM] + [VM] * (ranks + ranks // 2) + [AN] * len(deps),
        out_specs=VM,
        compiler_params=pltpu.CompilerParams(vmem_limit_bytes=24 * 2**20),
        cost_estimate=BRIEF,
    )(at, *whole, *halves, *deps)


def patches_kernel(at_ref, *refs):
    ins, out_ref = refs[:-1], refs[-1]
    ranks = len(ins) // 2
    for i in range(ranks // 2):
        out_ref[3 * i + 1] = jnp.zeros(out_ref.shape[1:], f32)
    for i in range(ranks):
        src = at_ref[1] ^ i
        out_ref[3 * (src // 2) + 2 * (src % 2)] = ins[i][...].astype(f32)
        out_ref[3 * (src // 2) + 1] += ins[ranks + i][...].astype(f32)


def place_patches(at, parts_a, parts_b):
    shape = (3 * len(parts_a) // 2,) + parts_a[0].shape
    return pl.pallas_call(
        patches_kernel,
        out_shape=jax.ShapeDtypeStruct(shape, f32),
        in_specs=[SM] + [VM] * (2 * len(parts_a)),
        out_specs=VM,
        compiler_params=pltpu.CompilerParams(vmem_limit_bytes=24 * 2**20),
        cost_estimate=BRIEF,
    )(at, *parts_a, *parts_b)


CP = 32


def place(perm, toks, TR, TC):
    own, ext = TR * TC, perm.shape[2]
    tok = lax.broadcasted_iota(jnp.int32, (toks, 1), 0)
    row = jnp.where(tok < own, tok // TC, jnp.where(tok < own + TR, tok - own, TR))
    col = jnp.where(
        tok < own, tok % TC, jnp.where(tok < own + TR, TC, tok - own - TR)
    )
    real = tok <= own + TR + TC
    pixel = lax.broadcasted_iota(jnp.int32, (toks, ext), 1)
    for a in range(2):
        for b in range(2):
            ok = real & ((row < TR) | (a == 0)) & ((col < TC) | (b == 0))
            at = jnp.where(ok, (2 * row + a) * (2 * TC + 1) + 2 * col + b, -1)
            perm[2 * a + b] = jnp.where(pixel == at, 1.0, 0.0).astype(bf16)


def pixel_grad_kernel(cot_ref, w_ref, *refs, TR, TC):
    out_ref, perm = refs[-2:]

    @pl.when(pl.program_id(0) == 0)
    def _():
        place(perm, out_ref.shape[1], TR, TC)

    grad = dot(cot_ref[0], w_ref[0], NT)
    hi = grad.astype(bf16)
    lo = (grad - hi.astype(f32)).astype(bf16)
    parts = [dot(perm[i], hi, NT) + dot(perm[i], lo, NT) for i in range(4)]
    out_ref[0] = jnp.concatenate(parts, axis=1)


def pixel_sample_kernel(x_ref, w_ref, *refs, TR, TC):
    out_ref, perm = refs[-2:]

    @pl.when(pl.program_id(0) == 0)
    def _():
        place(perm, x_ref.shape[1], TR, TC)

    x = x_ref[0]
    window = sum(dot(x[:, i * CP : (i + 1) * CP], perm[i], TN) for i in range(4))
    out_ref[0] = dot(window.astype(bf16), w_ref[0], NN).astype(bf16)


def per_plane(body, first, weights, out_rows, out_lanes, out_type, toks, TR, TC, deps=()):
    planes, ext, samples = weights.shape

    def whole(shape):
        return pl.BlockSpec((1,) + shape, lambda i: (i, 0, 0))

    return pl.pallas_call(
        functools.partial(body, TR=TR, TC=TC),
        grid=(planes,),
        out_shape=jax.ShapeDtypeStruct((planes, out_rows, out_lanes), out_type),
        in_specs=[whole(first.shape[1:]), whole((ext, samples))] + [AN] * len(deps),
        out_specs=whole((out_rows, out_lanes)),
        scratch_shapes=[pltpu.VMEM((4, toks, ext), bf16)],
        compiler_params=pltpu.CompilerParams(vmem_limit_bytes=24 * 2**20),
        cost_estimate=BRIEF,
    )(first, weights, *deps)


def swap_seq(value):
    return lax.all_to_all(value, "seq", split_axis=0, concat_axis=0, tiled=True)


def swap_mp(value):
    return lax.all_to_all(value, "mp", split_axis=0, concat_axis=0, tiled=True)


def swap_all(value):
    return lax.all_to_all(value, ("seq", "mp"), split_axis=0, concat_axis=0, tiled=True)


def swap_pair(value):
    count = lax.axis_size("mp")
    return lax.ppermute(value, "mp", [(i, i ^ 1) for i in range(count)])


def gather_rows(piece):
    return lax.all_gather(piece, ("mp", "seq"), axis=0, tiled=False)


def bundle_part(bundle, at, rows):
    pieces, _, D = bundle.shape
    if rows % 16 == 0 and at % rows == 0:
        return bundle, ((pieces, rows, D), (0, at // rows, 0))
    value = bundle[:, at : at + rows].reshape(1, -1, D)
    return value, (value.shape, None)


def by_step(part, steps):
    (pieces, rows, D), at = part[1]
    if pieces > 1:
        return part[0], pl.BlockSpec((pieces // steps, rows, D), lambda i: (i, at[1], 0))
    return part[0], pl.BlockSpec((1, rows // steps, D), lambda i: (0, i, 0))


def reduce_rows(value):
    return lax.psum_scatter(value, "seq", scatter_dimension=0, tiled=True)


def to_ranks(blocks):
    moves = [[(i, i ^ step) for i in range(len(blocks))] for step in range(len(blocks))]
    return [v if i == 0 else lax.ppermute(v, "mp", moves[i]) for i, v in enumerate(blocks)]


def to_halves(blocks):
    pairs = len(blocks)
    arrived = []
    for step in range(pairs):
        moves = [(2 * p + h, pairs * h + (p ^ step)) for p in range(pairs) for h in range(2)]
        arrived.append(lax.ppermute(blocks[step], "mp", moves))
    return arrived


def sum_ranks(value):
    return lax.psum_scatter(value, "mp", scatter_dimension=1, tiled=True).astype(f32)


def gather_pieces(value):
    shares = lax.axis_size("seq")
    pieces = []
    for step in range(0, shares, 2):
        moves = [(i, i ^ step) for i in range(shares)]
        pieces.append(value if step == 0 else lax.ppermute(value, "seq", moves))
    cores = [(i, i ^ 1) for i in range(shares)]
    return [p for piece in pieces for p in (piece, lax.ppermute(piece, "seq", cores))]


def per_device(
    tokens,
    patches,
    counts,
    norm_gains,
    norm_shifts,
    cross_query,
    cross_kv,
    cross_out,
    self_qkv,
    self_out,
    mlp_up,
    mlp_down,
    decoder,
    sample_weights,
    tokens_cot,
    sample_cot,
):
    objects, R, D = tokens.shape
    S, M = lax.axis_size("seq"), lax.axis_size("mp")
    s, m = lax.axis_index("seq"), lax.axis_index("mp")
    pairs = M // 2
    if objects != 3 * pairs or S != 2 * M or D % (HD * S) != 0:
        raise ValueError("unexpected sizes")
    pair, half = m // 2, m % 2
    at_a, at_b = 3 * pair + 2 * half, 3 * pair + 1
    RB = R // 2
    RS = R + RB
    rows = [R, RB]
    W = D // S
    hpd = W // HD
    slots, width = patches.shape[1], patches.shape[2]
    slot_total = slots * S
    row_total = R * S

    def pick(arr):
        whole = lax.dynamic_index_in_dim(arr, at_b, 0, keepdims=False)
        return [
            lax.dynamic_index_in_dim(arr, at_a, 0, keepdims=False),
            lax.dynamic_slice_in_dim(whole, half * RB, RB, 0),
        ]

    def mine(arr, axis):
        share = arr.shape[axis] // S
        return lax.dynamic_slice_in_dim(arr, s * share, share, axis)

    channels = decoder.shape[1]
    local_dec = jnp.pad(decoder.transpose(2, 1, 0), ((0, 0), (0, CP - channels), (0, 0)))
    part = S // 2
    qkv_piece = lax.dynamic_slice_in_dim(self_qkv, s // part * W, W, 2).reshape(D, 3 * W)
    qkv_piece = lax.dynamic_slice_in_dim(qkv_piece, s % part * (3 * W // part), 3 * W // part, 1)
    per = D // (S * M)
    dec_rows = 4 * CP // S
    kv_rows = 2 * per
    at = s * kv_rows
    kv_piece = lax.dynamic_slice(
        cross_kv, (0, (at // W) % 2, at // (2 * W) * W + at % W), (width, 1, kv_rows)
    )
    kv_piece = jnp.pad(kv_piece[:, 0].T, ((0, 0), (0, D - width)))
    lead = gather_rows(jnp.concatenate([kv_piece, mine(cross_query, 1).T], axis=0))
    w_kv, w_query = bundle_part(lead, 0, kv_rows), bundle_part(lead, kv_rows, per)
    first = gather_rows(
        jnp.concatenate(
            [qkv_piece.T, mine(cross_out, 0)], axis=0
        )
    )
    up_rows = mlp_up.shape[1] // S
    second = gather_rows(
        jnp.concatenate(
            [
                mine(mlp_up, 1).T,
                mine(mlp_down, 0),
                mine(self_out, 0),
                mine(local_dec.reshape(-1, D), 0),
            ],
            axis=0,
        )
    )
    steps = 8
    w_up = by_step(bundle_part(second, 0, up_rows), steps)
    w_down = by_step(bundle_part(second, up_rows, up_rows), steps)
    w_triple = by_step(bundle_part(first, 0, 3 * per), S)
    w_cross_out = bundle_part(first, 3 * per, per)
    w_self_out = bundle_part(second, 2 * up_rows, per)
    w_dec = bundle_part(second, 2 * up_rows + per, dec_rows)

    x0 = pick(tokens)
    norms = [jnp.stack([norm_gains[i], norm_shifts[i]]) for i in range(3)]
    at = jnp.stack([s, m])
    both = [lax.dynamic_index_in_dim(patches, o, 0, keepdims=False) for o in (at_a, at_b)]
    patch_pieces = gather_pieces(jnp.concatenate(both, axis=0))
    TC = PLANE // 4
    TR = PLANE * 4 // S
    own, rim = TR * TC, TR * TC + TR
    toks = -(-(rim + TC + 1) // 32) * 32
    planes = objects * 3
    weights_in = sample_weights.reshape(planes, *sample_weights.shape[3:])
    cot_in = sample_cot.reshape(planes, channels, -1)
    cot_in = jnp.pad(cot_in, ((0, 0), (0, CP - channels), (0, 0)))
    ext = per_plane(pixel_grad_kernel, cot_in, weights_in, toks, 4 * CP, f32, toks, TR, TC)
    ways = {
        1: [i for i in range(S) if i % 4 != 3],
        4: [i for i in range(S) if i + 4 < S],
        5: [i for i in range(S) if i % 4 != 3 and i + 4 < S],
    }
    rights = lax.ppermute(ext[:, own:rim], "seq", [(i, i + 1) for i in ways[1]])
    belows = lax.ppermute(ext[:, rim : rim + TC], "seq", [(i, i + 4) for i in ways[4]])
    corner = lax.ppermute(ext[:, rim + TC : rim + TC + 1], "seq", [(i, i + 5) for i in ways[5]])
    grid = ext[:, :own].reshape(planes, TR, TC, -1)
    belows = jnp.concatenate([belows[:, :1] + corner, belows[:, 1:]], axis=1)
    grid = grid + jnp.pad(rights[:, :, None], ((0, 0), (0, 0), (0, TC - 1), (0, 0)))
    grid = grid + jnp.pad(belows[:, None], ((0, 0), (0, TR - 1), (0, 0), (0, 0)))
    KA, KB = R // S, RB // S
    cu = 4 * CP
    grad_pix = grid.astype(bf16).reshape(pairs, 3, S, KA, cu)
    gp_a = jnp.stack([grad_pix[:, 0], grad_pix[:, 2]], axis=1).transpose(2, 0, 1, 3, 4)
    gp_b = grad_pix[:, 1].reshape(pairs, S, 2, KB, cu).transpose(1, 0, 2, 3, 4)
    sent = jnp.concatenate([gp_a, gp_b], axis=3).reshape(S * M, KA + KB, cu)

    q1, keys_one, n1, w_query, w_kv = start(
        at, x0, norms[0], w_kv, w_query, patch_pieces, W, [sent]
    )
    heads_one = swap_seq(q1)
    back = swap_all(hold(sent, [heads_one]))
    d_pix = back.reshape(S, M, KA + KB, cu).transpose(2, 0, 1, 3).reshape(RS, M * cu)

    limits = [
        jnp.stack([lax.dynamic_index_in_dim(counts, o, 0, keepdims=False), jnp.int32(0)])
        for o in (at_a, at_b)
    ]
    kv_one = [(slots, (i * slots, 0), (i * slots, W), 0) for i in range(2)]
    o1, res1 = [], []
    for i in range(2):
        out, res = attend(
            limits[i],
            [heads_one, keys_one],
            S,
            (0, rows[i], i * R, 0),
            [(1,) + kv_one[i]],
            slot_total,
            hpd,
            False,
            [(back,), ()][i],
        )
        o1.append(out)
        res1.append(res)

    mids = [
        middle(swap_seq(o1[i].reshape(S, rows[i], W)), x0[i], norms[1], w_cross_out, w_triple)
        for i in range(2)
    ]
    x1, n2, a1, t2 = zip(*mids)

    heads_two = [swap_seq(v) for v in t2]
    pair_kv = swap_pair(heads_two[1][:, :, W:])
    wide = jnp.array([row_total, 0], jnp.int32)
    kv_a2 = (R, (0, W), (0, 2 * W), 0)
    kv_b2 = (RB, (0, W), (0, 2 * W), 0)
    kv_p2 = (RB, (0, 0), (0, W), row_total // 2)
    o_a2, res_a2 = attend(
        wide, [heads_two[0]], S, (0, R, 0, 0), [(0,) + kv_a2], row_total, hpd, True
    )
    o_b2, res_b2 = attend(
        wide,
        [heads_two[1], pair_kv],
        S,
        (0, RB, 0, 0),
        [(0,) + kv_b2, (1,) + kv_p2],
        row_total,
        hpd,
        True,
        [o_a2],
    )
    a2_a = swap_seq(o_a2.reshape(S, R, W))
    a2 = [a2_a, swap_seq(hold(o_b2.reshape(S, RB, W), [a2_a]))]

    hidden = mlp_up.shape[1] * M
    n3, a2, g, du, x3b, pix, e3, d2, e2, da2, sums_three = feed_forward(
        a2,
        x1,
        pick(tokens_cot),
        d_pix,
        norms[2],
        w_self_out,
        w_dec,
        w_up,
        w_down,
        hidden,
        steps,
    )

    da2 = swap_seq(da2)
    grads_one = weight_grads([[(n3, du)], [(e3, g)], [(e2, a2)], [(x3b, d_pix)]], M)
    grads_one = hold(grads_one, [da2])
    pix = hold(pix, [grads_one])
    dt2_a = attend_back(
        wide,
        [res_a2, da2, o_a2, heads_two[0]],
        S,
        (R, 0),
        [(3,) + kv_a2],
        row_total,
        hpd,
        True,
        [grads_one],
        "lanes",
    )
    grads_one = reduce_rows(grads_one)
    pix = pix.reshape(KA + KB, S, M, cu).transpose(1, 2, 0, 3)
    got = swap_all(pix.reshape(S * M, KA + KB, cu)).reshape(S, pairs, 2, KA + KB, cu)
    half_total = row_total // 2
    kv_p2 = (RB, (0, 0), (0, W), 0)
    dq_p2, dkv_p2 = attend_back(
        wide,
        [res_b2, da2, o_b2, pair_kv],
        S,
        (RB, R),
        [(3,) + kv_p2],
        half_total,
        hpd,
        True,
        [dt2_a, got],
    )
    given = swap_pair(dkv_p2)
    dq_b2, dkv_b2 = attend_back(
        wide,
        [res_b2, da2, o_b2, heads_two[1]],
        S,
        (RB, R),
        [(3,) + kv_b2],
        half_total,
        hpd,
        True,
        [dq_p2],
    )
    dq_b2 = (dq_b2.astype(f32) + dq_p2.astype(f32)).astype(bf16)
    dkv_b2 = (dkv_b2.astype(f32) + given.astype(f32)).astype(bf16)
    dt2 = [
        swap_seq(dt2_a),
        jnp.concatenate([dq_b2, dkv_b2], axis=1).reshape(S, RB, 3 * W),
    ]

    def below(i, deps):
        return middle_back(
            dt2[i], x1[i], d2, (0, R // RB)[i], norms[1], w_cross_out, w_triple, deps
        )

    def cross_back(i, da1, deps):
        return attend_back(
            limits[i],
            [res1[i], da1, o1[i], keys_one],
            S,
            (rows[i], 0),
            [(3,) + kv_one[i]],
            slot_total,
            hpd,
            False,
            deps,
            "rows",
        )

    low_a = below(0, [dq_b2, given])
    x3b = hold(x3b, [low_a[0]])
    blocks_a, blocks_b = x3b[:R].reshape(M, R // M, D), x3b[R:].reshape(pairs, R // M, D)
    blocks_a = [lax.dynamic_index_in_dim(blocks_a, m ^ i, 0, keepdims=False) for i in range(M)]
    blocks_b = [
        lax.dynamic_index_in_dim(blocks_b, pair ^ i, 0, keepdims=False) for i in range(pairs)
    ]
    blocks_a, blocks_b = to_ranks(blocks_a), to_halves(blocks_b)
    da1_a = swap_seq(low_a[2])
    dt2[1] = swap_seq(hold(dt2[1], [da1_a]))
    cross_a = cross_back(0, da1_a, [])
    grads_one = sum_ranks(hold(grads_one, [da1_a]))
    low_b = below(1, [cross_a])
    got_a = swap_seq(cross_a)
    da1_b = swap_seq(hold(low_b[2], [got_a]))
    d1, e1, da1, sums_two = zip(low_a, low_b)

    grads_two = weight_grads(
        [[(n2[i], dt2[i]) for i in range(2)], [(e1[i], a1[i]) for i in range(2)]], M, [grads_one, got_a] + blocks_a + blocks_b
    )
    *sent_a, part_a, share, lift = end(
        at, got_a, 0, w_query, w_kv, x0[0], n1, d1[0], norm_gains[:1], M, [grads_two]
    )
    cross_b = cross_back(1, da1_b, [grads_two, part_a])
    grads_two = reduce_rows(grads_two)
    got_b = swap_seq(cross_b)

    two = sums_two[0] + sums_two[1]
    small = jnp.concatenate([two, sums_three], axis=0)
    sent_a, part_a = to_ranks(sent_a), to_ranks([part_a] * M)
    by_head = finish(at, [cross_a, cross_b], rows, patch_pieces, [cross_b])
    heads = by_head.shape[1]
    *sent_b, part_b, final = end(
        at,
        got_b,
        R // RB,
        w_query,
        w_kv,
        x0[1],
        n1,
        d1[1],
        norm_gains[:1],
        pairs,
        [],
        [share, lift, small, by_head],
    )
    got_last = swap_seq(final)
    grad_tokens = place_rows(at, sent_a, to_halves(sent_b), f32)
    patch_grad = place_patches(at, part_a, to_ranks([part_b] * M))
    px_a = got[:, :, :, :KA].transpose(1, 2, 0, 3, 4).reshape(pairs, 2, S * KA, cu)
    px_b = got[:, :, :, KA:].transpose(1, 0, 2, 3, 4).reshape(pairs, S * KA, cu)
    tile = jnp.stack([px_a[:, 0], px_b, px_a[:, 1]], axis=1).reshape(planes, TR, TC, cu)
    rights = lax.ppermute(tile[:, :, 0], "seq", [(i + 1, i) for i in ways[1]])
    belows = lax.ppermute(tile[:, 0], "seq", [(i + 4, i) for i in ways[4]])
    corner = lax.ppermute(tile[:, 0, :1], "seq", [(i + 5, i) for i in ways[5]])
    fill = jnp.zeros((planes, toks - rim - TC - 1, cu), bf16)
    ext = jnp.concatenate([tile.reshape(planes, own, cu), rights, belows, corner, fill], axis=1)
    ext = hold(ext, [final])
    tokens_out = place_rows(at, blocks_a, blocks_b, bf16, [final])
    sampled = per_plane(
        pixel_sample_kernel, ext, weights_in, CP, weights_in.shape[2], bf16, toks, TR, TC
    )
    sampled = sampled[:, :channels].reshape(objects, 3, channels, 1, -1)

    final = last(to_ranks(mix(at, got_last, M, heads, [sampled, tokens_out])), heads)
    grad_cross_query, grad_keys, grad_values, small = final
    grad_cross_kv = jnp.stack([grad_keys, grad_values], axis=1)

    grads_two = sum_ranks(grads_two)
    ff = hidden // M
    grad_mlp_up, grad_mlp_down = grads_one[:, :ff], grads_one[:, ff : 2 * ff].T
    grad_self_out = grads_one[:, 2 * ff : 2 * ff + D // M].T
    grad_decoder = grads_one[:, 2 * ff + D // M :]
    grad_decoder = grad_decoder.reshape(D // S, 4, CP)[:, :, :channels].transpose(0, 2, 1)
    grad_self_qkv = grads_two[:, : 3 * D // M].reshape(D // S, 2, 3, W).transpose(0, 2, 1, 3)
    grad_cross_out = grads_two[:, 3 * D // M :].T

    return (
        tokens_out,
        sampled,
        grad_tokens,
        patch_grad,
        jnp.stack([small[0], small[2], small[4]]),
        jnp.stack([small[1], small[3]]),
        small[5],
        grad_cross_query,
        grad_cross_kv,
        grad_cross_out,
        grad_self_qkv.reshape(D // S, 3, -1),
        grad_self_out,
        grad_mlp_up,
        grad_mlp_down,
        grad_decoder,
    )


def solution(mesh):
    return jax.shard_map(
        per_device,
        mesh=mesh,
        in_specs=(
            P(None, "seq", None),
            P(None, "seq", None),
            P(),
            P(),
            P(),
            P(None, "mp"),
            P(None, None, "mp"),
            P("mp", None),
            P(None, None, "mp"),
            P("mp", None),
            P(None, "mp"),
            P("mp", None),
            P(None, "mp", None),
            P(None, None, "seq", None, None),
            P(None, "seq", None),
            P(None, None, "mp", "seq", None),
        ),
        out_specs=(
            P(None, ("seq", "mp"), None),
            P(None, None, "mp", "seq", None),
            P(None, ("seq", "mp"), None),
            P(None, "seq", None),
            P(None, "seq"),
            P(None, "seq"),
            P("seq"),
            P("seq", "mp"),
            P("seq", None, "mp"),
            P("mp", "seq"),
            P("seq", None, "mp"),
            P("mp", "seq"),
            P("seq", "mp"),
            P("mp", "seq"),
            P("seq", "mp", None),
        ),
        check_vma=False,
    )
```

```python
import functools
import math

import jax
import jax.numpy as jnp
from jax import lax
from jax.experimental import pallas as pl
from jax.experimental.pallas import tpu as pltpu
from jax.sharding import PartitionSpec as P


PLANE = 32
HD = 64
LANES = 128
norm_eps = 1e-05
f32 = jnp.float32
bf16 = jnp.bfloat16

NT = (((1,), (1,)), ((), ()))
NN = (((1,), (0,)), ((), ()))
TN = (((0,), (0,)), ((), ()))


def dot(a, b, dims):
    return lax.dot_general(a, b, dims, preferred_element_type=f32)


def mm(a, b):
    return jnp.dot(a, b, preferred_element_type=f32)


def split3(v):
    hi = v.astype(bf16).astype(f32)
    rest = v - hi
    mid = rest.astype(bf16).astype(f32)
    return hi, mid, rest - mid


def spread(base, cols):
    lane = lax.broadcasted_iota(jnp.int32, (base.shape[0], HD), 1)
    tail = jnp.zeros((base.shape[0], HD), f32)
    for at, col in cols.items():
        tail = jnp.where(lane == at, col, tail)
    return jnp.concatenate([base, tail], axis=1).astype(bf16)


def load_keys(n_ref, kv_specs, refs, ka, va, hpd, blocks):
    for ref_at, rows, k_at, v_at, base in kv_specs:
        src = refs[ref_at]

        def build(i, _):
            natural = base + (i ^ n_ref[1]) * rows
            dst = pl.ds(pl.multiple_of(natural, 16), rows)
            slot = natural + lax.broadcasted_iota(jnp.int32, (rows, 1), 0)
            mask = jnp.where(slot < n_ref[0], 0.0, -1e30).astype(f32)
            for h in range(hpd):
                k = src[i, k_at[0] : k_at[0] + rows, k_at[1] + h * HD : k_at[1] + (h + 1) * HD]
                v = src[i, v_at[0] : v_at[0] + rows, v_at[1] + h * HD : v_at[1] + (h + 1) * HD]
                ka[h, dst, :] = spread(k.astype(f32), {0: 1.0, 1: 1.0, 2: 1.0, 3: mask})
                va[h, dst, :] = spread(v.astype(f32), {0: 1.0, 1: 1.0, 2: 1.0})
            return 0

        lax.fori_loop(0, blocks, build, 0)


def fwd_kernel(n_ref, *refs, n_in, blocks, q_spec, kv_specs, hpd, bq, kc, fixed):
    ins, (o_ref, qa_ref, ka, va) = refs[:n_in], refs[-4:]
    load_keys(n_ref, kv_specs, ins, ka, va, hpd, blocks)
    q_at, rows_q, q_off, q_lane = q_spec

    def build(i, _):
        dst = pl.ds(pl.multiple_of((i ^ n_ref[1]) * rows_q, 16), rows_q)
        for h in range(hpd):
            q = ins[q_at][i, q_off : q_off + rows_q, q_lane + h * HD : q_lane + (h + 1) * HD]
            qa_ref[h, dst, :] = spread(q.astype(f32) * (1.0 / math.sqrt(HD)), {3: 1.0})
        return 0

    lax.fori_loop(0, blocks, build, 0)
    total = ka.shape[1]

    def block(b, _):
        rows = pl.ds(pl.multiple_of(b * bq, bq), bq)

        def chunk(c, carry):
            cols = pl.ds(pl.multiple_of(c * kc, kc), kc)
            out = []
            for h in range(hpd):
                m, acc = carry[h]
                s = dot(qa_ref[h, rows, :], ka[h, cols, :], NT)
                top = jnp.maximum(m, jnp.max(s, axis=1, keepdims=True))
                p = jnp.exp(s - top).astype(bf16)
                out.append((top, acc * jnp.exp(m - top) + dot(p, va[h, cols, :], NN)))
            return tuple(out)

        carry = ((jnp.full((bq, 1), -1e30, f32), jnp.zeros((bq, LANES), f32)),) * hpd
        if fixed:
            for c in range(total // kc):
                carry = chunk(c, carry)
        else:
            carry = lax.fori_loop(0, (n_ref[0] + kc - 1) // kc, chunk, carry)
        outs = []
        for h in range(hpd):
            m, acc = carry[h]
            norm = acc[:, HD : HD + 1]
            outs.append(acc[:, :HD] / norm)
            hi, mid, lo = split3(-(m + jnp.log(norm)))
            qa_ref[h, rows, :] = spread(
                qa_ref[h, rows, :HD].astype(f32), {0: hi, 1: mid, 2: lo, 3: 1.0}
            )
        o_ref[rows, :] = jnp.concatenate(outs, axis=1).astype(bf16)
        return 0

    lax.fori_loop(0, qa_ref.shape[1] // bq, block, 0)


def bwd_kernel(n_ref, *refs, n_in, n_dep, blocks, do_spec, kv_specs, hpd, bq, kc, fixed, form):
    ins, (*outs, ka, va, da, dk, dv, dq) = refs[:n_in], refs[n_in + n_dep :]
    qa_ref, do_ref, o_ref = ins[:3]
    load_keys(n_ref, kv_specs, ins, ka, va, hpd, blocks)
    rows_q, do_off = do_spec

    def build(i, _):
        rows = pl.ds(pl.multiple_of(i * rows_q, 16), rows_q)
        for h in range(hpd):
            d = do_ref[i, do_off : do_off + rows_q, h * HD : (h + 1) * HD].astype(f32)
            o = o_ref[rows, h * HD : (h + 1) * HD].astype(f32)
            hi, mid, lo = split3(-jnp.sum(d * o, axis=1, keepdims=True))
            da[h, rows, :] = spread(d, {0: hi, 1: mid, 2: lo})
        return 0

    lax.fori_loop(0, blocks, build, 0)
    dk[...] = jnp.zeros_like(dk)
    dv[...] = jnp.zeros_like(dv)
    total = ka.shape[1]
    steps = total // kc if fixed else (n_ref[0] + kc - 1) // kc

    def block(b, _):
        rows = pl.ds(pl.multiple_of(b * bq, bq), bq)

        def chunk(c, dqs):
            cols = pl.ds(pl.multiple_of(c * kc, kc), kc)
            out = []
            for h in range(hpd):
                k, q, d = ka[h, cols, :], qa_ref[h, rows, :], da[h, rows, :]
                p = jnp.exp(dot(k, q, NT))
                dp = dot(va[h, cols, :], d, NT)
                dv[h, cols, :] += dot(p.astype(bf16), d, NN)
                g = (p * dp).astype(bf16)
                dk[h, cols, :] += dot(g, q, NN)
                out.append(dqs[h] + dot(k, g, TN))
            return tuple(out)

        dqs = lax.fori_loop(0, steps, chunk, (jnp.zeros((LANES, bq), f32),) * hpd)
        grad = jnp.concatenate([v[:HD, :] for v in dqs], axis=0).T
        dq[rows, :] = (grad * (1.0 / math.sqrt(HD))).astype(bf16)
        return 0

    lax.fori_loop(0, qa_ref.shape[1] // bq, block, 0)
    step = total // blocks

    def finish(i, _):
        rows = pl.ds(pl.multiple_of(i * step, 16), step)
        q_rows = pl.ds(pl.multiple_of(i * rows_q, 16), rows_q)
        k, v = [
            jnp.concatenate([d[h, rows, :HD] for h in range(hpd)], axis=1).astype(bf16)
            for d in (dk, dv)
        ]
        if form == "split":
            outs[0][q_rows, :] = dq[q_rows, :]
            outs[1][rows, :] = jnp.concatenate([k, v], axis=1)
        elif form == "lanes":
            outs[0][i] = jnp.concatenate([dq[q_rows, :], k, v], axis=1)
        else:
            outs[0][i, :rows_q, :] = dq[q_rows, :]
            outs[0][i, rows_q : rows_q + step, :] = k
            outs[0][i, rows_q + step :, :] = v
        return 0

    lax.fori_loop(0, blocks, finish, 0)


VM = pl.BlockSpec(memory_space=pltpu.VMEM)
SM = pl.BlockSpec(memory_space=pltpu.SMEM)
BRIEF = pl.CostEstimate(flops=10**6, bytes_accessed=10**5, transcendentals=0)
AN = pl.BlockSpec(memory_space=pl.ANY)


def fit(rows, most):
    return math.gcd(rows, most)


def attend(limits, ins, blocks, q_spec, kv_specs, total, hpd, fixed, deps=()):
    queries = blocks * q_spec[1]
    kc = fit(total, 1024 if fixed else 512)
    body = functools.partial(
        fwd_kernel,
        n_in=len(ins),
        blocks=blocks,
        q_spec=q_spec,
        kv_specs=kv_specs,
        hpd=hpd,
        bq=fit(queries, 512),
        kc=kc,
        fixed=fixed,
    )
    work = hpd * queries * total
    return pl.pallas_call(
        body,
        out_shape=(
            jax.ShapeDtypeStruct((queries, hpd * HD), bf16),
            jax.ShapeDtypeStruct((hpd, queries, LANES), bf16),
        ),
        in_specs=[SM] + [VM] * len(ins) + [AN] * len(deps),
        out_specs=(VM, VM),
        scratch_shapes=[pltpu.VMEM((hpd, total, LANES), bf16)] * 2,
        compiler_params=pltpu.CompilerParams(vmem_limit_bytes=44 * 2**20),
        cost_estimate=BRIEF,
    )(limits, *ins, *deps)


def attend_back(limits, ins, blocks, do_spec, kv_specs, total, hpd, fixed, deps=(), form="split"):
    queries = blocks * do_spec[0]
    W, step = hpd * HD, total // blocks
    shapes = {
        "split": [(queries, W), (total, 2 * W)],
        "lanes": [(blocks, step, 3 * W)],
        "rows": [(blocks, do_spec[0] + 2 * step, W)],
    }[form]
    body = functools.partial(
        bwd_kernel,
        n_in=len(ins),
        n_dep=len(deps),
        blocks=blocks,
        do_spec=do_spec,
        kv_specs=kv_specs,
        hpd=hpd,
        bq=fit(queries, 512),
        kc=fit(total, 512),
        fixed=fixed,
        form=form,
    )
    out = pl.pallas_call(
        body,
        out_shape=tuple(jax.ShapeDtypeStruct(v, bf16) for v in shapes),
        in_specs=[SM] + [VM] * len(ins) + [AN] * len(deps),
        out_specs=(VM,) * len(shapes),
        scratch_shapes=[pltpu.VMEM((hpd, total, LANES), bf16)] * 2
        + [pltpu.VMEM((hpd, queries, LANES), bf16)]
        + [pltpu.VMEM((hpd, total, LANES), f32)] * 2
        + [pltpu.VMEM((queries, W), bf16)],
        compiler_params=pltpu.CompilerParams(vmem_limit_bytes=52 * 2**20),
        cost_estimate=BRIEF,
    )(limits, *ins, *deps)
    return out if len(out) > 1 else out[0]


def norm_parts(values):
    center = values - jnp.mean(values, axis=-1, keepdims=True)
    scale = lax.rsqrt(jnp.mean(center * center, axis=-1, keepdims=True) + norm_eps)
    return center * scale, scale


def layer_norm(values, gain_row, shift_row):
    return (norm_parts(values)[0] * gain_row + shift_row).astype(bf16)


def norm_back(values, gain_row, grad_out):
    unit, scale = norm_parts(values)
    lifted = grad_out * gain_row
    grad_in = scale * (
        lifted
        - jnp.mean(lifted, axis=-1, keepdims=True)
        - unit * jnp.mean(lifted * unit, axis=-1, keepdims=True)
    )
    gain = jnp.sum(grad_out * unit, axis=0, keepdims=True)
    return grad_in, gain, jnp.sum(grad_out, axis=0, keepdims=True)


def flat(ref):
    return ref[...].reshape(-1, ref.shape[-1])


def joined(ref):
    return jnp.concatenate([ref[i] for i in range(ref.shape[0])], axis=1)


def once(shape, index=None):
    at = (0,) * len(shape) if index is None else index
    return pl.BlockSpec(shape, lambda i: at, pipeline_mode=pl.Buffered(1))


def held(shape):
    return pl.BlockSpec(shape, lambda i: (0,) * len(shape))


def mid_kernel(a_ref, x_ref, norm_ref, wo_ref, wt_ref, *refs):
    x1_ref, n_ref, ac_ref, t_ref = refs[-4:]

    @pl.when(pl.program_id(0) == 0)
    def _():
        a = joined(a_ref)
        ac_ref[...] = a
        x1 = x_ref[...].astype(f32) + dot(a, flat(wo_ref), NN)
        x1_ref[...] = x1
        n_ref[...] = layer_norm(x1, norm_ref[0:1, :], norm_ref[1:2, :])

    t_ref[0] = dot(n_ref[...], flat(wt_ref), NT).astype(bf16)


def middle(a, x, norm, w_out, w_triple, deps=()):
    S, rows, W = a.shape
    D = S * W
    return pl.pallas_call(
        mid_kernel,
        grid=(S,),
        out_shape=(
            jax.ShapeDtypeStruct((rows, D), f32),
            jax.ShapeDtypeStruct((rows, D), bf16),
            jax.ShapeDtypeStruct((rows, D), bf16),
            jax.ShapeDtypeStruct((S, rows, 3 * W), bf16),
        ),
        in_specs=[
            once((S, rows, W)),
            once((rows, D)),
            once((2, D)),
            once(*w_out[1]),
            w_triple[1],
        ]
        + [AN] * len(deps),
        out_specs=(
            held((rows, D)),
            held((rows, D)),
            held((rows, D)),
            pl.BlockSpec((1, rows, 3 * W), lambda i: (i, 0, 0)),
        ),
        compiler_params=pltpu.CompilerParams(vmem_limit_bytes=40 * 2**20),
        cost_estimate=BRIEF,
    )(a, x, norm, w_out[0], w_triple[0], *deps)


def mlp_kernel(
    aa_ref,
    ab_ref,
    xa_ref,
    xb_ref,
    ca_ref,
    cb_ref,
    dp_ref,
    norm_ref,
    ws_ref,
    wd_ref,
    up_ref,
    down_ref,
    n_ref,
    ac_ref,
    g_ref,
    du_ref,
    x3_ref,
    pix_ref,
    e3_ref,
    d2_ref,
    e2_ref,
    da_ref,
    sum_ref,
    x2,
    d3,
    acc,
    back,
    *,
    steps,
):
    step = pl.program_id(0)
    R = xa_ref.shape[0]
    S, _, W = aa_ref.shape

    @pl.when(step == 0)
    def _():
        for rows, a_ref, x_ref, c_ref in (
            (slice(0, R), aa_ref, xa_ref, ca_ref),
            (slice(R, x2.shape[0]), ab_ref, xb_ref, cb_ref),
        ):
            a = joined(a_ref)
            ac_ref[rows, :] = a
            x = x_ref[...] + dot(a, flat(ws_ref), NN)
            x2[rows, :] = x
            n_ref[rows, :] = layer_norm(x, norm_ref[0:1, :], norm_ref[1:2, :])
            d = c_ref[...].astype(f32) + dot(dp_ref[rows, :], flat(wd_ref), NN)
            d3[rows, :] = d
            e3_ref[rows, :] = d.astype(bf16)
        acc[...] = jnp.zeros_like(acc)
        back[...] = jnp.zeros_like(back)

    up = flat(up_ref)
    down = flat(down_ref)
    u = dot(n_ref[...], up, NT)
    slope = math.sqrt(2.0 / math.pi)
    square = u * u
    bend = jnp.tanh(slope * u * (1.0 + 0.044715 * square))
    half = 0.5 * (1.0 + bend)
    g = (u * half).astype(bf16)
    rise = half + 0.5 * slope * u * (1.0 - bend * bend) * (1.0 + 0.134145 * square)
    du = (dot(e3_ref[...], down, NT) * rise).astype(bf16)
    g_ref[...] = g
    du_ref[...] = du
    acc[...] += dot(g, down, NN)
    back[...] += dot(du, up, NN)

    @pl.when(step == steps - 1)
    def _():
        x3 = (x2[...] + acc[...]).astype(bf16)
        x3_ref[...] = x3
        pix_ref[...] = dot(x3, flat(wd_ref), NT).astype(bf16)
        grad_in, gain, shift = norm_back(x2[...], norm_ref[0:1, :], back[...])
        d2 = d3[...] + grad_in
        d2_ref[...] = d2
        e2 = d2.astype(bf16)
        e2_ref[...] = e2
        sum_ref[...] = jnp.concatenate([gain, shift], axis=0)
        da = dot(e2, flat(ws_ref), NT).astype(bf16)
        for i in range(S):
            da_ref[i] = da[:, i * W : (i + 1) * W]


def feed_forward(a, x1, cot, d_pix, norm, w_out, w_dec, w_up, w_down, hidden, steps):
    S, R, W = a[0].shape
    RB = a[1].shape[1]
    D, total, pixels = S * W, R + RB, d_pix.shape[1]
    part = hidden // steps
    row = jax.ShapeDtypeStruct((total, D), bf16)
    wide = jax.ShapeDtypeStruct((total, hidden), bf16)
    blocked = pl.BlockSpec((total, part), lambda i: (0, i))
    full = held((total, D))
    return pl.pallas_call(
        functools.partial(mlp_kernel, steps=steps),
        grid=(steps,),
        out_shape=(
            row,
            row,
            wide,
            wide,
            row,
            jax.ShapeDtypeStruct((total, pixels), bf16),
            row,
            jax.ShapeDtypeStruct((total, D), f32),
            row,
            jax.ShapeDtypeStruct((S, total, W), bf16),
            jax.ShapeDtypeStruct((2, D), f32),
        ),
        in_specs=[
            once((S, R, W)),
            once((S, RB, W)),
            once((R, D)),
            once((RB, D)),
            once((R, D)),
            once((RB, D)),
            once((total, pixels)),
            once((2, D)),
            once(*w_out[1]),
            once(*w_dec[1]),
            w_up[1],
            w_down[1],
        ],
        out_specs=(
            full,
            full,
            blocked,
            blocked,
            full,
            held((total, pixels)),
            full,
            full,
            full,
            held((S, total, W)),
            held((2, D)),
        ),
        scratch_shapes=[pltpu.VMEM((total, D), f32)] * 4,
        compiler_params=pltpu.CompilerParams(vmem_limit_bytes=60 * 2**20),
        cost_estimate=BRIEF,
    )(*a, *x1, *cot, d_pix, norm, w_out[0], w_dec[0], w_up[0], w_down[0])


def hold_kernel(*refs):
    pass


def hold(value, deps):
    return pl.pallas_call(
        hold_kernel,
        out_shape=jax.ShapeDtypeStruct(value.shape, value.dtype),
        in_specs=[AN] * (1 + len(deps)),
        out_specs=AN,
        input_output_aliases={0: 0},
        cost_estimate=BRIEF,
    )(value, *deps)


def back_kernel(
    t_ref, x_ref, d_ref, norm_ref, wo_ref, wt_ref, *refs, steps
):
    d1_ref, e_ref, da_ref, sum_ref, acc = refs[-5:]
    step = pl.program_id(0)
    part = dot(t_ref[0], flat(wt_ref), NN)

    @pl.when(step == 0)
    def _():
        acc[...] = part

    @pl.when(step > 0)
    def _():
        acc[...] += part

    @pl.when(step == steps - 1)
    def _():
        grad_in, gain, shift = norm_back(x_ref[...], norm_ref[0:1, :], acc[...])
        d1 = d_ref[...] + grad_in
        d1_ref[...] = d1
        e = d1.astype(bf16)
        e_ref[...] = e
        sum_ref[...] = jnp.concatenate([gain, shift], axis=0)
        da = dot(e, flat(wo_ref), NT).astype(bf16)
        W = da_ref.shape[2]
        for i in range(steps):
            da_ref[i] = da[:, i * W : (i + 1) * W]


def middle_back(t, x1, d2, at, norm, w_out, w_triple, deps=()):
    S, rows, wide = t.shape
    D = x1.shape[1]
    W = wide // 3
    return pl.pallas_call(
        functools.partial(back_kernel, steps=S),
        grid=(S,),
        out_shape=(
            jax.ShapeDtypeStruct((rows, D), f32),
            jax.ShapeDtypeStruct((rows, D), bf16),
            jax.ShapeDtypeStruct((S, rows, W), bf16),
            jax.ShapeDtypeStruct((2, D), f32),
        ),
        in_specs=[
            pl.BlockSpec((1, rows, wide), lambda i: (i, 0, 0)),
            once((rows, D)),
            once((rows, D), (at, 0)),
            once((2, D)),
            once(*w_out[1]),
            w_triple[1],
        ]
        + [AN] * len(deps),
        out_specs=(
            held((rows, D)),
            held((rows, D)),
            held((S, rows, W)),
            held((2, D)),
        ),
        scratch_shapes=[pltpu.VMEM((rows, D), f32)],
        compiler_params=pltpu.CompilerParams(vmem_limit_bytes=40 * 2**20),
        cost_estimate=BRIEF,
    )(t, x1, d2, norm, w_out[0], w_triple[0], *deps)


def grads_kernel(*refs, shape, widths):
    count = sum(shape)
    lefts, rights = refs[:count], refs[count : 2 * count]
    out_ref, turned = refs[-1 - count], refs[-count:]

    @pl.when(pl.program_id(0) == 0)
    def _():
        for left, t in zip(lefts, turned):
            t[...] = left[...].T

    at = n = 0
    for pieces, width in zip(shape, widths):
        total = 0.0
        for i in range(n, n + pieces):
            right = joined(rights[i]) if len(rights[i].shape) == 3 else rights[i][...]
            total += dot(turned[i][...], right, NN)
        out_ref[:, at : at + width] = total.astype(bf16)
        at, n = at + width, n + pieces


def weight_grads(terms, ranks, deps=()):
    pieces = [p for term in terms for p in term]
    shape = [len(term) for term in terms]
    widths = [term[0][1].size // term[0][0].shape[0] // ranks for term in terms]
    D, per = pieces[0][0].shape[1], sum(widths)
    lefts = [p[0] for p in pieces]
    rights = [p[1] for p in pieces]
    work = sum(p[0].shape[0] for p in pieces) * D * per * ranks // len(pieces)
    return pl.pallas_call(
        functools.partial(grads_kernel, shape=shape, widths=widths),
        grid=(ranks,),
        out_shape=jax.ShapeDtypeStruct((D, per * ranks), bf16),
        in_specs=[once(v.shape) for v in lefts]
        + [
            pl.BlockSpec((v.shape[0] // ranks,) + v.shape[1:], lambda i: (i, 0, 0))
            if v.ndim == 3
            else pl.BlockSpec((v.shape[0], v.shape[1] // ranks), lambda i: (0, i))
            for v in rights
        ]
        + [AN] * len(deps),
        out_specs=pl.BlockSpec((D, per), lambda i: (0, i)),
        scratch_shapes=[pltpu.VMEM(v.shape[::-1], bf16) for v in lefts],
        compiler_params=pltpu.CompilerParams(vmem_limit_bytes=56 * 2**20),
        cost_estimate=BRIEF,
    )(*lefts, *rights, *deps)


def start_kernel(at_ref, xa_ref, xb_ref, norm_ref, wk_ref, wq_in, *refs, pieces, width):
    p_in, (q_ref, k_ref, n_ref, wq_ref, wkv_ref) = refs[:pieces], refs[-5:]
    seq = at_ref[0]
    R = xa_ref.shape[0]
    W = q_ref.shape[2]
    wq_ref[...] = flat(wq_in)
    wkv_ref[...] = flat(wk_ref)[:, :width]
    for block, x_ref in ((slice(0, R), xa_ref), (slice(R, n_ref.shape[0]), xb_ref)):
        n_ref[block, :] = layer_norm(x_ref[...].astype(f32), norm_ref[0:1, :], norm_ref[1:2, :])
    for i in range(pieces):
        q_ref[i] = dot(n_ref[...], wq_ref[i * W : (i + 1) * W, :], NT).astype(bf16)
    own = wkv_ref[pl.ds(pl.multiple_of(seq * 2 * W, 16), 2 * W), :]
    for i in range(pieces):
        k_ref[seq ^ i] = dot(p_in[i][...], own, NT).astype(bf16)


def start(at, x0, norm, w_kv, w_query, patch_pieces, W, deps):
    S, D = len(patch_pieces), x0[0].shape[1]
    total = x0[0].shape[0] + x0[1].shape[0]
    slots, width = patch_pieces[0].shape
    whole = [x0[0].shape, x0[1].shape, norm.shape]
    outs = [(S, total, W), (S, slots, 2 * W), (total, D), (D, D), (2 * D, width)]
    return pl.pallas_call(
        functools.partial(start_kernel, pieces=S, width=width),
        grid=(1,),
        out_shape=tuple(jax.ShapeDtypeStruct(v, bf16) for v in outs),
        in_specs=[SM]
        + [once(v) for v in whole]
        + [once(*w_kv[1]), once(*w_query[1])]
        + [once((slots, width))] * S
        + [AN] * len(deps),
        out_specs=tuple(held(v) for v in outs),
        compiler_params=pltpu.CompilerParams(vmem_limit_bytes=56 * 2**20),
        cost_estimate=BRIEF,
    )(at, *x0, norm, w_kv[0], w_query[0], *patch_pieces, *deps)


def finish_kernel(at_ref, a_ref, b_ref, *refs, pieces, rows):
    p_in, out_ref = refs[:pieces], refs[-1]
    seq = at_ref[0]
    W = a_ref.shape[2]
    slots = (a_ref.shape[1] - rows[0]) // 2
    sums = [0.0, 0.0]
    for i in range(pieces):
        for j, (ref, at) in enumerate(((a_ref, rows[0]), (b_ref, rows[1]))):
            p = p_in[i][j * slots : (j + 1) * slots, :]
            for k in range(2):
                sums[k] += dot(ref[seq ^ i, at + k * slots : at + (k + 1) * slots, :], p, TN)
    wide = sums[0].shape[1] // pieces
    for k in range(2):
        grad = sums[k].T.astype(bf16)
        for i in range(pieces):
            out_ref[i, k * wide : (k + 1) * wide, :] = grad[i * wide : (i + 1) * wide, :]


def finish(at, cross, rows, patch_pieces, deps):
    S, _, W = cross[0].shape
    out = (S, 2 * patch_pieces[0].shape[1] // S, W)
    return pl.pallas_call(
        functools.partial(finish_kernel, pieces=S, rows=rows),
        out_shape=jax.ShapeDtypeStruct(out, bf16),
        in_specs=[SM] + [VM] * (2 + S) + [AN] * len(deps),
        out_specs=VM,
        compiler_params=pltpu.CompilerParams(vmem_limit_bytes=32 * 2**20),
        cost_estimate=BRIEF,
    )(at, *cross, *patch_pieces, *deps)


def pack_lanes(ref, at, value):
    rows = value.shape[0]
    for i in range(value.shape[1] // LANES):
        ref[at + i * rows : at + (i + 1) * rows, :] = value[:, i * LANES : (i + 1) * LANES]


def unpack_lanes(ref, at, rows, columns):
    parts = [ref[at + i * rows : at + (i + 1) * rows, :] for i in range(columns // LANES)]
    return jnp.concatenate(parts, axis=1)


def end_kernel(
    at_ref, g_ref, wq_ref, wkv_ref, x_ref, n_ref, d_ref, gain_ref, *refs, blocks, more, n_dep
):
    extra, refs = refs[:more], refs[more + n_dep :]
    outs, refs = refs[:blocks], refs[blocks:]
    if more:
        part_ref, refs = refs[0], refs[1:]
    outs_more, (n_t, dq, total) = refs[:-3], refs[-3:]
    S, _, W = g_ref.shape
    rows = x_ref.shape[0]
    slots = (g_ref.shape[1] - rows) // 2
    own = rows // blocks
    dq[...] = jnp.concatenate([g_ref[i, :rows, :] for i in range(S)], axis=1)
    n_t[...] = n_ref[...].T
    grad, gain, shift = norm_back(
        x_ref[...].astype(f32), gain_ref[...], dot(dq[...], wq_ref[...], NN)
    )
    total[...] = d_ref[...] + grad
    place = at_ref[1] // 2 if more else at_ref[1]
    keys = []
    for i in range(S):
        keys += [g_ref[i, rows : rows + slots, :], g_ref[i, rows + slots :, :]]
    part = dot(jnp.concatenate(keys, axis=1), wkv_ref[...], NN).astype(bf16)
    for i in range(blocks):
        block = total[pl.ds(pl.multiple_of((place ^ i) * own, 8), own), :].astype(bf16)
        if more:
            outs[i][...] = block
        else:
            pack_lanes(outs[i], 0, block)
            pack_lanes(outs[i], own * block.shape[1] // LANES, part)
    if more:
        part_ref[...] = part
    lift = jnp.concatenate([gain, shift], axis=0)
    tall = n_t.shape[0] // S
    for i in range(0, S, 2):
        pair = dot(n_t[...], dq[:, i * W : (i + 2) * W], NN)
        if more:
            pair += extra[0][i // 2]
            for j in range(S):
                block = pair[j * tall : (j + 1) * tall, :].astype(bf16)
                outs_more[0][j, i * tall : (i + 1) * tall, :] = block[:, :W]
                outs_more[0][j, (i + 1) * tall : (i + 2) * tall, :] = block[:, W:]
        else:
            outs_more[0][i // 2] = pair
    if not more:
        outs_more[1][...] = lift
        return
    at = S * tall
    heads = extra[3].shape[1]
    zero = jnp.zeros((2, n_t.shape[0]), f32)
    sums = jnp.concatenate([lift + extra[1][...], extra[2][...], zero], axis=0)
    hi = sums.astype(bf16).astype(f32)
    both = jnp.concatenate([hi, sums - hi], axis=0).astype(bf16)
    for j in range(S):
        outs_more[0][j, at : at + heads, :] = extra[3][j]
        outs_more[0][j, at + heads :, :] = both[:, j * W : (j + 1) * W]


def end(at, got, place, w_query, w_kv, x0, n1, d1, gain, blocks, deps, more=()):
    S, _, W = got.shape
    rows, D = x0.shape
    slots, width = (got.shape[1] - rows) // 2, w_kv.shape[1]
    own = rows // blocks
    if more:
        outs = [((own, D), bf16)] * blocks + [((slots, width), bf16)]
        outs += [((S, D + more[3].shape[1] + 16, W), bf16)]
    else:
        outs = [(((own * D + slots * width) // LANES, LANES), bf16)] * blocks
        outs += [((S // 2, D, 2 * W), f32), ((2, D), f32)]
    whole = [got, w_query, w_kv, x0, n1, d1, gain, *more]
    specs = [once(v.shape) for v in whole]
    specs[4] = once((rows, D), (place, 0))
    return pl.pallas_call(
        functools.partial(end_kernel, blocks=blocks, more=len(more), n_dep=len(deps)),
        grid=(1,),
        out_shape=tuple(jax.ShapeDtypeStruct(*v) for v in outs),
        in_specs=[SM] + specs + [AN] * len(deps),
        out_specs=tuple(held(v[0]) for v in outs),
        scratch_shapes=[
            pltpu.VMEM((D, rows), bf16),
            pltpu.VMEM((rows, D), bf16),
            pltpu.VMEM((rows, D), f32),
        ],
        compiler_params=pltpu.CompilerParams(vmem_limit_bytes=56 * 2**20),
        cost_estimate=BRIEF,
    )(at, *whole, *deps)


def mix_kernel(at_ref, x_ref, *refs, heads, ranks):
    outs = refs[-ranks:]
    S, rows, W = x_ref.shape
    blocks = rows - heads - 16
    pair = blocks // len(outs)
    small = sum(x_ref[j, blocks + heads :, :].astype(f32) for j in range(S))
    total = small[:8] + small[8:]
    hi = total.astype(bf16).astype(f32)
    for i in range(len(outs)):
        rank = at_ref[1] ^ i
        src = pl.ds(pl.multiple_of(rank * pair, 16), pair)
        outs[i][:pair, :] = sum(x_ref[j, src, :].astype(f32) for j in range(S)).astype(bf16)
        for k in range(2):
            outs[i][pair + k * heads : pair + (k + 1) * heads, :] = x_ref[
                2 * rank + k, blocks : blocks + heads, :
            ]
        outs[i][pair + 2 * heads :, :] = jnp.concatenate([hi, total - hi], axis=0).astype(bf16)


def mix(at, got, ranks, heads, deps):
    S, rows, W = got.shape
    shape = ((rows - heads - 16) // ranks + 2 * heads + 16, W)
    return pl.pallas_call(
        functools.partial(mix_kernel, heads=heads, ranks=ranks),
        out_shape=(jax.ShapeDtypeStruct(shape, bf16),) * ranks,
        in_specs=[SM, VM] + [AN] * len(deps),
        out_specs=(VM,) * ranks,
        compiler_params=pltpu.CompilerParams(vmem_limit_bytes=24 * 2**20),
        cost_estimate=BRIEF,
    )(at, got, *deps)


def last_kernel(*refs, heads):
    ins, (q_ref, k_ref, v_ref, small_ref) = refs[:-4], refs[-4:]
    total = sum(v[...].astype(f32) for v in ins)
    pair = total.shape[0] - 2 * heads - 16
    q_ref[...] = jnp.concatenate([total[: pair // 2], total[pair // 2 : pair]], axis=1)
    one, two = total[pair : pair + heads], total[pair + heads : pair + 2 * heads]
    k_ref[...] = jnp.concatenate([one[: heads // 2], two[: heads // 2]], axis=1)
    v_ref[...] = jnp.concatenate([one[heads // 2 :], two[heads // 2 :]], axis=1)
    small_ref[...] = total[pair + 2 * heads : pair + 2 * heads + 8] + total[pair + 2 * heads + 8 :]


def last(parts, heads):
    rows, W = parts[0].shape
    pair = rows - 2 * heads - 16
    outs = [(pair // 2, 2 * W), (heads // 2, 2 * W), (heads // 2, 2 * W), (8, W)]
    return pl.pallas_call(
        functools.partial(last_kernel, heads=heads),
        out_shape=tuple(jax.ShapeDtypeStruct(v, f32) for v in outs),
        in_specs=[VM] * len(parts),
        out_specs=(VM,) * 4,
        compiler_params=pltpu.CompilerParams(vmem_limit_bytes=24 * 2**20),
        cost_estimate=BRIEF,
    )(*parts)


def place_kernel(at_ref, *refs, ranks, packed):
    whole, halves, out_ref = refs[:ranks], refs[ranks : ranks + ranks // 2], refs[-1]
    _, own, D = out_ref.shape
    for i in range(ranks):
        src = at_ref[1] ^ i
        block = unpack_lanes(whole[i], 0, own, D) if packed else whole[i][...]
        out_ref[3 * (src // 2) + 2 * (src % 2)] = block.astype(out_ref.dtype)
    for i in range(ranks // 2):
        src = at_ref[1] % (ranks // 2) ^ i
        out_ref[3 * src + 1] = halves[i][...].astype(out_ref.dtype)


def place_rows(at, whole, halves, kind, deps=(), packed=False):
    ranks = len(whole)
    shape = (3 * ranks // 2,) + halves[0].shape
    return pl.pallas_call(
        functools.partial(place_kernel, ranks=ranks, packed=packed),
        out_shape=jax.ShapeDtypeStruct(shape, kind),
        in_specs=[SM] + [VM] * (ranks + ranks // 2) + [AN] * len(deps),
        out_specs=VM,
        compiler_params=pltpu.CompilerParams(vmem_limit_bytes=24 * 2**20),
        cost_estimate=BRIEF,
    )(at, *whole, *halves, *deps)


def patches_kernel(at_ref, *refs):
    ins, out_ref = refs[:-1], refs[-1]
    ranks = len(ins) // 2
    _, slots, width = out_ref.shape
    at = ins[0].shape[0] - slots * width // LANES
    for i in range(ranks // 2):
        out_ref[3 * i + 1] = jnp.zeros(out_ref.shape[1:], f32)
    for i in range(ranks):
        src = at_ref[1] ^ i
        block = unpack_lanes(ins[i], at, slots, width)
        out_ref[3 * (src // 2) + 2 * (src % 2)] = block.astype(f32)
        out_ref[3 * (src // 2) + 1] += ins[ranks + i][...].astype(f32)


def place_patches(at, parts_a, parts_b):
    shape = (3 * len(parts_a) // 2,) + parts_b[0].shape
    return pl.pallas_call(
        patches_kernel,
        out_shape=jax.ShapeDtypeStruct(shape, f32),
        in_specs=[SM] + [VM] * (2 * len(parts_a)),
        out_specs=VM,
        compiler_params=pltpu.CompilerParams(vmem_limit_bytes=24 * 2**20),
        cost_estimate=BRIEF,
    )(at, *parts_a, *parts_b)


CP = 32


def place(perm, toks, TR, TC):
    own, ext = TR * TC, perm.shape[2]
    tok = lax.broadcasted_iota(jnp.int32, (toks, 1), 0)
    row = jnp.where(tok < own, tok // TC, jnp.where(tok < own + TR, tok - own, TR))
    col = jnp.where(
        tok < own, tok % TC, jnp.where(tok < own + TR, TC, tok - own - TR)
    )
    real = tok <= own + TR + TC
    pixel = lax.broadcasted_iota(jnp.int32, (toks, ext), 1)
    for a in range(2):
        for b in range(2):
            ok = real & ((row < TR) | (a == 0)) & ((col < TC) | (b == 0))
            at = jnp.where(ok, (2 * row + a) * (2 * TC + 1) + 2 * col + b, -1)
            perm[2 * a + b] = jnp.where(pixel == at, 1.0, 0.0).astype(bf16)


def pixel_grad_kernel(cot_ref, w_ref, *refs, TR, TC):
    out_ref, perm = refs[-2:]

    @pl.when(pl.program_id(0) == 0)
    def _():
        place(perm, out_ref.shape[1], TR, TC)

    grad = dot(cot_ref[0], w_ref[0], NT)
    hi = grad.astype(bf16)
    lo = (grad - hi.astype(f32)).astype(bf16)
    parts = [dot(perm[i], hi, NT) + dot(perm[i], lo, NT) for i in range(4)]
    out_ref[0] = jnp.concatenate(parts, axis=1)


def pixel_sample_kernel(x_ref, w_ref, *refs, TR, TC):
    out_ref, perm = refs[-2:]

    @pl.when(pl.program_id(0) == 0)
    def _():
        place(perm, x_ref.shape[1], TR, TC)

    x = x_ref[0]
    window = sum(dot(x[:, i * CP : (i + 1) * CP], perm[i], TN) for i in range(4))
    out_ref[0] = dot(window.astype(bf16), w_ref[0], NN).astype(bf16)


def per_plane(body, first, weights, out_rows, out_lanes, out_type, toks, TR, TC, deps=()):
    planes, ext, samples = weights.shape

    def whole(shape):
        return pl.BlockSpec((1,) + shape, lambda i: (i, 0, 0))

    return pl.pallas_call(
        functools.partial(body, TR=TR, TC=TC),
        grid=(planes,),
        out_shape=jax.ShapeDtypeStruct((planes, out_rows, out_lanes), out_type),
        in_specs=[whole(first.shape[1:]), whole((ext, samples))] + [AN] * len(deps),
        out_specs=whole((out_rows, out_lanes)),
        scratch_shapes=[pltpu.VMEM((4, toks, ext), bf16)],
        compiler_params=pltpu.CompilerParams(vmem_limit_bytes=24 * 2**20),
        cost_estimate=BRIEF,
    )(first, weights, *deps)


def swap_seq(value):
    return lax.all_to_all(value, "seq", split_axis=0, concat_axis=0, tiled=True)


def swap_mp(value):
    return lax.all_to_all(value, "mp", split_axis=0, concat_axis=0, tiled=True)


def swap_all(value):
    return lax.all_to_all(value, ("seq", "mp"), split_axis=0, concat_axis=0, tiled=True)


def swap_pair(value):
    count = lax.axis_size("mp")
    return lax.ppermute(value, "mp", [(i, i ^ 1) for i in range(count)])


def gather_rows(piece):
    return lax.all_gather(piece, ("mp", "seq"), axis=0, tiled=False)


def bundle_part(bundle, at, rows):
    pieces, _, D = bundle.shape
    if rows % 16 == 0 and at % rows == 0:
        return bundle, ((pieces, rows, D), (0, at // rows, 0))
    value = bundle[:, at : at + rows].reshape(1, -1, D)
    return value, (value.shape, None)


def by_step(part, steps):
    (pieces, rows, D), at = part[1]
    if pieces > 1:
        return part[0], pl.BlockSpec((pieces // steps, rows, D), lambda i: (i, at[1], 0))
    return part[0], pl.BlockSpec((1, rows // steps, D), lambda i: (0, i, 0))


def reduce_rows(value):
    return lax.psum_scatter(value, "seq", scatter_dimension=0, tiled=True)


def to_ranks(blocks):
    moves = [[(i, i ^ step) for i in range(len(blocks))] for step in range(len(blocks))]
    return [v if i == 0 else lax.ppermute(v, "mp", moves[i]) for i, v in enumerate(blocks)]


def to_halves(blocks):
    pairs = len(blocks)
    arrived = []
    for step in range(pairs):
        moves = [(2 * p + h, pairs * h + (p ^ step)) for p in range(pairs) for h in range(2)]
        arrived.append(lax.ppermute(blocks[step], "mp", moves))
    return arrived


def sum_ranks(value):
    return lax.psum_scatter(value, "mp", scatter_dimension=1, tiled=True).astype(f32)


def gather_pieces(value):
    shares = lax.axis_size("seq")
    pieces = []
    for step in range(0, shares, 2):
        moves = [(i, i ^ step) for i in range(shares)]
        pieces.append(value if step == 0 else lax.ppermute(value, "seq", moves))
    cores = [(i, i ^ 1) for i in range(shares)]
    return [p for piece in pieces for p in (piece, lax.ppermute(piece, "seq", cores))]


def per_device(
    tokens,
    patches,
    counts,
    norm_gains,
    norm_shifts,
    cross_query,
    cross_kv,
    cross_out,
    self_qkv,
    self_out,
    mlp_up,
    mlp_down,
    decoder,
    sample_weights,
    tokens_cot,
    sample_cot,
):
    objects, R, D = tokens.shape
    S, M = lax.axis_size("seq"), lax.axis_size("mp")
    s, m = lax.axis_index("seq"), lax.axis_index("mp")
    pairs = M // 2
    if objects != 3 * pairs or S != 2 * M or D % (HD * S) != 0:
        raise ValueError("unexpected sizes")
    pair, half = m // 2, m % 2
    at_a, at_b = 3 * pair + 2 * half, 3 * pair + 1
    RB = R // 2
    RS = R + RB
    rows = [R, RB]
    W = D // S
    hpd = W // HD
    slots, width = patches.shape[1], patches.shape[2]
    slot_total = slots * S
    row_total = R * S

    def pick(arr):
        whole = lax.dynamic_index_in_dim(arr, at_b, 0, keepdims=False)
        return [
            lax.dynamic_index_in_dim(arr, at_a, 0, keepdims=False),
            lax.dynamic_slice_in_dim(whole, half * RB, RB, 0),
        ]

    def mine(arr, axis):
        share = arr.shape[axis] // S
        return lax.dynamic_slice_in_dim(arr, s * share, share, axis)

    channels = decoder.shape[1]
    local_dec = jnp.pad(decoder.transpose(2, 1, 0), ((0, 0), (0, CP - channels), (0, 0)))
    part = S // 2
    qkv_piece = lax.dynamic_slice_in_dim(self_qkv, s // part * W, W, 2).reshape(D, 3 * W)
    qkv_piece = lax.dynamic_slice_in_dim(qkv_piece, s % part * (3 * W // part), 3 * W // part, 1)
    per = D // (S * M)
    dec_rows = 4 * CP // S
    kv_rows = 2 * per
    at = s * kv_rows
    kv_piece = lax.dynamic_slice(
        cross_kv, (0, (at // W) % 2, at // (2 * W) * W + at % W), (width, 1, kv_rows)
    )
    kv_piece = jnp.pad(kv_piece[:, 0].T, ((0, 0), (0, D - width)))
    lead = gather_rows(jnp.concatenate([kv_piece, mine(cross_query, 1).T], axis=0))
    w_kv, w_query = bundle_part(lead, 0, kv_rows), bundle_part(lead, kv_rows, per)
    first = gather_rows(
        jnp.concatenate(
            [qkv_piece.T, mine(cross_out, 0)], axis=0
        )
    )
    up_rows = mlp_up.shape[1] // S
    second = gather_rows(
        jnp.concatenate(
            [
                mine(mlp_up, 1).T,
                mine(mlp_down, 0),
                mine(self_out, 0),
                mine(local_dec.reshape(-1, D), 0),
            ],
            axis=0,
        )
    )
    steps = 8
    w_up = by_step(bundle_part(second, 0, up_rows), steps)
    w_down = by_step(bundle_part(second, up_rows, up_rows), steps)
    w_triple = by_step(bundle_part(first, 0, 3 * per), S)
    w_cross_out = bundle_part(first, 3 * per, per)
    w_self_out = bundle_part(second, 2 * up_rows, per)
    w_dec = bundle_part(second, 2 * up_rows + per, dec_rows)

    x0 = pick(tokens)
    norms = [jnp.stack([norm_gains[i], norm_shifts[i]]) for i in range(3)]
    at = jnp.stack([s, m])
    both = [lax.dynamic_index_in_dim(patches, o, 0, keepdims=False) for o in (at_a, at_b)]
    patch_pieces = gather_pieces(jnp.concatenate(both, axis=0))
    TC = PLANE // 4
    TR = PLANE * 4 // S
    own, rim = TR * TC, TR * TC + TR
    toks = -(-(rim + TC + 1) // 32) * 32
    planes = objects * 3
    weights_in = sample_weights.reshape(planes, *sample_weights.shape[3:])
    cot_in = sample_cot.reshape(planes, channels, -1)
    cot_in = jnp.pad(cot_in, ((0, 0), (0, CP - channels), (0, 0)))
    ext = per_plane(pixel_grad_kernel, cot_in, weights_in, toks, 4 * CP, f32, toks, TR, TC)
    ways = {
        1: [i for i in range(S) if i % 4 != 3],
        4: [i for i in range(S) if i + 4 < S],
        5: [i for i in range(S) if i % 4 != 3 and i + 4 < S],
    }
    rights = lax.ppermute(ext[:, own:rim], "seq", [(i, i + 1) for i in ways[1]])
    belows = lax.ppermute(ext[:, rim : rim + TC], "seq", [(i, i + 4) for i in ways[4]])
    corner = lax.ppermute(ext[:, rim + TC : rim + TC + 1], "seq", [(i, i + 5) for i in ways[5]])
    grid = ext[:, :own].reshape(planes, TR, TC, -1)
    belows = jnp.concatenate([belows[:, :1] + corner, belows[:, 1:]], axis=1)
    grid = grid + jnp.pad(rights[:, :, None], ((0, 0), (0, 0), (0, TC - 1), (0, 0)))
    grid = grid + jnp.pad(belows[:, None], ((0, 0), (0, TR - 1), (0, 0), (0, 0)))
    KA, KB = R // S, RB // S
    cu = 4 * CP
    grad_pix = grid.astype(bf16).reshape(pairs, 3, S, KA, cu)
    gp_a = jnp.stack([grad_pix[:, 0], grad_pix[:, 2]], axis=1).transpose(2, 0, 1, 3, 4)
    gp_b = grad_pix[:, 1].reshape(pairs, S, 2, KB, cu).transpose(1, 0, 2, 3, 4)
    sent = jnp.concatenate([gp_a, gp_b], axis=3).reshape(S * M, KA + KB, cu)

    q1, keys_one, n1, w_query, w_kv = start(
        at, x0, norms[0], w_kv, w_query, patch_pieces, W, [sent]
    )
    heads_one = swap_seq(q1)
    back = swap_all(hold(sent, [heads_one]))
    d_pix = back.reshape(S, M, KA + KB, cu).transpose(2, 0, 1, 3).reshape(RS, M * cu)

    limits = [
        jnp.stack([lax.dynamic_index_in_dim(counts, o, 0, keepdims=False), jnp.int32(0)])
        for o in (at_a, at_b)
    ]
    kv_one = [(slots, (i * slots, 0), (i * slots, W), 0) for i in range(2)]
    o1, res1 = [], []
    for i in range(2):
        out, res = attend(
            limits[i],
            [heads_one, keys_one],
            S,
            (0, rows[i], i * R, 0),
            [(1,) + kv_one[i]],
            slot_total,
            hpd,
            False,
            [(back,), ()][i],
        )
        o1.append(out)
        res1.append(res)

    mids = [
        middle(swap_seq(o1[i].reshape(S, rows[i], W)), x0[i], norms[1], w_cross_out, w_triple)
        for i in range(2)
    ]
    x1, n2, a1, t2 = zip(*mids)

    heads_two = [swap_seq(v) for v in t2]
    pair_kv = swap_pair(heads_two[1][:, :, W:])
    wide = jnp.array([row_total, 0], jnp.int32)
    kv_a2 = (R, (0, W), (0, 2 * W), 0)
    kv_b2 = (RB, (0, W), (0, 2 * W), 0)
    kv_p2 = (RB, (0, 0), (0, W), row_total // 2)
    o_a2, res_a2 = attend(
        wide, [heads_two[0]], S, (0, R, 0, 0), [(0,) + kv_a2], row_total, hpd, True
    )
    o_b2, res_b2 = attend(
        wide,
        [heads_two[1], pair_kv],
        S,
        (0, RB, 0, 0),
        [(0,) + kv_b2, (1,) + kv_p2],
        row_total,
        hpd,
        True,
        [o_a2],
    )
    a2_a = swap_seq(o_a2.reshape(S, R, W))
    a2 = [a2_a, swap_seq(hold(o_b2.reshape(S, RB, W), [a2_a]))]

    hidden = mlp_up.shape[1] * M
    n3, a2, g, du, x3b, pix, e3, d2, e2, da2, sums_three = feed_forward(
        a2,
        x1,
        pick(tokens_cot),
        d_pix,
        norms[2],
        w_self_out,
        w_dec,
        w_up,
        w_down,
        hidden,
        steps,
    )

    da2 = swap_seq(da2)
    grads_one = weight_grads([[(n3, du)], [(e3, g)], [(e2, a2)], [(x3b, d_pix)]], M)
    grads_one = hold(grads_one, [da2])
    pix = hold(pix, [grads_one])
    dt2_a = attend_back(
        wide,
        [res_a2, da2, o_a2, heads_two[0]],
        S,
        (R, 0),
        [(3,) + kv_a2],
        row_total,
        hpd,
        True,
        [grads_one],
        "lanes",
    )
    grads_one = reduce_rows(grads_one)
    pix = pix.reshape(KA + KB, S, M, cu).transpose(1, 2, 0, 3)
    got = swap_all(pix.reshape(S * M, KA + KB, cu)).reshape(S, pairs, 2, KA + KB, cu)
    half_total = row_total // 2
    kv_p2 = (RB, (0, 0), (0, W), 0)
    dq_p2, dkv_p2 = attend_back(
        wide,
        [res_b2, da2, o_b2, pair_kv],
        S,
        (RB, R),
        [(3,) + kv_p2],
        half_total,
        hpd,
        True,
        [dt2_a, got],
    )
    given = swap_pair(dkv_p2)
    dq_b2, dkv_b2 = attend_back(
        wide,
        [res_b2, da2, o_b2, heads_two[1]],
        S,
        (RB, R),
        [(3,) + kv_b2],
        half_total,
        hpd,
        True,
        [dq_p2],
    )
    dq_b2 = (dq_b2.astype(f32) + dq_p2.astype(f32)).astype(bf16)
    dkv_b2 = (dkv_b2.astype(f32) + given.astype(f32)).astype(bf16)
    dt2 = [
        swap_seq(dt2_a),
        jnp.concatenate([dq_b2, dkv_b2], axis=1).reshape(S, RB, 3 * W),
    ]

    def below(i, deps):
        return middle_back(
            dt2[i], x1[i], d2, (0, R // RB)[i], norms[1], w_cross_out, w_triple, deps
        )

    def cross_back(i, da1, deps):
        return attend_back(
            limits[i],
            [res1[i], da1, o1[i], keys_one],
            S,
            (rows[i], 0),
            [(3,) + kv_one[i]],
            slot_total,
            hpd,
            False,
            deps,
            "rows",
        )

    low_a = below(0, [dq_b2, given])
    x3b = hold(x3b, [low_a[0]])
    blocks_a, blocks_b = x3b[:R].reshape(M, R // M, D), x3b[R:].reshape(pairs, R // M, D)
    blocks_a = [lax.dynamic_index_in_dim(blocks_a, m ^ i, 0, keepdims=False) for i in range(M)]
    blocks_b = [
        lax.dynamic_index_in_dim(blocks_b, pair ^ i, 0, keepdims=False) for i in range(pairs)
    ]
    blocks_a, blocks_b = to_ranks(blocks_a), to_halves(blocks_b)
    da1_a = swap_seq(low_a[2])
    dt2[1] = swap_seq(hold(dt2[1], [da1_a]))
    cross_a = cross_back(0, da1_a, [])
    grads_one = sum_ranks(hold(grads_one, [da1_a]))
    low_b = below(1, [cross_a])
    got_a = swap_seq(cross_a)
    da1_b = swap_seq(hold(low_b[2], [got_a]))
    d1, e1, da1, sums_two = zip(low_a, low_b)

    grads_two = weight_grads(
        [[(n2[i], dt2[i]) for i in range(2)], [(e1[i], a1[i]) for i in range(2)]], M, [grads_one, got_a] + blocks_a + blocks_b
    )
    *sent_a, share, lift = end(
        at, got_a, 0, w_query, w_kv, x0[0], n1, d1[0], norm_gains[:1], M, [grads_two]
    )
    cross_b = cross_back(1, da1_b, [grads_two, lift])
    grads_two = reduce_rows(grads_two)
    got_b = swap_seq(cross_b)

    two = sums_two[0] + sums_two[1]
    small = jnp.concatenate([two, sums_three], axis=0)
    px_a = got[:, :, :, :KA].transpose(1, 2, 0, 3, 4).reshape(pairs, 2, S * KA, cu)
    px_b = got[:, :, :, KA:].transpose(1, 0, 2, 3, 4).reshape(pairs, S * KA, cu)
    tile = jnp.stack([px_a[:, 0], px_b, px_a[:, 1]], axis=1).reshape(planes, TR, TC, cu)
    rights = lax.ppermute(tile[:, :, 0], "seq", [(i + 1, i) for i in ways[1]])
    belows = lax.ppermute(tile[:, 0], "seq", [(i + 4, i) for i in ways[4]])
    corner = lax.ppermute(tile[:, 0, :1], "seq", [(i + 5, i) for i in ways[5]])
    fill = jnp.zeros((planes, toks - rim - TC - 1, cu), bf16)
    ext = jnp.concatenate([tile.reshape(planes, own, cu), rights, belows, corner, fill], axis=1)
    sent_a = to_ranks(sent_a)
    by_head = finish(at, [cross_a, cross_b], rows, patch_pieces, [*sent_a, ext])
    heads = by_head.shape[1]
    *sent_b, part_b, final = end(
        at,
        got_b,
        R // RB,
        w_query,
        w_kv,
        x0[1],
        n1,
        d1[1],
        norm_gains[:1],
        pairs,
        [],
        [share, lift, small, by_head],
    )
    got_last = swap_seq(final)
    grad_tokens = place_rows(at, sent_a, to_halves(sent_b), f32, [], True)
    patch_grad = place_patches(at, sent_a, to_ranks([part_b] * M))
    ext = hold(ext, [final])
    tokens_out = place_rows(at, blocks_a, blocks_b, bf16, [final])
    sampled = per_plane(
        pixel_sample_kernel, ext, weights_in, CP, weights_in.shape[2], bf16, toks, TR, TC
    )
    sampled = sampled[:, :channels].reshape(objects, 3, channels, 1, -1)

    final = last(to_ranks(mix(at, got_last, M, heads, [sampled, tokens_out])), heads)
    grad_cross_query, grad_keys, grad_values, small = final
    grad_cross_kv = jnp.stack([grad_keys, grad_values], axis=1)

    grads_two = sum_ranks(grads_two)
    ff = hidden // M
    grad_mlp_up, grad_mlp_down = grads_one[:, :ff], grads_one[:, ff : 2 * ff].T
    grad_self_out = grads_one[:, 2 * ff : 2 * ff + D // M].T
    grad_decoder = grads_one[:, 2 * ff + D // M :]
    grad_decoder = grad_decoder.reshape(D // S, 4, CP)[:, :, :channels].transpose(0, 2, 1)
    grad_self_qkv = grads_two[:, : 3 * D // M].reshape(D // S, 2, 3, W).transpose(0, 2, 1, 3)
    grad_cross_out = grads_two[:, 3 * D // M :].T

    return (
        tokens_out,
        sampled,
        grad_tokens,
        patch_grad,
        jnp.stack([small[0], small[2], small[4]]),
        jnp.stack([small[1], small[3]]),
        small[5],
        grad_cross_query,
        grad_cross_kv,
        grad_cross_out,
        grad_self_qkv.reshape(D // S, 3, -1),
        grad_self_out,
        grad_mlp_up,
        grad_mlp_down,
        grad_decoder,
    )


def solution(mesh):
    return jax.shard_map(
        per_device,
        mesh=mesh,
        in_specs=(
            P(None, "seq", None),
            P(None, "seq", None),
            P(),
            P(),
            P(),
            P(None, "mp"),
            P(None, None, "mp"),
            P("mp", None),
            P(None, None, "mp"),
            P("mp", None),
            P(None, "mp"),
            P("mp", None),
            P(None, "mp", None),
            P(None, None, "seq", None, None),
            P(None, "seq", None),
            P(None, None, "mp", "seq", None),
        ),
        out_specs=(
            P(None, ("seq", "mp"), None),
            P(None, None, "mp", "seq", None),
            P(None, ("seq", "mp"), None),
            P(None, "seq", None),
            P(None, "seq"),
            P(None, "seq"),
            P("seq"),
            P("seq", "mp"),
            P("seq", None, "mp"),
            P("mp", "seq"),
            P("seq", None, "mp"),
            P("mp", "seq"),
            P("seq", "mp"),
            P("mp", "seq"),
            P("seq", "mp", None),
        ),
        check_vma=False,
    )
```

```python
import functools
import math

import jax
import jax.numpy as jnp
from jax import lax
from jax.experimental import pallas as pl
from jax.experimental.pallas import tpu as pltpu
from jax.sharding import PartitionSpec as P


PLANE = 32
HD = 64
LANES = 128
norm_eps = 1e-05
f32 = jnp.float32
bf16 = jnp.bfloat16

NT = (((1,), (1,)), ((), ()))
NN = (((1,), (0,)), ((), ()))
TN = (((0,), (0,)), ((), ()))


def dot(a, b, dims):
    return lax.dot_general(a, b, dims, preferred_element_type=f32)


def mm(a, b):
    return jnp.dot(a, b, preferred_element_type=f32)


def split3(v):
    hi = v.astype(bf16).astype(f32)
    rest = v - hi
    mid = rest.astype(bf16).astype(f32)
    return hi, mid, rest - mid


def spread(base, cols):
    lane = lax.broadcasted_iota(jnp.int32, (base.shape[0], HD), 1)
    tail = jnp.zeros((base.shape[0], HD), f32)
    for at, col in cols.items():
        tail = jnp.where(lane == at, col, tail)
    return jnp.concatenate([base, tail], axis=1).astype(bf16)


def load_keys(n_ref, kv_specs, refs, ka, va, hpd, blocks):
    for ref_at, rows, k_at, v_at, base in kv_specs:
        src = refs[ref_at]

        def build(i, _):
            natural = base + (i ^ n_ref[1]) * rows
            dst = pl.ds(pl.multiple_of(natural, 16), rows)
            slot = natural + lax.broadcasted_iota(jnp.int32, (rows, 1), 0)
            mask = jnp.where(slot < n_ref[0], 0.0, -1e30).astype(f32)
            for h in range(hpd):
                k = src[i, k_at[0] : k_at[0] + rows, k_at[1] + h * HD : k_at[1] + (h + 1) * HD]
                v = src[i, v_at[0] : v_at[0] + rows, v_at[1] + h * HD : v_at[1] + (h + 1) * HD]
                ka[h, dst, :] = spread(k.astype(f32), {0: 1.0, 1: 1.0, 2: 1.0, 3: mask})
                va[h, dst, :] = spread(v.astype(f32), {0: 1.0, 1: 1.0, 2: 1.0})
            return 0

        lax.fori_loop(0, blocks, build, 0)


def fwd_kernel(n_ref, *refs, n_in, blocks, q_spec, kv_specs, hpd, bq, kc, fixed):
    ins, (o_ref, qa_ref, ka, va) = refs[:n_in], refs[-4:]
    load_keys(n_ref, kv_specs, ins, ka, va, hpd, blocks)
    q_at, rows_q, q_off, q_lane = q_spec

    def build(i, _):
        dst = pl.ds(pl.multiple_of((i ^ n_ref[1]) * rows_q, 16), rows_q)
        for h in range(hpd):
            q = ins[q_at][i, q_off : q_off + rows_q, q_lane + h * HD : q_lane + (h + 1) * HD]
            qa_ref[h, dst, :] = spread(q.astype(f32) * (1.0 / math.sqrt(HD)), {3: 1.0})
        return 0

    lax.fori_loop(0, blocks, build, 0)
    total = ka.shape[1]

    def block(b, _):
        rows = pl.ds(pl.multiple_of(b * bq, bq), bq)

        def chunk(c, carry):
            cols = pl.ds(pl.multiple_of(c * kc, kc), kc)
            out = []
            for h in range(hpd):
                m, acc = carry[h]
                s = dot(qa_ref[h, rows, :], ka[h, cols, :], NT)
                top = jnp.maximum(m, jnp.max(s, axis=1, keepdims=True))
                p = jnp.exp(s - top).astype(bf16)
                out.append((top, acc * jnp.exp(m - top) + dot(p, va[h, cols, :], NN)))
            return tuple(out)

        carry = ((jnp.full((bq, 1), -1e30, f32), jnp.zeros((bq, LANES), f32)),) * hpd
        if fixed:
            for c in range(total // kc):
                carry = chunk(c, carry)
        else:
            carry = lax.fori_loop(0, (n_ref[0] + kc - 1) // kc, chunk, carry)
        outs = []
        for h in range(hpd):
            m, acc = carry[h]
            norm = acc[:, HD : HD + 1]
            outs.append(acc[:, :HD] / norm)
            hi, mid, lo = split3(-(m + jnp.log(norm)))
            qa_ref[h, rows, :] = spread(
                qa_ref[h, rows, :HD].astype(f32), {0: hi, 1: mid, 2: lo, 3: 1.0}
            )
        o_ref[rows, :] = jnp.concatenate(outs, axis=1).astype(bf16)
        return 0

    lax.fori_loop(0, qa_ref.shape[1] // bq, block, 0)


def bwd_kernel(n_ref, *refs, n_in, n_dep, blocks, do_spec, kv_specs, hpd, bq, kc, fixed, form):
    ins, (*outs, ka, va, da, dk, dv, dq) = refs[:n_in], refs[n_in + n_dep :]
    qa_ref, do_ref, o_ref = ins[:3]
    load_keys(n_ref, kv_specs, ins, ka, va, hpd, blocks)
    rows_q, do_off = do_spec

    def build(i, _):
        rows = pl.ds(pl.multiple_of(i * rows_q, 16), rows_q)
        for h in range(hpd):
            d = do_ref[i, do_off : do_off + rows_q, h * HD : (h + 1) * HD].astype(f32)
            o = o_ref[rows, h * HD : (h + 1) * HD].astype(f32)
            hi, mid, lo = split3(-jnp.sum(d * o, axis=1, keepdims=True))
            da[h, rows, :] = spread(d, {0: hi, 1: mid, 2: lo})
        return 0

    lax.fori_loop(0, blocks, build, 0)
    dk[...] = jnp.zeros_like(dk)
    dv[...] = jnp.zeros_like(dv)
    total = ka.shape[1]
    steps = total // kc if fixed else (n_ref[0] + kc - 1) // kc

    def block(b, _):
        rows = pl.ds(pl.multiple_of(b * bq, bq), bq)

        def chunk(c, dqs):
            cols = pl.ds(pl.multiple_of(c * kc, kc), kc)
            out = []
            for h in range(hpd):
                k, q, d = ka[h, cols, :], qa_ref[h, rows, :], da[h, rows, :]
                p = jnp.exp(dot(k, q, NT))
                dp = dot(va[h, cols, :], d, NT)
                dv[h, cols, :] += dot(p.astype(bf16), d, NN)
                g = (p * dp).astype(bf16)
                dk[h, cols, :] += dot(g, q, NN)
                out.append(dqs[h] + dot(k, g, TN))
            return tuple(out)

        dqs = lax.fori_loop(0, steps, chunk, (jnp.zeros((LANES, bq), f32),) * hpd)
        grad = jnp.concatenate([v[:HD, :] for v in dqs], axis=0).T
        dq[rows, :] = (grad * (1.0 / math.sqrt(HD))).astype(bf16)
        return 0

    lax.fori_loop(0, qa_ref.shape[1] // bq, block, 0)
    step = total // blocks

    def finish(i, _):
        rows = pl.ds(pl.multiple_of(i * step, 16), step)
        q_rows = pl.ds(pl.multiple_of(i * rows_q, 16), rows_q)
        k, v = [
            jnp.concatenate([d[h, rows, :HD] for h in range(hpd)], axis=1).astype(bf16)
            for d in (dk, dv)
        ]
        if form == "split":
            outs[0][q_rows, :] = dq[q_rows, :]
            outs[1][rows, :] = jnp.concatenate([k, v], axis=1)
        elif form == "lanes":
            outs[0][i] = jnp.concatenate([dq[q_rows, :], k, v], axis=1)
        else:
            outs[0][i, :rows_q, :] = dq[q_rows, :]
            outs[0][i, rows_q : rows_q + step, :] = k
            outs[0][i, rows_q + step :, :] = v
        return 0

    lax.fori_loop(0, blocks, finish, 0)


VM = pl.BlockSpec(memory_space=pltpu.VMEM)
SM = pl.BlockSpec(memory_space=pltpu.SMEM)
BRIEF = pl.CostEstimate(flops=10**6, bytes_accessed=10**5, transcendentals=0)
AN = pl.BlockSpec(memory_space=pl.ANY)


def fit(rows, most):
    return math.gcd(rows, most)


def attend(limits, ins, blocks, q_spec, kv_specs, total, hpd, fixed, deps=()):
    queries = blocks * q_spec[1]
    kc = fit(total, 1024 if fixed else 512)
    body = functools.partial(
        fwd_kernel,
        n_in=len(ins),
        blocks=blocks,
        q_spec=q_spec,
        kv_specs=kv_specs,
        hpd=hpd,
        bq=fit(queries, 512),
        kc=kc,
        fixed=fixed,
    )
    work = hpd * queries * total
    return pl.pallas_call(
        body,
        out_shape=(
            jax.ShapeDtypeStruct((queries, hpd * HD), bf16),
            jax.ShapeDtypeStruct((hpd, queries, LANES), bf16),
        ),
        in_specs=[SM] + [VM] * len(ins) + [AN] * len(deps),
        out_specs=(VM, VM),
        scratch_shapes=[pltpu.VMEM((hpd, total, LANES), bf16)] * 2,
        compiler_params=pltpu.CompilerParams(vmem_limit_bytes=44 * 2**20),
        cost_estimate=BRIEF,
    )(limits, *ins, *deps)


def attend_back(limits, ins, blocks, do_spec, kv_specs, total, hpd, fixed, deps=(), form="split"):
    queries = blocks * do_spec[0]
    W, step = hpd * HD, total // blocks
    shapes = {
        "split": [(queries, W), (total, 2 * W)],
        "lanes": [(blocks, step, 3 * W)],
        "rows": [(blocks, do_spec[0] + 2 * step, W)],
    }[form]
    body = functools.partial(
        bwd_kernel,
        n_in=len(ins),
        n_dep=len(deps),
        blocks=blocks,
        do_spec=do_spec,
        kv_specs=kv_specs,
        hpd=hpd,
        bq=fit(queries, 512),
        kc=fit(total, 1024 if fixed else 512),
        fixed=fixed,
        form=form,
    )
    out = pl.pallas_call(
        body,
        out_shape=tuple(jax.ShapeDtypeStruct(v, bf16) for v in shapes),
        in_specs=[SM] + [VM] * len(ins) + [AN] * len(deps),
        out_specs=(VM,) * len(shapes),
        scratch_shapes=[pltpu.VMEM((hpd, total, LANES), bf16)] * 2
        + [pltpu.VMEM((hpd, queries, LANES), bf16)]
        + [pltpu.VMEM((hpd, total, LANES), f32)] * 2
        + [pltpu.VMEM((queries, W), bf16)],
        compiler_params=pltpu.CompilerParams(vmem_limit_bytes=52 * 2**20),
        cost_estimate=BRIEF,
    )(limits, *ins, *deps)
    return out if len(out) > 1 else out[0]


def norm_parts(values):
    center = values - jnp.mean(values, axis=-1, keepdims=True)
    scale = lax.rsqrt(jnp.mean(center * center, axis=-1, keepdims=True) + norm_eps)
    return center * scale, scale


def layer_norm(values, gain_row, shift_row):
    return (norm_parts(values)[0] * gain_row + shift_row).astype(bf16)


def norm_back(values, gain_row, grad_out):
    unit, scale = norm_parts(values)
    lifted = grad_out * gain_row
    grad_in = scale * (
        lifted
        - jnp.mean(lifted, axis=-1, keepdims=True)
        - unit * jnp.mean(lifted * unit, axis=-1, keepdims=True)
    )
    gain = jnp.sum(grad_out * unit, axis=0, keepdims=True)
    return grad_in, gain, jnp.sum(grad_out, axis=0, keepdims=True)


def flat(ref):
    return ref[...].reshape(-1, ref.shape[-1])


def joined(ref):
    return jnp.concatenate([ref[i] for i in range(ref.shape[0])], axis=1)


def once(shape, index=None):
    at = (0,) * len(shape) if index is None else index
    return pl.BlockSpec(shape, lambda i: at, pipeline_mode=pl.Buffered(1))


def held(shape):
    return pl.BlockSpec(shape, lambda i: (0,) * len(shape))


def mid_kernel(a_ref, x_ref, norm_ref, wo_ref, wt_ref, *refs):
    x1_ref, n_ref, ac_ref, t_ref = refs[-4:]

    @pl.when(pl.program_id(0) == 0)
    def _():
        a = joined(a_ref)
        ac_ref[...] = a
        x1 = x_ref[...].astype(f32) + dot(a, flat(wo_ref), NN)
        x1_ref[...] = x1
        n_ref[...] = layer_norm(x1, norm_ref[0:1, :], norm_ref[1:2, :])

    t_ref[0] = dot(n_ref[...], flat(wt_ref), NT).astype(bf16)


def middle(a, x, norm, w_out, w_triple, deps=()):
    S, rows, W = a.shape
    D = S * W
    return pl.pallas_call(
        mid_kernel,
        grid=(S,),
        out_shape=(
            jax.ShapeDtypeStruct((rows, D), f32),
            jax.ShapeDtypeStruct((rows, D), bf16),
            jax.ShapeDtypeStruct((rows, D), bf16),
            jax.ShapeDtypeStruct((S, rows, 3 * W), bf16),
        ),
        in_specs=[
            once((S, rows, W)),
            once((rows, D)),
            once((2, D)),
            once(*w_out[1]),
            w_triple[1],
        ]
        + [AN] * len(deps),
        out_specs=(
            held((rows, D)),
            held((rows, D)),
            held((rows, D)),
            pl.BlockSpec((1, rows, 3 * W), lambda i: (i, 0, 0)),
        ),
        compiler_params=pltpu.CompilerParams(vmem_limit_bytes=40 * 2**20),
        cost_estimate=BRIEF,
    )(a, x, norm, w_out[0], w_triple[0], *deps)


def mlp_kernel(
    aa_ref,
    ab_ref,
    xa_ref,
    xb_ref,
    ca_ref,
    cb_ref,
    dp_ref,
    norm_ref,
    ws_ref,
    wd_ref,
    up_ref,
    down_ref,
    n_ref,
    ac_ref,
    g_ref,
    du_ref,
    x3_ref,
    pix_ref,
    e3_ref,
    d2_ref,
    e2_ref,
    da_ref,
    sum_ref,
    x2,
    d3,
    acc,
    back,
    *,
    steps,
):
    step = pl.program_id(0)
    R = xa_ref.shape[0]
    S, _, W = aa_ref.shape

    @pl.when(step == 0)
    def _():
        for rows, a_ref, x_ref, c_ref in (
            (slice(0, R), aa_ref, xa_ref, ca_ref),
            (slice(R, x2.shape[0]), ab_ref, xb_ref, cb_ref),
        ):
            a = joined(a_ref)
            ac_ref[rows, :] = a
            x = x_ref[...] + dot(a, flat(ws_ref), NN)
            x2[rows, :] = x
            n_ref[rows, :] = layer_norm(x, norm_ref[0:1, :], norm_ref[1:2, :])
            d = c_ref[...].astype(f32) + dot(dp_ref[rows, :], flat(wd_ref), NN)
            d3[rows, :] = d
            e3_ref[rows, :] = d.astype(bf16)
        acc[...] = jnp.zeros_like(acc)
        back[...] = jnp.zeros_like(back)

    up = flat(up_ref)
    down = flat(down_ref)
    u = dot(n_ref[...], up, NT)
    slope = math.sqrt(2.0 / math.pi)
    square = u * u
    bend = jnp.tanh(slope * u * (1.0 + 0.044715 * square))
    half = 0.5 * (1.0 + bend)
    g = (u * half).astype(bf16)
    rise = half + 0.5 * slope * u * (1.0 - bend * bend) * (1.0 + 0.134145 * square)
    du = (dot(e3_ref[...], down, NT) * rise).astype(bf16)
    g_ref[...] = g
    du_ref[...] = du
    acc[...] += dot(g, down, NN)
    back[...] += dot(du, up, NN)

    @pl.when(step == steps - 1)
    def _():
        x3 = (x2[...] + acc[...]).astype(bf16)
        x3_ref[...] = x3
        pix_ref[...] = dot(x3, flat(wd_ref), NT).astype(bf16)
        grad_in, gain, shift = norm_back(x2[...], norm_ref[0:1, :], back[...])
        d2 = d3[...] + grad_in
        d2_ref[...] = d2
        e2 = d2.astype(bf16)
        e2_ref[...] = e2
        sum_ref[...] = jnp.concatenate([gain, shift], axis=0)
        da = dot(e2, flat(ws_ref), NT).astype(bf16)
        for i in range(S):
            da_ref[i] = da[:, i * W : (i + 1) * W]


def feed_forward(a, x1, cot, d_pix, norm, w_out, w_dec, w_up, w_down, hidden, steps):
    S, R, W = a[0].shape
    RB = a[1].shape[1]
    D, total, pixels = S * W, R + RB, d_pix.shape[1]
    part = hidden // steps
    row = jax.ShapeDtypeStruct((total, D), bf16)
    wide = jax.ShapeDtypeStruct((total, hidden), bf16)
    blocked = pl.BlockSpec((total, part), lambda i: (0, i))
    full = held((total, D))
    return pl.pallas_call(
        functools.partial(mlp_kernel, steps=steps),
        grid=(steps,),
        out_shape=(
            row,
            row,
            wide,
            wide,
            row,
            jax.ShapeDtypeStruct((total, pixels), bf16),
            row,
            jax.ShapeDtypeStruct((total, D), f32),
            row,
            jax.ShapeDtypeStruct((S, total, W), bf16),
            jax.ShapeDtypeStruct((2, D), f32),
        ),
        in_specs=[
            once((S, R, W)),
            once((S, RB, W)),
            once((R, D)),
            once((RB, D)),
            once((R, D)),
            once((RB, D)),
            once((total, pixels)),
            once((2, D)),
            once(*w_out[1]),
            once(*w_dec[1]),
            w_up[1],
            w_down[1],
        ],
        out_specs=(
            full,
            full,
            blocked,
            blocked,
            full,
            held((total, pixels)),
            full,
            full,
            full,
            held((S, total, W)),
            held((2, D)),
        ),
        scratch_shapes=[pltpu.VMEM((total, D), f32)] * 4,
        compiler_params=pltpu.CompilerParams(vmem_limit_bytes=60 * 2**20),
        cost_estimate=BRIEF,
    )(*a, *x1, *cot, d_pix, norm, w_out[0], w_dec[0], w_up[0], w_down[0])


def hold_kernel(*refs):
    pass


def hold(value, deps):
    return pl.pallas_call(
        hold_kernel,
        out_shape=jax.ShapeDtypeStruct(value.shape, value.dtype),
        in_specs=[AN] * (1 + len(deps)),
        out_specs=AN,
        input_output_aliases={0: 0},
        cost_estimate=BRIEF,
    )(value, *deps)


def back_kernel(
    t_ref, x_ref, d_ref, norm_ref, wo_ref, wt_ref, *refs, steps
):
    d1_ref, e_ref, da_ref, sum_ref, acc = refs[-5:]
    step = pl.program_id(0)
    part = dot(t_ref[0], flat(wt_ref), NN)

    @pl.when(step == 0)
    def _():
        acc[...] = part

    @pl.when(step > 0)
    def _():
        acc[...] += part

    @pl.when(step == steps - 1)
    def _():
        grad_in, gain, shift = norm_back(x_ref[...], norm_ref[0:1, :], acc[...])
        d1 = d_ref[...] + grad_in
        d1_ref[...] = d1
        e = d1.astype(bf16)
        e_ref[...] = e
        sum_ref[...] = jnp.concatenate([gain, shift], axis=0)
        da = dot(e, flat(wo_ref), NT).astype(bf16)
        W = da_ref.shape[2]
        for i in range(steps):
            da_ref[i] = da[:, i * W : (i + 1) * W]


def middle_back(t, x1, d2, at, norm, w_out, w_triple, deps=()):
    S, rows, wide = t.shape
    D = x1.shape[1]
    W = wide // 3
    return pl.pallas_call(
        functools.partial(back_kernel, steps=S),
        grid=(S,),
        out_shape=(
            jax.ShapeDtypeStruct((rows, D), f32),
            jax.ShapeDtypeStruct((rows, D), bf16),
            jax.ShapeDtypeStruct((S, rows, W), bf16),
            jax.ShapeDtypeStruct((2, D), f32),
        ),
        in_specs=[
            pl.BlockSpec((1, rows, wide), lambda i: (i, 0, 0)),
            once((rows, D)),
            once((rows, D), (at, 0)),
            once((2, D)),
            once(*w_out[1]),
            w_triple[1],
        ]
        + [AN] * len(deps),
        out_specs=(
            held((rows, D)),
            held((rows, D)),
            held((S, rows, W)),
            held((2, D)),
        ),
        scratch_shapes=[pltpu.VMEM((rows, D), f32)],
        compiler_params=pltpu.CompilerParams(vmem_limit_bytes=40 * 2**20),
        cost_estimate=BRIEF,
    )(t, x1, d2, norm, w_out[0], w_triple[0], *deps)


def grads_kernel(*refs, shape, widths):
    count = sum(shape)
    lefts, rights = refs[:count], refs[count : 2 * count]
    out_ref, turned = refs[-1 - count], refs[-count:]

    @pl.when(pl.program_id(0) == 0)
    def _():
        for left, t in zip(lefts, turned):
            t[...] = left[...].T

    at = n = 0
    for pieces, width in zip(shape, widths):
        total = 0.0
        for i in range(n, n + pieces):
            right = joined(rights[i]) if len(rights[i].shape) == 3 else rights[i][...]
            total += dot(turned[i][...], right, NN)
        out_ref[:, at : at + width] = total.astype(bf16)
        at, n = at + width, n + pieces


def weight_grads(terms, ranks, deps=()):
    pieces = [p for term in terms for p in term]
    shape = [len(term) for term in terms]
    widths = [term[0][1].size // term[0][0].shape[0] // ranks for term in terms]
    D, per = pieces[0][0].shape[1], sum(widths)
    lefts = [p[0] for p in pieces]
    rights = [p[1] for p in pieces]
    work = sum(p[0].shape[0] for p in pieces) * D * per * ranks // len(pieces)
    return pl.pallas_call(
        functools.partial(grads_kernel, shape=shape, widths=widths),
        grid=(ranks,),
        out_shape=jax.ShapeDtypeStruct((D, per * ranks), bf16),
        in_specs=[once(v.shape) for v in lefts]
        + [
            pl.BlockSpec((v.shape[0] // ranks,) + v.shape[1:], lambda i: (i, 0, 0))
            if v.ndim == 3
            else pl.BlockSpec((v.shape[0], v.shape[1] // ranks), lambda i: (0, i))
            for v in rights
        ]
        + [AN] * len(deps),
        out_specs=pl.BlockSpec((D, per), lambda i: (0, i)),
        scratch_shapes=[pltpu.VMEM(v.shape[::-1], bf16) for v in lefts],
        compiler_params=pltpu.CompilerParams(vmem_limit_bytes=56 * 2**20),
        cost_estimate=BRIEF,
    )(*lefts, *rights, *deps)


def start_kernel(at_ref, xa_ref, xb_ref, norm_ref, wk_ref, *refs, pieces, width):
    p_in, (q_ref, k_ref, n_ref, wq_ref, wkv_ref) = refs[:pieces], refs[-5:]
    seq = at_ref[0]
    R = xa_ref.shape[0]
    W = q_ref.shape[2]
    groups, per = wk_ref.shape[0], wq_ref.shape[0] // wk_ref.shape[0]
    size = wkv_ref.shape[0] // groups
    for i in range(groups):
        wq_ref[i * per : (i + 1) * per, :] = wk_ref[i, :per, :]
        kept = wk_ref.shape[1] - per
        wkv_ref[i * size : i * size + kept, :] = wk_ref[i, per:, :width]
        if kept < size:
            tall = size - kept
            tail = [wk_ref[i, at : at + tall, width:] for at in range(per, per + kept, tall)]
            wkv_ref[i * size + kept : (i + 1) * size, :] = jnp.concatenate(tail, axis=1)
    for block, x_ref in ((slice(0, R), xa_ref), (slice(R, n_ref.shape[0]), xb_ref)):
        n_ref[block, :] = layer_norm(x_ref[...].astype(f32), norm_ref[0:1, :], norm_ref[1:2, :])
    for i in range(pieces):
        q_ref[i] = dot(n_ref[...], wq_ref[i * W : (i + 1) * W, :], NT).astype(bf16)
    own = wkv_ref[pl.ds(pl.multiple_of(seq * 2 * W, 16), 2 * W), :]
    for i in range(pieces):
        k_ref[seq ^ i] = dot(p_in[i][...], own, NT).astype(bf16)


def start(at, x0, norm, lead, patch_pieces, W, deps):
    S, D = len(patch_pieces), x0[0].shape[1]
    total = x0[0].shape[0] + x0[1].shape[0]
    slots, width = patch_pieces[0].shape
    whole = [x0[0].shape, x0[1].shape, norm.shape]
    outs = [(S, total, W), (S, slots, 2 * W), (total, D), (D, D), (2 * D, width)]
    return pl.pallas_call(
        functools.partial(start_kernel, pieces=S, width=width),
        grid=(1,),
        out_shape=tuple(jax.ShapeDtypeStruct(v, bf16) for v in outs),
        in_specs=[SM]
        + [once(v) for v in whole]
        + [once(lead.shape)]
        + [once((slots, width))] * S
        + [AN] * len(deps),
        out_specs=tuple(held(v) for v in outs),
        compiler_params=pltpu.CompilerParams(vmem_limit_bytes=56 * 2**20),
        cost_estimate=BRIEF,
    )(at, *x0, norm, lead, *patch_pieces, *deps)


def finish_kernel(at_ref, a_ref, b_ref, *refs, pieces, rows):
    p_in, out_ref = refs[:pieces], refs[-1]
    seq = at_ref[0]
    W = a_ref.shape[2]
    slots = (a_ref.shape[1] - rows[0]) // 2
    sums = [0.0, 0.0]
    for i in range(pieces):
        for j, (ref, at) in enumerate(((a_ref, rows[0]), (b_ref, rows[1]))):
            p = p_in[i][j * slots : (j + 1) * slots, :]
            for k in range(2):
                sums[k] += dot(ref[seq ^ i, at + k * slots : at + (k + 1) * slots, :], p, TN)
    wide = sums[0].shape[1] // pieces
    for k in range(2):
        grad = sums[k].T.astype(bf16)
        for i in range(pieces):
            out_ref[i, k * wide : (k + 1) * wide, :] = grad[i * wide : (i + 1) * wide, :]


def finish(at, cross, rows, patch_pieces, deps):
    S, _, W = cross[0].shape
    out = (S, 2 * patch_pieces[0].shape[1] // S, W)
    return pl.pallas_call(
        functools.partial(finish_kernel, pieces=S, rows=rows),
        out_shape=jax.ShapeDtypeStruct(out, bf16),
        in_specs=[SM] + [VM] * (2 + S) + [AN] * len(deps),
        out_specs=VM,
        compiler_params=pltpu.CompilerParams(vmem_limit_bytes=32 * 2**20),
        cost_estimate=BRIEF,
    )(at, *cross, *patch_pieces, *deps)


def pack_lanes(ref, at, value):
    rows = value.shape[0]
    for i in range(value.shape[1] // LANES):
        ref[at + i * rows : at + (i + 1) * rows, :] = value[:, i * LANES : (i + 1) * LANES]


def unpack_lanes(ref, at, rows, columns):
    parts = [ref[at + i * rows : at + (i + 1) * rows, :] for i in range(columns // LANES)]
    return jnp.concatenate(parts, axis=1)


def end_kernel(
    at_ref, g_ref, wq_ref, wkv_ref, x_ref, n_ref, d_ref, gain_ref, *refs, blocks, more, n_dep
):
    extra, refs = refs[:more], refs[more + n_dep :]
    outs, refs = refs[:blocks], refs[blocks:]
    if more:
        part_ref, refs = refs[0], refs[1:]
    outs_more, (n_t, dq, total) = refs[:-3], refs[-3:]
    S, _, W = g_ref.shape
    rows = x_ref.shape[0]
    slots = (g_ref.shape[1] - rows) // 2
    own = rows // blocks
    dq[...] = jnp.concatenate([g_ref[i, :rows, :] for i in range(S)], axis=1)
    n_t[...] = n_ref[...].T
    grad, gain, shift = norm_back(
        x_ref[...].astype(f32), gain_ref[...], dot(dq[...], wq_ref[...], NN)
    )
    total[...] = d_ref[...] + grad
    place = at_ref[1] // 2 if more else at_ref[1]
    keys = []
    for i in range(S):
        keys += [g_ref[i, rows : rows + slots, :], g_ref[i, rows + slots :, :]]
    part = dot(jnp.concatenate(keys, axis=1), wkv_ref[...], NN).astype(bf16)
    for i in range(blocks):
        block = total[pl.ds(pl.multiple_of((place ^ i) * own, 8), own), :].astype(bf16)
        if more:
            outs[i][...] = block
        else:
            pack_lanes(outs[i], 0, block)
            pack_lanes(outs[i], own * block.shape[1] // LANES, part)
    if more:
        part_ref[...] = part
    lift = jnp.concatenate([gain, shift], axis=0)
    tall = n_t.shape[0] // S
    for i in range(0, S, 2):
        pair = dot(n_t[...], dq[:, i * W : (i + 2) * W], NN)
        if more:
            pair += extra[0][i // 2]
            for j in range(S):
                block = pair[j * tall : (j + 1) * tall, :].astype(bf16)
                outs_more[0][j, i * tall : (i + 1) * tall, :] = block[:, :W]
                outs_more[0][j, (i + 1) * tall : (i + 2) * tall, :] = block[:, W:]
        else:
            outs_more[0][i // 2] = pair
    if not more:
        outs_more[1][...] = lift
        return
    at = S * tall
    heads = extra[3].shape[1]
    zero = jnp.zeros((2, n_t.shape[0]), f32)
    sums = jnp.concatenate([lift + extra[1][...], extra[2][...], zero], axis=0)
    hi = sums.astype(bf16).astype(f32)
    both = jnp.concatenate([hi, sums - hi], axis=0).astype(bf16)
    for j in range(S):
        outs_more[0][j, at : at + heads, :] = extra[3][j]
        outs_more[0][j, at + heads :, :] = both[:, j * W : (j + 1) * W]


def end(at, got, place, w_query, w_kv, x0, n1, d1, gain, blocks, deps, more=()):
    S, _, W = got.shape
    rows, D = x0.shape
    slots, width = (got.shape[1] - rows) // 2, w_kv.shape[1]
    own = rows // blocks
    if more:
        outs = [((own, D), bf16)] * blocks + [((slots, width), bf16)]
        outs += [((S, D + more[3].shape[1] + 16, W), bf16)]
    else:
        outs = [(((own * D + slots * width) // LANES, LANES), bf16)] * blocks
        outs += [((S // 2, D, 2 * W), f32), ((2, D), f32)]
    whole = [got, w_query, w_kv, x0, n1, d1, gain, *more]
    specs = [once(v.shape) for v in whole]
    specs[4] = once((rows, D), (place, 0))
    return pl.pallas_call(
        functools.partial(end_kernel, blocks=blocks, more=len(more), n_dep=len(deps)),
        grid=(1,),
        out_shape=tuple(jax.ShapeDtypeStruct(*v) for v in outs),
        in_specs=[SM] + specs + [AN] * len(deps),
        out_specs=tuple(held(v[0]) for v in outs),
        scratch_shapes=[
            pltpu.VMEM((D, rows), bf16),
            pltpu.VMEM((rows, D), bf16),
            pltpu.VMEM((rows, D), f32),
        ],
        compiler_params=pltpu.CompilerParams(vmem_limit_bytes=56 * 2**20),
        cost_estimate=BRIEF,
    )(at, *whole, *deps)


def mix_kernel(at_ref, x_ref, *refs, heads, ranks):
    outs = refs[-ranks:]
    S, rows, W = x_ref.shape
    blocks = rows - heads - 16
    pair = blocks // len(outs)
    small = sum(x_ref[j, blocks + heads :, :].astype(f32) for j in range(S))
    total = small[:8] + small[8:]
    hi = total.astype(bf16).astype(f32)
    for i in range(len(outs)):
        rank = at_ref[1] ^ i
        src = pl.ds(pl.multiple_of(rank * pair, 16), pair)
        outs[i][:pair, :] = sum(x_ref[j, src, :].astype(f32) for j in range(S)).astype(bf16)
        for k in range(2):
            outs[i][pair + k * heads : pair + (k + 1) * heads, :] = x_ref[
                2 * rank + k, blocks : blocks + heads, :
            ]
        outs[i][pair + 2 * heads :, :] = jnp.concatenate([hi, total - hi], axis=0).astype(bf16)


def mix(at, got, ranks, heads, deps):
    S, rows, W = got.shape
    shape = ((rows - heads - 16) // ranks + 2 * heads + 16, W)
    return pl.pallas_call(
        functools.partial(mix_kernel, heads=heads, ranks=ranks),
        out_shape=(jax.ShapeDtypeStruct(shape, bf16),) * ranks,
        in_specs=[SM, VM] + [AN] * len(deps),
        out_specs=(VM,) * ranks,
        compiler_params=pltpu.CompilerParams(vmem_limit_bytes=24 * 2**20),
        cost_estimate=BRIEF,
    )(at, got, *deps)


def last_kernel(*refs, heads):
    ins, (q_ref, k_ref, v_ref, small_ref) = refs[:-4], refs[-4:]
    total = sum(v[...].astype(f32) for v in ins)
    pair = total.shape[0] - 2 * heads - 16
    q_ref[...] = jnp.concatenate([total[: pair // 2], total[pair // 2 : pair]], axis=1)
    one, two = total[pair : pair + heads], total[pair + heads : pair + 2 * heads]
    k_ref[...] = jnp.concatenate([one[: heads // 2], two[: heads // 2]], axis=1)
    v_ref[...] = jnp.concatenate([one[heads // 2 :], two[heads // 2 :]], axis=1)
    small_ref[...] = total[pair + 2 * heads : pair + 2 * heads + 8] + total[pair + 2 * heads + 8 :]


def last(parts, heads):
    rows, W = parts[0].shape
    pair = rows - 2 * heads - 16
    outs = [(pair // 2, 2 * W), (heads // 2, 2 * W), (heads // 2, 2 * W), (8, W)]
    return pl.pallas_call(
        functools.partial(last_kernel, heads=heads),
        out_shape=tuple(jax.ShapeDtypeStruct(v, f32) for v in outs),
        in_specs=[VM] * len(parts),
        out_specs=(VM,) * 4,
        compiler_params=pltpu.CompilerParams(vmem_limit_bytes=24 * 2**20),
        cost_estimate=BRIEF,
    )(*parts)


def place_kernel(at_ref, *refs, ranks, packed):
    whole, halves, out_ref = refs[:ranks], refs[ranks : ranks + ranks // 2], refs[-1]
    _, own, D = out_ref.shape
    for i in range(ranks):
        src = at_ref[1] ^ i
        block = unpack_lanes(whole[i], 0, own, D) if packed else whole[i][...]
        out_ref[3 * (src // 2) + 2 * (src % 2)] = block.astype(out_ref.dtype)
    for i in range(ranks // 2):
        src = at_ref[1] % (ranks // 2) ^ i
        out_ref[3 * src + 1] = halves[i][...].astype(out_ref.dtype)


def place_rows(at, whole, halves, kind, deps=(), packed=False):
    ranks = len(whole)
    shape = (3 * ranks // 2,) + halves[0].shape
    return pl.pallas_call(
        functools.partial(place_kernel, ranks=ranks, packed=packed),
        out_shape=jax.ShapeDtypeStruct(shape, kind),
        in_specs=[SM] + [VM] * (ranks + ranks // 2) + [AN] * len(deps),
        out_specs=VM,
        compiler_params=pltpu.CompilerParams(vmem_limit_bytes=24 * 2**20),
        cost_estimate=BRIEF,
    )(at, *whole, *halves, *deps)


def patches_kernel(at_ref, *refs):
    ins, out_ref = refs[:-1], refs[-1]
    ranks = len(ins) // 2
    _, slots, width = out_ref.shape
    at = ins[0].shape[0] - slots * width // LANES
    for i in range(ranks // 2):
        out_ref[3 * i + 1] = jnp.zeros(out_ref.shape[1:], f32)
    for i in range(ranks):
        src = at_ref[1] ^ i
        block = unpack_lanes(ins[i], at, slots, width)
        out_ref[3 * (src // 2) + 2 * (src % 2)] = block.astype(f32)
        out_ref[3 * (src // 2) + 1] += ins[ranks + i][...].astype(f32)


def place_patches(at, parts_a, parts_b):
    shape = (3 * len(parts_a) // 2,) + parts_b[0].shape
    return pl.pallas_call(
        patches_kernel,
        out_shape=jax.ShapeDtypeStruct(shape, f32),
        in_specs=[SM] + [VM] * (2 * len(parts_a)),
        out_specs=VM,
        compiler_params=pltpu.CompilerParams(vmem_limit_bytes=24 * 2**20),
        cost_estimate=BRIEF,
    )(at, *parts_a, *parts_b)


CP = 32


def place(perm, toks, TR, TC):
    own, ext = TR * TC, perm.shape[2]
    tok = lax.broadcasted_iota(jnp.int32, (toks, 1), 0)
    row = jnp.where(tok < own, tok // TC, jnp.where(tok < own + TR, tok - own, TR))
    col = jnp.where(
        tok < own, tok % TC, jnp.where(tok < own + TR, TC, tok - own - TR)
    )
    real = tok <= own + TR + TC
    pixel = lax.broadcasted_iota(jnp.int32, (toks, ext), 1)
    for a in range(2):
        for b in range(2):
            ok = real & ((row < TR) | (a == 0)) & ((col < TC) | (b == 0))
            at = jnp.where(ok, (2 * row + a) * (2 * TC + 1) + 2 * col + b, -1)
            perm[2 * a + b] = jnp.where(pixel == at, 1.0, 0.0).astype(bf16)


def pixel_grad_kernel(cot_ref, w_ref, *refs, TR, TC):
    out_ref, perm = refs[-2:]

    @pl.when(pl.program_id(0) == 0)
    def _():
        place(perm, out_ref.shape[1], TR, TC)

    grad = dot(cot_ref[0], w_ref[0], NT)
    hi = grad.astype(bf16)
    lo = (grad - hi.astype(f32)).astype(bf16)
    parts = [dot(perm[i], hi, NT) + dot(perm[i], lo, NT) for i in range(4)]
    out_ref[0] = jnp.concatenate(parts, axis=1)


def pixel_sample_kernel(x_ref, w_ref, *refs, TR, TC):
    out_ref, perm = refs[-2:]

    @pl.when(pl.program_id(0) == 0)
    def _():
        place(perm, x_ref.shape[1], TR, TC)

    x = x_ref[0]
    window = sum(dot(x[:, i * CP : (i + 1) * CP], perm[i], TN) for i in range(4))
    out_ref[0] = dot(window.astype(bf16), w_ref[0], NN).astype(bf16)


def per_plane(body, first, weights, out_rows, out_lanes, out_type, toks, TR, TC, deps=()):
    planes, ext, samples = weights.shape

    def whole(shape):
        return pl.BlockSpec((1,) + shape, lambda i: (i, 0, 0))

    return pl.pallas_call(
        functools.partial(body, TR=TR, TC=TC),
        grid=(planes,),
        out_shape=jax.ShapeDtypeStruct((planes, out_rows, out_lanes), out_type),
        in_specs=[whole(first.shape[1:]), whole((ext, samples))] + [AN] * len(deps),
        out_specs=whole((out_rows, out_lanes)),
        scratch_shapes=[pltpu.VMEM((4, toks, ext), bf16)],
        compiler_params=pltpu.CompilerParams(vmem_limit_bytes=24 * 2**20),
        cost_estimate=BRIEF,
    )(first, weights, *deps)


def swap_seq(value):
    return lax.all_to_all(value, "seq", split_axis=0, concat_axis=0, tiled=True)


def swap_mp(value):
    return lax.all_to_all(value, "mp", split_axis=0, concat_axis=0, tiled=True)


def swap_all(value):
    return lax.all_to_all(value, ("seq", "mp"), split_axis=0, concat_axis=0, tiled=True)


def swap_pair(value):
    count = lax.axis_size("mp")
    return lax.ppermute(value, "mp", [(i, i ^ 1) for i in range(count)])


def gather_rows(piece):
    return lax.all_gather(piece, ("mp", "seq"), axis=0, tiled=False)


def bundle_part(bundle, at, rows):
    pieces, _, D = bundle.shape
    if rows % 16 == 0 and at % rows == 0:
        return bundle, ((pieces, rows, D), (0, at // rows, 0))
    value = bundle[:, at : at + rows].reshape(1, -1, D)
    return value, (value.shape, None)


def by_step(part, steps):
    (pieces, rows, D), at = part[1]
    if pieces > 1:
        return part[0], pl.BlockSpec((pieces // steps, rows, D), lambda i: (i, at[1], 0))
    return part[0], pl.BlockSpec((1, rows // steps, D), lambda i: (0, i, 0))


def reduce_rows(value):
    return lax.psum_scatter(value, "seq", scatter_dimension=0, tiled=True)


def to_ranks(blocks):
    moves = [[(i, i ^ step) for i in range(len(blocks))] for step in range(len(blocks))]
    return [v if i == 0 else lax.ppermute(v, "mp", moves[i]) for i, v in enumerate(blocks)]


def to_halves(blocks):
    pairs = len(blocks)
    arrived = []
    for step in range(pairs):
        moves = [(2 * p + h, pairs * h + (p ^ step)) for p in range(pairs) for h in range(2)]
        arrived.append(lax.ppermute(blocks[step], "mp", moves))
    return arrived


def sum_ranks(value):
    return lax.psum_scatter(value, "mp", scatter_dimension=1, tiled=True).astype(f32)


def gather_pieces(value):
    shares = lax.axis_size("seq")
    pieces = []
    for step in range(0, shares, 2):
        moves = [(i, i ^ step) for i in range(shares)]
        pieces.append(value if step == 0 else lax.ppermute(value, "seq", moves))
    cores = [(i, i ^ 1) for i in range(shares)]
    return [p for piece in pieces for p in (piece, lax.ppermute(piece, "seq", cores))]


def per_device(
    tokens,
    patches,
    counts,
    norm_gains,
    norm_shifts,
    cross_query,
    cross_kv,
    cross_out,
    self_qkv,
    self_out,
    mlp_up,
    mlp_down,
    decoder,
    sample_weights,
    tokens_cot,
    sample_cot,
):
    objects, R, D = tokens.shape
    S, M = lax.axis_size("seq"), lax.axis_size("mp")
    s, m = lax.axis_index("seq"), lax.axis_index("mp")
    pairs = M // 2
    if objects != 3 * pairs or S != 2 * M or D % (HD * S) != 0:
        raise ValueError("unexpected sizes")
    pair, half = m // 2, m % 2
    at_a, at_b = 3 * pair + 2 * half, 3 * pair + 1
    RB = R // 2
    RS = R + RB
    rows = [R, RB]
    W = D // S
    hpd = W // HD
    slots, width = patches.shape[1], patches.shape[2]
    slot_total = slots * S
    row_total = R * S

    def pick(arr):
        whole = lax.dynamic_index_in_dim(arr, at_b, 0, keepdims=False)
        return [
            lax.dynamic_index_in_dim(arr, at_a, 0, keepdims=False),
            lax.dynamic_slice_in_dim(whole, half * RB, RB, 0),
        ]

    def mine(arr, axis):
        share = arr.shape[axis] // S
        return lax.dynamic_slice_in_dim(arr, s * share, share, axis)

    channels = decoder.shape[1]
    local_dec = jnp.pad(decoder.transpose(2, 1, 0), ((0, 0), (0, CP - channels), (0, 0)))
    part = S // 2
    qkv_piece = lax.dynamic_slice_in_dim(self_qkv, s // part * W, W, 2).reshape(D, 3 * W)
    qkv_piece = lax.dynamic_slice_in_dim(qkv_piece, s % part * (3 * W // part), 3 * W // part, 1)
    per = D // (S * M)
    dec_rows = 4 * CP // S
    kv_rows = 2 * per
    at = s * kv_rows
    kv_piece = lax.dynamic_slice(
        cross_kv, (0, (at // W) % 2, at // (2 * W) * W + at % W), (width, 1, kv_rows)
    )
    kv_piece = kv_piece[:, 0].T
    tail_rows = kv_rows - kv_rows * width // D
    if (kv_rows - tail_rows) % tail_rows == 0 and tail_rows % 16 == 0 and width % 128 == 0:
        folds = (kv_rows - tail_rows) // tail_rows
        tail = jnp.split(kv_piece[-tail_rows:], folds, axis=1)
        kv_piece = jnp.concatenate([kv_piece[:-tail_rows], jnp.concatenate(tail)], axis=1)
    else:
        kv_piece = jnp.pad(kv_piece, ((0, 0), (0, D - width)))
    kv_rows = kv_piece.shape[0]
    lead = [mine(cross_query, 1).T, kv_piece]
    lead = gather_rows(jnp.concatenate(lead, axis=0))
    first = gather_rows(
        jnp.concatenate(
            [qkv_piece.T, mine(cross_out, 0)], axis=0
        )
    )
    up_rows = mlp_up.shape[1] // S
    second = gather_rows(
        jnp.concatenate(
            [
                mine(mlp_up, 1).T,
                mine(mlp_down, 0),
                mine(self_out, 0),
                mine(local_dec.reshape(-1, D), 0),
            ],
            axis=0,
        )
    )
    steps = 8
    w_up = by_step(bundle_part(second, 0, up_rows), steps)
    w_down = by_step(bundle_part(second, up_rows, up_rows), steps)
    w_triple = by_step(bundle_part(first, 0, 3 * per), S)
    w_cross_out = bundle_part(first, 3 * per, per)
    w_self_out = bundle_part(second, 2 * up_rows, per)
    w_dec = bundle_part(second, 2 * up_rows + per, dec_rows)

    x0 = pick(tokens)
    norms = [jnp.stack([norm_gains[i], norm_shifts[i]]) for i in range(3)]
    at = jnp.stack([s, m])
    both = [lax.dynamic_index_in_dim(patches, o, 0, keepdims=False) for o in (at_a, at_b)]
    patch_pieces = gather_pieces(jnp.concatenate(both, axis=0))
    TC = PLANE // 4
    TR = PLANE * 4 // S
    own, rim = TR * TC, TR * TC + TR
    toks = -(-(rim + TC + 1) // 32) * 32
    planes = objects * 3
    weights_in = sample_weights.reshape(planes, *sample_weights.shape[3:])
    cot_in = sample_cot.reshape(planes, channels, -1)
    cot_in = jnp.pad(cot_in, ((0, 0), (0, CP - channels), (0, 0)))
    ext = per_plane(pixel_grad_kernel, cot_in, weights_in, toks, 4 * CP, f32, toks, TR, TC)
    ways = {
        1: [i for i in range(S) if i % 4 != 3],
        4: [i for i in range(S) if i + 4 < S],
        5: [i for i in range(S) if i % 4 != 3 and i + 4 < S],
    }
    rights = lax.ppermute(ext[:, own:rim], "seq", [(i, i + 1) for i in ways[1]])
    belows = lax.ppermute(ext[:, rim : rim + TC], "seq", [(i, i + 4) for i in ways[4]])
    corner = lax.ppermute(ext[:, rim + TC : rim + TC + 1], "seq", [(i, i + 5) for i in ways[5]])
    grid = ext[:, :own].reshape(planes, TR, TC, -1)
    belows = jnp.concatenate([belows[:, :1] + corner, belows[:, 1:]], axis=1)
    grid = grid + jnp.pad(rights[:, :, None], ((0, 0), (0, 0), (0, TC - 1), (0, 0)))
    grid = grid + jnp.pad(belows[:, None], ((0, 0), (0, TR - 1), (0, 0), (0, 0)))
    KA, KB = R // S, RB // S
    cu = 4 * CP
    grad_pix = grid.astype(bf16).reshape(pairs, 3, S, KA, cu)
    gp_a = jnp.stack([grad_pix[:, 0], grad_pix[:, 2]], axis=1).transpose(2, 0, 1, 3, 4)
    gp_b = grad_pix[:, 1].reshape(pairs, S, 2, KB, cu).transpose(1, 0, 2, 3, 4)
    sent = jnp.concatenate([gp_a, gp_b], axis=3).reshape(S * M, KA + KB, cu)

    q1, keys_one, n1, w_query, w_kv = start(
        at, x0, norms[0], lead, patch_pieces, W, [sent]
    )
    heads_one = swap_seq(q1)
    back = swap_all(hold(sent, [heads_one]))
    d_pix = back.reshape(S, M, KA + KB, cu).transpose(2, 0, 1, 3).reshape(RS, M * cu)

    limits = [
        jnp.stack([lax.dynamic_index_in_dim(counts, o, 0, keepdims=False), jnp.int32(0)])
        for o in (at_a, at_b)
    ]
    kv_one = [(slots, (i * slots, 0), (i * slots, W), 0) for i in range(2)]
    o1, res1 = [], []
    for i in range(2):
        out, res = attend(
            limits[i],
            [heads_one, keys_one],
            S,
            (0, rows[i], i * R, 0),
            [(1,) + kv_one[i]],
            slot_total,
            hpd,
            False,
            [(back,), ()][i],
        )
        o1.append(out)
        res1.append(res)

    mids = [
        middle(swap_seq(o1[i].reshape(S, rows[i], W)), x0[i], norms[1], w_cross_out, w_triple)
        for i in range(2)
    ]
    x1, n2, a1, t2 = zip(*mids)

    heads_two = [swap_seq(v) for v in t2]
    pair_kv = swap_pair(heads_two[1][:, :, W:])
    wide = jnp.array([row_total, 0], jnp.int32)
    kv_a2 = (R, (0, W), (0, 2 * W), 0)
    kv_b2 = (RB, (0, W), (0, 2 * W), 0)
    kv_p2 = (RB, (0, 0), (0, W), row_total // 2)
    o_a2, res_a2 = attend(
        wide, [heads_two[0]], S, (0, R, 0, 0), [(0,) + kv_a2], row_total, hpd, True
    )
    o_b2, res_b2 = attend(
        wide,
        [heads_two[1], pair_kv],
        S,
        (0, RB, 0, 0),
        [(0,) + kv_b2, (1,) + kv_p2],
        row_total,
        hpd,
        True,
        [o_a2],
    )
    a2_a = swap_seq(o_a2.reshape(S, R, W))
    a2 = [a2_a, swap_seq(hold(o_b2.reshape(S, RB, W), [a2_a]))]

    hidden = mlp_up.shape[1] * M
    n3, a2, g, du, x3b, pix, e3, d2, e2, da2, sums_three = feed_forward(
        a2,
        x1,
        pick(tokens_cot),
        d_pix,
        norms[2],
        w_self_out,
        w_dec,
        w_up,
        w_down,
        hidden,
        steps,
    )

    da2 = swap_seq(da2)
    grads_one = weight_grads([[(n3, du)], [(e3, g)], [(e2, a2)], [(x3b, d_pix)]], M)
    grads_one = hold(grads_one, [da2])
    pix = hold(pix, [grads_one])
    dt2_a = attend_back(
        wide,
        [res_a2, da2, o_a2, heads_two[0]],
        S,
        (R, 0),
        [(3,) + kv_a2],
        row_total,
        hpd,
        True,
        [grads_one],
        "lanes",
    )
    grads_one = reduce_rows(grads_one)
    pix = pix.reshape(KA + KB, S, M, cu).transpose(1, 2, 0, 3)
    got = swap_all(pix.reshape(S * M, KA + KB, cu)).reshape(S, pairs, 2, KA + KB, cu)
    half_total = row_total // 2
    kv_p2 = (RB, (0, 0), (0, W), 0)
    dq_p2, dkv_p2 = attend_back(
        wide,
        [res_b2, da2, o_b2, pair_kv],
        S,
        (RB, R),
        [(3,) + kv_p2],
        half_total,
        hpd,
        True,
        [dt2_a, got],
    )
    given = swap_pair(dkv_p2)
    dq_b2, dkv_b2 = attend_back(
        wide,
        [res_b2, da2, o_b2, heads_two[1]],
        S,
        (RB, R),
        [(3,) + kv_b2],
        half_total,
        hpd,
        True,
        [dq_p2],
    )
    dq_b2 = (dq_b2.astype(f32) + dq_p2.astype(f32)).astype(bf16)
    dkv_b2 = (dkv_b2.astype(f32) + given.astype(f32)).astype(bf16)
    dt2 = [
        swap_seq(dt2_a),
        jnp.concatenate([dq_b2, dkv_b2], axis=1).reshape(S, RB, 3 * W),
    ]

    def below(i, deps):
        return middle_back(
            dt2[i], x1[i], d2, (0, R // RB)[i], norms[1], w_cross_out, w_triple, deps
        )

    def cross_back(i, da1, deps):
        return attend_back(
            limits[i],
            [res1[i], da1, o1[i], keys_one],
            S,
            (rows[i], 0),
            [(3,) + kv_one[i]],
            slot_total,
            hpd,
            False,
            deps,
            "rows",
        )

    low_a = below(0, [dq_b2, given])
    x3b = hold(x3b, [low_a[0]])
    blocks_a, blocks_b = x3b[:R].reshape(M, R // M, D), x3b[R:].reshape(pairs, R // M, D)
    blocks_a = [lax.dynamic_index_in_dim(blocks_a, m ^ i, 0, keepdims=False) for i in range(M)]
    blocks_b = [
        lax.dynamic_index_in_dim(blocks_b, pair ^ i, 0, keepdims=False) for i in range(pairs)
    ]
    blocks_a, blocks_b = to_ranks(blocks_a), to_halves(blocks_b)
    da1_a = swap_seq(low_a[2])
    dt2[1] = swap_seq(hold(dt2[1], [da1_a]))
    cross_a = cross_back(0, da1_a, [])
    grads_one = sum_ranks(hold(grads_one, [da1_a]))
    low_b = below(1, [cross_a])
    got_a = swap_seq(cross_a)
    da1_b = swap_seq(hold(low_b[2], [got_a]))
    d1, e1, da1, sums_two = zip(low_a, low_b)

    grads_two = weight_grads(
        [[(n2[i], dt2[i]) for i in range(2)], [(e1[i], a1[i]) for i in range(2)]], M, [grads_one, got_a] + blocks_a + blocks_b
    )
    *sent_a, share, lift = end(
        at, got_a, 0, w_query, w_kv, x0[0], n1, d1[0], norm_gains[:1], M, [grads_two]
    )
    cross_b = cross_back(1, da1_b, [grads_two, lift])
    grads_two = reduce_rows(grads_two)
    got_b = swap_seq(cross_b)

    two = sums_two[0] + sums_two[1]
    small = jnp.concatenate([two, sums_three], axis=0)
    px_a = got[:, :, :, :KA].transpose(1, 2, 0, 3, 4).reshape(pairs, 2, S * KA, cu)
    px_b = got[:, :, :, KA:].transpose(1, 0, 2, 3, 4).reshape(pairs, S * KA, cu)
    tile = jnp.stack([px_a[:, 0], px_b, px_a[:, 1]], axis=1).reshape(planes, TR, TC, cu)
    rights = lax.ppermute(tile[:, :, 0], "seq", [(i + 1, i) for i in ways[1]])
    belows = lax.ppermute(tile[:, 0], "seq", [(i + 4, i) for i in ways[4]])
    corner = lax.ppermute(tile[:, 0, :1], "seq", [(i + 5, i) for i in ways[5]])
    fill = jnp.zeros((planes, toks - rim - TC - 1, cu), bf16)
    ext = jnp.concatenate([tile.reshape(planes, own, cu), rights, belows, corner, fill], axis=1)
    sent_a = to_ranks(sent_a)
    by_head = finish(at, [cross_a, cross_b], rows, patch_pieces, [*sent_a, ext])
    heads = by_head.shape[1]
    *sent_b, part_b, final = end(
        at,
        got_b,
        R // RB,
        w_query,
        w_kv,
        x0[1],
        n1,
        d1[1],
        norm_gains[:1],
        pairs,
        [],
        [share, lift, small, by_head],
    )
    got_last = swap_seq(final)
    grad_tokens = place_rows(at, sent_a, to_halves(sent_b), f32, [], True)
    patch_grad = place_patches(at, sent_a, to_ranks([part_b] * M))
    ext = hold(ext, [final])
    tokens_out = place_rows(at, blocks_a, blocks_b, bf16, [final])
    sampled = per_plane(
        pixel_sample_kernel, ext, weights_in, CP, weights_in.shape[2], bf16, toks, TR, TC
    )
    sampled = sampled[:, :channels].reshape(objects, 3, channels, 1, -1)

    final = last(to_ranks(mix(at, got_last, M, heads, [sampled, tokens_out])), heads)
    grad_cross_query, grad_keys, grad_values, small = final
    grad_cross_kv = jnp.stack([grad_keys, grad_values], axis=1)

    grads_two = sum_ranks(grads_two)
    ff = hidden // M
    grad_mlp_up, grad_mlp_down = grads_one[:, :ff], grads_one[:, ff : 2 * ff].T
    grad_self_out = grads_one[:, 2 * ff : 2 * ff + D // M].T
    grad_decoder = grads_one[:, 2 * ff + D // M :]
    grad_decoder = grad_decoder.reshape(D // S, 4, CP)[:, :, :channels].transpose(0, 2, 1)
    grad_self_qkv = grads_two[:, : 3 * D // M].reshape(D // S, 2, 3, W).transpose(0, 2, 1, 3)
    grad_cross_out = grads_two[:, 3 * D // M :].T

    return (
        tokens_out,
        sampled,
        grad_tokens,
        patch_grad,
        jnp.stack([small[0], small[2], small[4]]),
        jnp.stack([small[1], small[3]]),
        small[5],
        grad_cross_query,
        grad_cross_kv,
        grad_cross_out,
        grad_self_qkv.reshape(D // S, 3, -1),
        grad_self_out,
        grad_mlp_up,
        grad_mlp_down,
        grad_decoder,
    )


def solution(mesh):
    return jax.shard_map(
        per_device,
        mesh=mesh,
        in_specs=(
            P(None, "seq", None),
            P(None, "seq", None),
            P(),
            P(),
            P(),
            P(None, "mp"),
            P(None, None, "mp"),
            P("mp", None),
            P(None, None, "mp"),
            P("mp", None),
            P(None, "mp"),
            P("mp", None),
            P(None, "mp", None),
            P(None, None, "seq", None, None),
            P(None, "seq", None),
            P(None, None, "mp", "seq", None),
        ),
        out_specs=(
            P(None, ("seq", "mp"), None),
            P(None, None, "mp", "seq", None),
            P(None, ("seq", "mp"), None),
            P(None, "seq", None),
            P(None, "seq"),
            P(None, "seq"),
            P("seq"),
            P("seq", "mp"),
            P("seq", None, "mp"),
            P("mp", "seq"),
            P("seq", None, "mp"),
            P("mp", "seq"),
            P("seq", "mp"),
            P("mp", "seq"),
            P("seq", "mp", None),
        ),
        check_vma=False,
    )
```

```python
import functools
import math

import jax
import jax.numpy as jnp
from jax import lax
from jax.experimental import pallas as pl
from jax.experimental.pallas import tpu as pltpu
from jax.sharding import PartitionSpec as P


PLANE = 32
HD = 64
LANES = 128
norm_eps = 1e-05
f32 = jnp.float32
bf16 = jnp.bfloat16

NT = (((1,), (1,)), ((), ()))
NN = (((1,), (0,)), ((), ()))
TN = (((0,), (0,)), ((), ()))


def dot(a, b, dims):
    return lax.dot_general(a, b, dims, preferred_element_type=f32)


def mm(a, b):
    return jnp.dot(a, b, preferred_element_type=f32)


def split3(v):
    hi = v.astype(bf16).astype(f32)
    rest = v - hi
    mid = rest.astype(bf16).astype(f32)
    return hi, mid, rest - mid


def spread(base, cols):
    lane = lax.broadcasted_iota(jnp.int32, (base.shape[0], HD), 1)
    tail = jnp.zeros((base.shape[0], HD), f32)
    for at, col in cols.items():
        tail = jnp.where(lane == at, col, tail)
    return jnp.concatenate([base, tail], axis=1).astype(bf16)


def load_keys(n_ref, kv_specs, refs, ka, va, hpd, blocks):
    for ref_at, rows, k_at, v_at, base in kv_specs:
        src = refs[ref_at]

        def build(i, _):
            natural = base + (i ^ n_ref[1]) * rows
            dst = pl.ds(pl.multiple_of(natural, 16), rows)
            slot = natural + lax.broadcasted_iota(jnp.int32, (rows, 1), 0)
            mask = jnp.where(slot < n_ref[0], 0.0, -1e30).astype(f32)
            for h in range(hpd):
                k = src[i, k_at[0] : k_at[0] + rows, k_at[1] + h * HD : k_at[1] + (h + 1) * HD]
                v = src[i, v_at[0] : v_at[0] + rows, v_at[1] + h * HD : v_at[1] + (h + 1) * HD]
                ka[h, dst, :] = spread(k.astype(f32), {0: 1.0, 1: 1.0, 2: 1.0, 3: mask})
                va[h, dst, :] = spread(v.astype(f32), {0: 1.0, 1: 1.0, 2: 1.0})
            return 0

        lax.fori_loop(0, blocks, build, 0)


def fwd_kernel(n_ref, *refs, n_in, blocks, q_spec, kv_specs, hpd, bq, kc, fixed):
    ins, (o_ref, qa_ref, ka, va) = refs[:n_in], refs[-4:]
    load_keys(n_ref, kv_specs, ins, ka, va, hpd, blocks)
    q_at, rows_q, q_off, q_lane = q_spec

    def build(i, _):
        dst = pl.ds(pl.multiple_of((i ^ n_ref[1]) * rows_q, 16), rows_q)
        for h in range(hpd):
            q = ins[q_at][i, q_off : q_off + rows_q, q_lane + h * HD : q_lane + (h + 1) * HD]
            qa_ref[h, dst, :] = spread(q.astype(f32) * (1.0 / math.sqrt(HD)), {3: 1.0})
        return 0

    lax.fori_loop(0, blocks, build, 0)
    total = ka.shape[1]

    def block(b, _):
        rows = pl.ds(pl.multiple_of(b * bq, bq), bq)

        def chunk(c, carry):
            cols = pl.ds(pl.multiple_of(c * kc, kc), kc)
            out = []
            for h in range(hpd):
                m, acc = carry[h]
                s = dot(qa_ref[h, rows, :], ka[h, cols, :], NT)
                top = jnp.maximum(m, jnp.max(s, axis=1, keepdims=True))
                p = jnp.exp(s - top).astype(bf16)
                out.append((top, acc * jnp.exp(m - top) + dot(p, va[h, cols, :], NN)))
            return tuple(out)

        carry = ((jnp.full((bq, 1), -1e30, f32), jnp.zeros((bq, LANES), f32)),) * hpd
        if fixed:
            for c in range(total // kc):
                carry = chunk(c, carry)
        else:
            carry = lax.fori_loop(0, (n_ref[0] + kc - 1) // kc, chunk, carry)
        outs = []
        for h in range(hpd):
            m, acc = carry[h]
            norm = acc[:, HD : HD + 1]
            outs.append(acc[:, :HD] / norm)
            hi, mid, lo = split3(-(m + jnp.log(norm)))
            qa_ref[h, rows, :] = spread(
                qa_ref[h, rows, :HD].astype(f32), {0: hi, 1: mid, 2: lo, 3: 1.0}
            )
        o_ref[rows, :] = jnp.concatenate(outs, axis=1).astype(bf16)
        return 0

    lax.fori_loop(0, qa_ref.shape[1] // bq, block, 0)


def bwd_kernel(n_ref, *refs, n_in, n_dep, blocks, do_spec, kv_specs, hpd, bq, kc, fixed, form):
    ins, (*outs, ka, va, da, dk, dv, dq) = refs[:n_in], refs[n_in + n_dep :]
    qa_ref, do_ref, o_ref = ins[:3]
    load_keys(n_ref, kv_specs, ins, ka, va, hpd, blocks)
    rows_q, do_off = do_spec

    def build(i, _):
        rows = pl.ds(pl.multiple_of(i * rows_q, 16), rows_q)
        for h in range(hpd):
            d = do_ref[i, do_off : do_off + rows_q, h * HD : (h + 1) * HD].astype(f32)
            o = o_ref[rows, h * HD : (h + 1) * HD].astype(f32)
            hi, mid, lo = split3(-jnp.sum(d * o, axis=1, keepdims=True))
            da[h, rows, :] = spread(d, {0: hi, 1: mid, 2: lo})
        return 0

    lax.fori_loop(0, blocks, build, 0)
    dk[...] = jnp.zeros_like(dk)
    dv[...] = jnp.zeros_like(dv)
    total = ka.shape[1]
    steps = total // kc if fixed else (n_ref[0] + kc - 1) // kc

    def block(b, _):
        rows = pl.ds(pl.multiple_of(b * bq, bq), bq)

        def chunk(c, dqs):
            cols = pl.ds(pl.multiple_of(c * kc, kc), kc)
            out = []
            for h in range(hpd):
                k, q, d = ka[h, cols, :], qa_ref[h, rows, :], da[h, rows, :]
                p = jnp.exp(dot(k, q, NT))
                dp = dot(va[h, cols, :], d, NT)
                dv[h, cols, :] += dot(p.astype(bf16), d, NN)
                g = (p * dp).astype(bf16)
                dk[h, cols, :] += dot(g, q, NN)
                out.append(dqs[h] + dot(k, g, TN))
            return tuple(out)

        dqs = lax.fori_loop(0, steps, chunk, (jnp.zeros((LANES, bq), f32),) * hpd)
        grad = jnp.concatenate([v[:HD, :] for v in dqs], axis=0).T
        dq[rows, :] = (grad * (1.0 / math.sqrt(HD))).astype(bf16)
        return 0

    lax.fori_loop(0, qa_ref.shape[1] // bq, block, 0)
    step = total // blocks

    def finish(i, _):
        rows = pl.ds(pl.multiple_of(i * step, 16), step)
        q_rows = pl.ds(pl.multiple_of(i * rows_q, 16), rows_q)
        k, v = [
            jnp.concatenate([d[h, rows, :HD] for h in range(hpd)], axis=1).astype(bf16)
            for d in (dk, dv)
        ]
        if form == "split":
            outs[0][q_rows, :] = dq[q_rows, :]
            outs[1][rows, :] = jnp.concatenate([k, v], axis=1)
        elif form == "lanes":
            outs[0][i] = jnp.concatenate([dq[q_rows, :], k, v], axis=1)
        else:
            outs[0][i, :rows_q, :] = dq[q_rows, :]
            outs[0][i, rows_q : rows_q + step, :] = k
            outs[0][i, rows_q + step :, :] = v
        return 0

    lax.fori_loop(0, blocks, finish, 0)


VM = pl.BlockSpec(memory_space=pltpu.VMEM)
SM = pl.BlockSpec(memory_space=pltpu.SMEM)
BRIEF = pl.CostEstimate(flops=10**6, bytes_accessed=10**5, transcendentals=0)
AN = pl.BlockSpec(memory_space=pl.ANY)


def fit(rows, most):
    return math.gcd(rows, most)


def attend(limits, ins, blocks, q_spec, kv_specs, total, hpd, fixed, deps=()):
    queries = blocks * q_spec[1]
    kc = fit(total, 1024 if fixed else 512)
    body = functools.partial(
        fwd_kernel,
        n_in=len(ins),
        blocks=blocks,
        q_spec=q_spec,
        kv_specs=kv_specs,
        hpd=hpd,
        bq=fit(queries, 512),
        kc=kc,
        fixed=fixed,
    )
    work = hpd * queries * total
    return pl.pallas_call(
        body,
        out_shape=(
            jax.ShapeDtypeStruct((queries, hpd * HD), bf16),
            jax.ShapeDtypeStruct((hpd, queries, LANES), bf16),
        ),
        in_specs=[SM] + [VM] * len(ins) + [AN] * len(deps),
        out_specs=(VM, VM),
        scratch_shapes=[pltpu.VMEM((hpd, total, LANES), bf16)] * 2,
        compiler_params=pltpu.CompilerParams(vmem_limit_bytes=44 * 2**20),
        cost_estimate=BRIEF,
    )(limits, *ins, *deps)


def attend_back(limits, ins, blocks, do_spec, kv_specs, total, hpd, fixed, deps=(), form="split"):
    queries = blocks * do_spec[0]
    W, step = hpd * HD, total // blocks
    shapes = {
        "split": [(queries, W), (total, 2 * W)],
        "lanes": [(blocks, step, 3 * W)],
        "rows": [(blocks, do_spec[0] + 2 * step, W)],
    }[form]
    body = functools.partial(
        bwd_kernel,
        n_in=len(ins),
        n_dep=len(deps),
        blocks=blocks,
        do_spec=do_spec,
        kv_specs=kv_specs,
        hpd=hpd,
        bq=fit(queries, 512),
        kc=fit(total, 1024 if fixed else 512),
        fixed=fixed,
        form=form,
    )
    out = pl.pallas_call(
        body,
        out_shape=tuple(jax.ShapeDtypeStruct(v, bf16) for v in shapes),
        in_specs=[SM] + [VM] * len(ins) + [AN] * len(deps),
        out_specs=(VM,) * len(shapes),
        scratch_shapes=[pltpu.VMEM((hpd, total, LANES), bf16)] * 2
        + [pltpu.VMEM((hpd, queries, LANES), bf16)]
        + [pltpu.VMEM((hpd, total, LANES), f32)] * 2
        + [pltpu.VMEM((queries, W), bf16)],
        compiler_params=pltpu.CompilerParams(vmem_limit_bytes=52 * 2**20),
        cost_estimate=BRIEF,
    )(limits, *ins, *deps)
    return out if len(out) > 1 else out[0]


def norm_parts(values):
    center = values - jnp.mean(values, axis=-1, keepdims=True)
    scale = lax.rsqrt(jnp.mean(center * center, axis=-1, keepdims=True) + norm_eps)
    return center * scale, scale


def layer_norm(values, gain_row, shift_row):
    return (norm_parts(values)[0] * gain_row + shift_row).astype(bf16)


def norm_back(values, gain_row, grad_out):
    unit, scale = norm_parts(values)
    lifted = grad_out * gain_row
    grad_in = scale * (
        lifted
        - jnp.mean(lifted, axis=-1, keepdims=True)
        - unit * jnp.mean(lifted * unit, axis=-1, keepdims=True)
    )
    gain = jnp.sum(grad_out * unit, axis=0, keepdims=True)
    return grad_in, gain, jnp.sum(grad_out, axis=0, keepdims=True)


def flat(ref):
    return ref[...].reshape(-1, ref.shape[-1])


def joined(ref):
    return jnp.concatenate([ref[i] for i in range(ref.shape[0])], axis=1)


def once(shape, index=None):
    at = (0,) * len(shape) if index is None else index
    return pl.BlockSpec(shape, lambda i: at, pipeline_mode=pl.Buffered(1))


def held(shape):
    return pl.BlockSpec(shape, lambda i: (0,) * len(shape))


def mid_kernel(a_ref, x_ref, norm_ref, wo_ref, wt_ref, *refs):
    x1_ref, n_ref, ac_ref, t_ref = refs[-4:]

    @pl.when(pl.program_id(0) == 0)
    def _():
        a = joined(a_ref)
        ac_ref[...] = a
        x1 = x_ref[...].astype(f32) + dot(a, flat(wo_ref), NN)
        x1_ref[...] = x1
        n_ref[...] = layer_norm(x1, norm_ref[0:1, :], norm_ref[1:2, :])

    t_ref[0] = dot(n_ref[...], flat(wt_ref), NT).astype(bf16)


def middle(a, x, norm, w_out, w_triple, deps=()):
    S, rows, W = a.shape
    D = S * W
    return pl.pallas_call(
        mid_kernel,
        grid=(S,),
        out_shape=(
            jax.ShapeDtypeStruct((rows, D), f32),
            jax.ShapeDtypeStruct((rows, D), bf16),
            jax.ShapeDtypeStruct((rows, D), bf16),
            jax.ShapeDtypeStruct((S, rows, 3 * W), bf16),
        ),
        in_specs=[
            once((S, rows, W)),
            once((rows, D)),
            once((2, D)),
            once(*w_out[1]),
            w_triple[1],
        ]
        + [AN] * len(deps),
        out_specs=(
            held((rows, D)),
            held((rows, D)),
            held((rows, D)),
            pl.BlockSpec((1, rows, 3 * W), lambda i: (i, 0, 0)),
        ),
        compiler_params=pltpu.CompilerParams(vmem_limit_bytes=40 * 2**20),
        cost_estimate=BRIEF,
    )(a, x, norm, w_out[0], w_triple[0], *deps)


def mlp_kernel(
    aa_ref,
    ab_ref,
    xa_ref,
    xb_ref,
    ca_ref,
    cb_ref,
    dp_ref,
    norm_ref,
    ws_ref,
    wd_ref,
    up_ref,
    down_ref,
    n_ref,
    ac_ref,
    g_ref,
    du_ref,
    x3_ref,
    pix_ref,
    e3_ref,
    d2_ref,
    e2_ref,
    da_ref,
    sum_ref,
    x2,
    d3,
    acc,
    back,
    *,
    steps,
):
    step = pl.program_id(0)
    R = xa_ref.shape[0]
    S, _, W = aa_ref.shape

    @pl.when(step == 0)
    def _():
        for rows, a_ref, x_ref, c_ref in (
            (slice(0, R), aa_ref, xa_ref, ca_ref),
            (slice(R, x2.shape[0]), ab_ref, xb_ref, cb_ref),
        ):
            a = joined(a_ref)
            ac_ref[rows, :] = a
            x = x_ref[...] + dot(a, flat(ws_ref), NN)
            x2[rows, :] = x
            n_ref[rows, :] = layer_norm(x, norm_ref[0:1, :], norm_ref[1:2, :])
            d = c_ref[...].astype(f32) + dot(dp_ref[rows, :], flat(wd_ref), NN)
            d3[rows, :] = d
            e3_ref[rows, :] = d.astype(bf16)
        acc[...] = jnp.zeros_like(acc)
        back[...] = jnp.zeros_like(back)

    up = flat(up_ref)
    down = flat(down_ref)
    u = dot(n_ref[...], up, NT)
    slope = math.sqrt(2.0 / math.pi)
    square = u * u
    bend = jnp.tanh(slope * u * (1.0 + 0.044715 * square))
    half = 0.5 * (1.0 + bend)
    g = (u * half).astype(bf16)
    rise = half + 0.5 * slope * u * (1.0 - bend * bend) * (1.0 + 0.134145 * square)
    du = (dot(e3_ref[...], down, NT) * rise).astype(bf16)
    g_ref[...] = g
    du_ref[...] = du
    acc[...] += dot(g, down, NN)
    back[...] += dot(du, up, NN)

    @pl.when(step == steps - 1)
    def _():
        x3 = (x2[...] + acc[...]).astype(bf16)
        x3_ref[...] = x3
        pix_ref[...] = dot(x3, flat(wd_ref), NT).astype(bf16)
        grad_in, gain, shift = norm_back(x2[...], norm_ref[0:1, :], back[...])
        d2 = d3[...] + grad_in
        d2_ref[...] = d2
        e2 = d2.astype(bf16)
        e2_ref[...] = e2
        sum_ref[...] = jnp.concatenate([gain, shift], axis=0)
        da = dot(e2, flat(ws_ref), NT).astype(bf16)
        for i in range(S):
            da_ref[i] = da[:, i * W : (i + 1) * W]


def feed_forward(a, x1, cot, d_pix, norm, w_out, w_dec, w_up, w_down, hidden, steps):
    S, R, W = a[0].shape
    RB = a[1].shape[1]
    D, total, pixels = S * W, R + RB, d_pix.shape[1]
    part = hidden // steps
    row = jax.ShapeDtypeStruct((total, D), bf16)
    wide = jax.ShapeDtypeStruct((total, hidden), bf16)
    blocked = pl.BlockSpec((total, part), lambda i: (0, i))
    full = held((total, D))
    return pl.pallas_call(
        functools.partial(mlp_kernel, steps=steps),
        grid=(steps,),
        out_shape=(
            row,
            row,
            wide,
            wide,
            row,
            jax.ShapeDtypeStruct((total, pixels), bf16),
            row,
            jax.ShapeDtypeStruct((total, D), f32),
            row,
            jax.ShapeDtypeStruct((S, total, W), bf16),
            jax.ShapeDtypeStruct((2, D), f32),
        ),
        in_specs=[
            once((S, R, W)),
            once((S, RB, W)),
            once((R, D)),
            once((RB, D)),
            once((R, D)),
            once((RB, D)),
            once((total, pixels)),
            once((2, D)),
            once(*w_out[1]),
            once(*w_dec[1]),
            w_up[1],
            w_down[1],
        ],
        out_specs=(
            full,
            full,
            blocked,
            blocked,
            full,
            held((total, pixels)),
            full,
            full,
            full,
            held((S, total, W)),
            held((2, D)),
        ),
        scratch_shapes=[pltpu.VMEM((total, D), f32)] * 4,
        compiler_params=pltpu.CompilerParams(vmem_limit_bytes=60 * 2**20),
        cost_estimate=BRIEF,
    )(*a, *x1, *cot, d_pix, norm, w_out[0], w_dec[0], w_up[0], w_down[0])


def hold_kernel(*refs):
    pass


def hold(value, deps):
    return pl.pallas_call(
        hold_kernel,
        out_shape=jax.ShapeDtypeStruct(value.shape, value.dtype),
        in_specs=[AN] * (1 + len(deps)),
        out_specs=AN,
        input_output_aliases={0: 0},
        cost_estimate=BRIEF,
    )(value, *deps)


def back_kernel(
    t_ref, x_ref, d_ref, norm_ref, wo_ref, wt_ref, *refs, steps
):
    d1_ref, e_ref, da_ref, sum_ref, acc = refs[-5:]
    step = pl.program_id(0)
    part = dot(t_ref[0], flat(wt_ref), NN)

    @pl.when(step == 0)
    def _():
        acc[...] = part

    @pl.when(step > 0)
    def _():
        acc[...] += part

    @pl.when(step == steps - 1)
    def _():
        grad_in, gain, shift = norm_back(x_ref[...], norm_ref[0:1, :], acc[...])
        d1 = d_ref[...] + grad_in
        d1_ref[...] = d1
        e = d1.astype(bf16)
        e_ref[...] = e
        sum_ref[...] = jnp.concatenate([gain, shift], axis=0)
        da = dot(e, flat(wo_ref), NT).astype(bf16)
        W = da_ref.shape[2]
        for i in range(steps):
            da_ref[i] = da[:, i * W : (i + 1) * W]


def middle_back(t, x1, d2, at, norm, w_out, w_triple, deps=()):
    S, rows, wide = t.shape
    D = x1.shape[1]
    W = wide // 3
    return pl.pallas_call(
        functools.partial(back_kernel, steps=S),
        grid=(S,),
        out_shape=(
            jax.ShapeDtypeStruct((rows, D), f32),
            jax.ShapeDtypeStruct((rows, D), bf16),
            jax.ShapeDtypeStruct((S, rows, W), bf16),
            jax.ShapeDtypeStruct((2, D), f32),
        ),
        in_specs=[
            pl.BlockSpec((1, rows, wide), lambda i: (i, 0, 0)),
            once((rows, D)),
            once((rows, D), (at, 0)),
            once((2, D)),
            once(*w_out[1]),
            w_triple[1],
        ]
        + [AN] * len(deps),
        out_specs=(
            held((rows, D)),
            held((rows, D)),
            held((S, rows, W)),
            held((2, D)),
        ),
        scratch_shapes=[pltpu.VMEM((rows, D), f32)],
        compiler_params=pltpu.CompilerParams(vmem_limit_bytes=40 * 2**20),
        cost_estimate=BRIEF,
    )(t, x1, d2, norm, w_out[0], w_triple[0], *deps)


def grads_kernel(*refs, shape, widths):
    count = sum(shape)
    lefts, rights = refs[:count], refs[count : 2 * count]
    out_ref, turned = refs[-1 - count], refs[-count:]

    @pl.when(pl.program_id(0) == 0)
    def _():
        for left, t in zip(lefts, turned):
            t[...] = left[...].T

    at = n = 0
    for pieces, width in zip(shape, widths):
        total = 0.0
        for i in range(n, n + pieces):
            right = joined(rights[i]) if len(rights[i].shape) == 3 else rights[i][...]
            total += dot(turned[i][...], right, NN)
        out_ref[:, at : at + width] = total.astype(bf16)
        at, n = at + width, n + pieces


def weight_grads(terms, ranks, deps=()):
    pieces = [p for term in terms for p in term]
    shape = [len(term) for term in terms]
    widths = [term[0][1].size // term[0][0].shape[0] // ranks for term in terms]
    D, per = pieces[0][0].shape[1], sum(widths)
    lefts = [p[0] for p in pieces]
    rights = [p[1] for p in pieces]
    work = sum(p[0].shape[0] for p in pieces) * D * per * ranks // len(pieces)
    return pl.pallas_call(
        functools.partial(grads_kernel, shape=shape, widths=widths),
        grid=(ranks,),
        out_shape=jax.ShapeDtypeStruct((D, per * ranks), bf16),
        in_specs=[once(v.shape) for v in lefts]
        + [
            pl.BlockSpec((v.shape[0] // ranks,) + v.shape[1:], lambda i: (i, 0, 0))
            if v.ndim == 3
            else pl.BlockSpec((v.shape[0], v.shape[1] // ranks), lambda i: (0, i))
            for v in rights
        ]
        + [AN] * len(deps),
        out_specs=pl.BlockSpec((D, per), lambda i: (0, i)),
        scratch_shapes=[pltpu.VMEM(v.shape[::-1], bf16) for v in lefts],
        compiler_params=pltpu.CompilerParams(vmem_limit_bytes=56 * 2**20),
        cost_estimate=BRIEF,
    )(*lefts, *rights, *deps)


def start_kernel(at_ref, xa_ref, xb_ref, norm_ref, wk_ref, *refs, pieces, width):
    p_in, (q_ref, k_ref, n_ref, wq_ref, wkv_ref) = refs[:pieces], refs[-5:]
    seq = at_ref[0]
    R = xa_ref.shape[0]
    W = q_ref.shape[2]
    groups, per = wk_ref.shape[0], wq_ref.shape[0] // wk_ref.shape[0]
    size = wkv_ref.shape[0] // groups
    for i in range(groups):
        wq_ref[i * per : (i + 1) * per, :] = wk_ref[i, :per, :]
        kept = wk_ref.shape[1] - per
        wkv_ref[i * size : i * size + kept, :] = wk_ref[i, per:, :width]
        if kept < size:
            tall = size - kept
            tail = [wk_ref[i, at : at + tall, width:] for at in range(per, per + kept, tall)]
            wkv_ref[i * size + kept : (i + 1) * size, :] = jnp.concatenate(tail, axis=1)
    for block, x_ref in ((slice(0, R), xa_ref), (slice(R, n_ref.shape[0]), xb_ref)):
        n_ref[block, :] = layer_norm(x_ref[...].astype(f32), norm_ref[0:1, :], norm_ref[1:2, :])
    for i in range(pieces):
        q_ref[i] = dot(n_ref[...], wq_ref[i * W : (i + 1) * W, :], NT).astype(bf16)
    own = wkv_ref[pl.ds(pl.multiple_of(seq * 2 * W, 16), 2 * W), :]
    for i in range(pieces):
        k_ref[seq ^ i] = dot(p_in[i][...], own, NT).astype(bf16)


def start(at, x0, norm, lead, patch_pieces, W, deps):
    S, D = len(patch_pieces), x0[0].shape[1]
    total = x0[0].shape[0] + x0[1].shape[0]
    slots, width = patch_pieces[0].shape
    whole = [x0[0].shape, x0[1].shape, norm.shape]
    outs = [(S, total, W), (S, slots, 2 * W), (total, D), (D, D), (2 * D, width)]
    return pl.pallas_call(
        functools.partial(start_kernel, pieces=S, width=width),
        grid=(1,),
        out_shape=tuple(jax.ShapeDtypeStruct(v, bf16) for v in outs),
        in_specs=[SM]
        + [once(v) for v in whole]
        + [once(lead.shape)]
        + [once((slots, width))] * S
        + [AN] * len(deps),
        out_specs=tuple(held(v) for v in outs),
        compiler_params=pltpu.CompilerParams(vmem_limit_bytes=56 * 2**20),
        cost_estimate=BRIEF,
    )(at, *x0, norm, lead, *patch_pieces, *deps)


def finish_kernel(at_ref, a_ref, b_ref, *refs, pieces, rows):
    p_in, out_ref = refs[:pieces], refs[-1]
    seq = at_ref[0]
    W = a_ref.shape[2]
    slots = (a_ref.shape[1] - rows[0]) // 2
    sums = [0.0, 0.0]
    for i in range(pieces):
        for j, (ref, at) in enumerate(((a_ref, rows[0]), (b_ref, rows[1]))):
            p = p_in[i][j * slots : (j + 1) * slots, :]
            for k in range(2):
                sums[k] += dot(ref[seq ^ i, at + k * slots : at + (k + 1) * slots, :], p, TN)
    wide = sums[0].shape[1] // pieces
    for k in range(2):
        grad = sums[k].T.astype(bf16)
        for i in range(pieces):
            out_ref[i, k * wide : (k + 1) * wide, :] = grad[i * wide : (i + 1) * wide, :]


def finish(at, cross, rows, patch_pieces, deps):
    S, _, W = cross[0].shape
    out = (S, 2 * patch_pieces[0].shape[1] // S, W)
    return pl.pallas_call(
        functools.partial(finish_kernel, pieces=S, rows=rows),
        out_shape=jax.ShapeDtypeStruct(out, bf16),
        in_specs=[SM] + [VM] * (2 + S) + [AN] * len(deps),
        out_specs=VM,
        compiler_params=pltpu.CompilerParams(vmem_limit_bytes=32 * 2**20),
        cost_estimate=BRIEF,
    )(at, *cross, *patch_pieces, *deps)


def pack_lanes(ref, at, value):
    rows = value.shape[0]
    for i in range(value.shape[1] // LANES):
        ref[at + i * rows : at + (i + 1) * rows, :] = value[:, i * LANES : (i + 1) * LANES]


def unpack_lanes(ref, at, rows, columns):
    parts = [ref[at + i * rows : at + (i + 1) * rows, :] for i in range(columns // LANES)]
    return jnp.concatenate(parts, axis=1)


def end_kernel(
    at_ref, g_ref, wq_ref, wkv_ref, x_ref, n_ref, d_ref, gain_ref, *refs, blocks, more, n_dep
):
    extra, refs = refs[:more], refs[more + n_dep :]
    outs, refs = refs[:blocks], refs[blocks:]
    if more:
        part_ref, refs = refs[0], refs[1:]
    outs_more, (n_t, dq, total) = refs[:-3], refs[-3:]
    S, _, W = g_ref.shape
    rows = x_ref.shape[0]
    slots = (g_ref.shape[1] - rows) // 2
    own = rows // blocks
    dq[...] = jnp.concatenate([g_ref[i, :rows, :] for i in range(S)], axis=1)
    n_t[...] = n_ref[...].T
    grad, gain, shift = norm_back(
        x_ref[...].astype(f32), gain_ref[...], dot(dq[...], wq_ref[...], NN)
    )
    total[...] = d_ref[...] + grad
    place = at_ref[1] // 2 if more else at_ref[1]
    keys = []
    for i in range(S):
        keys += [g_ref[i, rows : rows + slots, :], g_ref[i, rows + slots :, :]]
    part = dot(jnp.concatenate(keys, axis=1), wkv_ref[...], NN).astype(bf16)
    for i in range(blocks):
        block = total[pl.ds(pl.multiple_of((place ^ i) * own, 8), own), :].astype(bf16)
        if more:
            outs[i][...] = block
        else:
            pack_lanes(outs[i], 0, block)
            pack_lanes(outs[i], own * block.shape[1] // LANES, part)
    if more:
        part_ref[...] = part
    lift = jnp.concatenate([gain, shift], axis=0)
    tall = n_t.shape[0] // S
    for i in range(0, S, 2):
        pair = dot(n_t[...], dq[:, i * W : (i + 2) * W], NN)
        if more:
            pair += extra[0][i // 2]
            for j in range(S):
                block = pair[j * tall : (j + 1) * tall, :].astype(bf16)
                outs_more[0][j, i * tall : (i + 1) * tall, :] = block[:, :W]
                outs_more[0][j, (i + 1) * tall : (i + 2) * tall, :] = block[:, W:]
        else:
            outs_more[0][i // 2] = pair
    if not more:
        outs_more[1][...] = lift
        return
    at = S * tall
    heads = extra[3].shape[1]
    zero = jnp.zeros((2, n_t.shape[0]), f32)
    sums = jnp.concatenate([lift + extra[1][...], extra[2][...], zero], axis=0)
    hi = sums.astype(bf16).astype(f32)
    both = jnp.concatenate([hi, sums - hi], axis=0).astype(bf16)
    for j in range(S):
        outs_more[0][j, at : at + heads, :] = extra[3][j]
        outs_more[0][j, at + heads :, :] = both[:, j * W : (j + 1) * W]


def end(at, got, place, w_query, w_kv, x0, n1, d1, gain, blocks, deps, more=()):
    S, _, W = got.shape
    rows, D = x0.shape
    slots, width = (got.shape[1] - rows) // 2, w_kv.shape[1]
    own = rows // blocks
    if more:
        outs = [((own, D), bf16)] * blocks + [((slots, width), bf16)]
        outs += [((S, D + more[3].shape[1] + 16, W), bf16)]
    else:
        outs = [(((own * D + slots * width) // LANES, LANES), bf16)] * blocks
        outs += [((S // 2, D, 2 * W), f32), ((2, D), f32)]
    whole = [got, w_query, w_kv, x0, n1, d1, gain, *more]
    specs = [once(v.shape) for v in whole]
    specs[4] = once((rows, D), (place, 0))
    return pl.pallas_call(
        functools.partial(end_kernel, blocks=blocks, more=len(more), n_dep=len(deps)),
        grid=(1,),
        out_shape=tuple(jax.ShapeDtypeStruct(*v) for v in outs),
        in_specs=[SM] + specs + [AN] * len(deps),
        out_specs=tuple(held(v[0]) for v in outs),
        scratch_shapes=[
            pltpu.VMEM((D, rows), bf16),
            pltpu.VMEM((rows, D), bf16),
            pltpu.VMEM((rows, D), f32),
        ],
        compiler_params=pltpu.CompilerParams(vmem_limit_bytes=56 * 2**20),
        cost_estimate=BRIEF,
    )(at, *whole, *deps)


def mix_kernel(at_ref, x_ref, *refs, heads, ranks):
    outs = refs[-ranks:]
    S, rows, W = x_ref.shape
    blocks = rows - heads - 16
    pair = blocks // len(outs)
    small = sum(x_ref[j, blocks + heads :, :].astype(f32) for j in range(S))
    total = small[:8] + small[8:]
    hi = total.astype(bf16).astype(f32)
    for i in range(len(outs)):
        rank = at_ref[1] ^ i
        src = pl.ds(pl.multiple_of(rank * pair, 16), pair)
        outs[i][:pair, :] = sum(x_ref[j, src, :].astype(f32) for j in range(S)).astype(bf16)
        for k in range(2):
            outs[i][pair + k * heads : pair + (k + 1) * heads, :] = x_ref[
                2 * rank + k, blocks : blocks + heads, :
            ]
        outs[i][pair + 2 * heads :, :] = jnp.concatenate([hi, total - hi], axis=0).astype(bf16)


def mix(at, got, ranks, heads, deps):
    S, rows, W = got.shape
    shape = ((rows - heads - 16) // ranks + 2 * heads + 16, W)
    return pl.pallas_call(
        functools.partial(mix_kernel, heads=heads, ranks=ranks),
        out_shape=(jax.ShapeDtypeStruct(shape, bf16),) * ranks,
        in_specs=[SM, VM] + [AN] * len(deps),
        out_specs=(VM,) * ranks,
        compiler_params=pltpu.CompilerParams(vmem_limit_bytes=24 * 2**20),
        cost_estimate=BRIEF,
    )(at, got, *deps)


def last_kernel(*refs, heads):
    ins, (q_ref, k_ref, v_ref, small_ref) = refs[:-4], refs[-4:]
    total = sum(v[...].astype(f32) for v in ins)
    pair = total.shape[0] - 2 * heads - 16
    q_ref[...] = jnp.concatenate([total[: pair // 2], total[pair // 2 : pair]], axis=1)
    one, two = total[pair : pair + heads], total[pair + heads : pair + 2 * heads]
    k_ref[...] = jnp.concatenate([one[: heads // 2], two[: heads // 2]], axis=1)
    v_ref[...] = jnp.concatenate([one[heads // 2 :], two[heads // 2 :]], axis=1)
    small_ref[...] = total[pair + 2 * heads : pair + 2 * heads + 8] + total[pair + 2 * heads + 8 :]


def last(parts, heads):
    rows, W = parts[0].shape
    pair = rows - 2 * heads - 16
    outs = [(pair // 2, 2 * W), (heads // 2, 2 * W), (heads // 2, 2 * W), (8, W)]
    return pl.pallas_call(
        functools.partial(last_kernel, heads=heads),
        out_shape=tuple(jax.ShapeDtypeStruct(v, f32) for v in outs),
        in_specs=[VM] * len(parts),
        out_specs=(VM,) * 4,
        compiler_params=pltpu.CompilerParams(vmem_limit_bytes=24 * 2**20),
        cost_estimate=BRIEF,
    )(*parts)


def place_kernel(at_ref, *refs, ranks, packed):
    whole, halves, out_ref = refs[:ranks], refs[ranks : ranks + ranks // 2], refs[-1]
    _, own, D = out_ref.shape
    for i in range(ranks):
        src = at_ref[1] ^ i
        block = unpack_lanes(whole[i], 0, own, D) if packed else whole[i][...]
        out_ref[3 * (src // 2) + 2 * (src % 2)] = block.astype(out_ref.dtype)
    for i in range(ranks // 2):
        src = at_ref[1] % (ranks // 2) ^ i
        out_ref[3 * src + 1] = halves[i][...].astype(out_ref.dtype)


def place_rows(at, whole, halves, kind, deps=(), packed=False):
    ranks = len(whole)
    shape = (3 * ranks // 2,) + halves[0].shape
    return pl.pallas_call(
        functools.partial(place_kernel, ranks=ranks, packed=packed),
        out_shape=jax.ShapeDtypeStruct(shape, kind),
        in_specs=[SM] + [VM] * (ranks + ranks // 2) + [AN] * len(deps),
        out_specs=VM,
        compiler_params=pltpu.CompilerParams(vmem_limit_bytes=24 * 2**20),
        cost_estimate=BRIEF,
    )(at, *whole, *halves, *deps)


def patches_kernel(at_ref, *refs):
    ins, out_ref = refs[:-1], refs[-1]
    ranks = len(ins) // 2
    _, slots, width = out_ref.shape
    at = ins[0].shape[0] - slots * width // LANES
    for i in range(ranks // 2):
        out_ref[3 * i + 1] = jnp.zeros(out_ref.shape[1:], f32)
    for i in range(ranks):
        src = at_ref[1] ^ i
        block = unpack_lanes(ins[i], at, slots, width)
        out_ref[3 * (src // 2) + 2 * (src % 2)] = block.astype(f32)
        out_ref[3 * (src // 2) + 1] += ins[ranks + i][...].astype(f32)


def place_patches(at, parts_a, parts_b):
    shape = (3 * len(parts_a) // 2,) + parts_b[0].shape
    return pl.pallas_call(
        patches_kernel,
        out_shape=jax.ShapeDtypeStruct(shape, f32),
        in_specs=[SM] + [VM] * (2 * len(parts_a)),
        out_specs=VM,
        compiler_params=pltpu.CompilerParams(vmem_limit_bytes=24 * 2**20),
        cost_estimate=BRIEF,
    )(at, *parts_a, *parts_b)


CP = 32


def place(perm, toks, TR, TC):
    own, ext = TR * TC, perm.shape[2]
    tok = lax.broadcasted_iota(jnp.int32, (toks, 1), 0)
    row = jnp.where(tok < own, tok // TC, jnp.where(tok < own + TR, tok - own, TR))
    col = jnp.where(
        tok < own, tok % TC, jnp.where(tok < own + TR, TC, tok - own - TR)
    )
    real = tok <= own + TR + TC
    pixel = lax.broadcasted_iota(jnp.int32, (toks, ext), 1)
    for a in range(2):
        for b in range(2):
            ok = real & ((row < TR) | (a == 0)) & ((col < TC) | (b == 0))
            at = jnp.where(ok, (2 * row + a) * (2 * TC + 1) + 2 * col + b, -1)
            perm[2 * a + b] = jnp.where(pixel == at, 1.0, 0.0).astype(bf16)


def pixel_grad_kernel(cot_ref, w_ref, *refs, TR, TC):
    out_ref, perm = refs[-2:]

    @pl.when(pl.program_id(0) == 0)
    def _():
        place(perm, out_ref.shape[1], TR, TC)

    grad = dot(cot_ref[0], w_ref[0], NT)
    hi = grad.astype(bf16)
    lo = (grad - hi.astype(f32)).astype(bf16)
    parts = [dot(perm[i], hi, NT) + dot(perm[i], lo, NT) for i in range(4)]
    out_ref[0] = jnp.concatenate(parts, axis=1)


def pixel_sample_kernel(x_ref, w_ref, *refs, TR, TC):
    out_ref, perm = refs[-2:]

    @pl.when(pl.program_id(0) == 0)
    def _():
        place(perm, x_ref.shape[1], TR, TC)

    x = x_ref[0]
    window = sum(dot(x[:, i * CP : (i + 1) * CP], perm[i], TN) for i in range(4))
    out_ref[0] = dot(window.astype(bf16), w_ref[0], NN).astype(bf16)


def per_plane(body, first, weights, out_rows, out_lanes, out_type, toks, TR, TC, deps=()):
    planes, ext, samples = weights.shape

    def whole(shape):
        return pl.BlockSpec((1,) + shape, lambda i: (i, 0, 0))

    return pl.pallas_call(
        functools.partial(body, TR=TR, TC=TC),
        grid=(planes,),
        out_shape=jax.ShapeDtypeStruct((planes, out_rows, out_lanes), out_type),
        in_specs=[whole(first.shape[1:]), whole((ext, samples))] + [AN] * len(deps),
        out_specs=whole((out_rows, out_lanes)),
        scratch_shapes=[pltpu.VMEM((4, toks, ext), bf16)],
        compiler_params=pltpu.CompilerParams(vmem_limit_bytes=24 * 2**20),
        cost_estimate=BRIEF,
    )(first, weights, *deps)


def swap_seq(value):
    return lax.all_to_all(value, "seq", split_axis=0, concat_axis=0, tiled=True)


def swap_mp(value):
    return lax.all_to_all(value, "mp", split_axis=0, concat_axis=0, tiled=True)


def swap_all(value):
    return lax.all_to_all(value, ("seq", "mp"), split_axis=0, concat_axis=0, tiled=True)


def swap_pair(value):
    count = lax.axis_size("mp")
    return lax.ppermute(value, "mp", [(i, i ^ 1) for i in range(count)])


def gather_rows(piece):
    return lax.all_gather(piece, ("mp", "seq"), axis=0, tiled=False)


def bundle_part(bundle, at, rows):
    pieces, _, D = bundle.shape
    if rows % 16 == 0 and at % rows == 0:
        return bundle, ((pieces, rows, D), (0, at // rows, 0))
    value = bundle[:, at : at + rows].reshape(1, -1, D)
    return value, (value.shape, None)


def by_step(part, steps):
    (pieces, rows, D), at = part[1]
    if pieces > 1:
        return part[0], pl.BlockSpec((pieces // steps, rows, D), lambda i: (i, at[1], 0))
    return part[0], pl.BlockSpec((1, rows // steps, D), lambda i: (0, i, 0))


def reduce_rows(value):
    return lax.psum_scatter(value, "seq", scatter_dimension=0, tiled=True)


def to_ranks(blocks):
    moves = [[(i, i ^ step) for i in range(len(blocks))] for step in range(len(blocks))]
    return [v if i == 0 else lax.ppermute(v, "mp", moves[i]) for i, v in enumerate(blocks)]


def to_halves(blocks):
    pairs = len(blocks)
    arrived = []
    for step in range(pairs):
        moves = [(2 * p + h, pairs * h + (p ^ step)) for p in range(pairs) for h in range(2)]
        arrived.append(lax.ppermute(blocks[step], "mp", moves))
    return arrived


def sum_ranks(value):
    return lax.psum_scatter(value, "mp", scatter_dimension=1, tiled=True).astype(f32)


def gather_pieces(value):
    shares = lax.axis_size("seq")
    pieces = []
    for step in range(0, shares, 2):
        moves = [(i, i ^ step) for i in range(shares)]
        pieces.append(value if step == 0 else lax.ppermute(value, "seq", moves))
    cores = [(i, i ^ 1) for i in range(shares)]
    return [p for piece in pieces for p in (piece, lax.ppermute(piece, "seq", cores))]


def per_device(
    tokens,
    patches,
    counts,
    norm_gains,
    norm_shifts,
    cross_query,
    cross_kv,
    cross_out,
    self_qkv,
    self_out,
    mlp_up,
    mlp_down,
    decoder,
    sample_weights,
    tokens_cot,
    sample_cot,
):
    objects, R, D = tokens.shape
    S, M = lax.axis_size("seq"), lax.axis_size("mp")
    s, m = lax.axis_index("seq"), lax.axis_index("mp")
    pairs = M // 2
    if objects != 3 * pairs or S != 2 * M or D % (HD * S) != 0:
        raise ValueError("unexpected sizes")
    pair, half = m // 2, m % 2
    at_a, at_b = 3 * pair + 2 * half, 3 * pair + 1
    RB = R // 2
    RS = R + RB
    rows = [R, RB]
    W = D // S
    hpd = W // HD
    slots, width = patches.shape[1], patches.shape[2]
    slot_total = slots * S
    row_total = R * S

    def pick(arr):
        whole = lax.dynamic_index_in_dim(arr, at_b, 0, keepdims=False)
        return [
            lax.dynamic_index_in_dim(arr, at_a, 0, keepdims=False),
            lax.dynamic_slice_in_dim(whole, half * RB, RB, 0),
        ]

    def mine(arr, axis):
        share = arr.shape[axis] // S
        return lax.dynamic_slice_in_dim(arr, s * share, share, axis)

    channels = decoder.shape[1]
    local_dec = jnp.pad(decoder.transpose(2, 1, 0), ((0, 0), (0, CP - channels), (0, 0)))
    part = S // 2
    qkv_piece = lax.dynamic_slice_in_dim(self_qkv, s // part * W, W, 2).reshape(D, 3 * W)
    qkv_piece = lax.dynamic_slice_in_dim(qkv_piece, s % part * (3 * W // part), 3 * W // part, 1)
    per = D // (S * M)
    dec_rows = 4 * CP // S
    kv_rows = 2 * per
    at = s * kv_rows
    kv_piece = lax.dynamic_slice(
        cross_kv, (0, (at // W) % 2, at // (2 * W) * W + at % W), (width, 1, kv_rows)
    )
    kv_piece = kv_piece[:, 0].T
    tail_rows = kv_rows - kv_rows * width // D
    if (kv_rows - tail_rows) % tail_rows == 0 and tail_rows % 16 == 0 and width % 128 == 0:
        folds = (kv_rows - tail_rows) // tail_rows
        tail = jnp.split(kv_piece[-tail_rows:], folds, axis=1)
        kv_piece = jnp.concatenate([kv_piece[:-tail_rows], jnp.concatenate(tail)], axis=1)
    else:
        kv_piece = jnp.pad(kv_piece, ((0, 0), (0, D - width)))
    kv_rows = kv_piece.shape[0]
    lead = [mine(cross_query, 1).T, kv_piece]
    lead = gather_rows(jnp.concatenate(lead, axis=0))
    first = gather_rows(
        jnp.concatenate(
            [qkv_piece.T, mine(cross_out, 0)], axis=0
        )
    )
    up_rows = mlp_up.shape[1] // S
    second = gather_rows(
        jnp.concatenate(
            [
                mine(mlp_up, 1).T,
                mine(mlp_down, 0),
                mine(self_out, 0),
                mine(local_dec.reshape(-1, D), 0),
            ],
            axis=0,
        )
    )
    steps = 8
    w_up = by_step(bundle_part(second, 0, up_rows), steps)
    w_down = by_step(bundle_part(second, up_rows, up_rows), steps)
    w_triple = by_step(bundle_part(first, 0, 3 * per), S)
    w_cross_out = bundle_part(first, 3 * per, per)
    w_self_out = bundle_part(second, 2 * up_rows, per)
    w_dec = bundle_part(second, 2 * up_rows + per, dec_rows)

    x0 = pick(tokens)
    norms = [jnp.stack([norm_gains[i], norm_shifts[i]]) for i in range(3)]
    at = jnp.stack([s, m])
    both = [lax.dynamic_index_in_dim(patches, o, 0, keepdims=False) for o in (at_a, at_b)]
    patch_pieces = gather_pieces(jnp.concatenate(both, axis=0))
    TC = PLANE // 4
    TR = PLANE * 4 // S
    own, rim = TR * TC, TR * TC + TR
    toks = -(-(rim + TC + 1) // 32) * 32
    planes = objects * 3
    weights_in = sample_weights.reshape(planes, *sample_weights.shape[3:])
    cot_in = sample_cot.reshape(planes, channels, -1)
    cot_in = jnp.pad(cot_in, ((0, 0), (0, CP - channels), (0, 0)))
    ext = per_plane(pixel_grad_kernel, cot_in, weights_in, toks, 4 * CP, f32, toks, TR, TC)
    ways = {
        1: [i for i in range(S) if i % 4 != 3],
        4: [i for i in range(S) if i + 4 < S],
        5: [i for i in range(S) if i % 4 != 3 and i + 4 < S],
    }
    rights = lax.ppermute(ext[:, own:rim], "seq", [(i, i + 1) for i in ways[1]])
    belows = lax.ppermute(ext[:, rim : rim + TC], "seq", [(i, i + 4) for i in ways[4]])
    corner = lax.ppermute(ext[:, rim + TC : rim + TC + 1], "seq", [(i, i + 5) for i in ways[5]])
    grid = ext[:, :own].reshape(planes, TR, TC, -1)
    belows = jnp.concatenate([belows[:, :1] + corner, belows[:, 1:]], axis=1)
    grid = grid + jnp.pad(rights[:, :, None], ((0, 0), (0, 0), (0, TC - 1), (0, 0)))
    grid = grid + jnp.pad(belows[:, None], ((0, 0), (0, TR - 1), (0, 0), (0, 0)))
    KA, KB = R // S, RB // S
    cu = 4 * CP
    grad_pix = grid.astype(bf16).reshape(pairs, 3, S, KA, cu)
    gp_a = jnp.stack([grad_pix[:, 0], grad_pix[:, 2]], axis=1).transpose(2, 0, 1, 3, 4)
    gp_b = grad_pix[:, 1].reshape(pairs, S, 2, KB, cu).transpose(1, 0, 2, 3, 4)
    sent = jnp.concatenate([gp_a, gp_b], axis=3).reshape(S * M, KA + KB, cu)

    q1, keys_one, n1, w_query, w_kv = start(
        at, x0, norms[0], lead, patch_pieces, W, [sent]
    )
    heads_one = swap_seq(q1)
    back = swap_all(hold(sent, [heads_one]))
    d_pix = back.reshape(S, M, KA + KB, cu).transpose(2, 0, 1, 3).reshape(RS, M * cu)

    limits = [
        jnp.stack([lax.dynamic_index_in_dim(counts, o, 0, keepdims=False), jnp.int32(0)])
        for o in (at_a, at_b)
    ]
    kv_one = [(slots, (i * slots, 0), (i * slots, W), 0) for i in range(2)]
    o1, res1 = [], []
    for i in range(2):
        out, res = attend(
            limits[i],
            [heads_one, keys_one],
            S,
            (0, rows[i], i * R, 0),
            [(1,) + kv_one[i]],
            slot_total,
            hpd,
            False,
            [(back,), ()][i],
        )
        o1.append(out)
        res1.append(res)

    mids = [
        middle(swap_seq(o1[i].reshape(S, rows[i], W)), x0[i], norms[1], w_cross_out, w_triple)
        for i in range(2)
    ]
    x1, n2, a1, t2 = zip(*mids)

    heads_two = [swap_seq(v) for v in t2]
    pair_kv = swap_pair(heads_two[1][:, :, W:])
    wide = jnp.array([row_total, 0], jnp.int32)
    kv_a2 = (R, (0, W), (0, 2 * W), 0)
    kv_b2 = (RB, (0, W), (0, 2 * W), 0)
    kv_p2 = (RB, (0, 0), (0, W), row_total // 2)
    o_a2, res_a2 = attend(
        wide, [heads_two[0]], S, (0, R, 0, 0), [(0,) + kv_a2], row_total, hpd, True
    )
    o_b2, res_b2 = attend(
        wide,
        [heads_two[1], pair_kv],
        S,
        (0, RB, 0, 0),
        [(0,) + kv_b2, (1,) + kv_p2],
        row_total,
        hpd,
        True,
        [o_a2],
    )
    a2_a = swap_seq(o_a2.reshape(S, R, W))
    a2 = [a2_a, swap_seq(hold(o_b2.reshape(S, RB, W), [a2_a]))]

    hidden = mlp_up.shape[1] * M
    n3, a2, g, du, x3b, pix, e3, d2, e2, da2, sums_three = feed_forward(
        a2,
        x1,
        pick(tokens_cot),
        d_pix,
        norms[2],
        w_self_out,
        w_dec,
        w_up,
        w_down,
        hidden,
        steps,
    )

    da2 = swap_seq(da2)
    grads_one = weight_grads([[(n3, du)], [(e3, g)], [(e2, a2)], [(x3b, d_pix)]], M)
    grads_one = hold(grads_one, [da2])
    pix = hold(pix, [grads_one])
    dt2_a = attend_back(
        wide,
        [res_a2, da2, o_a2, heads_two[0]],
        S,
        (R, 0),
        [(3,) + kv_a2],
        row_total,
        hpd,
        True,
        [grads_one],
        "lanes",
    )
    grads_one = reduce_rows(grads_one)
    pix = pix.reshape(KA + KB, S, M, cu).transpose(1, 2, 0, 3)
    got = swap_all(pix.reshape(S * M, KA + KB, cu)).reshape(S, pairs, 2, KA + KB, cu)
    half_total = row_total // 2
    kv_p2 = (RB, (0, 0), (0, W), 0)
    dq_p2, dkv_p2 = attend_back(
        wide,
        [res_b2, da2, o_b2, pair_kv],
        S,
        (RB, R),
        [(3,) + kv_p2],
        half_total,
        hpd,
        True,
        [dt2_a, got],
    )
    given = swap_pair(dkv_p2)
    dq_b2, dkv_b2 = attend_back(
        wide,
        [res_b2, da2, o_b2, heads_two[1]],
        S,
        (RB, R),
        [(3,) + kv_b2],
        half_total,
        hpd,
        True,
        [dq_p2],
    )
    dq_b2 = (dq_b2.astype(f32) + dq_p2.astype(f32)).astype(bf16)
    dkv_b2 = (dkv_b2.astype(f32) + given.astype(f32)).astype(bf16)
    dt2 = [
        swap_seq(dt2_a),
        jnp.concatenate([dq_b2, dkv_b2], axis=1).reshape(S, RB, 3 * W),
    ]

    def below(i, deps):
        return middle_back(
            dt2[i], x1[i], d2, (0, R // RB)[i], norms[1], w_cross_out, w_triple, deps
        )

    def cross_back(i, da1, deps):
        return attend_back(
            limits[i],
            [res1[i], da1, o1[i], keys_one],
            S,
            (rows[i], 0),
            [(3,) + kv_one[i]],
            slot_total,
            hpd,
            False,
            deps,
            "rows",
        )

    low_a = below(0, [dq_b2, given])
    x3b = hold(x3b, [low_a[0]])
    blocks_a, blocks_b = x3b[:R].reshape(M, R // M, D), x3b[R:].reshape(pairs, R // M, D)
    blocks_a = [lax.dynamic_index_in_dim(blocks_a, m ^ i, 0, keepdims=False) for i in range(M)]
    blocks_b = [
        lax.dynamic_index_in_dim(blocks_b, pair ^ i, 0, keepdims=False) for i in range(pairs)
    ]
    blocks_a, blocks_b = to_ranks(blocks_a), to_halves(blocks_b)
    da1_a = swap_seq(low_a[2])
    dt2[1] = swap_seq(hold(dt2[1], [da1_a]))
    cross_a = cross_back(0, da1_a, [])
    grads_one = sum_ranks(hold(grads_one, [da1_a]))
    low_b = below(1, [cross_a])
    got_a = swap_seq(cross_a)
    da1_b = swap_seq(hold(low_b[2], [got_a]))
    d1, e1, da1, sums_two = zip(low_a, low_b)

    grads_two = weight_grads(
        [[(n2[i], dt2[i]) for i in range(2)], [(e1[i], a1[i]) for i in range(2)]], M, [grads_one, got_a] + blocks_a + blocks_b
    )
    *sent_a, share, lift = end(
        at, got_a, 0, w_query, w_kv, x0[0], n1, d1[0], norm_gains[:1], M, [grads_two]
    )
    cross_b = cross_back(1, da1_b, [grads_two, lift])
    grads_two = reduce_rows(grads_two)
    got_b = swap_seq(cross_b)

    two = sums_two[0] + sums_two[1]
    small = jnp.concatenate([two, sums_three], axis=0)
    px_a = got[:, :, :, :KA].transpose(1, 2, 0, 3, 4).reshape(pairs, 2, S * KA, cu)
    px_b = got[:, :, :, KA:].transpose(1, 0, 2, 3, 4).reshape(pairs, S * KA, cu)
    tile = jnp.stack([px_a[:, 0], px_b, px_a[:, 1]], axis=1).reshape(planes, TR, TC, cu)
    rights = lax.ppermute(tile[:, :, 0], "seq", [(i + 1, i) for i in ways[1]])
    belows = lax.ppermute(tile[:, 0], "seq", [(i + 4, i) for i in ways[4]])
    corner = lax.ppermute(tile[:, 0, :1], "seq", [(i + 5, i) for i in ways[5]])
    fill = jnp.zeros((planes, toks - rim - TC - 1, cu), bf16)
    ext = jnp.concatenate([tile.reshape(planes, own, cu), rights, belows, corner, fill], axis=1)
    sent_a = to_ranks(sent_a)
    by_head = finish(at, [cross_a, cross_b], rows, patch_pieces, [ext])
    heads = by_head.shape[1]
    *sent_b, part_b, final = end(
        at,
        got_b,
        R // RB,
        w_query,
        w_kv,
        x0[1],
        n1,
        d1[1],
        norm_gains[:1],
        pairs,
        sent_a,
        [share, lift, small, by_head],
    )
    got_last = swap_seq(final)
    grad_tokens = place_rows(at, sent_a, to_halves(sent_b), f32, [], True)
    patch_grad = place_patches(at, sent_a, to_ranks([part_b] * M))
    ext = hold(ext, [final])
    tokens_out = place_rows(at, blocks_a, blocks_b, bf16, [final])
    sampled = per_plane(
        pixel_sample_kernel, ext, weights_in, CP, weights_in.shape[2], bf16, toks, TR, TC
    )
    sampled = sampled[:, :channels].reshape(objects, 3, channels, 1, -1)

    final = last(to_ranks(mix(at, got_last, M, heads, [sampled, tokens_out])), heads)
    grad_cross_query, grad_keys, grad_values, small = final
    grad_cross_kv = jnp.stack([grad_keys, grad_values], axis=1)

    grads_two = sum_ranks(grads_two)
    ff = hidden // M
    grad_mlp_up, grad_mlp_down = grads_one[:, :ff], grads_one[:, ff : 2 * ff].T
    grad_self_out = grads_one[:, 2 * ff : 2 * ff + D // M].T
    grad_decoder = grads_one[:, 2 * ff + D // M :]
    grad_decoder = grad_decoder.reshape(D // S, 4, CP)[:, :, :channels].transpose(0, 2, 1)
    grad_self_qkv = grads_two[:, : 3 * D // M].reshape(D // S, 2, 3, W).transpose(0, 2, 1, 3)
    grad_cross_out = grads_two[:, 3 * D // M :].T

    return (
        tokens_out,
        sampled,
        grad_tokens,
        patch_grad,
        jnp.stack([small[0], small[2], small[4]]),
        jnp.stack([small[1], small[3]]),
        small[5],
        grad_cross_query,
        grad_cross_kv,
        grad_cross_out,
        grad_self_qkv.reshape(D // S, 3, -1),
        grad_self_out,
        grad_mlp_up,
        grad_mlp_down,
        grad_decoder,
    )


def solution(mesh):
    return jax.shard_map(
        per_device,
        mesh=mesh,
        in_specs=(
            P(None, "seq", None),
            P(None, "seq", None),
            P(),
            P(),
            P(),
            P(None, "mp"),
            P(None, None, "mp"),
            P("mp", None),
            P(None, None, "mp"),
            P("mp", None),
            P(None, "mp"),
            P("mp", None),
            P(None, "mp", None),
            P(None, None, "seq", None, None),
            P(None, "seq", None),
            P(None, None, "mp", "seq", None),
        ),
        out_specs=(
            P(None, ("seq", "mp"), None),
            P(None, None, "mp", "seq", None),
            P(None, ("seq", "mp"), None),
            P(None, "seq", None),
            P(None, "seq"),
            P(None, "seq"),
            P("seq"),
            P("seq", "mp"),
            P("seq", None, "mp"),
            P("mp", "seq"),
            P("seq", None, "mp"),
            P("mp", "seq"),
            P("seq", "mp"),
            P("mp", "seq"),
            P("seq", "mp", None),
        ),
        check_vma=False,
    )
```
